32 devices in a mesh: pts: 8 (over z, x), cams: 4 (over y, core).
Axes of the slice: x: 2, y: 2, z: 4, core: 2. Of those that a mesh axis runs over, the one named last changes fastest.
Arguments:
- camera_jacobian: float32 [18, 131072], P(None, ('pts', 'cams')), may hold values from -3 to 3
- point_jacobian: float32 [6, 131072], P(None, ('pts', 'cams')), may hold values from -6 to 6
- residual: float32 [2, 131072], P(None, ('pts', 'cams')), may hold values from -6 to 6
- observed_slot: int32 [131072], P(('pts', 'cams')), may hold values from 0 to 1023, as said below
- observed_point: int32 [131072], P(('pts', 'cams')), may hold values from 0 to 4095, as said below
- send_list: int32 [32, 4, 256], P(('pts', 'cams')), may hold values from 0 to 8191, as said below
Outputs:
- camera_step: float32 [9, 32768], P(None, 'cams')
- point_step: float32 [3, 131072], P(None, ('pts', 'cams'))
The draws below stay inside these ranges and needn't reach their ends.
Inputs may be any that keep to these rules, and one draw needn't show every extreme that they name: `observed_slot`: an observation on device d = p * 4 + c with value s names entry s % 256 of send_list[p * 4 + s // 256, c]. In each such list only a leading run of entries is named, at least 64 long; for every device one list is named up to its last entry. `observed_point`: on every device both the first and the last of its 4096 points are observed. `send_list`: entry j of every list lies in the (j % 8)-th of 8 equal runs of an owner's 8192 cameras, that is, its value v has v // 1024 == j % 8.
All inputs are finite; a program needn't handle non-finite values.
Results may differ from the reference program's by a relative error of at most 0.0001.
Values sent between devices are 32-bit elements; how exact they have to be, the bound alone decides.
No kernel may reach another device: no remote copies, remote signals or barrier semaphores. Data moves between devices by JAX's collectives and lax.ppermute only.
A program may use at most 64 MiB of HBM per device.

```python
import jax
import jax.numpy as jnp

CP = 9
CAM_OWN = 8192
SLOT = 256
OBS_DEV = 4096
PT_DEV = 4096
ITERS = 3
NCAM = 32768
NPT = 131072
NOBS = 131072
N_PTS = 8
N_CAMS = 4


def draw_observed_slot(key, part):
    key = jax.random.fold_in(key, 11)
    devices = N_PTS * N_CAMS
    first, second, third, fourth = jax.random.split(key, 4)
    device = jnp.arange(devices, dtype=jnp.int32)
    home = (device % N_CAMS + 3 * (device // N_CAMS)) % N_CAMS
    counts = jax.random.randint(first, (devices, N_CAMS), SLOT // 4, SLOT)
    column = jnp.arange(N_CAMS, dtype=jnp.int32)[None, :]
    counts = jnp.where(column == home[:, None], SLOT, counts)
    homeward = jax.random.randint(second, (devices, OBS_DEV), 0, 2)
    elsewhere = jax.random.randint(third, (devices, OBS_DEV), 0, N_CAMS)
    owner = jnp.where(homeward == 1, home[:, None], elsewhere)
    limit = jnp.take_along_axis(counts, owner, axis=1)
    within = jax.random.randint(fourth, (devices, OBS_DEV), 0, 1 << 20) % limit
    slots = owner * SLOT + within
    slots = slots.at[:, 0].set(home * SLOT + SLOT - 1)
    slots = slots.at[:, 1].set(0)
    return slots.reshape(-1).astype(jnp.int32)


def draw_observed_point(key, part):
    key = jax.random.fold_in(key, 17)
    devices = N_PTS * N_CAMS
    local = jax.random.randint(key, (devices, OBS_DEV), 0, PT_DEV)
    local = local.at[:, 2].set(PT_DEV - 1)
    local = local.at[:, 3].set(0)
    return local.reshape(-1).astype(jnp.int32)


def draw_send_list(key, part):
    key = jax.random.fold_in(key, 23)
    share = CAM_OWN // N_PTS
    within = jax.random.randint(key, (N_PTS * N_CAMS, N_CAMS, SLOT), 0, share)
    column = jnp.arange(SLOT, dtype=jnp.int32) % N_PTS
    lists = column[None, None, :] * share + within
    lists = lists.at[0, 0, 0].set(0)
    lists = lists.at[0, 0, N_PTS - 1].set(CAM_OWN - 1)
    return lists.astype(jnp.int32)


def block_levels(stream_key, dims, cuts, low, largest):
    level = 1.0
    for axis_at, parts in cuts:
        draws = jax.random.uniform(jax.random.fold_in(jax.random.fold_in(stream_key, 6), axis_at), (parts,), jnp.float32, low / len(cuts), largest / len(cuts))
        level = level * jnp.repeat(jnp.exp(draws), dims[axis_at] // parts).reshape((-1,) + (1,) * (len(dims) - 1 - axis_at))
    return level


def centred(stream_key, shape, scale, most, shards=(), kind=jnp.bfloat16):
    result = scale * jax.random.normal(stream_key, shape, jnp.float32)
    if shards:
        result = result * block_levels(stream_key, shape, shards, -0.22, 0.18)
    return jnp.clip(result, -most, most).astype(kind)


def setup_inputs(seed: int = 0) -> dict:
    key_list = jax.random.split(jax.random.key(seed), 7)
    camera_jacobian = centred(key_list[0], (2 * CP, NOBS), (OBS_DEV * N_PTS // CAM_OWN) ** -0.5, 3.0, ((1, 32),), jnp.float32)
    point_jacobian = centred(key_list[1], (6, NOBS), 1.0, 6.0, ((1, 32),), jnp.float32)
    residual = centred(key_list[2], (2, NOBS), 1.0, 6.0, ((1, 32),), jnp.float32)
    observed_slot = draw_observed_slot(jax.random.fold_in(key_list[6], 71), 0)
    observed_point = draw_observed_point(jax.random.fold_in(key_list[6], 71), 0)
    send_list = draw_send_list(jax.random.fold_in(key_list[6], 71), 0)
    return dict(camera_jacobian=camera_jacobian, point_jacobian=point_jacobian, residual=residual, observed_slot=observed_slot, observed_point=observed_point, send_list=send_list)


damping_camera = 1.0
damping_point = 1.0


def spread(values, index, count):
    return jnp.zeros((values.shape[0], count), values.dtype).at[:, index].add(values)


def camera_apply(jacobian, gathered):
    return jnp.sum(jacobian.reshape(2, 9, -1) * gathered[None], axis=1)


def camera_transpose(jacobian, errors):
    return jnp.sum(jacobian.reshape(2, 9, -1) * errors[:, None], axis=0)


def point_apply(jacobian, values):
    return jnp.sum(jacobian.reshape(2, 3, -1) * values[None], axis=1)


def point_transpose(jacobian, errors):
    return jnp.sum(jacobian.reshape(2, 3, -1) * errors[:, None], axis=0)


def point_inverse(jacobian, points, count):
    blocks = jacobian.reshape(2, 3, -1)
    first, second, third = blocks[:, 0], blocks[:, 1], blocks[:, 2]
    outer = jnp.stack([first * first, first * second, first * third, second * second, second * third, third * third]).sum(axis=1)
    normal = spread(outer, points, count)
    top_left = normal[0] + damping_point
    top_mid = normal[1]
    top_right = normal[2]
    mid_mid = normal[3] + damping_point
    mid_right = normal[4]
    low_right = normal[5] + damping_point
    adjugate = jnp.stack([
        mid_mid * low_right - mid_right * mid_right,
        top_right * mid_right - top_mid * low_right,
        top_mid * mid_right - top_right * mid_mid,
        top_left * low_right - top_right * top_right,
        top_mid * top_right - top_left * mid_right,
        top_left * mid_mid - top_mid * top_mid])
    determinant = top_left * adjugate[0] + top_mid * adjugate[1] + top_right * adjugate[2]
    return adjugate / determinant[None]


def point_solve(inverse, values):
    first = inverse[0] * values[0] + inverse[1] * values[1] + inverse[2] * values[2]
    second = inverse[1] * values[0] + inverse[3] * values[1] + inverse[4] * values[2]
    third = inverse[2] * values[0] + inverse[4] * values[1] + inverse[5] * values[2]
    return jnp.stack([first, second, third])


def reference(camera_jacobian, point_jacobian, residual, observed_slot, observed_point, send_list):
    total = camera_jacobian.shape[1]
    device = jnp.arange(total, dtype=jnp.int32) // OBS_DEV
    owner = observed_slot // SLOT
    sender = (device // N_CAMS) * N_CAMS + owner
    local = send_list[sender, device % N_CAMS, observed_slot % SLOT]
    camera = (owner * CAM_OWN + local).astype(jnp.int32)
    point_index = (device * PT_DEV + observed_point).astype(jnp.int32)
    inverse = point_inverse(point_jacobian, point_index, NPT)

    def schur(direction):
        gathered = camera_apply(camera_jacobian, direction[:, camera])
        folded = point_solve(inverse, spread(point_transpose(point_jacobian, gathered), point_index, NPT))
        errors = gathered - point_apply(point_jacobian, folded[:, point_index])
        return spread(camera_transpose(camera_jacobian, errors), camera, NCAM) + damping_camera * direction

    point_gradient = spread(point_transpose(point_jacobian, residual), point_index, NPT)
    eliminated = point_solve(inverse, point_gradient)
    errors = residual - point_apply(point_jacobian, eliminated[:, point_index])
    right_side = -spread(camera_transpose(camera_jacobian, errors), camera, NCAM)
    blocks = camera_jacobian.reshape(2, 9, -1)
    squares = jnp.sum(blocks * blocks, axis=0)
    precondition = 1.0 / (spread(squares, camera, NCAM) + damping_camera)
    solution = jnp.zeros((9, NCAM), jnp.float32)
    remainder = right_side
    scaled = precondition * remainder
    direction = scaled
    product = jnp.sum(remainder * scaled)
    for iteration in range(ITERS):
        image = schur(direction)
        step_size = product / jnp.sum(direction * image)
        solution = solution + step_size * direction
        remainder = remainder - step_size * image
        scaled = precondition * remainder
        renewed = jnp.sum(remainder * scaled)
        direction = scaled + (renewed / product) * direction
        product = renewed
    gathered = camera_apply(camera_jacobian, solution[:, camera])
    point_step = -point_solve(inverse, point_gradient + spread(point_transpose(point_jacobian, gathered), point_index, NPT))
    return solution, point_step
```

```python
import functools

import jax
import jax.numpy as jnp
from jax import lax
from jax.experimental import pallas as pl
from jax.experimental.pallas import tpu as pltpu
from jax.sharding import PartitionSpec as P

CP = 9
CAM_OWN = 8192
PT_DEV = 4096
ITERS = 3
LANES = 128
SUB = 8
PT_LO = 256
PT_HI = PT_DEV // PT_LO
PT_ROWS = PT_DEV // LANES
PIECES = 3
VMEM_LIMIT = 40 * 1024 * 1024

damping_camera = 1.0
damping_point = 1.0

f32 = jnp.float32
bf16 = jnp.bfloat16


class Sizes:
    def __init__(self, pts, cams, slot, obs):
        self.pts, self.cams, self.slot, self.obs = pts, cams, slot, obs
        self.devices = pts * cams
        self.block = slot // pts
        assert cams * self.block == LANES and LANES % pts == 0
        self.rows = obs // LANES
        self.run = CAM_OWN // pts
        self.run_rows = self.run // LANES
        self.own_rows = max(SUB, self.run_rows)
        self.groups = -(-CP // cams)
        self.first_groups = -(-2 * CP // cams)
        self.message = 4
        self.first_message = 4 if self.first_groups < 4 else 8
        assert self.groups * cams > CP


def sub_iota(rows):
    return lax.broadcasted_iota(jnp.int32, (rows, LANES), 0)


def lane_iota(rows):
    return lax.broadcasted_iota(jnp.int32, (rows, LANES), 1)


def cut(value):
    parts = []
    for _ in range(PIECES - 1):
        part = value.astype(bf16).astype(f32)
        parts.append(part)
        value = value - part
    parts.append(value)
    return parts


def swap_blocks(rows, block, wanted):
    which = lane_iota(rows[0].shape[0]) // block
    result = []
    for q in range(wanted):
        total = None
        for c, value in enumerate(rows):
            shift = ((c - q) * block) % LANES
            moved = pltpu.roll(value, shift, axis=1) if shift else value
            total = jnp.where(which == c, moved, 0.0 if total is None else total)
        result.append(total)
    return result


def gather_rows(row, count, high, low, comps):
    result = [None] * comps
    for k in range(count):
        here = high == k
        for c in range(comps):
            source = jnp.broadcast_to(row(c, k), high.shape)
            found = jnp.take_along_axis(source, low, axis=1, mode="promise_in_bounds")
            result[c] = found if k == 0 else jnp.where(here, found, result[c])
    return result


def build(index, parts, high, low, high_count, low_count, spread_ref, place_ref):
    columns = pl.ds(pl.multiple_of(index * LANES, LANES), LANES)
    mask = jnp.broadcast_to(high, (high_count, LANES)) == sub_iota(high_count)
    together = max(1, 16 // high_count)
    for start in range(0, len(parts), together):
        pieces = [
            jnp.where(mask, jnp.broadcast_to(part, (high_count, LANES)), 0.0)
            for part in parts[start : start + together]
        ]
        while len(pieces) < together:
            pieces.append(jnp.zeros((high_count, LANES), f32))
        tile = pieces[0] if together == 1 else jnp.concatenate(pieces, axis=0)
        spread_ref[start * high_count : start * high_count + tile.shape[0], columns] = tile.astype(bf16)
    place = jnp.broadcast_to(low, (low_count, LANES)) == sub_iota(low_count)
    place_ref[:low_count, columns] = jnp.where(place, 1.0, 0.0).astype(bf16)


def spread_rows(parts, high_count):
    return -(-parts * high_count // 16) * 16


def scatter(parts, entries, high_count, low_count, spread_ref, place_ref):
    rows = spread_rows(parts, high_count)
    return lax.dot_general(
        spread_ref[:rows, :entries],
        place_ref[:low_count, :entries],
        (((1,), (1,)), ((), ())),
        preferred_element_type=f32,
    )


def joined(result, comp, high_count, pieces=PIECES):
    first = comp * pieces * high_count
    total = result[first + (pieces - 1) * high_count : first + pieces * high_count]
    for piece in reversed(range(pieces - 1)):
        total = total + result[first + piece * high_count : first + (piece + 1) * high_count]
    return total


def point_rows(value):
    return jnp.concatenate([value[:, :LANES], value[:, LANES:]], axis=0)


def point_place(point):
    high = point >> 8
    return high + ((point >> 7) & 1) * PT_HI, point & (LANES - 1), high, point & (PT_LO - 1)


def slot_place(slot, sizes):
    within = slot % sizes.slot
    return within % sizes.pts, (slot // sizes.slot) * sizes.block + within // sizes.pts


def solve(inverse, values):
    first = inverse[0] * values[0] + inverse[1] * values[1] + inverse[2] * values[2]
    second = inverse[1] * values[0] + inverse[3] * values[1] + inverse[4] * values[2]
    third = inverse[2] * values[0] + inverse[4] * values[1] + inverse[5] * values[2]
    return first, second, third


def write_messages(fields, scalar, groups, message, out_ref, sizes, extra=None):
    which = lane_iota(sizes.pts) // sizes.block
    for g in range(groups):
        rows = fields[g * sizes.cams : (g + 1) * sizes.cams]
        moved = swap_partial(rows, sizes)
        for c in range(sizes.cams):
            value = moved[c]
            if g == groups - 1 and scalar is not None:
                value = jnp.where(which == sizes.cams - 1, scalar, value)
            out_ref[pl.ds(c * message + g, sizes.pts, stride=sizes.cams * message), :] = value
    for g in range(groups, message):
        for c in range(sizes.cams):
            value = extra if (extra is not None and g == groups) else jnp.zeros((sizes.pts, LANES), f32)
            out_ref[pl.ds(c * message + g, sizes.pts, stride=sizes.cams * message), :] = value


def swap_partial(rows, sizes):
    return swap_blocks(rows, sizes.block, sizes.cams)


def read_row(in_ref, c, g, message, sizes):
    return in_ref[pl.ds(c * message + g, sizes.pts, stride=sizes.cams * message), :]


def read_messages(in_ref, count, message, sizes):
    fields = []
    group = 0
    while len(fields) < count:
        rows = [read_row(in_ref, c, group, message, sizes) for c in range(sizes.cams)]
        fields += swap_blocks(rows, sizes.block, min(sizes.cams, count - len(fields)))
        group += 1
    return fields


def read_scalar(in_ref, groups, message, sizes):
    total = read_row(in_ref, 0, groups - 1, message, sizes)
    for c in range(1, sizes.cams):
        total = total + read_row(in_ref, c, groups - 1, message, sizes)
    chosen = jnp.where(lane_iota(sizes.pts) == LANES - 1, total, 0.0)
    return jnp.sum(chosen, keepdims=True)


def setup_kernel(sizes, jac_ref, pjac_ref, res_ref, slot_ref, point_ref, list_ref,
                 out_ref, a_ref, b_ref, inv_ref, grad_ref,
                 r_ref, table_ref, spread_ref, place_ref):
    rows = sizes.rows
    for j in range(rows):
        columns = slice(j * LANES, (j + 1) * LANES)
        for start in range(0, 2 * CP, SUB):
            size = min(SUB, 2 * CP - start)
            a_ref[pl.ds(start * rows + j, size, stride=rows), :] = jac_ref[start : start + size, columns]
        b_ref[pl.ds(j, 6, stride=rows), :] = pjac_ref[:, columns]
        r_ref[pl.ds(j, 2, stride=rows), :] = res_ref[:, columns]

    def at(ref, comp, group):
        return ref[pl.ds(pl.multiple_of(comp * rows + group * SUB, SUB), SUB), :]

    def first(group, carry):
        b = [at(b_ref, k, group) for k in range(6)]
        r = [at(r_ref, k, group) for k in range(2)]
        point = point_ref[pl.ds(pl.multiple_of(group * SUB, SUB), SUB), :]
        _, _, high, low = point_place(point)
        values = [b[i] * b[j] + b[3 + i] * b[3 + j] for i, j in ((0, 0), (0, 1), (0, 2), (1, 1), (1, 2), (2, 2))]
        values += [b[i] * r[0] + b[3 + i] * r[1] for i in range(3)]
        parts = [part for value in values for part in cut(value)]
        for s in range(SUB):
            build(group * SUB + s, [part[s : s + 1] for part in parts], high[s : s + 1], low[s : s + 1],
                  PT_HI, PT_LO, spread_ref, place_ref)
        return carry

    lax.fori_loop(0, rows // SUB, first, 0)
    result = scatter(9 * PIECES, sizes.obs, PT_HI, PT_LO, spread_ref, place_ref)
    normal = [point_rows(joined(result, k, PT_HI)) for k in range(9)]
    top_left = normal[0] + damping_point
    top_mid = normal[1]
    top_right = normal[2]
    mid_mid = normal[3] + damping_point
    mid_right = normal[4]
    low_right = normal[5] + damping_point
    adjugate = [
        mid_mid * low_right - mid_right * mid_right,
        top_right * mid_right - top_mid * low_right,
        top_mid * mid_right - top_right * mid_mid,
        top_left * low_right - top_right * top_right,
        top_mid * top_right - top_left * mid_right,
        top_left * mid_mid - top_mid * top_mid,
    ]
    determinant = top_left * adjugate[0] + top_mid * adjugate[1] + top_right * adjugate[2]
    inverse = [value / determinant for value in adjugate]
    for k in range(6):
        inv_ref[k] = inverse[k]
    for k in range(3):
        grad_ref[k] = normal[6 + k]
    eliminated = solve(inverse, normal[6:])
    for k in range(3):
        table_ref[k] = eliminated[k]

    def second(group, carry):
        point = point_ref[pl.ds(pl.multiple_of(group * SUB, SUB), SUB), :]
        high, low, _, _ = point_place(point)
        at_point = gather_rows(lambda c, k: table_ref[c, k : k + 1, :], PT_ROWS, high, low, 3)
        b = [at(b_ref, k, group) for k in range(6)]
        errors = [at(r_ref, i, group) - sum(b[3 * i + k] * at_point[k] for k in range(3)) for i in range(2)]
        a = [at(a_ref, k, group) for k in range(2 * CP)]
        values = [a[k] * errors[0] + a[CP + k] * errors[1] for k in range(CP)]
        values += [a[k] * a[k] + a[CP + k] * a[CP + k] for k in range(CP)]
        parts = [part for value in values for part in cut(value)]
        high, low = slot_place(slot_ref[pl.ds(pl.multiple_of(group * SUB, SUB), SUB), :], sizes)
        for s in range(SUB):
            build(group * SUB + s, [part[s : s + 1] for part in parts], high[s : s + 1], low[s : s + 1],
                  sizes.pts, LANES, spread_ref, place_ref)
        return carry

    lax.fori_loop(0, rows // SUB, second, 0)
    result = scatter(2 * CP * PIECES, sizes.obs, sizes.pts, LANES, spread_ref, place_ref)
    fields = [joined(result, k, sizes.pts) for k in range(2 * CP)]

    pieces = sizes.slot // LANES
    lane = lane_iota(1)
    for c in range(sizes.cams):
        for half in range(pieces):
            value = list_ref[c : c + 1, half * LANES : (half + 1) * LANES]
            low = c * sizes.block + half * (LANES // sizes.pts) + lane // sizes.pts
            build(c * pieces + half, [(value >> 8).astype(f32), (value & 255).astype(f32)], lane % sizes.pts, low,
                  sizes.pts, LANES, spread_ref, place_ref)
    result = scatter(2, sizes.cams * sizes.slot, sizes.pts, LANES, spread_ref, place_ref)
    listed = result[: sizes.pts] * 256.0 + result[sizes.pts : 2 * sizes.pts]
    write_messages(fields, None, sizes.first_groups, sizes.first_message, out_ref, sizes, extra=listed)


def entries_scatter(fields, entry, sizes, spread_ref, place_ref):
    high, low = entry // LANES, entry % LANES
    parts = [part for value in fields for part in cut(value)]
    for p in range(sizes.pts):
        build(p, [part[p : p + 1] for part in parts], high[p : p + 1], low[p : p + 1],
              sizes.own_rows, LANES, spread_ref, place_ref)
    result = scatter(len(parts), sizes.pts * LANES, sizes.own_rows, LANES, spread_ref, place_ref)
    return [joined(result, k, sizes.own_rows) for k in range(len(fields))]


def send_owned(scaled, partial, entry, out_ref, table_ref, sizes):
    for k in range(CP):
        table_ref[k] = scaled[k]
    fields = gather_rows(lambda c, k: table_ref[c, k : k + 1, :], sizes.run_rows, entry // LANES, entry % LANES, CP)
    write_messages(fields, partial, sizes.groups, sizes.message, out_ref, sizes)


def dot_fields(left, right):
    return jnp.sum(sum(a * b for a, b in zip(left, right)), keepdims=True)


def first_owner_kernel(sizes, column_ref, in_ref, out_ref, entry_ref, pre_ref, rem_ref,
                       table_ref, spread_ref, place_ref):
    listed = jnp.zeros((sizes.pts, LANES), f32)
    for c in range(sizes.cams):
        row = read_row(in_ref, c, sizes.first_groups, sizes.first_message, sizes)
        listed = jnp.where(column_ref[0] == c, row, listed)
    entry = listed.astype(jnp.int32) % sizes.run
    entry_ref[...] = entry
    fields = read_messages(in_ref, 2 * CP, sizes.first_message, sizes)
    sums = entries_scatter(fields, entry, sizes, spread_ref, place_ref)
    remainder = [-value for value in sums[:CP]]
    precondition = [1.0 / (value + damping_camera) for value in sums[CP:]]
    scaled = [p * r for p, r in zip(precondition, remainder)]
    for k in range(CP):
        pre_ref[k] = precondition[k]
        rem_ref[k] = remainder[k]
    send_owned(scaled, dot_fields(remainder, scaled), entry, out_ref, table_ref, sizes)


def owner_kernel(sizes, start, in_ref, entry_ref, pre_ref, rem_ref, dir_ref, product_ref, *refs):
    if start:
        out_ref, new_rem_ref, new_sol_ref, step_ref, table_ref, spread_ref, place_ref = refs
    else:
        sol_ref, out_ref, new_rem_ref, new_sol_ref, step_ref, table_ref, spread_ref, place_ref = refs
    entry = entry_ref[...]
    fields = read_messages(in_ref, CP, sizes.message, sizes)
    curvature = read_scalar(in_ref, sizes.groups, sizes.message, sizes)
    step = product_ref[...] / jnp.broadcast_to(curvature, (SUB, LANES))
    step_ref[...] = step
    sums = entries_scatter(fields, entry, sizes, spread_ref, place_ref)
    remainder, scaled = [], []
    for k in range(CP):
        direction = dir_ref[k]
        moved = step[:1] * direction
        new_sol_ref[k] = moved if start else sol_ref[k] + moved
        value = rem_ref[k] - step[:1] * (sums[k] + damping_camera * direction)
        new_rem_ref[k] = value
        remainder.append(value)
        scaled.append(pre_ref[k] * value)
    send_owned(scaled, dot_fields(remainder, scaled), entry, out_ref, table_ref, sizes)


def schur_kernel(sizes, start, last, in_ref, a_ref, b_ref, inv_ref, slot_ref, point_ref, pre_ref, rem_ref, grad_ref, *refs):
    refs = list(refs)
    if not start:
        product_ref, at_slot_ref, dir_ref, step_ref, sum_ref = refs[:5]
        refs = refs[5:]
    out_ref, new_product_ref, new_at_slot_ref, new_dir_ref, new_sum_ref = refs[:5]
    new_grad_ref = None
    refs = refs[5:]
    if not start:
        new_grad_ref = refs.pop(0)
    q_ref, table_ref, spread_ref, place_ref = refs
    rows = sizes.rows

    def at(ref, comp, group):
        return ref[pl.ds(pl.multiple_of(comp * rows + group * SUB, SUB), SUB), :]

    def index(ref, group):
        return ref[pl.ds(pl.multiple_of(group * SUB, SUB), SUB), :]

    renewed = jnp.broadcast_to(read_scalar(in_ref, sizes.groups, sizes.message, sizes), (SUB, LANES))
    new_product_ref[...] = renewed
    fields = read_messages(in_ref, CP, sizes.message, sizes)
    beta = None if start else (renewed / product_ref[...])[:1]
    squares = None
    for k in range(CP):
        direction = pre_ref[k] * rem_ref[k]
        if start:
            new_at_slot_ref[k] = fields[k]
        else:
            new_at_slot_ref[k] = fields[k] + beta * at_slot_ref[k]
            direction = direction + beta * dir_ref[k]
        new_dir_ref[k] = direction
        squares = direction * direction if squares is None else squares + direction * direction

    def first(group, carry):
        high, low = slot_place(index(slot_ref, group), sizes)
        gathered = gather_rows(lambda c, k: new_at_slot_ref[c, k : k + 1, :], sizes.pts, high, low, CP)
        q = [sum(at(a_ref, i * CP + k, group) * gathered[k] for k in range(CP)) for i in range(2)]
        for i in range(2):
            q_ref[pl.ds(pl.multiple_of(i * rows + group * SUB, SUB), SUB), :] = q[i]
        values = [at(b_ref, k, group) * q[0] + at(b_ref, 3 + k, group) * q[1] for k in range(3)]
        parts = [part for value in values for part in cut(value)]
        _, _, high, low = point_place(index(point_ref, group))
        for s in range(SUB):
            build(group * SUB + s, [part[s : s + 1] for part in parts], high[s : s + 1], low[s : s + 1],
                  PT_HI, PT_LO, spread_ref, place_ref)
        return carry

    lax.fori_loop(0, rows // SUB, first, 0)
    result = scatter(3 * PIECES, sizes.obs, PT_HI, PT_LO, spread_ref, place_ref)
    sums = [point_rows(joined(result, k, PT_HI)) for k in range(3)]
    folded = solve([inv_ref[k] for k in range(6)], sums)
    for k in range(3):
        table_ref[k] = folded[k]
        new_sum_ref[k] = sums[k]
        if not start:
            new_grad_ref[k] = grad_ref[k] + step_ref[:1, :] * sum_ref[k]

    def second(group, inner):
        high, low, _, _ = point_place(index(point_ref, group))
        at_point = gather_rows(lambda c, k: table_ref[c, k : k + 1, :], PT_ROWS, high, low, 3)
        q = [at(q_ref, i, group) for i in range(2)]
        errors = [q[i] - sum(at(b_ref, 3 * i + k, group) * at_point[k] for k in range(3)) for i in range(2)]
        inner = inner + q[0] * errors[0] + q[1] * errors[1]
        if not last:
            values = [at(a_ref, k, group) * errors[0] + at(a_ref, CP + k, group) * errors[1] for k in range(CP)]
            parts = [part for value in values for part in cut(value)]
            high, low = slot_place(index(slot_ref, group), sizes)
            for s in range(SUB):
                build(group * SUB + s, [part[s : s + 1] for part in parts], high[s : s + 1], low[s : s + 1],
                      sizes.pts, LANES, spread_ref, place_ref)
        return inner

    inner = lax.fori_loop(0, rows // SUB, second, jnp.zeros((SUB, LANES), f32))
    partial = jnp.sum(inner, keepdims=True) + damping_camera * jnp.sum(squares, keepdims=True)
    if last:
        out_ref[...] = jnp.broadcast_to(partial, (sizes.devices, LANES))
        return
    result = scatter(CP * PIECES, sizes.obs, sizes.pts, LANES, spread_ref, place_ref)
    fields = [joined(result, k, sizes.pts) for k in range(CP)]
    write_messages(fields, partial, sizes.groups, sizes.message, out_ref, sizes)


def final_kernel(sizes, in_ref, product_ref, all_ref, inv_ref, grad_ref, sum_ref, cam_ref, pt_ref, table_ref):
    curvature = jnp.sum(jnp.where(lane_iota(sizes.devices) == 0, in_ref[...], 0.0), keepdims=True)
    step = (product_ref[...] / jnp.broadcast_to(curvature, (SUB, LANES)))[:1]
    per = 2 * CP * sizes.own_rows
    for r in range(sizes.pts):
        for h in range(sizes.run_rows):
            columns = slice((r * sizes.run_rows + h) * LANES, (r * sizes.run_rows + h + 1) * LANES)
            for start in range(0, CP, SUB):
                size = min(SUB, CP - start)
                first = r * per + start * sizes.own_rows + h
                base = all_ref[pl.ds(first, size, stride=sizes.own_rows), :]
                direction = all_ref[pl.ds(first + CP * sizes.own_rows, size, stride=sizes.own_rows), :]
                cam_ref[start : start + size, columns] = base + step * direction
    total = [grad_ref[k] + step * sum_ref[k] for k in range(3)]
    solved = solve([inv_ref[k] for k in range(6)], total)
    for k in range(3):
        table_ref[k * PT_ROWS : (k + 1) * PT_ROWS, :] = -solved[k]
    for row in range(PT_ROWS):
        half, high = row // PT_HI, row % PT_HI
        chunk = high * (PT_LO // LANES) + half
        pt_ref[:, chunk * LANES : (chunk + 1) * LANES] = table_ref[pl.ds(row, 3, stride=PT_ROWS), :]


def shape(*dims, dtype=f32):
    return jax.ShapeDtypeStruct(dims, dtype)


def call(kernel, name, inputs, outputs, scratch, scalars=()):
    vmem = pl.BlockSpec(memory_space=pltpu.VMEM)
    smem = pl.BlockSpec(memory_space=pltpu.SMEM)
    return pl.pallas_call(
        kernel,
        name=name,
        out_shape=outputs,
        in_specs=[smem] * len(scalars) + [vmem] * len(inputs),
        out_specs=[vmem] * len(outputs),
        scratch_shapes=scratch,
        compiler_params=pltpu.CompilerParams(vmem_limit_bytes=VMEM_LIMIT),
    )(*scalars, *inputs)


def body(camera_jacobian, point_jacobian, residual, observed_slot, observed_point, send_list):
    sizes = Sizes(lax.axis_size("pts"), lax.axis_size("cams"), send_list.shape[2], camera_jacobian.shape[1])
    axes = ("pts", "cams")
    rows = sizes.rows
    slot = observed_slot.reshape(rows, LANES)
    point = observed_point.reshape(rows, LANES)
    column = lax.axis_index("cams").astype(jnp.int32).reshape(1)

    def exchange(messages):
        return lax.all_to_all(messages, axes, split_axis=0, concat_axis=0, tiled=True)

    def factors(high_rows, low_rows, entries):
        return [pltpu.VMEM((high_rows, entries), bf16), pltpu.VMEM((low_rows, entries), bf16)]

    point_table = shape(3, PT_ROWS, LANES)
    owned = shape(CP, sizes.own_rows, LANES)
    messages = shape(sizes.devices * sizes.message, LANES)
    scalar = shape(SUB, LANES)
    owned_scratch = pltpu.VMEM((CP, sizes.own_rows, LANES), f32)
    point_scratch = pltpu.VMEM((3, PT_ROWS, LANES), f32)
    entries = sizes.pts * LANES

    first, a, b, inverse, gradient = call(
        functools.partial(setup_kernel, sizes),
        "setup",
        [camera_jacobian, point_jacobian, residual, slot, point, send_list[0]],
        [
            shape(sizes.devices * sizes.first_message, LANES),
            shape(2 * CP * rows, LANES),
            shape(6 * rows, LANES),
            shape(6, PT_ROWS, LANES),
            point_table,
        ],
        [pltpu.VMEM((2 * rows, LANES), f32), point_scratch]
        + factors(max(spread_rows(9 * PIECES, PT_HI), spread_rows(2 * CP * PIECES, sizes.pts)), PT_LO, sizes.obs),
    )
    out, entry, precondition, remainder = call(
        functools.partial(first_owner_kernel, sizes),
        "first_owner",
        [exchange(first)],
        [messages, shape(sizes.pts, LANES, dtype=jnp.int32), owned, owned],
        [owned_scratch] + factors(spread_rows(2 * CP * PIECES, sizes.own_rows), LANES, entries),
        scalars=[column],
    )
    schur_scratch = [pltpu.VMEM((2 * rows, LANES), f32), point_scratch] + factors(
        max(spread_rows(3 * PIECES, PT_HI), spread_rows(CP * PIECES, sizes.pts)), PT_LO, sizes.obs
    )
    at_slot = shape(CP, sizes.pts, LANES)
    product = slots = direction = step = sums = solution_ = None
    for iteration in range(ITERS):
        start, last = iteration == 0, iteration == ITERS - 1
        earlier = [] if start else [product, slots, direction, step, sums]
        results = call(
            functools.partial(schur_kernel, sizes, start, last),
            "schur_last" if last else "schur",
            [exchange(out), a, b, inverse, slot, point, precondition, remainder, gradient] + earlier,
            [shape(sizes.devices, LANES) if last else messages, scalar, at_slot, owned, point_table]
            + ([] if start else [point_table]),
            schur_scratch,
        )
        out, product, slots, direction, sums = results[:5]
        if not start:
            gradient = results[5]
        if last:
            break
        out, remainder, solution_, step = call(
            functools.partial(owner_kernel, sizes, start),
            "owner",
            [exchange(out), entry, precondition, remainder, direction, product] + ([] if start else [solution_]),
            [messages, owned, owned, scalar],
            [owned_scratch] + factors(spread_rows(CP * PIECES, sizes.own_rows), LANES, entries),
        )
    both = jnp.concatenate([solution_, direction]).reshape(2 * CP * sizes.own_rows, LANES)
    gathered = lax.all_gather(both, "pts", axis=0, tiled=True)
    return call(
        functools.partial(final_kernel, sizes),
        "final",
        [exchange(out), product, gathered, inverse, gradient, sums],
        [shape(CP, CAM_OWN), shape(3, PT_DEV)],
        [pltpu.VMEM((3 * PT_ROWS, LANES), f32)],
    )


def solution(mesh):
    return jax.shard_map(
        lambda *arguments: tuple(body(*arguments)),
        mesh=mesh,
        in_specs=(
            P(None, ("pts", "cams")),
            P(None, ("pts", "cams")),
            P(None, ("pts", "cams")),
            P(("pts", "cams")),
            P(("pts", "cams")),
            P(("pts", "cams"), None, None),
        ),
        out_specs=(P(None, "cams"), P(None, ("pts", "cams"))),
        check_vma=False,
    )
```

```python
import functools

import jax
import jax.numpy as jnp
from jax import lax
from jax.experimental import pallas as pl
from jax.experimental.pallas import tpu as pltpu
from jax.sharding import PartitionSpec as P

CP = 9
CAM_OWN = 8192
PT_DEV = 4096
ITERS = 3
LANES = 128
SUB = 8
PT_LO = 256
PT_HI = PT_DEV // PT_LO
PT_ROWS = PT_DEV // LANES
PIECES = 3
VMEM_LIMIT = 40 * 1024 * 1024

damping_camera = 1.0
damping_point = 1.0

f32 = jnp.float32
bf16 = jnp.bfloat16


class Sizes:
    def __init__(self, pts, cams, slot, obs):
        self.pts, self.cams, self.slot, self.obs = pts, cams, slot, obs
        self.devices = pts * cams
        self.block = slot // pts
        assert cams * self.block == LANES and LANES % pts == 0
        self.rows = obs // LANES
        self.run = CAM_OWN // pts
        self.run_rows = self.run // LANES
        self.own_rows = max(SUB, self.run_rows)
        self.groups = -(-CP // cams)
        self.first_groups = -(-2 * CP // cams)
        self.message = self.groups
        self.first_message = self.first_groups + 1
        assert self.groups * cams > CP


def sub_iota(rows):
    return lax.broadcasted_iota(jnp.int32, (rows, LANES), 0)


def lane_iota(rows):
    return lax.broadcasted_iota(jnp.int32, (rows, LANES), 1)


def cut(value):
    parts = []
    for _ in range(PIECES - 1):
        part = value.astype(bf16).astype(f32)
        parts.append(part)
        value = value - part
    parts.append(value)
    return parts


def swap_blocks(rows, block, wanted):
    which = lane_iota(rows[0].shape[0]) // block
    result = []
    for q in range(wanted):
        total = None
        for c, value in enumerate(rows):
            shift = ((c - q) * block) % LANES
            moved = pltpu.roll(value, shift, axis=1) if shift else value
            total = jnp.where(which == c, moved, 0.0 if total is None else total)
        result.append(total)
    return result


def gather_rows(row, count, high, low, comps):
    result = [None] * comps
    for k in range(count):
        here = high == k
        for c in range(comps):
            source = jnp.broadcast_to(row(c, k), high.shape)
            found = jnp.take_along_axis(source, low, axis=1, mode="promise_in_bounds")
            result[c] = found if k == 0 else jnp.where(here, found, result[c])
    return result


def build(index, parts, high, low, high_count, low_count, spread_ref, place_ref):
    columns = pl.ds(pl.multiple_of(index * LANES, LANES), LANES)
    mask = jnp.broadcast_to(high, (high_count, LANES)) == sub_iota(high_count)
    together = max(1, 16 // high_count)
    for start in range(0, len(parts), together):
        pieces = [
            jnp.where(mask, jnp.broadcast_to(part, (high_count, LANES)), 0.0)
            for part in parts[start : start + together]
        ]
        while len(pieces) < together:
            pieces.append(jnp.zeros((high_count, LANES), f32))
        tile = pieces[0] if together == 1 else jnp.concatenate(pieces, axis=0)
        spread_ref[start * high_count : start * high_count + tile.shape[0], columns] = tile.astype(bf16)
    place = jnp.broadcast_to(low, (low_count, LANES)) == sub_iota(low_count)
    place_ref[:low_count, columns] = jnp.where(place, 1.0, 0.0).astype(bf16)


def spread_rows(parts, high_count):
    return -(-parts * high_count // 16) * 16


def scatter(parts, entries, high_count, low_count, spread_ref, place_ref):
    rows = spread_rows(parts, high_count)
    return lax.dot_general(
        spread_ref[:rows, :entries],
        place_ref[:low_count, :entries],
        (((1,), (1,)), ((), ())),
        preferred_element_type=f32,
    )


def joined(result, comp, high_count, pieces=PIECES):
    first = comp * pieces * high_count
    total = result[first + (pieces - 1) * high_count : first + pieces * high_count]
    for piece in reversed(range(pieces - 1)):
        total = total + result[first + piece * high_count : first + (piece + 1) * high_count]
    return total


def point_rows(value):
    return jnp.concatenate([value[:, :LANES], value[:, LANES:]], axis=0)


def point_place(point):
    high = point >> 8
    return high + ((point >> 7) & 1) * PT_HI, point & (LANES - 1), high, point & (PT_LO - 1)


def slot_place(slot, sizes):
    within = slot % sizes.slot
    return within % sizes.pts, (slot // sizes.slot) * sizes.block + within // sizes.pts


def solve(inverse, values):
    first = inverse[0] * values[0] + inverse[1] * values[1] + inverse[2] * values[2]
    second = inverse[1] * values[0] + inverse[3] * values[1] + inverse[4] * values[2]
    third = inverse[2] * values[0] + inverse[4] * values[1] + inverse[5] * values[2]
    return first, second, third


def write_messages(fields, scalar, groups, message, out_ref, sizes, extra=None):
    which = lane_iota(sizes.pts) // sizes.block
    for g in range(groups):
        rows = fields[g * sizes.cams : (g + 1) * sizes.cams]
        moved = swap_partial(rows, sizes)
        for c in range(sizes.cams):
            value = moved[c]
            if g == groups - 1 and scalar is not None:
                value = jnp.where(which == sizes.cams - 1, scalar, value)
            out_ref[pl.ds(c * message + g, sizes.pts, stride=sizes.cams * message), :] = value
    for g in range(groups, message):
        for c in range(sizes.cams):
            value = extra if (extra is not None and g == groups) else jnp.zeros((sizes.pts, LANES), f32)
            out_ref[pl.ds(c * message + g, sizes.pts, stride=sizes.cams * message), :] = value


def swap_partial(rows, sizes):
    return swap_blocks(rows, sizes.block, sizes.cams)


def read_row(in_ref, c, g, message, sizes):
    return in_ref[pl.ds(c * message + g, sizes.pts, stride=sizes.cams * message), :]


def read_messages(in_ref, count, message, sizes):
    fields = []
    group = 0
    while len(fields) < count:
        rows = [read_row(in_ref, c, group, message, sizes) for c in range(sizes.cams)]
        fields += swap_blocks(rows, sizes.block, min(sizes.cams, count - len(fields)))
        group += 1
    return fields


def read_scalar(in_ref, groups, message, sizes):
    total = read_row(in_ref, 0, groups - 1, message, sizes)
    for c in range(1, sizes.cams):
        total = total + read_row(in_ref, c, groups - 1, message, sizes)
    chosen = jnp.where(lane_iota(sizes.pts) == LANES - 1, total, 0.0)
    return jnp.sum(chosen, keepdims=True)


def setup_kernel(sizes, *refs):
    sources, refs = refs[:6], refs[6:]
    out_ref, a_ref, b_ref, inv_ref, grad_ref = refs[:5]
    r_ref, table_ref, spread_ref, place_ref = refs[5:9]
    jac_ref, pjac_ref, res_ref, slot_ref, point_ref, list_ref = refs[9:15]
    semaphores = refs[15]
    rows = sizes.rows
    copies = [pltpu.make_async_copy(source, target, semaphores.at[k]) for k, (source, target) in enumerate(zip(sources, refs[9:15]))]
    for copy in copies:
        copy.start()
    for copy in copies:
        copy.wait()
    for j in range(rows):
        columns = slice(j * LANES, (j + 1) * LANES)
        for start in range(0, 2 * CP, SUB):
            size = min(SUB, 2 * CP - start)
            a_ref[pl.ds(start * rows + j, size, stride=rows), :] = jac_ref[start : start + size, columns]
        b_ref[pl.ds(j, 6, stride=rows), :] = pjac_ref[:, columns]
        r_ref[pl.ds(j, 2, stride=rows), :] = res_ref[:, columns]

    def at(ref, comp, group):
        return ref[pl.ds(pl.multiple_of(comp * rows + group * SUB, SUB), SUB), :]

    def first(group, carry):
        b = [at(b_ref, k, group) for k in range(6)]
        r = [at(r_ref, k, group) for k in range(2)]
        point = point_ref[pl.ds(pl.multiple_of(group * SUB, SUB), SUB), :]
        _, _, high, low = point_place(point)
        values = [b[i] * b[j] + b[3 + i] * b[3 + j] for i, j in ((0, 0), (0, 1), (0, 2), (1, 1), (1, 2), (2, 2))]
        values += [b[i] * r[0] + b[3 + i] * r[1] for i in range(3)]
        parts = [part for value in values for part in cut(value)]
        for s in range(SUB):
            build(group * SUB + s, [part[s : s + 1] for part in parts], high[s : s + 1], low[s : s + 1],
                  PT_HI, PT_LO, spread_ref, place_ref)
        return carry

    lax.fori_loop(0, rows // SUB, first, 0)
    result = scatter(9 * PIECES, sizes.obs, PT_HI, PT_LO, spread_ref, place_ref)
    normal = [point_rows(joined(result, k, PT_HI)) for k in range(9)]
    top_left = normal[0] + damping_point
    top_mid = normal[1]
    top_right = normal[2]
    mid_mid = normal[3] + damping_point
    mid_right = normal[4]
    low_right = normal[5] + damping_point
    adjugate = [
        mid_mid * low_right - mid_right * mid_right,
        top_right * mid_right - top_mid * low_right,
        top_mid * mid_right - top_right * mid_mid,
        top_left * low_right - top_right * top_right,
        top_mid * top_right - top_left * mid_right,
        top_left * mid_mid - top_mid * top_mid,
    ]
    determinant = top_left * adjugate[0] + top_mid * adjugate[1] + top_right * adjugate[2]
    inverse = [value / determinant for value in adjugate]
    for k in range(6):
        inv_ref[k] = inverse[k]
    for k in range(3):
        grad_ref[k] = normal[6 + k]
    eliminated = solve(inverse, normal[6:])
    for k in range(3):
        table_ref[k] = eliminated[k]

    def second(group, carry):
        point = point_ref[pl.ds(pl.multiple_of(group * SUB, SUB), SUB), :]
        high, low, _, _ = point_place(point)
        at_point = gather_rows(lambda c, k: table_ref[c, k : k + 1, :], PT_ROWS, high, low, 3)
        b = [at(b_ref, k, group) for k in range(6)]
        errors = [at(r_ref, i, group) - sum(b[3 * i + k] * at_point[k] for k in range(3)) for i in range(2)]
        a = [at(a_ref, k, group) for k in range(2 * CP)]
        values = [a[k] * errors[0] + a[CP + k] * errors[1] for k in range(CP)]
        values += [a[k] * a[k] + a[CP + k] * a[CP + k] for k in range(CP)]
        parts = [part for value in values for part in cut(value)]
        high, low = slot_place(slot_ref[pl.ds(pl.multiple_of(group * SUB, SUB), SUB), :], sizes)
        for s in range(SUB):
            build(group * SUB + s, [part[s : s + 1] for part in parts], high[s : s + 1], low[s : s + 1],
                  sizes.pts, LANES, spread_ref, place_ref)
        return carry

    lax.fori_loop(0, rows // SUB, second, 0)
    result = scatter(2 * CP * PIECES, sizes.obs, sizes.pts, LANES, spread_ref, place_ref)
    fields = [joined(result, k, sizes.pts) for k in range(2 * CP)]

    pieces = sizes.slot // LANES
    lane = lane_iota(1)
    for c in range(sizes.cams):
        for half in range(pieces):
            value = list_ref[c : c + 1, half * LANES : (half + 1) * LANES]
            low = c * sizes.block + half * (LANES // sizes.pts) + lane // sizes.pts
            build(c * pieces + half, [(value >> 8).astype(f32), (value & 255).astype(f32)], lane % sizes.pts, low,
                  sizes.pts, LANES, spread_ref, place_ref)
    result = scatter(2, sizes.cams * sizes.slot, sizes.pts, LANES, spread_ref, place_ref)
    listed = result[: sizes.pts] * 256.0 + result[sizes.pts : 2 * sizes.pts]
    write_messages(fields, None, sizes.first_groups, sizes.first_message, out_ref, sizes, extra=listed)


def entries_scatter(fields, entry, sizes, spread_ref, place_ref):
    high, low = entry // LANES, entry % LANES
    parts = [part for value in fields for part in cut(value)]
    for p in range(sizes.pts):
        build(p, [part[p : p + 1] for part in parts], high[p : p + 1], low[p : p + 1],
              sizes.own_rows, LANES, spread_ref, place_ref)
    result = scatter(len(parts), sizes.pts * LANES, sizes.own_rows, LANES, spread_ref, place_ref)
    return [joined(result, k, sizes.own_rows) for k in range(len(fields))]


def send_owned(scaled, partial, entry, out_ref, table_ref, sizes):
    for k in range(CP):
        table_ref[k] = scaled[k]
    fields = gather_rows(lambda c, k: table_ref[c, k : k + 1, :], sizes.run_rows, entry // LANES, entry % LANES, CP)
    write_messages(fields, partial, sizes.groups, sizes.message, out_ref, sizes)


def dot_fields(left, right):
    return jnp.sum(sum(a * b for a, b in zip(left, right)), keepdims=True)


def first_owner_kernel(sizes, column_ref, in_ref, out_ref, entry_ref, pre_ref, rem_ref,
                       table_ref, spread_ref, place_ref):
    listed = jnp.zeros((sizes.pts, LANES), f32)
    for c in range(sizes.cams):
        row = read_row(in_ref, c, sizes.first_groups, sizes.first_message, sizes)
        listed = jnp.where(column_ref[0] == c, row, listed)
    entry = listed.astype(jnp.int32) % sizes.run
    entry_ref[...] = entry
    fields = read_messages(in_ref, 2 * CP, sizes.first_message, sizes)
    sums = entries_scatter(fields, entry, sizes, spread_ref, place_ref)
    remainder = [-value for value in sums[:CP]]
    precondition = [1.0 / (value + damping_camera) for value in sums[CP:]]
    scaled = [p * r for p, r in zip(precondition, remainder)]
    for k in range(CP):
        pre_ref[k] = precondition[k]
        rem_ref[k] = remainder[k]
    send_owned(scaled, dot_fields(remainder, scaled), entry, out_ref, table_ref, sizes)


def owner_kernel(sizes, start, in_ref, entry_ref, pre_ref, rem_ref, dir_ref, product_ref, *refs):
    if start:
        out_ref, new_rem_ref, new_sol_ref, step_ref, table_ref, spread_ref, place_ref = refs
    else:
        sol_ref, out_ref, new_rem_ref, new_sol_ref, step_ref, table_ref, spread_ref, place_ref = refs
    entry = entry_ref[...]
    fields = read_messages(in_ref, CP, sizes.message, sizes)
    curvature = read_scalar(in_ref, sizes.groups, sizes.message, sizes)
    step = product_ref[...] / jnp.broadcast_to(curvature, (SUB, LANES))
    step_ref[...] = step
    sums = entries_scatter(fields, entry, sizes, spread_ref, place_ref)
    remainder, scaled = [], []
    for k in range(CP):
        direction = dir_ref[k]
        moved = step[:1] * direction
        new_sol_ref[k] = moved if start else sol_ref[k] + moved
        value = rem_ref[k] - step[:1] * (sums[k] + damping_camera * direction)
        new_rem_ref[k] = value
        remainder.append(value)
        scaled.append(pre_ref[k] * value)
    send_owned(scaled, dot_fields(remainder, scaled), entry, out_ref, table_ref, sizes)


def schur_kernel(sizes, start, last, in_ref, a_ref, b_ref, inv_ref, slot_ref, point_ref, pre_ref, rem_ref, grad_ref, *refs):
    refs = list(refs)
    if not start:
        product_ref, at_slot_ref, dir_ref, step_ref, sum_ref = refs[:5]
        refs = refs[5:]
    out_ref, new_product_ref, new_at_slot_ref, new_dir_ref, new_sum_ref = refs[:5]
    new_grad_ref = None
    refs = refs[5:]
    if not start:
        new_grad_ref = refs.pop(0)
    q_ref, table_ref, spread_ref, place_ref = refs
    rows = sizes.rows

    def at(ref, comp, group):
        return ref[pl.ds(pl.multiple_of(comp * rows + group * SUB, SUB), SUB), :]

    def index(ref, group):
        return ref[pl.ds(pl.multiple_of(group * SUB, SUB), SUB), :]

    renewed = jnp.broadcast_to(read_scalar(in_ref, sizes.groups, sizes.message, sizes), (SUB, LANES))
    new_product_ref[...] = renewed
    fields = read_messages(in_ref, CP, sizes.message, sizes)
    beta = None if start else (renewed / product_ref[...])[:1]
    squares = None
    for k in range(CP):
        direction = pre_ref[k] * rem_ref[k]
        if start:
            new_at_slot_ref[k] = fields[k]
        else:
            new_at_slot_ref[k] = fields[k] + beta * at_slot_ref[k]
            direction = direction + beta * dir_ref[k]
        new_dir_ref[k] = direction
        squares = direction * direction if squares is None else squares + direction * direction

    def first(group, carry):
        high, low = slot_place(index(slot_ref, group), sizes)
        gathered = gather_rows(lambda c, k: new_at_slot_ref[c, k : k + 1, :], sizes.pts, high, low, CP)
        q = [sum(at(a_ref, i * CP + k, group) * gathered[k] for k in range(CP)) for i in range(2)]
        for i in range(2):
            q_ref[pl.ds(pl.multiple_of(i * rows + group * SUB, SUB), SUB), :] = q[i]
        values = [at(b_ref, k, group) * q[0] + at(b_ref, 3 + k, group) * q[1] for k in range(3)]
        parts = [part for value in values for part in cut(value)]
        _, _, high, low = point_place(index(point_ref, group))
        for s in range(SUB):
            build(group * SUB + s, [part[s : s + 1] for part in parts], high[s : s + 1], low[s : s + 1],
                  PT_HI, PT_LO, spread_ref, place_ref)
        return carry

    lax.fori_loop(0, rows // SUB, first, 0)
    result = scatter(3 * PIECES, sizes.obs, PT_HI, PT_LO, spread_ref, place_ref)
    sums = [point_rows(joined(result, k, PT_HI)) for k in range(3)]
    folded = solve([inv_ref[k] for k in range(6)], sums)
    for k in range(3):
        table_ref[k] = folded[k]
        new_sum_ref[k] = sums[k]
        if not start:
            new_grad_ref[k] = grad_ref[k] + step_ref[:1, :] * sum_ref[k]

    def second(group, inner):
        high, low, _, _ = point_place(index(point_ref, group))
        at_point = gather_rows(lambda c, k: table_ref[c, k : k + 1, :], PT_ROWS, high, low, 3)
        q = [at(q_ref, i, group) for i in range(2)]
        errors = [q[i] - sum(at(b_ref, 3 * i + k, group) * at_point[k] for k in range(3)) for i in range(2)]
        inner = inner + q[0] * errors[0] + q[1] * errors[1]
        if not last:
            values = [at(a_ref, k, group) * errors[0] + at(a_ref, CP + k, group) * errors[1] for k in range(CP)]
            parts = [part for value in values for part in cut(value)]
            high, low = slot_place(index(slot_ref, group), sizes)
            for s in range(SUB):
                build(group * SUB + s, [part[s : s + 1] for part in parts], high[s : s + 1], low[s : s + 1],
                      sizes.pts, LANES, spread_ref, place_ref)
        return inner

    inner = lax.fori_loop(0, rows // SUB, second, jnp.zeros((SUB, LANES), f32))
    partial = jnp.sum(inner, keepdims=True) + damping_camera * jnp.sum(squares, keepdims=True)
    if last:
        out_ref[...] = jnp.broadcast_to(partial, (sizes.devices, LANES))
        return
    result = scatter(CP * PIECES, sizes.obs, sizes.pts, LANES, spread_ref, place_ref)
    fields = [joined(result, k, sizes.pts) for k in range(CP)]
    write_messages(fields, partial, sizes.groups, sizes.message, out_ref, sizes)


def tail_kernel(sizes, in_ref, pre_ref, rem_ref, dir_ref, product_ref, sol_ref, out_ref):
    renewed = jnp.broadcast_to(read_scalar(in_ref, sizes.groups, sizes.message, sizes), (SUB, LANES))
    beta = (renewed / product_ref[...])[:1]
    for k in range(CP):
        direction = pre_ref[k] * rem_ref[k] + beta * dir_ref[k]
        for p in range(sizes.pts):
            first = (p * 2 * CP + k) * sizes.own_rows
            out_ref[first : first + sizes.own_rows, :] = sol_ref[k]
            first += CP * sizes.own_rows
            out_ref[first : first + sizes.own_rows, :] = direction


def final_kernel(sizes, in_ref, product_ref, all_ref, inv_ref, grad_ref, sum_ref, cam_ref, pt_ref, table_ref):
    curvature = jnp.sum(jnp.where(lane_iota(sizes.devices) == 0, in_ref[...], 0.0), keepdims=True)
    step = (product_ref[...] / jnp.broadcast_to(curvature, (SUB, LANES)))[:1]
    per = 2 * CP * sizes.own_rows
    for r in range(sizes.pts):
        for h in range(sizes.run_rows):
            columns = slice((r * sizes.run_rows + h) * LANES, (r * sizes.run_rows + h + 1) * LANES)
            for start in range(0, CP, SUB):
                size = min(SUB, CP - start)
                first = r * per + start * sizes.own_rows + h
                base = all_ref[pl.ds(first, size, stride=sizes.own_rows), :]
                direction = all_ref[pl.ds(first + CP * sizes.own_rows, size, stride=sizes.own_rows), :]
                cam_ref[start : start + size, columns] = base + step * direction
    total = [grad_ref[k] + step * sum_ref[k] for k in range(3)]
    solved = solve([inv_ref[k] for k in range(6)], total)
    for k in range(3):
        table_ref[k * PT_ROWS : (k + 1) * PT_ROWS, :] = -solved[k]
    for row in range(PT_ROWS):
        half, high = row // PT_HI, row % PT_HI
        chunk = high * (PT_LO // LANES) + half
        pt_ref[:, chunk * LANES : (chunk + 1) * LANES] = table_ref[pl.ds(row, 3, stride=PT_ROWS), :]


def shape(*dims, dtype=f32):
    return jax.ShapeDtypeStruct(dims, dtype)


def call(kernel, name, inputs, outputs, scratch, scalars=(), inputs_at=pltpu.VMEM, cost=None):
    vmem = pl.BlockSpec(memory_space=pltpu.VMEM)
    given = pl.BlockSpec(memory_space=inputs_at)
    smem = pl.BlockSpec(memory_space=pltpu.SMEM)
    return pl.pallas_call(
        kernel,
        name=name,
        out_shape=outputs,
        in_specs=[smem] * len(scalars) + [given] * len(inputs),
        out_specs=[vmem] * len(outputs),
        scratch_shapes=scratch,
        cost_estimate=cost,
        compiler_params=pltpu.CompilerParams(vmem_limit_bytes=VMEM_LIMIT),
    )(*scalars, *inputs)


def body(camera_jacobian, point_jacobian, residual, observed_slot, observed_point, send_list):
    sizes = Sizes(lax.axis_size("pts"), lax.axis_size("cams"), send_list.shape[2], camera_jacobian.shape[1])
    axes = ("pts", "cams")
    rows = sizes.rows
    slot = observed_slot.reshape(rows, LANES)
    point = observed_point.reshape(rows, LANES)
    column = lax.axis_index("cams").astype(jnp.int32).reshape(1)

    def exchange(messages):
        width = messages.size // sizes.devices
        flat = messages.reshape(sizes.devices, 1, width)
        return lax.all_to_all(flat, axes, split_axis=0, concat_axis=0, tiled=True).reshape(messages.shape)

    def factors(high_rows, low_rows, entries):
        return [pltpu.VMEM((high_rows, entries), bf16), pltpu.VMEM((low_rows, entries), bf16)]

    point_table = shape(3, PT_ROWS, LANES)
    owned = shape(CP, sizes.own_rows, LANES)
    messages = shape(sizes.devices * sizes.message, LANES)
    scalar = shape(SUB, LANES)
    owned_scratch = pltpu.VMEM((CP, sizes.own_rows, LANES), f32)
    point_scratch = pltpu.VMEM((3, PT_ROWS, LANES), f32)
    entries = sizes.pts * LANES

    given = [camera_jacobian, point_jacobian, residual, slot, point, send_list[0]]
    first, a, b, inverse, gradient = call(
        functools.partial(setup_kernel, sizes),
        "setup",
        given,
        [
            shape(sizes.devices * sizes.first_message, LANES),
            shape(2 * CP * rows, LANES),
            shape(6 * rows, LANES),
            shape(6, PT_ROWS, LANES),
            point_table,
        ],
        [pltpu.VMEM((2 * rows, LANES), f32), point_scratch]
        + factors(max(spread_rows(9 * PIECES, PT_HI), spread_rows(2 * CP * PIECES, sizes.pts)), PT_LO, sizes.obs)
        + [pltpu.VMEM(value.shape, value.dtype) for value in given]
        + [pltpu.SemaphoreType.DMA((len(given),))],
        inputs_at=pltpu.HBM,
    )
    out, entry, precondition, remainder = call(
        functools.partial(first_owner_kernel, sizes),
        "first_owner",
        [exchange(first)],
        [messages, shape(sizes.pts, LANES, dtype=jnp.int32), owned, owned],
        [owned_scratch] + factors(spread_rows(2 * CP * PIECES, sizes.own_rows), LANES, entries),
        scalars=[column],
    )
    schur_scratch = [pltpu.VMEM((2 * rows, LANES), f32), point_scratch] + factors(
        max(spread_rows(3 * PIECES, PT_HI), spread_rows(CP * PIECES, sizes.pts)), PT_LO, sizes.obs
    )
    at_slot = shape(CP, sizes.pts, LANES)
    product = slots = direction = step = sums = solution_ = None
    for iteration in range(ITERS):
        start, last = iteration == 0, iteration == ITERS - 1
        earlier = [] if start else [product, slots, direction, step, sums]
        arrived = exchange(out)
        if last:
            (both,) = call(
                functools.partial(tail_kernel, sizes),
                "tail",
                [arrived, precondition, remainder, direction, product, solution_],
                [shape(sizes.pts * 2 * CP * sizes.own_rows, LANES)],
                [],
            )
            gathered = lax.all_to_all(
                both.reshape(sizes.pts, -1, LANES), "pts", split_axis=0, concat_axis=0, tiled=True
            ).reshape(both.shape)
        results = call(
            functools.partial(schur_kernel, sizes, start, last),
            "schur_last" if last else "schur",
            [arrived, a, b, inverse, slot, point, precondition, remainder, gradient] + earlier,
            [shape(sizes.devices, LANES) if last else messages, scalar, at_slot, owned, point_table]
            + ([] if start else [point_table]),
            schur_scratch,
            cost=pl.CostEstimate(flops=2_000_000_000, bytes_accessed=10_000_000, transcendentals=0),
        )
        out, product, slots, direction, sums = results[:5]
        if not start:
            gradient = results[5]
        if last:
            break
        out, remainder, solution_, step = call(
            functools.partial(owner_kernel, sizes, start),
            "owner",
            [exchange(out), entry, precondition, remainder, direction, product] + ([] if start else [solution_]),
            [messages, owned, owned, scalar],
            [owned_scratch] + factors(spread_rows(CP * PIECES, sizes.own_rows), LANES, entries),
        )
    return call(
        functools.partial(final_kernel, sizes),
        "final",
        [exchange(out), product, gathered, inverse, gradient, sums],
        [shape(CP, CAM_OWN), shape(3, PT_DEV)],
        [pltpu.VMEM((3 * PT_ROWS, LANES), f32)],
    )


def solution(mesh):
    return jax.shard_map(
        lambda *arguments: tuple(body(*arguments)),
        mesh=mesh,
        in_specs=(
            P(None, ("pts", "cams")),
            P(None, ("pts", "cams")),
            P(None, ("pts", "cams")),
            P(("pts", "cams")),
            P(("pts", "cams")),
            P(("pts", "cams"), None, None),
        ),
        out_specs=(P(None, "cams"), P(None, ("pts", "cams"))),
        check_vma=False,
    )
```

```python
import functools

import jax
import jax.numpy as jnp
from jax import lax
from jax.experimental import pallas as pl
from jax.experimental.pallas import tpu as pltpu
from jax.sharding import PartitionSpec as P

CP = 9
CAM_OWN = 8192
PT_DEV = 4096
ITERS = 3
LANES = 128
SUB = 8
PT_LO = 256
PT_HI = PT_DEV // PT_LO
PT_ROWS = PT_DEV // LANES
PIECES = 3
VMEM_LIMIT = 40 * 1024 * 1024

damping_camera = 1.0
damping_point = 1.0

f32 = jnp.float32
bf16 = jnp.bfloat16


class Sizes:
    def __init__(self, pts, cams, slot, obs):
        self.pts, self.cams, self.slot, self.obs = pts, cams, slot, obs
        self.devices = pts * cams
        self.block = slot // pts
        assert cams * self.block == LANES and LANES % pts == 0
        self.rows = obs // LANES
        self.run = CAM_OWN // pts
        self.run_rows = self.run // LANES
        self.own_rows = max(SUB, self.run_rows)
        self.groups = -(-CP // cams)
        self.first_groups = -(-2 * CP // cams)
        self.message = self.groups
        self.first_message = self.first_groups + 1
        assert self.groups * cams > CP


def sub_iota(rows):
    return lax.broadcasted_iota(jnp.int32, (rows, LANES), 0)


def lane_iota(rows):
    return lax.broadcasted_iota(jnp.int32, (rows, LANES), 1)


def cut(value):
    parts = []
    for _ in range(PIECES - 1):
        part = value.astype(bf16).astype(f32)
        parts.append(part)
        value = value - part
    parts.append(value)
    return parts


def swap_blocks(rows, block, wanted):
    which = lane_iota(rows[0].shape[0]) // block
    result = []
    for q in range(wanted):
        total = None
        for c, value in enumerate(rows):
            shift = ((c - q) * block) % LANES
            moved = pltpu.roll(value, shift, axis=1) if shift else value
            total = jnp.where(which == c, moved, 0.0 if total is None else total)
        result.append(total)
    return result


def gather_rows(row, count, high, low, comps):
    result = [None] * comps
    for k in range(count):
        here = high == k
        for c in range(comps):
            source = jnp.broadcast_to(row(c, k), high.shape)
            found = jnp.take_along_axis(source, low, axis=1, mode="promise_in_bounds")
            result[c] = found if k == 0 else jnp.where(here, found, result[c])
    return result


def build(index, parts, high, low, high_count, low_count, spread_ref, place_ref):
    columns = pl.ds(pl.multiple_of(index * LANES, LANES), LANES)
    mask = jnp.broadcast_to(high, (high_count, LANES)) == sub_iota(high_count)
    together = max(1, 16 // high_count)
    for start in range(0, len(parts), together):
        pieces = [
            jnp.where(mask, jnp.broadcast_to(part, (high_count, LANES)), 0.0)
            for part in parts[start : start + together]
        ]
        while len(pieces) < together:
            pieces.append(jnp.zeros((high_count, LANES), f32))
        tile = pieces[0] if together == 1 else jnp.concatenate(pieces, axis=0)
        spread_ref[start * high_count : start * high_count + tile.shape[0], columns] = tile.astype(bf16)
    place = jnp.broadcast_to(low, (low_count, LANES)) == sub_iota(low_count)
    place_ref[:low_count, columns] = jnp.where(place, 1.0, 0.0).astype(bf16)


def spread_rows(parts, high_count):
    return -(-parts * high_count // 16) * 16


def scatter(parts, entries, high_count, low_count, spread_ref, place_ref):
    rows = spread_rows(parts, high_count)
    return lax.dot_general(
        spread_ref[:rows, :entries],
        place_ref[:low_count, :entries],
        (((1,), (1,)), ((), ())),
        preferred_element_type=f32,
    )


def joined(result, comp, high_count, pieces=PIECES):
    first = comp * pieces * high_count
    total = result[first + (pieces - 1) * high_count : first + pieces * high_count]
    for piece in reversed(range(pieces - 1)):
        total = total + result[first + piece * high_count : first + (piece + 1) * high_count]
    return total


def point_rows(value):
    return jnp.concatenate([value[:, :LANES], value[:, LANES:]], axis=0)


def point_place(point):
    high = point >> 8
    return high + ((point >> 7) & 1) * PT_HI, point & (LANES - 1), high, point & (PT_LO - 1)


def slot_place(slot, sizes):
    within = slot % sizes.slot
    return within % sizes.pts, (slot // sizes.slot) * sizes.block + within // sizes.pts


def solve(inverse, values):
    first = inverse[0] * values[0] + inverse[1] * values[1] + inverse[2] * values[2]
    second = inverse[1] * values[0] + inverse[3] * values[1] + inverse[4] * values[2]
    third = inverse[2] * values[0] + inverse[4] * values[1] + inverse[5] * values[2]
    return first, second, third


def write_messages(fields, scalar, groups, message, out_ref, sizes, extra=None):
    which = lane_iota(sizes.pts) // sizes.block
    for g in range(groups):
        rows = fields[g * sizes.cams : (g + 1) * sizes.cams]
        moved = swap_partial(rows, sizes)
        for c in range(sizes.cams):
            value = moved[c]
            if g == groups - 1 and scalar is not None:
                value = jnp.where(which == sizes.cams - 1, scalar, value)
            out_ref[pl.ds(c * message + g, sizes.pts, stride=sizes.cams * message), :] = value
    for g in range(groups, message):
        for c in range(sizes.cams):
            value = extra if (extra is not None and g == groups) else jnp.zeros((sizes.pts, LANES), f32)
            out_ref[pl.ds(c * message + g, sizes.pts, stride=sizes.cams * message), :] = value


def swap_partial(rows, sizes):
    return swap_blocks(rows, sizes.block, sizes.cams)


def read_row(in_ref, c, g, message, sizes):
    return in_ref[pl.ds(c * message + g, sizes.pts, stride=sizes.cams * message), :]


def read_messages(in_ref, count, message, sizes):
    fields = []
    group = 0
    while len(fields) < count:
        rows = [read_row(in_ref, c, group, message, sizes) for c in range(sizes.cams)]
        fields += swap_blocks(rows, sizes.block, min(sizes.cams, count - len(fields)))
        group += 1
    return fields


def read_scalar(in_ref, groups, message, sizes):
    total = read_row(in_ref, 0, groups - 1, message, sizes)
    for c in range(1, sizes.cams):
        total = total + read_row(in_ref, c, groups - 1, message, sizes)
    chosen = jnp.where(lane_iota(sizes.pts) == LANES - 1, total, 0.0)
    return jnp.sum(chosen, keepdims=True)


def setup_kernel(sizes, *refs):
    sources, refs = refs[:6], refs[6:]
    out_ref, a_ref, b_ref, inv_ref, grad_ref = refs[:5]
    r_ref, table_ref, spread_ref, place_ref = refs[5:9]
    jac_ref, pjac_ref, res_ref, slot_ref, point_ref, list_ref = refs[9:15]
    semaphores = refs[15]
    rows = sizes.rows
    copies = [pltpu.make_async_copy(source, target, semaphores.at[k]) for k, (source, target) in enumerate(zip(sources, refs[9:15]))]
    for copy in copies:
        copy.start()
    for copy in copies:
        copy.wait()
    for j in range(rows):
        columns = slice(j * LANES, (j + 1) * LANES)
        for start in range(0, 2 * CP, SUB):
            size = min(SUB, 2 * CP - start)
            a_ref[pl.ds(start * rows + j, size, stride=rows), :] = jac_ref[start : start + size, columns]
        b_ref[pl.ds(j, 6, stride=rows), :] = pjac_ref[:, columns]
        r_ref[pl.ds(j, 2, stride=rows), :] = res_ref[:, columns]

    def at(ref, comp, group):
        return ref[pl.ds(pl.multiple_of(comp * rows + group * SUB, SUB), SUB), :]

    def first(group, carry):
        b = [at(b_ref, k, group) for k in range(6)]
        r = [at(r_ref, k, group) for k in range(2)]
        point = point_ref[pl.ds(pl.multiple_of(group * SUB, SUB), SUB), :]
        _, _, high, low = point_place(point)
        values = [b[i] * b[j] + b[3 + i] * b[3 + j] for i, j in ((0, 0), (0, 1), (0, 2), (1, 1), (1, 2), (2, 2))]
        values += [b[i] * r[0] + b[3 + i] * r[1] for i in range(3)]
        parts = [part for value in values for part in cut(value)]
        for s in range(SUB):
            build(group * SUB + s, [part[s : s + 1] for part in parts], high[s : s + 1], low[s : s + 1],
                  PT_HI, PT_LO, spread_ref, place_ref)
        return carry

    lax.fori_loop(0, rows // SUB, first, 0)
    result = scatter(9 * PIECES, sizes.obs, PT_HI, PT_LO, spread_ref, place_ref)
    normal = [point_rows(joined(result, k, PT_HI)) for k in range(9)]
    top_left = normal[0] + damping_point
    top_mid = normal[1]
    top_right = normal[2]
    mid_mid = normal[3] + damping_point
    mid_right = normal[4]
    low_right = normal[5] + damping_point
    adjugate = [
        mid_mid * low_right - mid_right * mid_right,
        top_right * mid_right - top_mid * low_right,
        top_mid * mid_right - top_right * mid_mid,
        top_left * low_right - top_right * top_right,
        top_mid * top_right - top_left * mid_right,
        top_left * mid_mid - top_mid * top_mid,
    ]
    determinant = top_left * adjugate[0] + top_mid * adjugate[1] + top_right * adjugate[2]
    inverse = [value / determinant for value in adjugate]
    for k in range(6):
        inv_ref[k] = inverse[k]
    for k in range(3):
        grad_ref[k] = normal[6 + k]
    eliminated = solve(inverse, normal[6:])
    for k in range(3):
        table_ref[k] = eliminated[k]

    def second(group, carry):
        point = point_ref[pl.ds(pl.multiple_of(group * SUB, SUB), SUB), :]
        high, low, _, _ = point_place(point)
        at_point = gather_rows(lambda c, k: table_ref[c, k : k + 1, :], PT_ROWS, high, low, 3)
        b = [at(b_ref, k, group) for k in range(6)]
        errors = [at(r_ref, i, group) - sum(b[3 * i + k] * at_point[k] for k in range(3)) for i in range(2)]
        a = [at(a_ref, k, group) for k in range(2 * CP)]
        values = [a[k] * errors[0] + a[CP + k] * errors[1] for k in range(CP)]
        values += [a[k] * a[k] + a[CP + k] * a[CP + k] for k in range(CP)]
        parts = [part for value in values for part in cut(value)]
        high, low = slot_place(slot_ref[pl.ds(pl.multiple_of(group * SUB, SUB), SUB), :], sizes)
        for s in range(SUB):
            build(group * SUB + s, [part[s : s + 1] for part in parts], high[s : s + 1], low[s : s + 1],
                  sizes.pts, LANES, spread_ref, place_ref)
        return carry

    lax.fori_loop(0, rows // SUB, second, 0)
    result = scatter(2 * CP * PIECES, sizes.obs, sizes.pts, LANES, spread_ref, place_ref)
    fields = [joined(result, k, sizes.pts) for k in range(2 * CP)]

    pieces = sizes.slot // LANES
    lane = lane_iota(1)
    for c in range(sizes.cams):
        for half in range(pieces):
            value = list_ref[c : c + 1, half * LANES : (half + 1) * LANES]
            low = c * sizes.block + half * (LANES // sizes.pts) + lane // sizes.pts
            build(c * pieces + half, [(value >> 8).astype(f32), (value & 255).astype(f32)], lane % sizes.pts, low,
                  sizes.pts, LANES, spread_ref, place_ref)
    result = scatter(2, sizes.cams * sizes.slot, sizes.pts, LANES, spread_ref, place_ref)
    listed = result[: sizes.pts] * 256.0 + result[sizes.pts : 2 * sizes.pts]
    write_messages(fields, None, sizes.first_groups, sizes.first_message, out_ref, sizes, extra=listed)


def entries_scatter(fields, entry, sizes, spread_ref, place_ref):
    high, low = entry // LANES, entry % LANES
    parts = [part for value in fields for part in cut(value)]
    for p in range(sizes.pts):
        build(p, [part[p : p + 1] for part in parts], high[p : p + 1], low[p : p + 1],
              sizes.own_rows, LANES, spread_ref, place_ref)
    result = scatter(len(parts), sizes.pts * LANES, sizes.own_rows, LANES, spread_ref, place_ref)
    return [joined(result, k, sizes.own_rows) for k in range(len(fields))]


def send_owned(scaled, partial, entry, out_ref, table_ref, sizes):
    for k in range(CP):
        table_ref[k] = scaled[k]
    fields = gather_rows(lambda c, k: table_ref[c, k : k + 1, :], sizes.run_rows, entry // LANES, entry % LANES, CP)
    write_messages(fields, partial, sizes.groups, sizes.message, out_ref, sizes)


def dot_fields(left, right):
    return jnp.sum(sum(a * b for a, b in zip(left, right)), keepdims=True)


def first_owner_kernel(sizes, column_ref, in_ref, out_ref, entry_ref, pre_ref, rem_ref,
                       table_ref, spread_ref, place_ref):
    listed = jnp.zeros((sizes.pts, LANES), f32)
    for c in range(sizes.cams):
        row = read_row(in_ref, c, sizes.first_groups, sizes.first_message, sizes)
        listed = jnp.where(column_ref[0] == c, row, listed)
    entry = listed.astype(jnp.int32) % sizes.run
    entry_ref[...] = entry
    fields = read_messages(in_ref, 2 * CP, sizes.first_message, sizes)
    sums = entries_scatter(fields, entry, sizes, spread_ref, place_ref)
    remainder = [-value for value in sums[:CP]]
    precondition = [1.0 / (value + damping_camera) for value in sums[CP:]]
    scaled = [p * r for p, r in zip(precondition, remainder)]
    for k in range(CP):
        pre_ref[k] = precondition[k]
        rem_ref[k] = remainder[k]
    send_owned(scaled, dot_fields(remainder, scaled), entry, out_ref, table_ref, sizes)


def owner_kernel(sizes, start, in_ref, entry_ref, pre_ref, rem_ref, dir_ref, product_ref, *refs):
    if start:
        out_ref, new_rem_ref, new_sol_ref, step_ref, table_ref, spread_ref, place_ref = refs
    else:
        sol_ref, out_ref, new_rem_ref, new_sol_ref, step_ref, table_ref, spread_ref, place_ref = refs
    entry = entry_ref[...]
    fields = read_messages(in_ref, CP, sizes.message, sizes)
    curvature = read_scalar(in_ref, sizes.groups, sizes.message, sizes)
    step = product_ref[...] / jnp.broadcast_to(curvature, (SUB, LANES))
    step_ref[...] = step
    sums = entries_scatter(fields, entry, sizes, spread_ref, place_ref)
    remainder, scaled = [], []
    for k in range(CP):
        direction = dir_ref[k]
        moved = step[:1] * direction
        new_sol_ref[k] = moved if start else sol_ref[k] + moved
        value = rem_ref[k] - step[:1] * (sums[k] + damping_camera * direction)
        new_rem_ref[k] = value
        remainder.append(value)
        scaled.append(pre_ref[k] * value)
    send_owned(scaled, dot_fields(remainder, scaled), entry, out_ref, table_ref, sizes)


def schur_kernel(sizes, start, last, in_ref, a_ref, b_ref, inv_ref, slot_ref, point_ref, pre_ref, rem_ref, grad_ref, *refs):
    refs = list(refs)
    if not start:
        product_ref, at_slot_ref, dir_ref, step_ref, sum_ref = refs[:5]
        refs = refs[5:]
    out_ref, new_product_ref, new_at_slot_ref, new_dir_ref, new_sum_ref = refs[:5]
    new_grad_ref = None
    refs = refs[5:]
    if not start:
        new_grad_ref = refs.pop(0)
    q_ref, table_ref, spread_ref, place_ref = refs
    rows = sizes.rows

    def at(ref, comp, group):
        return ref[pl.ds(pl.multiple_of(comp * rows + group * SUB, SUB), SUB), :]

    def index(ref, group):
        return ref[pl.ds(pl.multiple_of(group * SUB, SUB), SUB), :]

    renewed = jnp.broadcast_to(read_scalar(in_ref, sizes.groups, sizes.message, sizes), (SUB, LANES))
    new_product_ref[...] = renewed
    fields = read_messages(in_ref, CP, sizes.message, sizes)
    beta = None if start else (renewed / product_ref[...])[:1]
    squares = None
    for k in range(CP):
        direction = pre_ref[k] * rem_ref[k]
        if start:
            new_at_slot_ref[k] = fields[k]
        else:
            new_at_slot_ref[k] = fields[k] + beta * at_slot_ref[k]
            direction = direction + beta * dir_ref[k]
        new_dir_ref[k] = direction
        squares = direction * direction if squares is None else squares + direction * direction

    def first(group, carry):
        high, low = slot_place(index(slot_ref, group), sizes)
        gathered = gather_rows(lambda c, k: new_at_slot_ref[c, k : k + 1, :], sizes.pts, high, low, CP)
        q = [sum(at(a_ref, i * CP + k, group) * gathered[k] for k in range(CP)) for i in range(2)]
        for i in range(2):
            q_ref[pl.ds(pl.multiple_of(i * rows + group * SUB, SUB), SUB), :] = q[i]
        values = [at(b_ref, k, group) * q[0] + at(b_ref, 3 + k, group) * q[1] for k in range(3)]
        parts = [part for value in values for part in cut(value)]
        _, _, high, low = point_place(index(point_ref, group))
        for s in range(SUB):
            build(group * SUB + s, [part[s : s + 1] for part in parts], high[s : s + 1], low[s : s + 1],
                  PT_HI, PT_LO, spread_ref, place_ref)
        return carry

    lax.fori_loop(0, rows // SUB, first, 0)
    result = scatter(3 * PIECES, sizes.obs, PT_HI, PT_LO, spread_ref, place_ref)
    sums = [point_rows(joined(result, k, PT_HI)) for k in range(3)]
    folded = solve([inv_ref[k] for k in range(6)], sums)
    for k in range(3):
        table_ref[k] = folded[k]
        new_sum_ref[k] = sums[k]
        if not start:
            new_grad_ref[k] = grad_ref[k] + step_ref[:1, :] * sum_ref[k]

    def second(group, inner):
        high, low, _, _ = point_place(index(point_ref, group))
        at_point = gather_rows(lambda c, k: table_ref[c, k : k + 1, :], PT_ROWS, high, low, 3)
        q = [at(q_ref, i, group) for i in range(2)]
        errors = [q[i] - sum(at(b_ref, 3 * i + k, group) * at_point[k] for k in range(3)) for i in range(2)]
        inner = inner + q[0] * errors[0] + q[1] * errors[1]
        if not last:
            values = [at(a_ref, k, group) * errors[0] + at(a_ref, CP + k, group) * errors[1] for k in range(CP)]
            parts = [part for value in values for part in cut(value)]
            high, low = slot_place(index(slot_ref, group), sizes)
            for s in range(SUB):
                build(group * SUB + s, [part[s : s + 1] for part in parts], high[s : s + 1], low[s : s + 1],
                      sizes.pts, LANES, spread_ref, place_ref)
        return inner

    inner = lax.fori_loop(0, rows // SUB, second, jnp.zeros((SUB, LANES), f32))
    partial = jnp.sum(inner, keepdims=True) + damping_camera * jnp.sum(squares, keepdims=True)
    if last:
        out_ref[...] = jnp.broadcast_to(partial, (sizes.devices, LANES))
        return
    result = scatter(CP * PIECES, sizes.obs, sizes.pts, LANES, spread_ref, place_ref)
    fields = [joined(result, k, sizes.pts) for k in range(CP)]
    write_messages(fields, partial, sizes.groups, sizes.message, out_ref, sizes)


def tail_kernel(sizes, in_ref, pre_ref, rem_ref, dir_ref, product_ref, sol_ref, out_ref):
    renewed = jnp.broadcast_to(read_scalar(in_ref, sizes.groups, sizes.message, sizes), (SUB, LANES))
    beta = (renewed / product_ref[...])[:1]
    for k in range(CP):
        direction = pre_ref[k] * rem_ref[k] + beta * dir_ref[k]
        first = k * sizes.own_rows
        out_ref[first : first + sizes.own_rows, :] = sol_ref[k]
        first += CP * sizes.own_rows
        out_ref[first : first + sizes.own_rows, :] = direction


def final_kernel(sizes, run_ref, in_ref, product_ref, inv_ref, grad_ref, sum_ref, *refs):
    all_refs = refs[: sizes.pts]
    cam_ref, pt_ref, table_ref = refs[sizes.pts :]
    curvature = jnp.sum(jnp.where(lane_iota(sizes.devices) == 0, in_ref[...], 0.0), keepdims=True)
    step = (product_ref[...] / jnp.broadcast_to(curvature, (SUB, LANES)))[:1]
    for k, all_ref in enumerate(all_refs):
        base_column = (run_ref[0] ^ k) * sizes.run
        for h in range(sizes.run_rows):
            columns = pl.ds(pl.multiple_of(base_column + h * LANES, LANES), LANES)
            for start in range(0, CP, SUB):
                size = min(SUB, CP - start)
                first = start * sizes.own_rows + h
                base = all_ref[pl.ds(first, size, stride=sizes.own_rows), :]
                direction = all_ref[pl.ds(first + CP * sizes.own_rows, size, stride=sizes.own_rows), :]
                cam_ref[start : start + size, columns] = base + step * direction
    total = [grad_ref[k] + step * sum_ref[k] for k in range(3)]
    solved = solve([inv_ref[k] for k in range(6)], total)
    for k in range(3):
        table_ref[k * PT_ROWS : (k + 1) * PT_ROWS, :] = -solved[k]
    for row in range(PT_ROWS):
        half, high = row // PT_HI, row % PT_HI
        chunk = high * (PT_LO // LANES) + half
        pt_ref[:, chunk * LANES : (chunk + 1) * LANES] = table_ref[pl.ds(row, 3, stride=PT_ROWS), :]


def shape(*dims, dtype=f32):
    return jax.ShapeDtypeStruct(dims, dtype)


def call(kernel, name, inputs, outputs, scratch, scalars=(), inputs_at=pltpu.VMEM, cost=None):
    vmem = pl.BlockSpec(memory_space=pltpu.VMEM)
    given = pl.BlockSpec(memory_space=inputs_at)
    smem = pl.BlockSpec(memory_space=pltpu.SMEM)
    return pl.pallas_call(
        kernel,
        name=name,
        out_shape=outputs,
        in_specs=[smem] * len(scalars) + [given] * len(inputs),
        out_specs=[vmem] * len(outputs),
        scratch_shapes=scratch,
        cost_estimate=cost,
        compiler_params=pltpu.CompilerParams(vmem_limit_bytes=VMEM_LIMIT),
    )(*scalars, *inputs)


def body(camera_jacobian, point_jacobian, residual, observed_slot, observed_point, send_list):
    sizes = Sizes(lax.axis_size("pts"), lax.axis_size("cams"), send_list.shape[2], camera_jacobian.shape[1])
    axes = ("pts", "cams")
    rows = sizes.rows
    slot = observed_slot.reshape(rows, LANES)
    point = observed_point.reshape(rows, LANES)
    column = lax.axis_index("cams").astype(jnp.int32).reshape(1)

    def exchange(messages):
        width = messages.size // sizes.devices
        flat = messages.reshape(sizes.devices, 1, width)
        return lax.all_to_all(flat, axes, split_axis=0, concat_axis=0, tiled=True).reshape(messages.shape)

    def factors(high_rows, low_rows, entries):
        return [pltpu.VMEM((high_rows, entries), bf16), pltpu.VMEM((low_rows, entries), bf16)]

    point_table = shape(3, PT_ROWS, LANES)
    owned = shape(CP, sizes.own_rows, LANES)
    messages = shape(sizes.devices * sizes.message, LANES)
    scalar = shape(SUB, LANES)
    owned_scratch = pltpu.VMEM((CP, sizes.own_rows, LANES), f32)
    point_scratch = pltpu.VMEM((3, PT_ROWS, LANES), f32)
    entries = sizes.pts * LANES

    given = [
        pltpu.with_memory_space_constraint(value, pltpu.HBM)
        for value in (camera_jacobian, point_jacobian, residual, slot, point, send_list[0])
    ]
    first, a, b, inverse, gradient = call(
        functools.partial(setup_kernel, sizes),
        "setup",
        given,
        [
            shape(sizes.devices * sizes.first_message, LANES),
            shape(2 * CP * rows, LANES),
            shape(6 * rows, LANES),
            shape(6, PT_ROWS, LANES),
            point_table,
        ],
        [pltpu.VMEM((2 * rows, LANES), f32), point_scratch]
        + factors(max(spread_rows(9 * PIECES, PT_HI), spread_rows(2 * CP * PIECES, sizes.pts)), PT_LO, sizes.obs)
        + [pltpu.VMEM(value.shape, value.dtype) for value in given]
        + [pltpu.SemaphoreType.DMA((len(given),))],
        inputs_at=pl.ANY,
    )
    out, entry, precondition, remainder = call(
        functools.partial(first_owner_kernel, sizes),
        "first_owner",
        [exchange(first)],
        [messages, shape(sizes.pts, LANES, dtype=jnp.int32), owned, owned],
        [owned_scratch] + factors(spread_rows(2 * CP * PIECES, sizes.own_rows), LANES, entries),
        scalars=[column],
    )
    schur_scratch = [pltpu.VMEM((2 * rows, LANES), f32), point_scratch] + factors(
        max(spread_rows(3 * PIECES, PT_HI), spread_rows(CP * PIECES, sizes.pts)), PT_LO, sizes.obs
    )
    at_slot = shape(CP, sizes.pts, LANES)
    product = slots = direction = step = sums = solution_ = None
    for iteration in range(ITERS):
        start, last = iteration == 0, iteration == ITERS - 1
        earlier = [] if start else [product, slots, direction, step, sums]
        arrived = exchange(out)
        if last:
            (both,) = call(
                functools.partial(tail_kernel, sizes),
                "tail",
                [arrived, precondition, remainder, direction, product, solution_],
                [shape(2 * CP * sizes.own_rows, LANES)],
                [],
            )
            gathered = [both] + [
                lax.ppermute(both, "pts", [(p, p ^ k) for p in range(sizes.pts)]) for k in range(1, sizes.pts)
            ]
        results = call(
            functools.partial(schur_kernel, sizes, start, last),
            "schur_last" if last else "schur",
            [arrived, a, b, inverse, slot, point, precondition, remainder, gradient] + earlier,
            [shape(sizes.devices, LANES) if last else messages, scalar, at_slot, owned, point_table]
            + ([] if start else [point_table]),
            schur_scratch,
            cost=pl.CostEstimate(flops=2_000_000_000, bytes_accessed=10_000_000, transcendentals=0),
        )
        out, product, slots, direction, sums = results[:5]
        if not start:
            gradient = results[5]
        if last:
            break
        out, remainder, solution_, step = call(
            functools.partial(owner_kernel, sizes, start),
            "owner",
            [exchange(out), entry, precondition, remainder, direction, product] + ([] if start else [solution_]),
            [messages, owned, owned, scalar],
            [owned_scratch] + factors(spread_rows(CP * PIECES, sizes.own_rows), LANES, entries),
        )
    return call(
        functools.partial(final_kernel, sizes),
        "final",
        [exchange(out), product, inverse, gradient, sums] + gathered,
        [shape(CP, CAM_OWN), shape(3, PT_DEV)],
        [pltpu.VMEM((3 * PT_ROWS, LANES), f32)],
        scalars=[lax.axis_index("pts").astype(jnp.int32).reshape(1)],
    )


def solution(mesh):
    return jax.shard_map(
        lambda *arguments: tuple(body(*arguments)),
        mesh=mesh,
        in_specs=(
            P(None, ("pts", "cams")),
            P(None, ("pts", "cams")),
            P(None, ("pts", "cams")),
            P(("pts", "cams")),
            P(("pts", "cams")),
            P(("pts", "cams"), None, None),
        ),
        out_specs=(P(None, "cams"), P(None, ("pts", "cams"))),
        check_vma=False,
    )
```

```python
import functools

import jax
import jax.numpy as jnp
from jax import lax
from jax.experimental import pallas as pl
from jax.experimental.pallas import tpu as pltpu
from jax.sharding import PartitionSpec as P

CP = 9
CAM_OWN = 8192
PT_DEV = 4096
ITERS = 3
LANES = 128
SUB = 8
PT_LO = 256
PT_HI = PT_DEV // PT_LO
PT_ROWS = PT_DEV // LANES
PIECES = 3
NEAR = 2
VMEM_LIMIT = 40 * 1024 * 1024

damping_camera = 1.0
damping_point = 1.0

f32 = jnp.float32
bf16 = jnp.bfloat16


class Sizes:
    def __init__(self, pts, cams, slot, obs):
        self.pts, self.cams, self.slot, self.obs = pts, cams, slot, obs
        self.devices = pts * cams
        self.block = slot // pts
        assert cams * self.block == LANES and LANES % pts == 0
        self.rows = obs // LANES
        self.run = CAM_OWN // pts
        self.run_rows = self.run // LANES
        self.own_rows = max(SUB, self.run_rows)
        self.groups = -(-CP // cams)
        self.first_groups = -(-2 * CP // cams)
        self.message = self.groups
        self.first_message = self.first_groups + 1
        assert self.groups * cams > CP


def sub_iota(rows):
    return lax.broadcasted_iota(jnp.int32, (rows, LANES), 0)


def lane_iota(rows):
    return lax.broadcasted_iota(jnp.int32, (rows, LANES), 1)


def cut(value):
    parts = []
    for _ in range(PIECES - 1):
        part = value.astype(bf16).astype(f32)
        parts.append(part)
        value = value - part
    parts.append(value)
    return parts


def swap_blocks(rows, block, wanted):
    which = lane_iota(rows[0].shape[0]) // block
    result = []
    for q in range(wanted):
        total = None
        for c, value in enumerate(rows):
            shift = ((c - q) * block) % LANES
            moved = pltpu.roll(value, shift, axis=1) if shift else value
            total = jnp.where(which == c, moved, 0.0 if total is None else total)
        result.append(total)
    return result


def gather_rows(row, count, high, low, comps):
    result = [None] * comps
    for k in range(count):
        here = high == k
        for c in range(comps):
            source = jnp.broadcast_to(row(c, k), high.shape)
            found = jnp.take_along_axis(source, low, axis=1, mode="promise_in_bounds")
            result[c] = found if k == 0 else jnp.where(here, found, result[c])
    return result


def build(index, parts, high, low, high_count, low_count, spread_ref, place_ref):
    columns = pl.ds(pl.multiple_of(index * LANES, LANES), LANES)
    mask = jnp.broadcast_to(high, (high_count, LANES)) == sub_iota(high_count)
    together = max(1, 16 // high_count)
    for start in range(0, len(parts), together):
        pieces = [
            jnp.where(mask, jnp.broadcast_to(part, (high_count, LANES)), 0.0)
            for part in parts[start : start + together]
        ]
        while len(pieces) < together:
            pieces.append(jnp.zeros((high_count, LANES), f32))
        tile = pieces[0] if together == 1 else jnp.concatenate(pieces, axis=0)
        spread_ref[start * high_count : start * high_count + tile.shape[0], columns] = tile.astype(bf16)
    place = jnp.broadcast_to(low, (low_count, LANES)) == sub_iota(low_count)
    place_ref[:low_count, columns] = jnp.where(place, 1.0, 0.0).astype(bf16)


def spread_rows(parts, high_count):
    return -(-parts * high_count // 16) * 16


def scatter(parts, entries, high_count, low_count, spread_ref, place_ref):
    rows = spread_rows(parts, high_count)
    return lax.dot_general(
        spread_ref[:rows, :entries],
        place_ref[:low_count, :entries],
        (((1,), (1,)), ((), ())),
        preferred_element_type=f32,
    )


def joined(result, comp, high_count, pieces=PIECES):
    first = comp * pieces * high_count
    total = result[first + (pieces - 1) * high_count : first + pieces * high_count]
    for piece in reversed(range(pieces - 1)):
        total = total + result[first + piece * high_count : first + (piece + 1) * high_count]
    return total


def point_rows(value):
    return jnp.concatenate([value[:, :LANES], value[:, LANES:]], axis=0)


def point_place(point):
    high = point >> 8
    return high + ((point >> 7) & 1) * PT_HI, point & (LANES - 1), high, point & (PT_LO - 1)


def slot_place(slot, sizes):
    within = slot % sizes.slot
    return within % sizes.pts, (slot // sizes.slot) * sizes.block + within // sizes.pts


def solve(inverse, values):
    first = inverse[0] * values[0] + inverse[1] * values[1] + inverse[2] * values[2]
    second = inverse[1] * values[0] + inverse[3] * values[1] + inverse[4] * values[2]
    third = inverse[2] * values[0] + inverse[4] * values[1] + inverse[5] * values[2]
    return first, second, third


def write_messages(fields, scalar, groups, message, out_ref, sizes, extra=None):
    which = lane_iota(sizes.pts) // sizes.block
    for g in range(groups):
        rows = fields[g * sizes.cams : (g + 1) * sizes.cams]
        moved = swap_partial(rows, sizes)
        for c in range(sizes.cams):
            value = moved[c]
            if g == groups - 1 and scalar is not None:
                value = jnp.where(which == sizes.cams - 1, scalar, value)
            out_ref[pl.ds(c * message + g, sizes.pts, stride=sizes.cams * message), :] = value
    for g in range(groups, message):
        for c in range(sizes.cams):
            value = extra if (extra is not None and g == groups) else jnp.zeros((sizes.pts, LANES), f32)
            out_ref[pl.ds(c * message + g, sizes.pts, stride=sizes.cams * message), :] = value


def swap_partial(rows, sizes):
    return swap_blocks(rows, sizes.block, sizes.cams)


def read_row(in_ref, c, g, message, sizes):
    return in_ref[pl.ds(c * message + g, sizes.pts, stride=sizes.cams * message), :]


def read_messages(in_ref, count, message, sizes):
    fields = []
    group = 0
    while len(fields) < count:
        rows = [read_row(in_ref, c, group, message, sizes) for c in range(sizes.cams)]
        fields += swap_blocks(rows, sizes.block, min(sizes.cams, count - len(fields)))
        group += 1
    return fields


def read_scalar(in_ref, groups, message, sizes):
    total = read_row(in_ref, 0, groups - 1, message, sizes)
    for c in range(1, sizes.cams):
        total = total + read_row(in_ref, c, groups - 1, message, sizes)
    chosen = jnp.where(lane_iota(sizes.pts) == LANES - 1, total, 0.0)
    return jnp.sum(chosen, keepdims=True)


def setup_kernel(sizes, *refs):
    sources, refs = refs[:6], refs[6:]
    out_ref, a_ref, b_ref, inv_ref, grad_ref = refs[:5]
    r_ref, table_ref, spread_ref, place_ref = refs[5:9]
    jac_ref, pjac_ref, res_ref, slot_ref, point_ref, list_ref = refs[9:15]
    semaphores = refs[15]
    rows = sizes.rows
    copies = [pltpu.make_async_copy(source, target, semaphores.at[k]) for k, (source, target) in enumerate(zip(sources, refs[9:15]))]
    for copy in copies:
        copy.start()
    for copy in copies:
        copy.wait()
    for j in range(rows):
        columns = slice(j * LANES, (j + 1) * LANES)
        for start in range(0, 2 * CP, SUB):
            size = min(SUB, 2 * CP - start)
            a_ref[pl.ds(start * rows + j, size, stride=rows), :] = jac_ref[start : start + size, columns]
        b_ref[pl.ds(j, 6, stride=rows), :] = pjac_ref[:, columns]
        r_ref[pl.ds(j, 2, stride=rows), :] = res_ref[:, columns]

    def at(ref, comp, group):
        return ref[pl.ds(pl.multiple_of(comp * rows + group * SUB, SUB), SUB), :]

    def first(group, carry):
        b = [at(b_ref, k, group) for k in range(6)]
        r = [at(r_ref, k, group) for k in range(2)]
        point = point_ref[pl.ds(pl.multiple_of(group * SUB, SUB), SUB), :]
        _, _, high, low = point_place(point)
        values = [b[i] * b[j] + b[3 + i] * b[3 + j] for i, j in ((0, 0), (0, 1), (0, 2), (1, 1), (1, 2), (2, 2))]
        values += [b[i] * r[0] + b[3 + i] * r[1] for i in range(3)]
        parts = [part for value in values for part in cut(value)]
        for s in range(SUB):
            build(group * SUB + s, [part[s : s + 1] for part in parts], high[s : s + 1], low[s : s + 1],
                  PT_HI, PT_LO, spread_ref, place_ref)
        return carry

    lax.fori_loop(0, rows // SUB, first, 0)
    result = scatter(9 * PIECES, sizes.obs, PT_HI, PT_LO, spread_ref, place_ref)
    normal = [point_rows(joined(result, k, PT_HI)) for k in range(9)]
    top_left = normal[0] + damping_point
    top_mid = normal[1]
    top_right = normal[2]
    mid_mid = normal[3] + damping_point
    mid_right = normal[4]
    low_right = normal[5] + damping_point
    adjugate = [
        mid_mid * low_right - mid_right * mid_right,
        top_right * mid_right - top_mid * low_right,
        top_mid * mid_right - top_right * mid_mid,
        top_left * low_right - top_right * top_right,
        top_mid * top_right - top_left * mid_right,
        top_left * mid_mid - top_mid * top_mid,
    ]
    determinant = top_left * adjugate[0] + top_mid * adjugate[1] + top_right * adjugate[2]
    inverse = [value / determinant for value in adjugate]
    for k in range(6):
        inv_ref[k] = inverse[k]
    for k in range(3):
        grad_ref[k] = normal[6 + k]
    eliminated = solve(inverse, normal[6:])
    for k in range(3):
        table_ref[k] = eliminated[k]

    def second(group, carry):
        point = point_ref[pl.ds(pl.multiple_of(group * SUB, SUB), SUB), :]
        high, low, _, _ = point_place(point)
        at_point = gather_rows(lambda c, k: table_ref[c, k : k + 1, :], PT_ROWS, high, low, 3)
        b = [at(b_ref, k, group) for k in range(6)]
        errors = [at(r_ref, i, group) - sum(b[3 * i + k] * at_point[k] for k in range(3)) for i in range(2)]
        a = [at(a_ref, k, group) for k in range(2 * CP)]
        values = [a[k] * errors[0] + a[CP + k] * errors[1] for k in range(CP)]
        values += [a[k] * a[k] + a[CP + k] * a[CP + k] for k in range(CP)]
        parts = [part for value in values for part in cut(value)]
        high, low = slot_place(slot_ref[pl.ds(pl.multiple_of(group * SUB, SUB), SUB), :], sizes)
        for s in range(SUB):
            build(group * SUB + s, [part[s : s + 1] for part in parts], high[s : s + 1], low[s : s + 1],
                  sizes.pts, LANES, spread_ref, place_ref)
        return carry

    lax.fori_loop(0, rows // SUB, second, 0)
    result = scatter(2 * CP * PIECES, sizes.obs, sizes.pts, LANES, spread_ref, place_ref)
    fields = [joined(result, k, sizes.pts) for k in range(2 * CP)]

    pieces = sizes.slot // LANES
    lane = lane_iota(1)
    for c in range(sizes.cams):
        for half in range(pieces):
            value = list_ref[c : c + 1, half * LANES : (half + 1) * LANES]
            low = c * sizes.block + half * (LANES // sizes.pts) + lane // sizes.pts
            build(c * pieces + half, [(value >> 8).astype(f32), (value & 255).astype(f32)], lane % sizes.pts, low,
                  sizes.pts, LANES, spread_ref, place_ref)
    result = scatter(2, sizes.cams * sizes.slot, sizes.pts, LANES, spread_ref, place_ref)
    listed = result[: sizes.pts] * 256.0 + result[sizes.pts : 2 * sizes.pts]
    write_messages(fields, None, sizes.first_groups, sizes.first_message, out_ref, sizes, extra=listed)


def entries_scatter(fields, entry, sizes, spread_ref, place_ref):
    high, low = entry // LANES, entry % LANES
    parts = [part for value in fields for part in cut(value)]
    for p in range(sizes.pts):
        build(p, [part[p : p + 1] for part in parts], high[p : p + 1], low[p : p + 1],
              sizes.own_rows, LANES, spread_ref, place_ref)
    result = scatter(len(parts), sizes.pts * LANES, sizes.own_rows, LANES, spread_ref, place_ref)
    return [joined(result, k, sizes.own_rows) for k in range(len(fields))]


def send_owned(scaled, partial, entry, out_ref, table_ref, sizes):
    for k in range(CP):
        table_ref[k] = scaled[k]
    fields = gather_rows(lambda c, k: table_ref[c, k : k + 1, :], sizes.run_rows, entry // LANES, entry % LANES, CP)
    write_messages(fields, partial, sizes.groups, sizes.message, out_ref, sizes)


def dot_fields(left, right):
    return jnp.sum(sum(a * b for a, b in zip(left, right)), keepdims=True)


def first_owner_kernel(sizes, column_ref, in_ref, out_ref, entry_ref, pre_ref, rem_ref,
                       table_ref, spread_ref, place_ref):
    listed = jnp.zeros((sizes.pts, LANES), f32)
    for c in range(sizes.cams):
        row = read_row(in_ref, c, sizes.first_groups, sizes.first_message, sizes)
        listed = jnp.where(column_ref[0] == c, row, listed)
    entry = listed.astype(jnp.int32) % sizes.run
    entry_ref[...] = entry
    fields = read_messages(in_ref, 2 * CP, sizes.first_message, sizes)
    sums = entries_scatter(fields, entry, sizes, spread_ref, place_ref)
    remainder = [-value for value in sums[:CP]]
    precondition = [1.0 / (value + damping_camera) for value in sums[CP:]]
    scaled = [p * r for p, r in zip(precondition, remainder)]
    for k in range(CP):
        pre_ref[k] = precondition[k]
        rem_ref[k] = remainder[k]
    send_owned(scaled, dot_fields(remainder, scaled), entry, out_ref, table_ref, sizes)


def owner_kernel(sizes, start, final, in_ref, entry_ref, pre_ref, rem_ref, dir_ref, product_ref, *refs):
    refs = list(refs)
    sol_ref = None if start else refs.pop(0)
    out_ref, new_rem_ref, new_sol_ref, step_ref = refs[:4]
    fields_ref = refs[4] if final else None
    table_ref, spread_ref, place_ref = refs[-3:]
    entry = entry_ref[...]
    fields = read_messages(in_ref, CP, sizes.message, sizes)
    curvature = read_scalar(in_ref, sizes.groups, sizes.message, sizes)
    step = product_ref[...] / jnp.broadcast_to(curvature, (SUB, LANES))
    step_ref[...] = step
    sums = entries_scatter(fields, entry, sizes, spread_ref, place_ref)
    remainder, scaled = [], []
    for k in range(CP):
        direction = dir_ref[k]
        moved = step[:1] * direction
        moved = moved if start else sol_ref[k] + moved
        new_sol_ref[k] = moved
        value = rem_ref[k] - step[:1] * (sums[k] + damping_camera * direction)
        new_rem_ref[k] = value
        remainder.append(value)
        scaled.append(pre_ref[k] * value)
        if final:
            for j, field in enumerate((moved, direction, scaled[k])):
                first = (j * CP + k) * sizes.own_rows
                fields_ref[first : first + sizes.own_rows, :] = field
    send_owned(scaled, dot_fields(remainder, scaled), entry, out_ref, table_ref, sizes)


def schur_kernel(sizes, start, last, in_ref, a_ref, b_ref, inv_ref, slot_ref, point_ref, pre_ref, rem_ref, grad_ref, *refs):
    refs = list(refs)
    if not start:
        product_ref, at_slot_ref, dir_ref, step_ref, sum_ref = refs[:5]
        refs = refs[5:]
    out_ref, new_product_ref, new_at_slot_ref, new_dir_ref, new_sum_ref = refs[:5]
    new_grad_ref = None
    refs = refs[5:]
    if not start:
        new_grad_ref = refs.pop(0)
    q_ref, table_ref, spread_ref, place_ref = refs
    rows = sizes.rows

    def at(ref, comp, group):
        return ref[pl.ds(pl.multiple_of(comp * rows + group * SUB, SUB), SUB), :]

    def index(ref, group):
        return ref[pl.ds(pl.multiple_of(group * SUB, SUB), SUB), :]

    renewed = jnp.broadcast_to(read_scalar(in_ref, sizes.groups, sizes.message, sizes), (SUB, LANES))
    new_product_ref[...] = renewed
    fields = read_messages(in_ref, CP, sizes.message, sizes)
    beta = None if start else (renewed / product_ref[...])[:1]
    squares = None
    for k in range(CP):
        direction = pre_ref[k] * rem_ref[k]
        if start:
            new_at_slot_ref[k] = fields[k]
        else:
            new_at_slot_ref[k] = fields[k] + beta * at_slot_ref[k]
            direction = direction + beta * dir_ref[k]
        new_dir_ref[k] = direction
        squares = direction * direction if squares is None else squares + direction * direction

    def first(group, carry):
        high, low = slot_place(index(slot_ref, group), sizes)
        gathered = gather_rows(lambda c, k: new_at_slot_ref[c, k : k + 1, :], sizes.pts, high, low, CP)
        q = [sum(at(a_ref, i * CP + k, group) * gathered[k] for k in range(CP)) for i in range(2)]
        for i in range(2):
            q_ref[pl.ds(pl.multiple_of(i * rows + group * SUB, SUB), SUB), :] = q[i]
        values = [at(b_ref, k, group) * q[0] + at(b_ref, 3 + k, group) * q[1] for k in range(3)]
        parts = [part for value in values for part in cut(value)]
        _, _, high, low = point_place(index(point_ref, group))
        for s in range(SUB):
            build(group * SUB + s, [part[s : s + 1] for part in parts], high[s : s + 1], low[s : s + 1],
                  PT_HI, PT_LO, spread_ref, place_ref)
        return carry

    lax.fori_loop(0, rows // SUB, first, 0)
    result = scatter(3 * PIECES, sizes.obs, PT_HI, PT_LO, spread_ref, place_ref)
    sums = [point_rows(joined(result, k, PT_HI)) for k in range(3)]
    folded = solve([inv_ref[k] for k in range(6)], sums)
    for k in range(3):
        table_ref[k] = folded[k]
        new_sum_ref[k] = sums[k]
        if not start:
            new_grad_ref[k] = grad_ref[k] + step_ref[:1, :] * sum_ref[k]

    def second(group, inner):
        high, low, _, _ = point_place(index(point_ref, group))
        at_point = gather_rows(lambda c, k: table_ref[c, k : k + 1, :], PT_ROWS, high, low, 3)
        q = [at(q_ref, i, group) for i in range(2)]
        errors = [q[i] - sum(at(b_ref, 3 * i + k, group) * at_point[k] for k in range(3)) for i in range(2)]
        inner = inner + q[0] * errors[0] + q[1] * errors[1]
        if not last:
            values = [at(a_ref, k, group) * errors[0] + at(a_ref, CP + k, group) * errors[1] for k in range(CP)]
            parts = [part for value in values for part in cut(value)]
            high, low = slot_place(index(slot_ref, group), sizes)
            for s in range(SUB):
                build(group * SUB + s, [part[s : s + 1] for part in parts], high[s : s + 1], low[s : s + 1],
                      sizes.pts, LANES, spread_ref, place_ref)
        return inner

    inner = lax.fori_loop(0, rows // SUB, second, jnp.zeros((SUB, LANES), f32))
    partial = jnp.sum(inner, keepdims=True) + damping_camera * jnp.sum(squares, keepdims=True)
    if last:
        out_ref[...] = jnp.broadcast_to(partial, (sizes.devices, LANES))
        return
    result = scatter(CP * PIECES, sizes.obs, sizes.pts, LANES, spread_ref, place_ref)
    fields = [joined(result, k, sizes.pts) for k in range(CP)]
    write_messages(fields, partial, sizes.groups, sizes.message, out_ref, sizes)


def tail_kernel(sizes, in_ref, product_ref, own_ref, other_ref, out_ref):
    renewed = jnp.broadcast_to(read_scalar(in_ref, sizes.groups, sizes.message, sizes), (SUB, LANES))
    beta = (renewed / product_ref[...])[:1]
    field = CP * sizes.own_rows
    for j, ref in enumerate((own_ref, other_ref)):
        first = j * 2 * field
        out_ref[first : first + field, :] = ref[:field, :]
        out_ref[first + field : first + 2 * field, :] = ref[2 * field :, :] + beta * ref[field : 2 * field, :]


def final_kernel(sizes, masks, run_ref, in_ref, product_ref, inv_ref, grad_ref, sum_ref, *refs):
    all_refs = refs[: len(masks)]
    cam_ref, pt_ref, table_ref = refs[len(masks) :]
    curvature = jnp.sum(jnp.where(lane_iota(sizes.devices) == 0, in_ref[...], 0.0), keepdims=True)
    step = (product_ref[...] / jnp.broadcast_to(curvature, (SUB, LANES)))[:1]
    for all_ref, pair in zip(all_refs, masks):
        for j, mask in enumerate(pair):
            base_column = (run_ref[0] ^ mask) * sizes.run
            for h in range(sizes.run_rows):
                columns = pl.ds(pl.multiple_of(base_column + h * LANES, LANES), LANES)
                for start in range(0, CP, SUB):
                    size = min(SUB, CP - start)
                    first = (j * 2 * CP + start) * sizes.own_rows + h
                    base = all_ref[pl.ds(first, size, stride=sizes.own_rows), :]
                    direction = all_ref[pl.ds(first + CP * sizes.own_rows, size, stride=sizes.own_rows), :]
                    cam_ref[start : start + size, columns] = base + step * direction
    total = [grad_ref[k] + step * sum_ref[k] for k in range(3)]
    solved = solve([inv_ref[k] for k in range(6)], total)
    for k in range(3):
        table_ref[k * PT_ROWS : (k + 1) * PT_ROWS, :] = -solved[k]
    for row in range(PT_ROWS):
        half, high = row // PT_HI, row % PT_HI
        chunk = high * (PT_LO // LANES) + half
        pt_ref[:, chunk * LANES : (chunk + 1) * LANES] = table_ref[pl.ds(row, 3, stride=PT_ROWS), :]


def shape(*dims, dtype=f32):
    return jax.ShapeDtypeStruct(dims, dtype)


def call(kernel, name, inputs, outputs, scratch, scalars=(), inputs_at=pltpu.VMEM, cost=None):
    vmem = pl.BlockSpec(memory_space=pltpu.VMEM)
    given = pl.BlockSpec(memory_space=inputs_at)
    smem = pl.BlockSpec(memory_space=pltpu.SMEM)
    return pl.pallas_call(
        kernel,
        name=name,
        out_shape=outputs,
        in_specs=[smem] * len(scalars) + [given] * len(inputs),
        out_specs=[vmem] * len(outputs),
        scratch_shapes=scratch,
        cost_estimate=cost,
        compiler_params=pltpu.CompilerParams(vmem_limit_bytes=VMEM_LIMIT),
    )(*scalars, *inputs)


def body(camera_jacobian, point_jacobian, residual, observed_slot, observed_point, send_list):
    sizes = Sizes(lax.axis_size("pts"), lax.axis_size("cams"), send_list.shape[2], camera_jacobian.shape[1])
    axes = ("pts", "cams")
    rows = sizes.rows
    slot = observed_slot.reshape(rows, LANES)
    point = observed_point.reshape(rows, LANES)
    column = lax.axis_index("cams").astype(jnp.int32).reshape(1)

    def exchange(messages):
        width = messages.size // sizes.devices
        flat = messages.reshape(sizes.devices, 1, width)
        return lax.all_to_all(flat, axes, split_axis=0, concat_axis=0, tiled=True).reshape(messages.shape)

    def flipped(value, flip):
        return lax.ppermute(value, "pts", [(p, p ^ flip) for p in range(sizes.pts)])

    def factors(high_rows, low_rows, entries):
        return [pltpu.VMEM((high_rows, entries), bf16), pltpu.VMEM((low_rows, entries), bf16)]

    point_table = shape(3, PT_ROWS, LANES)
    owned = shape(CP, sizes.own_rows, LANES)
    messages = shape(sizes.devices * sizes.message, LANES)
    scalar = shape(SUB, LANES)
    owned_scratch = pltpu.VMEM((CP, sizes.own_rows, LANES), f32)
    point_scratch = pltpu.VMEM((3, PT_ROWS, LANES), f32)
    entries = sizes.pts * LANES

    given = [
        pltpu.with_memory_space_constraint(value, pltpu.HBM)
        for value in (camera_jacobian, point_jacobian, residual, slot, point, send_list[0])
    ]
    first, a, b, inverse, gradient = call(
        functools.partial(setup_kernel, sizes),
        "setup",
        given,
        [
            shape(sizes.devices * sizes.first_message, LANES),
            shape(2 * CP * rows, LANES),
            shape(6 * rows, LANES),
            shape(6, PT_ROWS, LANES),
            point_table,
        ],
        [pltpu.VMEM((2 * rows, LANES), f32), point_scratch]
        + factors(max(spread_rows(9 * PIECES, PT_HI), spread_rows(2 * CP * PIECES, sizes.pts)), PT_LO, sizes.obs)
        + [pltpu.VMEM(value.shape, value.dtype) for value in given]
        + [pltpu.SemaphoreType.DMA((len(given),))],
        inputs_at=pl.ANY,
    )
    out, entry, precondition, remainder = call(
        functools.partial(first_owner_kernel, sizes),
        "first_owner",
        [exchange(first)],
        [messages, shape(sizes.pts, LANES, dtype=jnp.int32), owned, owned],
        [owned_scratch] + factors(spread_rows(2 * CP * PIECES, sizes.own_rows), LANES, entries),
        scalars=[column],
    )
    schur_scratch = [pltpu.VMEM((2 * rows, LANES), f32), point_scratch] + factors(
        max(spread_rows(3 * PIECES, PT_HI), spread_rows(CP * PIECES, sizes.pts)), PT_LO, sizes.obs
    )
    at_slot = shape(CP, sizes.pts, LANES)
    product = slots = direction = step = sums = solution_ = None
    for iteration in range(ITERS):
        start, last = iteration == 0, iteration == ITERS - 1
        earlier = [] if start else [product, slots, direction, step, sums]
        if last:
            neighbour = flipped(fields, NEAR)
        arrived = exchange(out)
        if last:
            (both,) = call(
                functools.partial(tail_kernel, sizes),
                "tail",
                [arrived, product, fields, neighbour],
                [shape(4 * CP * sizes.own_rows, LANES)],
                [],
            )
            flips = [1 << bit for bit in range(sizes.pts.bit_length() - 1) if 1 << bit != NEAR]
            flips = flips[1:] + flips[:1]
            early = {flip: flipped(both, flip) for flip in (flips[0], flips[-1])}
        results = call(
            functools.partial(schur_kernel, sizes, start, last),
            "schur_last" if last else "schur",
            [arrived, a, b, inverse, slot, point, precondition, remainder, gradient] + earlier,
            [shape(sizes.devices, LANES) if last else messages, scalar, at_slot, owned, point_table]
            + ([] if start else [point_table]),
            schur_scratch,
            cost=pl.CostEstimate(flops=2_000_000_000, bytes_accessed=10_000_000, transcendentals=0),
        )
        out, product, slots, direction, sums = results[:5]
        if not start:
            gradient = results[5]
        if last:
            early[flips[0]], out = lax.optimization_barrier((early[flips[0]], out))
            gathered, masks = [both], [(0, NEAR)]
            for flip in flips:
                gathered += [early[flip] if value is both and flip in early else flipped(value, flip) for value in gathered]
                masks += [tuple(mask ^ flip for mask in pair) for pair in masks]
            break
        final = iteration == ITERS - 2
        out, remainder, solution_, step, *rest = call(
            functools.partial(owner_kernel, sizes, start, final),
            "owner_final" if final else "owner",
            [exchange(out), entry, precondition, remainder, direction, product] + ([] if start else [solution_]),
            [messages, owned, owned, scalar] + ([shape(3 * CP * sizes.own_rows, LANES)] if final else []),
            [owned_scratch] + factors(spread_rows(CP * PIECES, sizes.own_rows), LANES, entries),
        )
        fields = rest[0] if final else None
    return call(
        functools.partial(final_kernel, sizes, masks),
        "final",
        [exchange(out), product, inverse, gradient, sums] + gathered,
        [shape(CP, CAM_OWN), shape(3, PT_DEV)],
        [pltpu.VMEM((3 * PT_ROWS, LANES), f32)],
        scalars=[lax.axis_index("pts").astype(jnp.int32).reshape(1)],
    )


def solution(mesh):
    return jax.shard_map(
        lambda *arguments: tuple(body(*arguments)),
        mesh=mesh,
        in_specs=(
            P(None, ("pts", "cams")),
            P(None, ("pts", "cams")),
            P(None, ("pts", "cams")),
            P(("pts", "cams")),
            P(("pts", "cams")),
            P(("pts", "cams"), None, None),
        ),
        out_specs=(P(None, "cams"), P(None, ("pts", "cams"))),
        check_vma=False,
    )
```

```python
import functools

import jax
import jax.numpy as jnp
from jax import lax
from jax.experimental import pallas as pl
from jax.experimental.pallas import tpu as pltpu
from jax.sharding import PartitionSpec as P

CP = 9
CAM_OWN = 8192
PT_DEV = 4096
ITERS = 3
LANES = 128
SUB = 8
PT_LO = 256
PT_HI = PT_DEV // PT_LO
PT_ROWS = PT_DEV // LANES
PIECES = 2
FINE = 3
NEAR = 2
VMEM_LIMIT = 24 * 1024 * 1024

damping_camera = 1.0
damping_point = 1.0

f32 = jnp.float32
bf16 = jnp.bfloat16


class Sizes:
    def __init__(self, pts, cams, slot, obs):
        self.pts, self.cams, self.slot, self.obs = pts, cams, slot, obs
        self.devices = pts * cams
        self.block = slot // pts
        assert cams * self.block == LANES and LANES % pts == 0
        self.rows = obs // LANES
        self.run = CAM_OWN // pts
        self.run_rows = self.run // LANES
        self.own_rows = max(SUB, self.run_rows)
        self.groups = -(-CP // cams)
        self.first_groups = -(-2 * CP // cams)
        self.message = self.groups
        self.first_message = self.first_groups + 1
        assert self.groups * cams > CP


def sub_iota(rows):
    return lax.broadcasted_iota(jnp.int32, (rows, LANES), 0)


def lane_iota(rows):
    return lax.broadcasted_iota(jnp.int32, (rows, LANES), 1)


def cut(value, pieces=PIECES):
    parts = []
    for _ in range(pieces - 1):
        part = value.astype(bf16).astype(f32)
        parts.append(part)
        value = value - part
    parts.append(value)
    return parts


def swap_blocks(rows, block, wanted):
    which = lane_iota(rows[0].shape[0]) // block
    result = []
    for q in range(wanted):
        total = None
        for c, value in enumerate(rows):
            shift = ((c - q) * block) % LANES
            moved = pltpu.roll(value, shift, axis=1) if shift else value
            total = jnp.where(which == c, moved, 0.0 if total is None else total)
        result.append(total)
    return result


def gather_rows(row, count, high, low, comps):
    result = [None] * comps
    for k in range(count):
        here = high == k
        for c in range(comps):
            source = jnp.broadcast_to(row(c, k), high.shape)
            found = jnp.take_along_axis(source, low, axis=1, mode="promise_in_bounds")
            result[c] = found if k == 0 else jnp.where(here, found, result[c])
    return result


def spread_row(index, parts, high, high_count, spread_ref):
    columns = pl.ds(pl.multiple_of(index * LANES, LANES), LANES)
    mask = jnp.broadcast_to(high, (high_count, LANES)) == sub_iota(high_count)
    together = max(1, 16 // high_count)
    for start in range(0, len(parts), together):
        pieces = [
            jnp.where(mask, jnp.broadcast_to(part, (high_count, LANES)), 0.0)
            for part in parts[start : start + together]
        ]
        while len(pieces) < together:
            pieces.append(jnp.zeros((high_count, LANES), f32))
        tile = pieces[0] if together == 1 else jnp.concatenate(pieces, axis=0)
        spread_ref[start * high_count : start * high_count + tile.shape[0], columns] = tile.astype(bf16)


def place_row(index, low, low_count, place_ref):
    columns = pl.ds(pl.multiple_of(index * LANES, LANES), LANES)
    place = jnp.broadcast_to(low, (low_count, LANES)) == sub_iota(low_count)
    place_ref[:low_count, columns] = jnp.where(place, 1.0, 0.0).astype(bf16)


def keep_parts(parts, parts_ref):
    for k, part in enumerate(parts):
        parts_ref[k * SUB : (k + 1) * SUB, :] = part


def part_rows(count, s, parts_ref):
    return [parts_ref[k * SUB + s : k * SUB + s + 1, :] for k in range(count)]


def spread_rows(parts, high_count):
    return -(-parts * high_count // 16) * 16


def scatter(parts, entries, high_count, low_count, spread_ref, place_ref):
    rows = spread_rows(parts, high_count)
    return lax.dot_general(
        spread_ref[:rows, :entries],
        place_ref[:low_count, :entries],
        (((1,), (1,)), ((), ())),
        preferred_element_type=f32,
    )


def joined(result, count, high_count, pieces=None):
    pieces = pieces or [PIECES] * count
    values, first = [], 0
    for number in pieces:
        rows = [result[first + k * high_count : first + (k + 1) * high_count] for k in range(number)]
        first += number * high_count
        total = rows[-1]
        for row in reversed(rows[:-1]):
            total = total + row
        values.append(total)
    return values


def point_rows(value):
    return jnp.concatenate([value[:, :LANES], value[:, LANES:]], axis=0)


def point_place(point):
    return (point >> 8) + ((point >> 7) & 1) * PT_HI, point & (LANES - 1)


def slot_place(slot, sizes):
    within = slot % sizes.slot
    return within % sizes.pts, (slot // sizes.slot) * sizes.block + within // sizes.pts


def solve(inverse, values):
    first = inverse[0] * values[0] + inverse[1] * values[1] + inverse[2] * values[2]
    second = inverse[1] * values[0] + inverse[3] * values[1] + inverse[4] * values[2]
    third = inverse[2] * values[0] + inverse[4] * values[1] + inverse[5] * values[2]
    return first, second, third


def write_messages(fields, scalar, groups, message, out_ref, sizes, extra=None):
    which = lane_iota(sizes.pts) // sizes.block
    for g in range(groups):
        rows = fields[g * sizes.cams : (g + 1) * sizes.cams]
        moved = swap_partial(rows, sizes)
        for c in range(sizes.cams):
            value = moved[c]
            if g == groups - 1 and scalar is not None:
                value = jnp.where(which == sizes.cams - 1, scalar, value)
            out_ref[pl.ds(c * message + g, sizes.pts, stride=sizes.cams * message), :] = value
    for g in range(groups, message):
        for c in range(sizes.cams):
            value = extra if (extra is not None and g == groups) else jnp.zeros((sizes.pts, LANES), f32)
            out_ref[pl.ds(c * message + g, sizes.pts, stride=sizes.cams * message), :] = value


def swap_partial(rows, sizes):
    return swap_blocks(rows, sizes.block, sizes.cams)


def read_row(in_ref, c, g, message, sizes):
    return in_ref[pl.ds(c * message + g, sizes.pts, stride=sizes.cams * message), :]


def read_messages(in_ref, count, message, sizes):
    fields = []
    group = 0
    while len(fields) < count:
        rows = [read_row(in_ref, c, group, message, sizes) for c in range(sizes.cams)]
        fields += swap_blocks(rows, sizes.block, min(sizes.cams, count - len(fields)))
        group += 1
    return fields


def read_scalar(in_ref, groups, message, sizes):
    total = read_row(in_ref, 0, groups - 1, message, sizes)
    for c in range(1, sizes.cams):
        total = total + read_row(in_ref, c, groups - 1, message, sizes)
    chosen = jnp.where(lane_iota(sizes.pts) == LANES - 1, total, 0.0)
    return jnp.sum(chosen, keepdims=True)


def setup_kernel(sizes, *refs):
    sources, refs = refs[:6], refs[6:]
    out_ref, a_ref, b_ref, inv_ref, grad_ref, place_point_ref, place_slot_ref = refs[:7]
    r_ref, table_ref, parts_ref, spread_ref, place_list_ref = refs[7:12]
    jac_ref, pjac_ref, res_ref, slot_ref, point_ref, list_ref = refs[12:18]
    semaphores = refs[18]
    rows = sizes.rows
    copies = [
        pltpu.make_async_copy(source, target, semaphores.at[k])
        for k, (source, target) in enumerate(zip(sources, refs[12:18]))
    ]
    for copy in copies:
        copy.start()
    for copy in copies:
        copy.wait()
    for j in range(rows):
        columns = slice(j * LANES, (j + 1) * LANES)
        for start in range(0, 2 * CP, SUB):
            size = min(SUB, 2 * CP - start)
            a_ref[pl.ds(start * rows + j, size, stride=rows), :] = jac_ref[start : start + size, columns]
        b_ref[pl.ds(j, 6, stride=rows), :] = pjac_ref[:, columns]
        r_ref[pl.ds(j, 2, stride=rows), :] = res_ref[:, columns]

    def at(ref, comp, group):
        return ref[pl.ds(pl.multiple_of(comp * rows + group * SUB, SUB), SUB), :]

    normal_pieces = [FINE] * 6 + [PIECES] * 3

    def first(group, carry):
        b = [at(b_ref, k, group) for k in range(6)]
        r = [at(r_ref, k, group) for k in range(2)]
        values = [b[i] * b[j] + b[3 + i] * b[3 + j] for i, j in ((0, 0), (0, 1), (0, 2), (1, 1), (1, 2), (2, 2))]
        values += [b[i] * r[0] + b[3 + i] * r[1] for i in range(3)]
        parts = [part for value, pieces in zip(values, normal_pieces) for part in cut(value, pieces)]
        keep_parts(parts, parts_ref)
        for s in range(SUB):
            row = group * SUB + s
            point = point_ref[pl.ds(row, 1), :]
            spread_row(row, part_rows(len(parts), s, parts_ref), point >> 8, PT_HI, spread_ref)
            place_row(row, point & (PT_LO - 1), PT_LO, place_point_ref)
        return carry

    lax.fori_loop(0, rows // SUB, first, 0)
    result = scatter(sum(normal_pieces), sizes.obs, PT_HI, PT_LO, spread_ref, place_point_ref)
    normal = [point_rows(value) for value in joined(result, 9, PT_HI, normal_pieces)]
    top_left = normal[0] + damping_point
    top_mid = normal[1]
    top_right = normal[2]
    mid_mid = normal[3] + damping_point
    mid_right = normal[4]
    low_right = normal[5] + damping_point
    adjugate = [
        mid_mid * low_right - mid_right * mid_right,
        top_right * mid_right - top_mid * low_right,
        top_mid * mid_right - top_right * mid_mid,
        top_left * low_right - top_right * top_right,
        top_mid * top_right - top_left * mid_right,
        top_left * mid_mid - top_mid * top_mid,
    ]
    determinant = top_left * adjugate[0] + top_mid * adjugate[1] + top_right * adjugate[2]
    inverse = [value / determinant for value in adjugate]
    for k in range(6):
        inv_ref[k] = inverse[k]
    for k in range(3):
        grad_ref[k] = normal[6 + k]
    eliminated = solve(inverse, normal[6:])
    for k in range(3):
        table_ref[k] = eliminated[k]

    def second(group, carry):
        point = point_ref[pl.ds(pl.multiple_of(group * SUB, SUB), SUB), :]
        high, low = point_place(point)
        at_point = gather_rows(lambda c, k: table_ref[c, k : k + 1, :], PT_ROWS, high, low, 3)
        b = [at(b_ref, k, group) for k in range(6)]
        errors = [at(r_ref, i, group) - sum(b[3 * i + k] * at_point[k] for k in range(3)) for i in range(2)]
        a = [at(a_ref, k, group) for k in range(2 * CP)]
        values = [a[k] * errors[0] + a[CP + k] * errors[1] for k in range(CP)]
        values += [a[k] * a[k] + a[CP + k] * a[CP + k] for k in range(CP)]
        parts = [part for value in values for part in cut(value)]
        keep_parts(parts, parts_ref)
        for s in range(SUB):
            row = group * SUB + s
            high, low = slot_place(slot_ref[pl.ds(row, 1), :], sizes)
            spread_row(row, part_rows(len(parts), s, parts_ref), high, sizes.pts, spread_ref)
            place_row(row, low, LANES, place_slot_ref)
        return carry

    lax.fori_loop(0, rows // SUB, second, 0)
    result = scatter(2 * CP * PIECES, sizes.obs, sizes.pts, LANES, spread_ref, place_slot_ref)
    fields = joined(result, 2 * CP, sizes.pts)

    pieces = sizes.slot // LANES
    lane = lane_iota(1)
    for c in range(sizes.cams):
        for half in range(pieces):
            value = list_ref[c : c + 1, half * LANES : (half + 1) * LANES]
            low = c * sizes.block + half * (LANES // sizes.pts) + lane // sizes.pts
            parts = [(value >> 8).astype(f32), (value & 255).astype(f32)]
            spread_row(c * pieces + half, parts, lane % sizes.pts, sizes.pts, spread_ref)
            place_row(c * pieces + half, low, LANES, place_list_ref)
    result = scatter(2, sizes.cams * sizes.slot, sizes.pts, LANES, spread_ref, place_list_ref)
    listed = result[: sizes.pts] * 256.0 + result[sizes.pts : 2 * sizes.pts]
    write_messages(fields, None, sizes.first_groups, sizes.first_message, out_ref, sizes, extra=listed)


def entries_scatter(fields, entry, sizes, spread_ref, place_ref):
    high, low = entry // LANES, entry % LANES
    parts = [part for value in fields for part in cut(value)]
    for p in range(sizes.pts):
        spread_row(p, [part[p : p + 1] for part in parts], high[p : p + 1], sizes.own_rows, spread_ref)
        place_row(p, low[p : p + 1], LANES, place_ref)
    result = scatter(len(parts), sizes.pts * LANES, sizes.own_rows, LANES, spread_ref, place_ref)
    return joined(result, len(fields), sizes.own_rows)


def send_owned(scaled, partial, entry, out_ref, table_ref, sizes):
    for k in range(CP):
        table_ref[k] = scaled[k]
    fields = gather_rows(lambda c, k: table_ref[c, k : k + 1, :], sizes.run_rows, entry // LANES, entry % LANES, CP)
    write_messages(fields, partial, sizes.groups, sizes.message, out_ref, sizes)


def dot_fields(left, right):
    return jnp.sum(sum(a * b for a, b in zip(left, right)), keepdims=True)


def first_owner_kernel(sizes, column_ref, in_ref, out_ref, entry_ref, pre_ref, rem_ref,
                       table_ref, spread_ref, place_ref):
    listed = jnp.zeros((sizes.pts, LANES), f32)
    for c in range(sizes.cams):
        row = read_row(in_ref, c, sizes.first_groups, sizes.first_message, sizes)
        listed = jnp.where(column_ref[0] == c, row, listed)
    entry = listed.astype(jnp.int32) % sizes.run
    entry_ref[...] = entry
    fields = read_messages(in_ref, 2 * CP, sizes.first_message, sizes)
    sums = entries_scatter(fields, entry, sizes, spread_ref, place_ref)
    remainder = [-value for value in sums[:CP]]
    precondition = [1.0 / (value + damping_camera) for value in sums[CP:]]
    scaled = [p * r for p, r in zip(precondition, remainder)]
    for k in range(CP):
        pre_ref[k] = precondition[k]
        rem_ref[k] = remainder[k]
    send_owned(scaled, dot_fields(remainder, scaled), entry, out_ref, table_ref, sizes)


def owner_kernel(sizes, start, final, in_ref, entry_ref, pre_ref, rem_ref, dir_ref, product_ref, *refs):
    refs = list(refs)
    sol_ref = None if start else refs.pop(0)
    out_ref, new_rem_ref, new_sol_ref, step_ref = refs[:4]
    fields_ref = refs[4] if final else None
    table_ref, spread_ref, place_ref = refs[-3:]
    entry = entry_ref[...]
    fields = read_messages(in_ref, CP, sizes.message, sizes)
    curvature = read_scalar(in_ref, sizes.groups, sizes.message, sizes)
    step = product_ref[...] / jnp.broadcast_to(curvature, (SUB, LANES))
    step_ref[...] = step
    sums = entries_scatter(fields, entry, sizes, spread_ref, place_ref)
    remainder, scaled = [], []
    for k in range(CP):
        direction = dir_ref[k]
        moved = step[:1] * direction
        moved = moved if start else sol_ref[k] + moved
        new_sol_ref[k] = moved
        value = rem_ref[k] - step[:1] * (sums[k] + damping_camera * direction)
        new_rem_ref[k] = value
        remainder.append(value)
        scaled.append(pre_ref[k] * value)
        if final:
            for j, field in enumerate((moved, direction, scaled[k])):
                first = (j * CP + k) * sizes.own_rows
                fields_ref[first : first + sizes.own_rows, :] = field
    send_owned(scaled, dot_fields(remainder, scaled), entry, out_ref, table_ref, sizes)


def schur_kernel(sizes, start, last, in_ref, a_ref, b_ref, inv_ref, slot_ref, point_ref,
                 place_point_ref, place_slot_ref, pre_ref, rem_ref, grad_ref, *refs):
    refs = list(refs)
    if not start:
        product_ref, at_slot_ref, dir_ref, step_ref, sum_ref = refs[:5]
        refs = refs[5:]
    out_ref, new_product_ref, new_at_slot_ref, new_dir_ref, new_sum_ref = refs[:5]
    new_grad_ref = None
    refs = refs[5:]
    if not start:
        new_grad_ref = refs.pop(0)
    q_ref, table_ref, parts_ref, spread_ref = refs
    rows = sizes.rows

    def at(ref, comp, group):
        return ref[pl.ds(pl.multiple_of(comp * rows + group * SUB, SUB), SUB), :]

    def index(ref, group):
        return ref[pl.ds(pl.multiple_of(group * SUB, SUB), SUB), :]

    renewed = jnp.broadcast_to(read_scalar(in_ref, sizes.groups, sizes.message, sizes), (SUB, LANES))
    new_product_ref[...] = renewed
    fields = read_messages(in_ref, CP, sizes.message, sizes)
    beta = None if start else (renewed / product_ref[...])[:1]
    squares = None
    for k in range(CP):
        direction = pre_ref[k] * rem_ref[k]
        if start:
            new_at_slot_ref[k] = fields[k]
        else:
            new_at_slot_ref[k] = fields[k] + beta * at_slot_ref[k]
            direction = direction + beta * dir_ref[k]
        new_dir_ref[k] = direction
        squares = direction * direction if squares is None else squares + direction * direction

    def first(group, carry):
        high, low = slot_place(index(slot_ref, group), sizes)
        gathered = gather_rows(lambda c, k: new_at_slot_ref[c, k : k + 1, :], sizes.pts, high, low, CP)
        q = [sum(at(a_ref, i * CP + k, group) * gathered[k] for k in range(CP)) for i in range(2)]
        for i in range(2):
            q_ref[pl.ds(pl.multiple_of(i * rows + group * SUB, SUB), SUB), :] = q[i]
        values = [at(b_ref, k, group) * q[0] + at(b_ref, 3 + k, group) * q[1] for k in range(3)]
        parts = [part for value in values for part in cut(value)]
        keep_parts(parts, parts_ref)
        for s in range(SUB):
            row = group * SUB + s
            spread_row(row, part_rows(len(parts), s, parts_ref), point_ref[pl.ds(row, 1), :] >> 8, PT_HI, spread_ref)
        return carry

    lax.fori_loop(0, rows // SUB, first, 0)
    result = scatter(3 * PIECES, sizes.obs, PT_HI, PT_LO, spread_ref, place_point_ref)
    sums = [point_rows(value) for value in joined(result, 3, PT_HI)]
    folded = solve([inv_ref[k] for k in range(6)], sums)
    for k in range(3):
        table_ref[k] = folded[k]
        new_sum_ref[k] = sums[k]
        if not start:
            new_grad_ref[k] = grad_ref[k] + step_ref[:1, :] * sum_ref[k]

    def second(group, inner):
        high, low = point_place(index(point_ref, group))
        at_point = gather_rows(lambda c, k: table_ref[c, k : k + 1, :], PT_ROWS, high, low, 3)
        q = [at(q_ref, i, group) for i in range(2)]
        errors = [q[i] - sum(at(b_ref, 3 * i + k, group) * at_point[k] for k in range(3)) for i in range(2)]
        inner = inner + q[0] * errors[0] + q[1] * errors[1]
        if not last:
            values = [at(a_ref, k, group) * errors[0] + at(a_ref, CP + k, group) * errors[1] for k in range(CP)]
            parts = [part for value in values for part in cut(value)]
            keep_parts(parts, parts_ref)
            for s in range(SUB):
                row = group * SUB + s
                high, _ = slot_place(slot_ref[pl.ds(row, 1), :], sizes)
                spread_row(row, part_rows(len(parts), s, parts_ref), high, sizes.pts, spread_ref)
        return inner

    inner = lax.fori_loop(0, rows // SUB, second, jnp.zeros((SUB, LANES), f32))
    partial = jnp.sum(inner, keepdims=True) + damping_camera * jnp.sum(squares, keepdims=True)
    if last:
        out_ref[...] = jnp.broadcast_to(partial, (sizes.devices, LANES))
        return
    result = scatter(CP * PIECES, sizes.obs, sizes.pts, LANES, spread_ref, place_slot_ref)
    fields = joined(result, CP, sizes.pts)
    write_messages(fields, partial, sizes.groups, sizes.message, out_ref, sizes)


def tail_kernel(sizes, in_ref, product_ref, own_ref, other_ref, out_ref):
    renewed = jnp.broadcast_to(read_scalar(in_ref, sizes.groups, sizes.message, sizes), (SUB, LANES))
    beta = (renewed / product_ref[...])[:1]
    field = CP * sizes.own_rows
    for j, ref in enumerate((own_ref, other_ref)):
        first = j * 2 * field
        out_ref[first : first + field, :] = ref[:field, :]
        out_ref[first + field : first + 2 * field, :] = ref[2 * field :, :] + beta * ref[field : 2 * field, :]


def final_kernel(sizes, masks, run_ref, in_ref, product_ref, inv_ref, grad_ref, sum_ref, *refs):
    all_refs = refs[: len(masks)]
    cam_ref, pt_ref, table_ref = refs[len(masks) :]
    curvature = jnp.sum(jnp.where(lane_iota(sizes.devices) == 0, in_ref[...], 0.0), keepdims=True)
    step = (product_ref[...] / jnp.broadcast_to(curvature, (SUB, LANES)))[:1]
    for all_ref, pair in zip(all_refs, masks):
        for j, mask in enumerate(pair):
            base_column = (run_ref[0] ^ mask) * sizes.run
            for h in range(sizes.run_rows):
                columns = pl.ds(pl.multiple_of(base_column + h * LANES, LANES), LANES)
                for start in range(0, CP, SUB):
                    size = min(SUB, CP - start)
                    first = (j * 2 * CP + start) * sizes.own_rows + h
                    base = all_ref[pl.ds(first, size, stride=sizes.own_rows), :]
                    direction = all_ref[pl.ds(first + CP * sizes.own_rows, size, stride=sizes.own_rows), :]
                    cam_ref[start : start + size, columns] = base + step * direction
    total = [grad_ref[k] + step * sum_ref[k] for k in range(3)]
    solved = solve([inv_ref[k] for k in range(6)], total)
    for k in range(3):
        table_ref[k * PT_ROWS : (k + 1) * PT_ROWS, :] = -solved[k]
    for row in range(PT_ROWS):
        half, high = row // PT_HI, row % PT_HI
        chunk = high * (PT_LO // LANES) + half
        pt_ref[:, chunk * LANES : (chunk + 1) * LANES] = table_ref[pl.ds(row, 3, stride=PT_ROWS), :]


def shape(*dims, dtype=f32):
    return jax.ShapeDtypeStruct(dims, dtype)


def call(kernel, name, inputs, outputs, scratch, scalars=(), inputs_at=pltpu.VMEM, cost=None):
    vmem = pl.BlockSpec(memory_space=pltpu.VMEM)
    given = pl.BlockSpec(memory_space=inputs_at)
    smem = pl.BlockSpec(memory_space=pltpu.SMEM)
    return pl.pallas_call(
        kernel,
        name=name,
        out_shape=outputs,
        in_specs=[smem] * len(scalars) + [given] * len(inputs),
        out_specs=[vmem] * len(outputs),
        scratch_shapes=scratch,
        cost_estimate=cost,
        compiler_params=pltpu.CompilerParams(vmem_limit_bytes=VMEM_LIMIT),
    )(*scalars, *inputs)


def body(camera_jacobian, point_jacobian, residual, observed_slot, observed_point, send_list):
    sizes = Sizes(lax.axis_size("pts"), lax.axis_size("cams"), send_list.shape[2], camera_jacobian.shape[1])
    axes = ("pts", "cams")
    rows = sizes.rows
    slot = observed_slot.reshape(rows, LANES)
    point = observed_point.reshape(rows, LANES)
    column = lax.axis_index("cams").astype(jnp.int32).reshape(1)

    def exchange(messages):
        width = messages.size // sizes.devices
        flat = messages.reshape(sizes.devices, 1, width)
        return lax.all_to_all(flat, axes, split_axis=0, concat_axis=0, tiled=True).reshape(messages.shape)

    def flipped(value, flip):
        return lax.ppermute(value, "pts", [(p, p ^ flip) for p in range(sizes.pts)])

    def factors(high_rows, low_rows, entries):
        return [pltpu.VMEM((high_rows, entries), bf16), pltpu.VMEM((low_rows, entries), bf16)]

    point_table = shape(3, PT_ROWS, LANES)
    owned = shape(CP, sizes.own_rows, LANES)
    messages = shape(sizes.devices * sizes.message, LANES)
    scalar = shape(SUB, LANES)
    owned_scratch = pltpu.VMEM((CP, sizes.own_rows, LANES), f32)
    point_scratch = pltpu.VMEM((3, PT_ROWS, LANES), f32)
    entries = sizes.pts * LANES

    def parts_scratch(count):
        return pltpu.VMEM((count * SUB, LANES), f32)


    given = [
        pltpu.with_memory_space_constraint(value, pltpu.HBM)
        for value in (camera_jacobian, point_jacobian, residual, slot, point, send_list[0])
    ]
    first, a, b, inverse, gradient, place_point, place_slot = call(
        functools.partial(setup_kernel, sizes),
        "setup",
        given,
        [
            shape(sizes.devices * sizes.first_message, LANES),
            shape(2 * CP * rows, LANES),
            shape(6 * rows, LANES),
            shape(6, PT_ROWS, LANES),
            point_table,
            shape(PT_LO, sizes.obs, dtype=bf16),
            shape(LANES, sizes.obs, dtype=bf16),
        ],
        [pltpu.VMEM((2 * rows, LANES), f32), point_scratch, parts_scratch(2 * CP * PIECES)]
        + [pltpu.VMEM((max(spread_rows(6 * FINE + 3 * PIECES, PT_HI), spread_rows(2 * CP * PIECES, sizes.pts)), sizes.obs), bf16)]
        + [pltpu.VMEM((LANES, sizes.cams * sizes.slot), bf16)]
        + [pltpu.VMEM(value.shape, value.dtype) for value in given]
        + [pltpu.SemaphoreType.DMA((len(given),))],
        inputs_at=pl.ANY,
    )
    out, entry, precondition, remainder = call(
        functools.partial(first_owner_kernel, sizes),
        "first_owner",
        [exchange(first)],
        [messages, shape(sizes.pts, LANES, dtype=jnp.int32), owned, owned],
        [owned_scratch] + factors(spread_rows(2 * CP * PIECES, sizes.own_rows), LANES, entries),
        scalars=[column],
    )
    schur_scratch = [pltpu.VMEM((2 * rows, LANES), f32), point_scratch, parts_scratch(CP * PIECES)]
    schur_scratch += [pltpu.VMEM((max(spread_rows(3 * PIECES, PT_HI), spread_rows(CP * PIECES, sizes.pts)), sizes.obs), bf16)]
    at_slot = shape(CP, sizes.pts, LANES)
    product = slots = direction = step = sums = solution_ = None
    for iteration in range(ITERS):
        start, last = iteration == 0, iteration == ITERS - 1
        earlier = [] if start else [product, slots, direction, step, sums]
        if last:
            neighbour = flipped(fields, NEAR)
        arrived = exchange(out)
        if last:
            (both,) = call(
                functools.partial(tail_kernel, sizes),
                "tail",
                [arrived, product, fields, neighbour],
                [shape(4 * CP * sizes.own_rows, LANES)],
                [],
            )
            flips = [1 << bit for bit in range(sizes.pts.bit_length() - 1) if 1 << bit != NEAR]
            flips = flips[1:] + flips[:1]
            early = {flip: flipped(both, flip) for flip in (flips[0], flips[-1])}
        results = call(
            functools.partial(schur_kernel, sizes, start, last),
            "schur_last" if last else "schur",
            [arrived, a, b, inverse, slot, point, place_point, place_slot, precondition, remainder, gradient]
            + earlier,
            [shape(sizes.devices, LANES) if last else messages, scalar, at_slot, owned, point_table]
            + ([] if start else [point_table]),
            schur_scratch,
            cost=pl.CostEstimate(flops=2_000_000_000, bytes_accessed=10_000_000, transcendentals=0),
        )
        out, product, slots, direction, sums = results[:5]
        if not start:
            gradient = results[5]
        if last:
            early[flips[0]], out = lax.optimization_barrier((early[flips[0]], out))
            gathered, masks = [both], [(0, NEAR)]
            for flip in flips:
                gathered += [early[flip] if value is both and flip in early else flipped(value, flip) for value in gathered]
                masks += [tuple(mask ^ flip for mask in pair) for pair in masks]
            break
        final = iteration == ITERS - 2
        out, remainder, solution_, step, *rest = call(
            functools.partial(owner_kernel, sizes, start, final),
            "owner_final" if final else "owner",
            [exchange(out), entry, precondition, remainder, direction, product] + ([] if start else [solution_]),
            [messages, owned, owned, scalar] + ([shape(3 * CP * sizes.own_rows, LANES)] if final else []),
            [owned_scratch] + factors(spread_rows(CP * PIECES, sizes.own_rows), LANES, entries),
        )
        fields = rest[0] if final else None
    return call(
        functools.partial(final_kernel, sizes, masks),
        "final",
        [exchange(out), product, inverse, gradient, sums] + gathered,
        [shape(CP, CAM_OWN), shape(3, PT_DEV)],
        [pltpu.VMEM((3 * PT_ROWS, LANES), f32)],
        scalars=[lax.axis_index("pts").astype(jnp.int32).reshape(1)],
    )


def solution(mesh):
    return jax.shard_map(
        lambda *arguments: tuple(body(*arguments)),
        mesh=mesh,
        in_specs=(
            P(None, ("pts", "cams")),
            P(None, ("pts", "cams")),
            P(None, ("pts", "cams")),
            P(("pts", "cams")),
            P(("pts", "cams")),
            P(("pts", "cams"), None, None),
        ),
        out_specs=(P(None, "cams"), P(None, ("pts", "cams"))),
        check_vma=False,
    )
```

```python
import functools

import jax
import jax.numpy as jnp
from jax import lax
from jax.experimental import pallas as pl
from jax.experimental.pallas import tpu as pltpu
from jax.sharding import PartitionSpec as P

CP = 9
CAM_OWN = 8192
PT_DEV = 4096
ITERS = 3
LANES = 128
SUB = 8
PT_LO = 256
PT_HI = PT_DEV // PT_LO
PIECES = 2
FINE = 3
NEAR = 2
VMEM_LIMIT = 24 * 1024 * 1024

damping_camera = 1.0
damping_point = 1.0

f32 = jnp.float32
bf16 = jnp.bfloat16


class Sizes:
    def __init__(self, pts, cams, slot, obs):
        self.pts, self.cams, self.slot, self.obs = pts, cams, slot, obs
        self.devices = pts * cams
        self.block = slot // pts
        assert cams * self.block == LANES and LANES % pts == 0
        self.rows = obs // LANES
        self.run = CAM_OWN // pts
        self.run_rows = self.run // LANES
        self.own_rows = max(SUB, self.run_rows)
        self.groups = -(-CP // cams)
        self.first_groups = -(-2 * CP // cams)
        self.message = self.groups
        self.first_message = self.first_groups + 1
        assert self.groups * cams > CP


def sub_iota(rows):
    return lax.broadcasted_iota(jnp.int32, (rows, LANES), 0)


def lane_iota(rows):
    return lax.broadcasted_iota(jnp.int32, (rows, LANES), 1)


def cut(value, pieces=PIECES):
    parts = []
    for _ in range(pieces - 1):
        part = value.astype(bf16).astype(f32)
        parts.append(part)
        value = value - part
    parts.append(value)
    return parts


def swap_blocks(rows, block, wanted):
    which = lane_iota(rows[0].shape[0]) // block
    result = []
    for q in range(wanted):
        total = None
        for c, value in enumerate(rows):
            shift = ((c - q) * block) % LANES
            moved = pltpu.roll(value, shift, axis=1) if shift else value
            total = jnp.where(which == c, moved, 0.0 if total is None else total)
        result.append(total)
    return result


def gather_rows(row, count, high, low, comps):
    result = [None] * comps
    for k in range(count):
        here = high == k
        for c in range(comps):
            source = jnp.broadcast_to(row(c, k), high.shape)
            found = jnp.take_along_axis(source, low, axis=1, mode="promise_in_bounds")
            result[c] = found if k == 0 else jnp.where(here, found, result[c])
    return result


def matmul_gather(group, tables, place_ref, high_of_row, high_count, picked_ref, found_ref):
    pieces = [piece for table in tables for piece in cut(table)]
    left = jnp.concatenate(pieces, axis=0).astype(bf16)
    rows = len(pieces) * high_count
    columns = pl.ds(pl.multiple_of(group * SUB * LANES, SUB * LANES), SUB * LANES)
    picked = jnp.dot(left, place_ref[:, columns], preferred_element_type=f32)
    for s in range(SUB):
        mask = jnp.broadcast_to(high_of_row(group * SUB + s), (high_count, LANES)) == sub_iota(high_count)
        mask = jnp.concatenate([mask.astype(f32)] * len(pieces), axis=0) > 0.5
        lanes = slice(s * LANES, (s + 1) * LANES)
        picked_ref[:rows, lanes] = jnp.where(mask, picked[:, lanes], 0.0).astype(bf16)
    padded = -(-len(tables) // SUB) * SUB
    owner = lax.broadcasted_iota(jnp.int32, (padded, rows), 1) // (PIECES * high_count)
    chosen = (owner == lax.broadcasted_iota(jnp.int32, (padded, rows), 0)).astype(f32).astype(bf16)
    total = jnp.dot(chosen, picked_ref[:rows, :], preferred_element_type=f32)
    for s in range(SUB):
        found_ref[s * padded : (s + 1) * padded, :] = total[:, s * LANES : (s + 1) * LANES]
    return [found_ref[pl.ds(c, SUB, stride=padded), :] for c in range(len(tables))]


def spread_row(index, parts, high, high_count, spread_ref):
    columns = pl.ds(pl.multiple_of(index * LANES, LANES), LANES)
    mask = jnp.broadcast_to(high, (high_count, LANES)) == sub_iota(high_count)
    together = max(1, 16 // high_count)
    for start in range(0, len(parts), together):
        pieces = [
            jnp.where(mask, jnp.broadcast_to(part, (high_count, LANES)), 0.0)
            for part in parts[start : start + together]
        ]
        while len(pieces) < together:
            pieces.append(jnp.zeros((high_count, LANES), f32))
        tile = pieces[0] if together == 1 else jnp.concatenate(pieces, axis=0)
        spread_ref[start * high_count : start * high_count + tile.shape[0], columns] = tile.astype(bf16)


def place_row(index, low, low_count, place_ref):
    columns = pl.ds(pl.multiple_of(index * LANES, LANES), LANES)
    place = jnp.broadcast_to(low, (low_count, LANES)) == sub_iota(low_count)
    place_ref[:low_count, columns] = jnp.where(place, 1.0, 0.0).astype(bf16)


def keep_parts(parts, parts_ref):
    for k, part in enumerate(parts):
        parts_ref[k * SUB : (k + 1) * SUB, :] = part


def part_rows(count, s, parts_ref):
    return [parts_ref[k * SUB + s : k * SUB + s + 1, :] for k in range(count)]


def spread_rows(parts, high_count):
    return -(-parts * high_count // 16) * 16


def scatter(parts, entries, high_count, low_count, spread_ref, place_ref):
    rows = spread_rows(parts, high_count)
    return lax.dot_general(
        spread_ref[:rows, :entries],
        place_ref[:low_count, :entries],
        (((1,), (1,)), ((), ())),
        preferred_element_type=f32,
    )


def joined(result, count, high_count, pieces=None):
    pieces = pieces or [PIECES] * count
    values, first = [], 0
    for number in pieces:
        rows = [result[first + k * high_count : first + (k + 1) * high_count] for k in range(number)]
        first += number * high_count
        total = rows[-1]
        for row in reversed(rows[:-1]):
            total = total + row
        values.append(total)
    return values


def slot_place(slot, sizes):
    within = slot % sizes.slot
    return within % sizes.pts, (slot // sizes.slot) * sizes.block + within // sizes.pts


def solve(inverse, values):
    first = inverse[0] * values[0] + inverse[1] * values[1] + inverse[2] * values[2]
    second = inverse[1] * values[0] + inverse[3] * values[1] + inverse[4] * values[2]
    third = inverse[2] * values[0] + inverse[4] * values[1] + inverse[5] * values[2]
    return first, second, third


def write_messages(fields, scalar, groups, message, out_ref, sizes, extra=None):
    which = lane_iota(sizes.pts) // sizes.block
    for g in range(groups):
        rows = fields[g * sizes.cams : (g + 1) * sizes.cams]
        moved = swap_partial(rows, sizes)
        for c in range(sizes.cams):
            value = moved[c]
            if g == groups - 1 and scalar is not None:
                value = jnp.where(which == sizes.cams - 1, scalar, value)
            out_ref[pl.ds(c * message + g, sizes.pts, stride=sizes.cams * message), :] = value
    for g in range(groups, message):
        for c in range(sizes.cams):
            value = extra if (extra is not None and g == groups) else jnp.zeros((sizes.pts, LANES), f32)
            out_ref[pl.ds(c * message + g, sizes.pts, stride=sizes.cams * message), :] = value


def swap_partial(rows, sizes):
    return swap_blocks(rows, sizes.block, sizes.cams)


def read_row(in_ref, c, g, message, sizes):
    return in_ref[pl.ds(c * message + g, sizes.pts, stride=sizes.cams * message), :]


def read_messages(in_ref, count, message, sizes):
    fields = []
    group = 0
    while len(fields) < count:
        rows = [read_row(in_ref, c, group, message, sizes) for c in range(sizes.cams)]
        fields += swap_blocks(rows, sizes.block, min(sizes.cams, count - len(fields)))
        group += 1
    return fields


def read_scalar(in_ref, groups, message, sizes):
    total = read_row(in_ref, 0, groups - 1, message, sizes)
    for c in range(1, sizes.cams):
        total = total + read_row(in_ref, c, groups - 1, message, sizes)
    chosen = jnp.where(lane_iota(sizes.pts) == LANES - 1, total, 0.0)
    return jnp.sum(chosen, keepdims=True)


def setup_kernel(sizes, *refs):
    sources, refs = refs[:6], refs[6:]
    out_ref, a_ref, b_ref, inv_ref, grad_ref, place_point_ref, place_slot_ref = refs[:7]
    new_slot_ref, new_point_ref = refs[7:9]
    r_ref, table_ref, parts_ref, spread_ref, place_list_ref, picked_ref, found_ref = refs[9:16]
    jac_ref, pjac_ref, res_ref, slot_ref, point_ref, list_ref = refs[16:22]
    semaphores = refs[22]
    rows = sizes.rows
    copies = [
        pltpu.make_async_copy(source, target, semaphores.at[k])
        for k, (source, target) in enumerate(zip(sources, refs[16:22]))
    ]
    for copy in copies:
        copy.start()
    for copy in copies:
        copy.wait()
    new_slot_ref[...] = slot_ref[...]
    new_point_ref[...] = point_ref[...]
    for j in range(rows):
        columns = slice(j * LANES, (j + 1) * LANES)
        for start in range(0, 2 * CP, SUB):
            size = min(SUB, 2 * CP - start)
            a_ref[pl.ds(start * rows + j, size, stride=rows), :] = jac_ref[start : start + size, columns]
        b_ref[pl.ds(j, 6, stride=rows), :] = pjac_ref[:, columns]
        r_ref[pl.ds(j, 2, stride=rows), :] = res_ref[:, columns]

    def at(ref, comp, group):
        return ref[pl.ds(pl.multiple_of(comp * rows + group * SUB, SUB), SUB), :]

    normal_pieces = [FINE] * 6 + [PIECES] * 3

    def first(group, carry):
        b = [at(b_ref, k, group) for k in range(6)]
        r = [at(r_ref, k, group) for k in range(2)]
        values = [b[i] * b[j] + b[3 + i] * b[3 + j] for i, j in ((0, 0), (0, 1), (0, 2), (1, 1), (1, 2), (2, 2))]
        values += [b[i] * r[0] + b[3 + i] * r[1] for i in range(3)]
        parts = [part for value, pieces in zip(values, normal_pieces) for part in cut(value, pieces)]
        keep_parts(parts, parts_ref)
        for s in range(SUB):
            row = group * SUB + s
            point = point_ref[pl.ds(row, 1), :]
            spread_row(row, part_rows(len(parts), s, parts_ref), point >> 8, PT_HI, spread_ref)
            place_row(row, point & (PT_LO - 1), PT_LO, place_point_ref)
        return carry

    lax.fori_loop(0, rows // SUB, first, 0)
    result = scatter(sum(normal_pieces), sizes.obs, PT_HI, PT_LO, spread_ref, place_point_ref)
    normal = joined(result, 9, PT_HI, normal_pieces)
    top_left = normal[0] + damping_point
    top_mid = normal[1]
    top_right = normal[2]
    mid_mid = normal[3] + damping_point
    mid_right = normal[4]
    low_right = normal[5] + damping_point
    adjugate = [
        mid_mid * low_right - mid_right * mid_right,
        top_right * mid_right - top_mid * low_right,
        top_mid * mid_right - top_right * mid_mid,
        top_left * low_right - top_right * top_right,
        top_mid * top_right - top_left * mid_right,
        top_left * mid_mid - top_mid * top_mid,
    ]
    determinant = top_left * adjugate[0] + top_mid * adjugate[1] + top_right * adjugate[2]
    inverse = [value / determinant for value in adjugate]
    for k in range(6):
        inv_ref[k] = inverse[k]
    for k in range(3):
        grad_ref[k] = normal[6 + k]
    eliminated = solve(inverse, normal[6:])
    for k in range(3):
        table_ref[k] = eliminated[k]

    def second(group, carry):
        at_point = matmul_gather(group, [table_ref[k] for k in range(3)], place_point_ref,
                                 lambda row: point_ref[pl.ds(row, 1), :] >> 8, PT_HI, picked_ref, found_ref)
        b = [at(b_ref, k, group) for k in range(6)]
        errors = [at(r_ref, i, group) - sum(b[3 * i + k] * at_point[k] for k in range(3)) for i in range(2)]
        a = [at(a_ref, k, group) for k in range(2 * CP)]
        values = [a[k] * errors[0] + a[CP + k] * errors[1] for k in range(CP)]
        values += [a[k] * a[k] + a[CP + k] * a[CP + k] for k in range(CP)]
        parts = [part for value in values for part in cut(value)]
        keep_parts(parts, parts_ref)
        for s in range(SUB):
            row = group * SUB + s
            high, low = slot_place(slot_ref[pl.ds(row, 1), :], sizes)
            spread_row(row, part_rows(len(parts), s, parts_ref), high, sizes.pts, spread_ref)
            place_row(row, low, LANES, place_slot_ref)
        return carry

    lax.fori_loop(0, rows // SUB, second, 0)
    result = scatter(2 * CP * PIECES, sizes.obs, sizes.pts, LANES, spread_ref, place_slot_ref)
    fields = joined(result, 2 * CP, sizes.pts)

    pieces = sizes.slot // LANES
    lane = lane_iota(1)
    for c in range(sizes.cams):
        for half in range(pieces):
            value = list_ref[c : c + 1, half * LANES : (half + 1) * LANES]
            low = c * sizes.block + half * (LANES // sizes.pts) + lane // sizes.pts
            parts = [(value >> 8).astype(f32), (value & 255).astype(f32)]
            spread_row(c * pieces + half, parts, lane % sizes.pts, sizes.pts, spread_ref)
            place_row(c * pieces + half, low, LANES, place_list_ref)
    result = scatter(2, sizes.cams * sizes.slot, sizes.pts, LANES, spread_ref, place_list_ref)
    listed = result[: sizes.pts] * 256.0 + result[sizes.pts : 2 * sizes.pts]
    write_messages(fields, None, sizes.first_groups, sizes.first_message, out_ref, sizes, extra=listed)


def entries_scatter(fields, entry, sizes, spread_ref, place_ref):
    high, low = entry // LANES, entry % LANES
    parts = [part for value in fields for part in cut(value)]
    for p in range(sizes.pts):
        spread_row(p, [part[p : p + 1] for part in parts], high[p : p + 1], sizes.own_rows, spread_ref)
        place_row(p, low[p : p + 1], LANES, place_ref)
    result = scatter(len(parts), sizes.pts * LANES, sizes.own_rows, LANES, spread_ref, place_ref)
    return joined(result, len(fields), sizes.own_rows)


def send_owned(scaled, partial, entry, out_ref, table_ref, sizes):
    for k in range(CP):
        table_ref[k] = scaled[k]
    fields = gather_rows(lambda c, k: table_ref[c, k : k + 1, :], sizes.run_rows, entry // LANES, entry % LANES, CP)
    write_messages(fields, partial, sizes.groups, sizes.message, out_ref, sizes)


def dot_fields(left, right):
    return jnp.sum(sum(a * b for a, b in zip(left, right)), keepdims=True)


def first_owner_kernel(sizes, column_ref, in_ref, out_ref, entry_ref, pre_ref, rem_ref,
                       table_ref, spread_ref, place_ref):
    listed = jnp.zeros((sizes.pts, LANES), f32)
    for c in range(sizes.cams):
        row = read_row(in_ref, c, sizes.first_groups, sizes.first_message, sizes)
        listed = jnp.where(column_ref[0] == c, row, listed)
    entry = listed.astype(jnp.int32) % sizes.run
    entry_ref[...] = entry
    fields = read_messages(in_ref, 2 * CP, sizes.first_message, sizes)
    sums = entries_scatter(fields, entry, sizes, spread_ref, place_ref)
    remainder = [-value for value in sums[:CP]]
    precondition = [1.0 / (value + damping_camera) for value in sums[CP:]]
    scaled = [p * r for p, r in zip(precondition, remainder)]
    for k in range(CP):
        pre_ref[k] = precondition[k]
        rem_ref[k] = remainder[k]
    send_owned(scaled, dot_fields(remainder, scaled), entry, out_ref, table_ref, sizes)


def owner_kernel(sizes, start, final, in_ref, entry_ref, pre_ref, rem_ref, dir_ref, product_ref, *refs):
    refs = list(refs)
    sol_ref = None if start else refs.pop(0)
    out_ref, new_rem_ref, new_sol_ref, step_ref = refs[:4]
    fields_ref = refs[4] if final else None
    table_ref, spread_ref, place_ref = refs[-3:]
    entry = entry_ref[...]
    fields = read_messages(in_ref, CP, sizes.message, sizes)
    curvature = read_scalar(in_ref, sizes.groups, sizes.message, sizes)
    step = product_ref[...] / jnp.broadcast_to(curvature, (SUB, LANES))
    step_ref[...] = step
    sums = entries_scatter(fields, entry, sizes, spread_ref, place_ref)
    remainder, scaled = [], []
    for k in range(CP):
        direction = dir_ref[k]
        moved = step[:1] * direction
        moved = moved if start else sol_ref[k] + moved
        new_sol_ref[k] = moved
        value = rem_ref[k] - step[:1] * (sums[k] + damping_camera * direction)
        new_rem_ref[k] = value
        remainder.append(value)
        scaled.append(pre_ref[k] * value)
        if final:
            for j, field in enumerate((moved, direction, scaled[k])):
                first = (j * CP + k) * sizes.own_rows
                fields_ref[first : first + sizes.own_rows, :] = field
    send_owned(scaled, dot_fields(remainder, scaled), entry, out_ref, table_ref, sizes)


def schur_kernel(sizes, start, last, in_ref, a_ref, b_ref, inv_ref, slot_ref, point_ref,
                 place_point_ref, place_slot_ref, pre_ref, rem_ref, grad_ref, *refs):
    refs = list(refs)
    if not start:
        product_ref, at_slot_ref, dir_ref, step_ref, sum_ref = refs[:5]
        refs = refs[5:]
    out_ref, new_product_ref, new_at_slot_ref, new_dir_ref, new_sum_ref = refs[:5]
    new_grad_ref = None
    refs = refs[5:]
    if not start:
        new_grad_ref = refs.pop(0)
    q_ref, table_ref, parts_ref, spread_ref, picked_ref, found_ref = refs
    rows = sizes.rows

    def at(ref, comp, group):
        return ref[pl.ds(pl.multiple_of(comp * rows + group * SUB, SUB), SUB), :]

    renewed = jnp.broadcast_to(read_scalar(in_ref, sizes.groups, sizes.message, sizes), (SUB, LANES))
    new_product_ref[...] = renewed
    fields = read_messages(in_ref, CP, sizes.message, sizes)
    beta = None if start else (renewed / product_ref[...])[:1]
    squares = None
    for k in range(CP):
        direction = pre_ref[k] * rem_ref[k]
        if start:
            new_at_slot_ref[k] = fields[k]
        else:
            new_at_slot_ref[k] = fields[k] + beta * at_slot_ref[k]
            direction = direction + beta * dir_ref[k]
        new_dir_ref[k] = direction
        squares = direction * direction if squares is None else squares + direction * direction

    def first(group, carry):
        gathered = matmul_gather(group, [new_at_slot_ref[k] for k in range(CP)], place_slot_ref,
                                 lambda row: slot_place(slot_ref[pl.ds(row, 1), :], sizes)[0], sizes.pts,
                                 picked_ref, found_ref)
        q = [sum(at(a_ref, i * CP + k, group) * gathered[k] for k in range(CP)) for i in range(2)]
        for i in range(2):
            q_ref[pl.ds(pl.multiple_of(i * rows + group * SUB, SUB), SUB), :] = q[i]
        values = [at(b_ref, k, group) * q[0] + at(b_ref, 3 + k, group) * q[1] for k in range(3)]
        parts = [part for value in values for part in cut(value)]
        keep_parts(parts, parts_ref)
        for s in range(SUB):
            row = group * SUB + s
            spread_row(row, part_rows(len(parts), s, parts_ref), point_ref[pl.ds(row, 1), :] >> 8, PT_HI, spread_ref)
        return carry

    lax.fori_loop(0, rows // SUB, first, 0)
    result = scatter(3 * PIECES, sizes.obs, PT_HI, PT_LO, spread_ref, place_point_ref)
    sums = joined(result, 3, PT_HI)
    folded = solve([inv_ref[k] for k in range(6)], sums)
    for k in range(3):
        table_ref[k] = folded[k]
        new_sum_ref[k] = sums[k]
        if not start:
            new_grad_ref[k] = grad_ref[k] + step_ref[:1, :1] * sum_ref[k]

    def second(group, inner):
        at_point = matmul_gather(group, [table_ref[k] for k in range(3)], place_point_ref,
                                 lambda row: point_ref[pl.ds(row, 1), :] >> 8, PT_HI, picked_ref, found_ref)
        q = [at(q_ref, i, group) for i in range(2)]
        errors = [q[i] - sum(at(b_ref, 3 * i + k, group) * at_point[k] for k in range(3)) for i in range(2)]
        inner = inner + q[0] * errors[0] + q[1] * errors[1]
        if not last:
            values = [at(a_ref, k, group) * errors[0] + at(a_ref, CP + k, group) * errors[1] for k in range(CP)]
            parts = [part for value in values for part in cut(value)]
            keep_parts(parts, parts_ref)
            for s in range(SUB):
                row = group * SUB + s
                high, _ = slot_place(slot_ref[pl.ds(row, 1), :], sizes)
                spread_row(row, part_rows(len(parts), s, parts_ref), high, sizes.pts, spread_ref)
        return inner

    inner = lax.fori_loop(0, rows // SUB, second, jnp.zeros((SUB, LANES), f32))
    partial = jnp.sum(inner, keepdims=True) + damping_camera * jnp.sum(squares, keepdims=True)
    if last:
        out_ref[...] = jnp.broadcast_to(partial, (sizes.devices, LANES))
        return
    result = scatter(CP * PIECES, sizes.obs, sizes.pts, LANES, spread_ref, place_slot_ref)
    fields = joined(result, CP, sizes.pts)
    write_messages(fields, partial, sizes.groups, sizes.message, out_ref, sizes)


def tail_kernel(sizes, in_ref, product_ref, own_ref, other_ref, out_ref):
    renewed = jnp.broadcast_to(read_scalar(in_ref, sizes.groups, sizes.message, sizes), (SUB, LANES))
    beta = (renewed / product_ref[...])[:1]
    field = CP * sizes.own_rows
    for j, ref in enumerate((own_ref, other_ref)):
        first = j * 2 * field
        out_ref[first : first + field, :] = ref[:field, :]
        out_ref[first + field : first + 2 * field, :] = ref[2 * field :, :] + beta * ref[field : 2 * field, :]


def final_kernel(sizes, masks, run_ref, in_ref, product_ref, inv_ref, grad_ref, sum_ref, *refs):
    all_refs = refs[: len(masks)]
    cam_ref, pt_ref, table_ref = refs[len(masks) :]
    curvature = jnp.sum(jnp.where(lane_iota(sizes.devices) == 0, in_ref[...], 0.0), keepdims=True)
    step = (product_ref[...] / jnp.broadcast_to(curvature, (SUB, LANES)))[:1]
    for all_ref, pair in zip(all_refs, masks):
        for j, mask in enumerate(pair):
            base_column = (run_ref[0] ^ mask) * sizes.run
            for h in range(sizes.run_rows):
                columns = pl.ds(pl.multiple_of(base_column + h * LANES, LANES), LANES)
                for start in range(0, CP, SUB):
                    size = min(SUB, CP - start)
                    first = (j * 2 * CP + start) * sizes.own_rows + h
                    base = all_ref[pl.ds(first, size, stride=sizes.own_rows), :]
                    direction = all_ref[pl.ds(first + CP * sizes.own_rows, size, stride=sizes.own_rows), :]
                    cam_ref[start : start + size, columns] = base + step * direction
    total = [grad_ref[k] + step[:, :1] * sum_ref[k] for k in range(3)]
    solved = solve([inv_ref[k] for k in range(6)], total)
    for k in range(3):
        table_ref[k * PT_HI : (k + 1) * PT_HI, :] = -solved[k]
    for row in range(PT_HI):
        for k in range(3):
            pt_ref[k : k + 1, row * PT_LO : (row + 1) * PT_LO] = table_ref[k * PT_HI + row : k * PT_HI + row + 1, :]


def shape(*dims, dtype=f32):
    return jax.ShapeDtypeStruct(dims, dtype)


def kept(*dims, dtype=f32):
    return pltpu.VMEM(dims, dtype)


def call(kernel, name, inputs, outputs, scratch, scalars=(), inputs_at=pltpu.VMEM, cost=None):
    vmem = pl.BlockSpec(memory_space=pltpu.VMEM)
    given = pl.BlockSpec(memory_space=inputs_at)
    smem = pl.BlockSpec(memory_space=pltpu.SMEM)
    return pl.pallas_call(
        kernel,
        name=name,
        out_shape=outputs,
        in_specs=[smem] * len(scalars) + [given] * len(inputs),
        out_specs=[vmem] * len(outputs),
        scratch_shapes=scratch,
        cost_estimate=cost,
        compiler_params=pltpu.CompilerParams(vmem_limit_bytes=VMEM_LIMIT),
    )(*scalars, *inputs)


def body(camera_jacobian, point_jacobian, residual, observed_slot, observed_point, send_list):
    sizes = Sizes(lax.axis_size("pts"), lax.axis_size("cams"), send_list.shape[2], camera_jacobian.shape[1])
    axes = ("pts", "cams")
    rows = sizes.rows
    slot = observed_slot.reshape(rows, LANES)
    point = observed_point.reshape(rows, LANES)
    column = lax.axis_index("cams").astype(jnp.int32).reshape(1)

    def exchange(messages):
        width = messages.size // sizes.devices
        flat = messages.reshape(sizes.devices, 1, width)
        return lax.all_to_all(flat, axes, split_axis=0, concat_axis=0, tiled=True).reshape(messages.shape)

    def flipped(value, flip):
        return lax.ppermute(value, "pts", [(p, p ^ flip) for p in range(sizes.pts)])

    def factors(high_rows, low_rows, entries):
        return [pltpu.VMEM((high_rows, entries), bf16), pltpu.VMEM((low_rows, entries), bf16)]

    point_table = kept(3, PT_HI, PT_LO)
    owned = kept(CP, sizes.own_rows, LANES)
    messages = kept(sizes.devices * sizes.message, LANES)
    scalar = kept(SUB, LANES)
    owned_scratch = pltpu.VMEM((CP, sizes.own_rows, LANES), f32)
    point_scratch = pltpu.VMEM((3, PT_HI, PT_LO), f32)
    entries = sizes.pts * LANES

    picked_rows = max(CP * PIECES * sizes.pts, 3 * PIECES * PT_HI)
    gather_scratch = [pltpu.VMEM((picked_rows, SUB * LANES), bf16), pltpu.VMEM((2 * SUB * SUB, LANES), f32)]

    def parts_scratch(count):
        return pltpu.VMEM((count * SUB, LANES), f32)


    given = [
        pltpu.with_memory_space_constraint(value, pltpu.HBM)
        for value in (camera_jacobian, point_jacobian, residual, slot, point, send_list[0])
    ]
    first, a, b, inverse, gradient, place_point, place_slot, slot, point = call(
        functools.partial(setup_kernel, sizes),
        "setup",
        given,
        [
            kept(sizes.devices * sizes.first_message, LANES),
            kept(2 * CP * rows, LANES),
            kept(6 * rows, LANES),
            kept(6, PT_HI, PT_LO),
            point_table,
            kept(PT_LO, sizes.obs, dtype=bf16),
            kept(LANES, sizes.obs, dtype=bf16),
            kept(rows, LANES, dtype=jnp.int32),
            kept(rows, LANES, dtype=jnp.int32),
        ],
        [pltpu.VMEM((2 * rows, LANES), f32), point_scratch, parts_scratch(2 * CP * PIECES)]
        + [pltpu.VMEM((max(spread_rows(6 * FINE + 3 * PIECES, PT_HI), spread_rows(2 * CP * PIECES, sizes.pts)), sizes.obs), bf16)]
        + [pltpu.VMEM((LANES, sizes.cams * sizes.slot), bf16)]
        + gather_scratch
        + [pltpu.VMEM(value.shape, value.dtype) for value in given]
        + [pltpu.SemaphoreType.DMA((len(given),))],
        inputs_at=pl.ANY,
    )
    out, entry, precondition, remainder = call(
        functools.partial(first_owner_kernel, sizes),
        "first_owner",
        [exchange(first)],
        [messages, kept(sizes.pts, LANES, dtype=jnp.int32), owned, owned],
        [owned_scratch] + factors(spread_rows(2 * CP * PIECES, sizes.own_rows), LANES, entries),
        scalars=[column],
    )
    schur_scratch = [pltpu.VMEM((2 * rows, LANES), f32), point_scratch, parts_scratch(CP * PIECES)]
    schur_scratch += [pltpu.VMEM((max(spread_rows(3 * PIECES, PT_HI), spread_rows(CP * PIECES, sizes.pts)), sizes.obs), bf16)]
    schur_scratch += gather_scratch
    at_slot = kept(CP, sizes.pts, LANES)
    product = slots = direction = step = sums = solution_ = None
    for iteration in range(ITERS):
        start, last = iteration == 0, iteration == ITERS - 1
        earlier = [] if start else [product, slots, direction, step, sums]
        if last:
            neighbour = flipped(fields, NEAR)
        arrived = exchange(out)
        if last:
            (both,) = call(
                functools.partial(tail_kernel, sizes),
                "tail",
                [arrived, product, fields, neighbour],
                [kept(4 * CP * sizes.own_rows, LANES)],
                [],
            )
            flips = [1 << bit for bit in range(sizes.pts.bit_length() - 1) if 1 << bit != NEAR]
            flips = flips[1:] + flips[:1]
            early = {flip: flipped(both, flip) for flip in (flips[0], flips[-1])}
        results = call(
            functools.partial(schur_kernel, sizes, start, last),
            "schur_last" if last else "schur",
            [arrived, a, b, inverse, slot, point, place_point, place_slot, precondition, remainder, gradient]
            + earlier,
            [kept(sizes.devices, LANES) if last else messages, scalar, at_slot, owned, point_table]
            + ([] if start else [point_table]),
            schur_scratch,
            cost=pl.CostEstimate(flops=2_000_000_000, bytes_accessed=10_000_000, transcendentals=0),
        )
        out, product, slots, direction, sums = results[:5]
        if not start:
            gradient = results[5]
        if last:
            early[flips[0]], out = lax.optimization_barrier((early[flips[0]], out))
            gathered, masks = [both], [(0, NEAR)]
            for flip in flips:
                gathered += [early[flip] if value is both and flip in early else flipped(value, flip) for value in gathered]
                masks += [tuple(mask ^ flip for mask in pair) for pair in masks]
            break
        final = iteration == ITERS - 2
        out, remainder, solution_, step, *rest = call(
            functools.partial(owner_kernel, sizes, start, final),
            "owner_final" if final else "owner",
            [exchange(out), entry, precondition, remainder, direction, product] + ([] if start else [solution_]),
            [messages, owned, owned, scalar] + ([kept(3 * CP * sizes.own_rows, LANES)] if final else []),
            [owned_scratch] + factors(spread_rows(CP * PIECES, sizes.own_rows), LANES, entries),
        )
        fields = rest[0] if final else None
    return call(
        functools.partial(final_kernel, sizes, masks),
        "final",
        [exchange(out), product, inverse, gradient, sums] + gathered,
        [shape(CP, CAM_OWN), shape(3, PT_DEV)],
        [pltpu.VMEM((3 * PT_HI, PT_LO), f32)],
        scalars=[lax.axis_index("pts").astype(jnp.int32).reshape(1)],
    )


def solution(mesh):
    return jax.shard_map(
        lambda *arguments: tuple(body(*arguments)),
        mesh=mesh,
        in_specs=(
            P(None, ("pts", "cams")),
            P(None, ("pts", "cams")),
            P(None, ("pts", "cams")),
            P(("pts", "cams")),
            P(("pts", "cams")),
            P(("pts", "cams"), None, None),
        ),
        out_specs=(P(None, "cams"), P(None, ("pts", "cams"))),
        check_vma=False,
    )
```

```python
import functools

import jax
import jax.numpy as jnp
from jax import lax
from jax.experimental import pallas as pl
from jax.experimental.pallas import tpu as pltpu
from jax.sharding import PartitionSpec as P

CP = 9
CAM_OWN = 8192
PT_DEV = 4096
ITERS = 3
LANES = 128
SUB = 8
PT_LO = 256
PT_HI = PT_DEV // PT_LO
PIECES = 2
FINE = 3
NEAR = 2
VMEM_LIMIT = 24 * 1024 * 1024

damping_camera = 1.0
damping_point = 1.0

f32 = jnp.float32
bf16 = jnp.bfloat16


class Sizes:
    def __init__(self, pts, cams, slot, obs):
        self.pts, self.cams, self.slot, self.obs = pts, cams, slot, obs
        self.devices = pts * cams
        self.block = slot // pts
        assert cams * self.block == LANES and LANES % pts == 0
        self.rows = obs // LANES
        self.run = CAM_OWN // pts
        self.run_rows = self.run // LANES
        self.own_rows = max(SUB, self.run_rows)
        self.groups = -(-CP // cams)
        self.first_groups = -(-2 * CP // cams)
        self.message = self.groups
        self.first_message = self.first_groups + 1
        assert self.groups * cams > CP


def sub_iota(rows):
    return lax.broadcasted_iota(jnp.int32, (rows, LANES), 0)


def lane_iota(rows):
    return lax.broadcasted_iota(jnp.int32, (rows, LANES), 1)


def cut(value, pieces=PIECES):
    parts = []
    for _ in range(pieces - 1):
        part = value.astype(bf16).astype(f32)
        parts.append(part)
        value = value - part
    parts.append(value)
    return parts


def swap_blocks(rows, block, wanted):
    which = lane_iota(rows[0].shape[0]) // block
    result = []
    for q in range(wanted):
        total = None
        for c, value in enumerate(rows):
            shift = ((c - q) * block) % LANES
            moved = pltpu.roll(value, shift, axis=1) if shift else value
            total = jnp.where(which == c, moved, 0.0 if total is None else total)
        result.append(total)
    return result


def gather_rows(row, count, high, low, comps):
    result = [None] * comps
    for k in range(count):
        here = high == k
        for c in range(comps):
            source = jnp.broadcast_to(row(c, k), high.shape)
            found = jnp.take_along_axis(source, low, axis=1, mode="promise_in_bounds")
            result[c] = found if k == 0 else jnp.where(here, found, result[c])
    return result


def gather_factors(tables):
    pieces = [piece for table in tables for piece in cut(table)]
    left = jnp.concatenate(pieces, axis=0).astype(bf16)
    padded, rows = -(-len(tables) // SUB) * SUB, left.shape[0]
    owner = lax.broadcasted_iota(jnp.int32, (padded, rows), 1) // (rows // len(tables))
    chosen = (owner == lax.broadcasted_iota(jnp.int32, (padded, rows), 0)).astype(f32).astype(bf16)
    return left, chosen


def matmul_gather(group, factors, count, place_ref, high_of_row, high_count, picked_ref, found_ref):
    left, chosen = factors
    rows, padded = left.shape[0], chosen.shape[0]
    width = SUB * LANES
    picked = jnp.dot(left, place_ref[:, group * width : (group + 1) * width], preferred_element_type=f32)
    for s in range(SUB):
        mask = jnp.broadcast_to(high_of_row(group * SUB + s), (high_count, LANES)) == sub_iota(high_count)
        for first in range(0, rows, high_count):
            block = picked[first : first + high_count, s * LANES : (s + 1) * LANES]
            columns = slice(group * width + s * LANES, group * width + (s + 1) * LANES)
            picked_ref[first : first + high_count, columns] = jnp.where(mask, block, 0.0).astype(bf16)
    total = jnp.dot(chosen, picked_ref[:rows, group * width : (group + 1) * width], preferred_element_type=f32)
    start = group * SUB * padded
    for s in range(SUB):
        found_ref[start + s * padded : start + (s + 1) * padded, :] = total[:, s * LANES : (s + 1) * LANES]
    return [found_ref[pl.ds(start + c, SUB, stride=padded), :] for c in range(count)]


def spread_row(index, parts, high, high_count, spread_ref):
    columns = slice(index * LANES, (index + 1) * LANES)
    mask = jnp.broadcast_to(high, (high_count, LANES)) == sub_iota(high_count)
    together = max(1, 16 // high_count)
    for start in range(0, len(parts), together):
        pieces = [
            jnp.where(mask, jnp.broadcast_to(part, (high_count, LANES)), 0.0)
            for part in parts[start : start + together]
        ]
        while len(pieces) < together:
            pieces.append(jnp.zeros((high_count, LANES), f32))
        tile = pieces[0] if together == 1 else jnp.concatenate(pieces, axis=0)
        spread_ref[start * high_count : start * high_count + tile.shape[0], columns] = tile.astype(bf16)


def place_row(index, low, low_count, place_ref):
    columns = slice(index * LANES, (index + 1) * LANES)
    place = jnp.broadcast_to(low, (low_count, LANES)) == sub_iota(low_count)
    place_ref[:low_count, columns] = jnp.where(place, 1.0, 0.0).astype(bf16)


def keep_parts(parts, group, parts_ref):
    for k, part in enumerate(parts):
        parts_ref[group, k * SUB : (k + 1) * SUB, :] = part


def part_rows(count, group, s, parts_ref):
    return [parts_ref[group, k * SUB + s : k * SUB + s + 1, :] for k in range(count)]


def spread_rows(parts, high_count):
    return -(-parts * high_count // 16) * 16


def scatter(parts, entries, high_count, low_count, spread_ref, place_ref):
    rows = spread_rows(parts, high_count)
    return lax.dot_general(
        spread_ref[:rows, :entries],
        place_ref[:low_count, :entries],
        (((1,), (1,)), ((), ())),
        preferred_element_type=f32,
    )


def joined(result, count, high_count, pieces=None):
    pieces = pieces or [PIECES] * count
    values, first = [], 0
    for number in pieces:
        rows = [result[first + k * high_count : first + (k + 1) * high_count] for k in range(number)]
        first += number * high_count
        total = rows[-1]
        for row in reversed(rows[:-1]):
            total = total + row
        values.append(total)
    return values


def slot_place(slot, sizes):
    within = slot % sizes.slot
    return within % sizes.pts, (slot // sizes.slot) * sizes.block + within // sizes.pts


def solve(inverse, values):
    first = inverse[0] * values[0] + inverse[1] * values[1] + inverse[2] * values[2]
    second = inverse[1] * values[0] + inverse[3] * values[1] + inverse[4] * values[2]
    third = inverse[2] * values[0] + inverse[4] * values[1] + inverse[5] * values[2]
    return first, second, third


def write_messages(fields, scalar, groups, message, out_ref, sizes, extra=None):
    which = lane_iota(sizes.pts) // sizes.block
    for g in range(groups):
        rows = fields[g * sizes.cams : (g + 1) * sizes.cams]
        moved = swap_partial(rows, sizes)
        for c in range(sizes.cams):
            value = moved[c]
            if g == groups - 1 and scalar is not None:
                value = jnp.where(which == sizes.cams - 1, scalar, value)
            out_ref[pl.ds(c * message + g, sizes.pts, stride=sizes.cams * message), :] = value
    for g in range(groups, message):
        for c in range(sizes.cams):
            value = extra if (extra is not None and g == groups) else jnp.zeros((sizes.pts, LANES), f32)
            out_ref[pl.ds(c * message + g, sizes.pts, stride=sizes.cams * message), :] = value


def swap_partial(rows, sizes):
    return swap_blocks(rows, sizes.block, sizes.cams)


def read_row(in_ref, c, g, message, sizes):
    return in_ref[pl.ds(c * message + g, sizes.pts, stride=sizes.cams * message), :]


def read_messages(in_ref, count, message, sizes):
    fields = []
    group = 0
    while len(fields) < count:
        rows = [read_row(in_ref, c, group, message, sizes) for c in range(sizes.cams)]
        fields += swap_blocks(rows, sizes.block, min(sizes.cams, count - len(fields)))
        group += 1
    return fields


def read_scalar(in_ref, groups, message, sizes):
    total = read_row(in_ref, 0, groups - 1, message, sizes)
    for c in range(1, sizes.cams):
        total = total + read_row(in_ref, c, groups - 1, message, sizes)
    chosen = jnp.where(lane_iota(sizes.pts) == LANES - 1, total, 0.0)
    return jnp.sum(chosen, keepdims=True)


def setup_kernel(sizes, *refs):
    sources, refs = refs[:6], refs[6:]
    out_ref, a_ref, b_ref, inv_ref, grad_ref, place_point_ref, new_slot_ref, new_point_ref = refs[:8]
    r_ref, parts_ref, spread_ref, picked_ref, found_ref, place_slot_ref, place_list_ref = refs[8:15]
    jac_ref, pjac_ref, res_ref, slot_ref, point_ref, list_ref = refs[15:21]
    semaphores = refs[21]
    rows = sizes.rows
    copies = [
        pltpu.make_async_copy(source, target, semaphores.at[k])
        for k, (source, target) in enumerate(zip(sources, refs[15:21]))
    ]
    for copy in copies:
        copy.start()
    for copy in copies:
        copy.wait()
    new_slot_ref[...] = slot_ref[...]
    new_point_ref[...] = point_ref[...]
    for j in range(rows):
        columns = slice(j * LANES, (j + 1) * LANES)
        for start in range(0, 2 * CP, SUB):
            size = min(SUB, 2 * CP - start)
            a_ref[pl.ds(start * rows + j, size, stride=rows), :] = jac_ref[start : start + size, columns]
        b_ref[pl.ds(j, 6, stride=rows), :] = pjac_ref[:, columns]
        r_ref[pl.ds(j, 2, stride=rows), :] = res_ref[:, columns]

    def at(ref, comp, group):
        return ref[comp * rows + group * SUB : comp * rows + (group + 1) * SUB, :]

    normal_pieces = [FINE] * 6 + [PIECES] * 3

    for group in range(rows // SUB):
        b = [at(b_ref, k, group) for k in range(6)]
        r = [at(r_ref, k, group) for k in range(2)]
        values = [b[i] * b[j] + b[3 + i] * b[3 + j] for i, j in ((0, 0), (0, 1), (0, 2), (1, 1), (1, 2), (2, 2))]
        values += [b[i] * r[0] + b[3 + i] * r[1] for i in range(3)]
        parts = [part for value, pieces in zip(values, normal_pieces) for part in cut(value, pieces)]
        keep_parts(parts, group, parts_ref)
        for s in range(SUB):
            row = group * SUB + s
            point = point_ref[row : row + 1, :]
            spread_row(row, part_rows(len(parts), group, s, parts_ref), point >> 8, PT_HI, spread_ref)
            place_row(row, point & (PT_LO - 1), PT_LO, place_point_ref)
    result = scatter(sum(normal_pieces), sizes.obs, PT_HI, PT_LO, spread_ref, place_point_ref)
    normal = joined(result, 9, PT_HI, normal_pieces)
    top_left = normal[0] + damping_point
    top_mid = normal[1]
    top_right = normal[2]
    mid_mid = normal[3] + damping_point
    mid_right = normal[4]
    low_right = normal[5] + damping_point
    adjugate = [
        mid_mid * low_right - mid_right * mid_right,
        top_right * mid_right - top_mid * low_right,
        top_mid * mid_right - top_right * mid_mid,
        top_left * low_right - top_right * top_right,
        top_mid * top_right - top_left * mid_right,
        top_left * mid_mid - top_mid * top_mid,
    ]
    determinant = top_left * adjugate[0] + top_mid * adjugate[1] + top_right * adjugate[2]
    inverse = [value / determinant for value in adjugate]
    for k in range(6):
        inv_ref[k] = inverse[k]
    for k in range(3):
        grad_ref[k] = normal[6 + k]
    eliminated = solve(inverse, normal[6:])
    picking = gather_factors(eliminated)
    for group in range(rows // SUB):
        at_point = matmul_gather(group, picking, 3, place_point_ref,
                                 lambda row: point_ref[row : row + 1, :] >> 8, PT_HI, picked_ref, found_ref)
        b = [at(b_ref, k, group) for k in range(6)]
        errors = [at(r_ref, i, group) - sum(b[3 * i + k] * at_point[k] for k in range(3)) for i in range(2)]
        a = [at(a_ref, k, group) for k in range(2 * CP)]
        values = [a[k] * errors[0] + a[CP + k] * errors[1] for k in range(CP)]
        values += [a[k] * a[k] + a[CP + k] * a[CP + k] for k in range(CP)]
        parts = [part for value in values for part in cut(value)]
        keep_parts(parts, group, parts_ref)
        for s in range(SUB):
            row = group * SUB + s
            high, low = slot_place(slot_ref[row : row + 1, :], sizes)
            spread_row(row, part_rows(len(parts), group, s, parts_ref), high, sizes.pts, spread_ref)
            place_row(row, low, LANES, place_slot_ref)
    result = scatter(2 * CP * PIECES, sizes.obs, sizes.pts, LANES, spread_ref, place_slot_ref)
    fields = joined(result, 2 * CP, sizes.pts)

    pieces = sizes.slot // LANES
    lane = lane_iota(1)
    for c in range(sizes.cams):
        for half in range(pieces):
            value = list_ref[c : c + 1, half * LANES : (half + 1) * LANES]
            low = c * sizes.block + half * (LANES // sizes.pts) + lane // sizes.pts
            parts = [(value >> 8).astype(f32), (value & 255).astype(f32)]
            spread_row(c * pieces + half, parts, lane % sizes.pts, sizes.pts, spread_ref)
            place_row(c * pieces + half, low, LANES, place_list_ref)
    result = scatter(2, sizes.cams * sizes.slot, sizes.pts, LANES, spread_ref, place_list_ref)
    listed = result[: sizes.pts] * 256.0 + result[sizes.pts : 2 * sizes.pts]
    write_messages(fields, None, sizes.first_groups, sizes.first_message, out_ref, sizes, extra=listed)


def entries_scatter(fields, entry, sizes, spread_ref, place_ref):
    high, low = entry // LANES, entry % LANES
    parts = [part for value in fields for part in cut(value)]
    for p in range(sizes.pts):
        spread_row(p, [part[p : p + 1] for part in parts], high[p : p + 1], sizes.own_rows, spread_ref)
        place_row(p, low[p : p + 1], LANES, place_ref)
    result = scatter(len(parts), sizes.pts * LANES, sizes.own_rows, LANES, spread_ref, place_ref)
    return joined(result, len(fields), sizes.own_rows)


def send_owned(scaled, partial, entry, out_ref, table_ref, sizes):
    for k in range(CP):
        table_ref[k] = scaled[k]
    fields = gather_rows(lambda c, k: table_ref[c, k : k + 1, :], sizes.run_rows, entry // LANES, entry % LANES, CP)
    write_messages(fields, partial, sizes.groups, sizes.message, out_ref, sizes)


def dot_fields(left, right):
    return jnp.sum(sum(a * b for a, b in zip(left, right)), keepdims=True)


def first_owner_kernel(sizes, column_ref, in_ref, out_ref, entry_ref, pre_ref, rem_ref,
                       table_ref, spread_ref, place_ref):
    listed = jnp.zeros((sizes.pts, LANES), f32)
    for c in range(sizes.cams):
        row = read_row(in_ref, c, sizes.first_groups, sizes.first_message, sizes)
        listed = jnp.where(column_ref[0] == c, row, listed)
    entry = listed.astype(jnp.int32) % sizes.run
    entry_ref[...] = entry
    fields = read_messages(in_ref, 2 * CP, sizes.first_message, sizes)
    sums = entries_scatter(fields, entry, sizes, spread_ref, place_ref)
    remainder = [-value for value in sums[:CP]]
    precondition = [1.0 / (value + damping_camera) for value in sums[CP:]]
    scaled = [p * r for p, r in zip(precondition, remainder)]
    for k in range(CP):
        pre_ref[k] = precondition[k]
        rem_ref[k] = remainder[k]
    send_owned(scaled, dot_fields(remainder, scaled), entry, out_ref, table_ref, sizes)


def owner_kernel(sizes, start, final, in_ref, entry_ref, pre_ref, rem_ref, dir_ref, product_ref, *refs):
    refs = list(refs)
    sol_ref = None if start else refs.pop(0)
    out_ref, new_rem_ref, new_sol_ref, step_ref = refs[:4]
    fields_ref = refs[4] if final else None
    table_ref, spread_ref, place_ref = refs[-3:]
    entry = entry_ref[...]
    fields = read_messages(in_ref, CP, sizes.message, sizes)
    curvature = read_scalar(in_ref, sizes.groups, sizes.message, sizes)
    step = product_ref[...] / jnp.broadcast_to(curvature, (SUB, LANES))
    step_ref[...] = step
    sums = entries_scatter(fields, entry, sizes, spread_ref, place_ref)
    remainder, scaled = [], []
    for k in range(CP):
        direction = dir_ref[k]
        moved = step[:1] * direction
        moved = moved if start else sol_ref[k] + moved
        new_sol_ref[k] = moved
        value = rem_ref[k] - step[:1] * (sums[k] + damping_camera * direction)
        new_rem_ref[k] = value
        remainder.append(value)
        scaled.append(pre_ref[k] * value)
        if final:
            for j, field in enumerate((moved, direction, scaled[k])):
                first = (j * CP + k) * sizes.own_rows
                fields_ref[first : first + sizes.own_rows, :] = field
    send_owned(scaled, dot_fields(remainder, scaled), entry, out_ref, table_ref, sizes)


def schur_kernel(sizes, start, last, in_ref, a_ref, b_ref, inv_ref, slot_ref, point_ref,
                 place_point_ref, pre_ref, rem_ref, grad_ref, *refs):
    refs = list(refs)
    if not start:
        product_ref, at_slot_ref, dir_ref, step_ref, sum_ref = refs[:5]
        refs = refs[5:]
    out_ref, new_product_ref, new_at_slot_ref, new_dir_ref, new_sum_ref = refs[:5]
    new_grad_ref = None
    refs = refs[5:]
    if not start:
        new_grad_ref = refs.pop(0)
    q_ref, parts_ref, spread_ref, picked_ref, found_ref, place_slot_ref = refs
    rows = sizes.rows

    def at(ref, comp, group):
        return ref[comp * rows + group * SUB : comp * rows + (group + 1) * SUB, :]

    renewed = jnp.broadcast_to(read_scalar(in_ref, sizes.groups, sizes.message, sizes), (SUB, LANES))
    new_product_ref[...] = renewed
    fields = read_messages(in_ref, CP, sizes.message, sizes)
    beta = None if start else (renewed / product_ref[...])[:1]
    squares = None
    for k in range(CP):
        direction = pre_ref[k] * rem_ref[k]
        if start:
            new_at_slot_ref[k] = fields[k]
        else:
            new_at_slot_ref[k] = fields[k] + beta * at_slot_ref[k]
            direction = direction + beta * dir_ref[k]
        new_dir_ref[k] = direction
        squares = direction * direction if squares is None else squares + direction * direction

    for group in range(rows // SUB):
        high, low = slot_place(slot_ref[group * SUB : (group + 1) * SUB, :], sizes)
        gathered = gather_rows(lambda c, k: new_at_slot_ref[c, k : k + 1, :], sizes.pts, high, low, CP)
        q = [sum(at(a_ref, i * CP + k, group) * gathered[k] for k in range(CP)) for i in range(2)]
        for i in range(2):
            q_ref[i * rows + group * SUB : i * rows + (group + 1) * SUB, :] = q[i]
        values = [at(b_ref, k, group) * q[0] + at(b_ref, 3 + k, group) * q[1] for k in range(3)]
        parts = [part for value in values for part in cut(value)]
        keep_parts(parts, group, parts_ref)
        for s in range(SUB):
            row = group * SUB + s
            spread_row(row, part_rows(len(parts), group, s, parts_ref), point_ref[row : row + 1, :] >> 8, PT_HI, spread_ref)
    result = scatter(3 * PIECES, sizes.obs, PT_HI, PT_LO, spread_ref, place_point_ref)
    sums = joined(result, 3, PT_HI)
    folded = solve([inv_ref[k] for k in range(6)], sums)
    for k in range(3):
        new_sum_ref[k] = sums[k]
        if not start:
            new_grad_ref[k] = grad_ref[k] + step_ref[:1, :1] * sum_ref[k]

    inner = None
    picking = gather_factors(folded)
    for group in range(rows // SUB):
        at_point = matmul_gather(group, picking, 3, place_point_ref,
                                 lambda row: point_ref[row : row + 1, :] >> 8, PT_HI, picked_ref, found_ref)
        q = [at(q_ref, i, group) for i in range(2)]
        errors = [q[i] - sum(at(b_ref, 3 * i + k, group) * at_point[k] for k in range(3)) for i in range(2)]
        here = q[0] * errors[0] + q[1] * errors[1]
        inner = here if inner is None else inner + here
        if not last:
            values = [at(a_ref, k, group) * errors[0] + at(a_ref, CP + k, group) * errors[1] for k in range(CP)]
            parts = [part for value in values for part in cut(value)]
            keep_parts(parts, group, parts_ref)
            for s in range(SUB):
                row = group * SUB + s
                high, low = slot_place(slot_ref[row : row + 1, :], sizes)
                spread_row(row, part_rows(len(parts), group, s, parts_ref), high, sizes.pts, spread_ref)
                place_row(row, low, LANES, place_slot_ref)
    partial = jnp.sum(inner, keepdims=True) + damping_camera * jnp.sum(squares, keepdims=True)
    if last:
        out_ref[...] = jnp.broadcast_to(partial, (sizes.devices, LANES))
        return
    result = scatter(CP * PIECES, sizes.obs, sizes.pts, LANES, spread_ref, place_slot_ref)
    fields = joined(result, CP, sizes.pts)
    write_messages(fields, partial, sizes.groups, sizes.message, out_ref, sizes)


def tail_kernel(sizes, in_ref, product_ref, own_ref, other_ref, out_ref):
    renewed = jnp.broadcast_to(read_scalar(in_ref, sizes.groups, sizes.message, sizes), (SUB, LANES))
    beta = (renewed / product_ref[...])[:1]
    field = CP * sizes.own_rows
    for j, ref in enumerate((own_ref, other_ref)):
        first = j * 2 * field
        out_ref[first : first + field, :] = ref[:field, :]
        out_ref[first + field : first + 2 * field, :] = ref[2 * field :, :] + beta * ref[field : 2 * field, :]


def final_kernel(sizes, masks, run_ref, in_ref, product_ref, inv_ref, grad_ref, sum_ref, *refs):
    all_refs = refs[: len(masks)]
    cam_ref, pt_ref, table_ref = refs[len(masks) :]
    curvature = jnp.sum(jnp.where(lane_iota(sizes.devices) == 0, in_ref[...], 0.0), keepdims=True)
    step = (product_ref[...] / jnp.broadcast_to(curvature, (SUB, LANES)))[:1]
    for all_ref, pair in zip(all_refs, masks):
        for j, mask in enumerate(pair):
            base_column = (run_ref[0] ^ mask) * sizes.run
            for h in range(sizes.run_rows):
                columns = pl.ds(pl.multiple_of(base_column + h * LANES, LANES), LANES)
                for start in range(0, CP, SUB):
                    size = min(SUB, CP - start)
                    first = (j * 2 * CP + start) * sizes.own_rows + h
                    base = all_ref[pl.ds(first, size, stride=sizes.own_rows), :]
                    direction = all_ref[pl.ds(first + CP * sizes.own_rows, size, stride=sizes.own_rows), :]
                    cam_ref[start : start + size, columns] = base + step * direction
    total = [grad_ref[k] + step[:, :1] * sum_ref[k] for k in range(3)]
    solved = solve([inv_ref[k] for k in range(6)], total)
    for k in range(3):
        table_ref[k * PT_HI : (k + 1) * PT_HI, :] = -solved[k]
    for row in range(PT_HI):
        for k in range(3):
            pt_ref[k : k + 1, row * PT_LO : (row + 1) * PT_LO] = table_ref[k * PT_HI + row : k * PT_HI + row + 1, :]


def shape(*dims, dtype=f32):
    return jax.ShapeDtypeStruct(dims, dtype)


def kept(*dims, dtype=f32):
    return pltpu.VMEM(dims, dtype)


def call(kernel, name, inputs, outputs, scratch, scalars=(), inputs_at=pltpu.VMEM, cost=None):
    vmem = pl.BlockSpec(memory_space=pltpu.VMEM)
    given = pl.BlockSpec(memory_space=inputs_at)
    smem = pl.BlockSpec(memory_space=pltpu.SMEM)
    return pl.pallas_call(
        kernel,
        name=name,
        out_shape=outputs,
        in_specs=[smem] * len(scalars) + [given] * len(inputs),
        out_specs=[vmem] * len(outputs),
        scratch_shapes=scratch,
        cost_estimate=cost,
        compiler_params=pltpu.CompilerParams(vmem_limit_bytes=VMEM_LIMIT),
    )(*scalars, *inputs)


def body(camera_jacobian, point_jacobian, residual, observed_slot, observed_point, send_list):
    sizes = Sizes(lax.axis_size("pts"), lax.axis_size("cams"), send_list.shape[2], camera_jacobian.shape[1])
    axes = ("pts", "cams")
    rows = sizes.rows
    slot = observed_slot.reshape(rows, LANES)
    point = observed_point.reshape(rows, LANES)
    column = lax.axis_index("cams").astype(jnp.int32).reshape(1)

    def exchange(messages):
        width = messages.size // sizes.devices
        flat = messages.reshape(sizes.devices, 1, width)
        return lax.all_to_all(flat, axes, split_axis=0, concat_axis=0, tiled=True).reshape(messages.shape)

    def flipped(value, flip):
        return lax.ppermute(value, "pts", [(p, p ^ flip) for p in range(sizes.pts)])

    def factors(high_rows, low_rows, entries):
        return [pltpu.VMEM((high_rows, entries), bf16), pltpu.VMEM((low_rows, entries), bf16)]

    point_table = kept(3, PT_HI, PT_LO)
    owned = kept(CP, sizes.own_rows, LANES)
    messages = kept(sizes.devices * sizes.message, LANES)
    scalar = kept(SUB, LANES)
    owned_scratch = pltpu.VMEM((CP, sizes.own_rows, LANES), f32)
    entries = sizes.pts * LANES

    gather_scratch = [
        pltpu.VMEM((3 * PIECES * PT_HI, sizes.obs), bf16),
        pltpu.VMEM((rows * SUB, LANES), f32),
        pltpu.VMEM((LANES, sizes.obs), bf16),
    ]

    def parts_scratch(count):
        return pltpu.VMEM((rows // SUB, count * SUB, LANES), f32)


    given = [
        pltpu.with_memory_space_constraint(value, pltpu.HBM)
        for value in (camera_jacobian, point_jacobian, residual, slot, point, send_list[0])
    ]
    first, a, b, inverse, gradient, place_point, slot, point = call(
        functools.partial(setup_kernel, sizes),
        "setup",
        given,
        [
            kept(sizes.devices * sizes.first_message, LANES),
            kept(2 * CP * rows, LANES),
            kept(6 * rows, LANES),
            kept(6, PT_HI, PT_LO),
            point_table,
            kept(PT_LO, sizes.obs, dtype=bf16),
            kept(rows, LANES, dtype=jnp.int32),
            kept(rows, LANES, dtype=jnp.int32),
        ],
        [pltpu.VMEM((2 * rows, LANES), f32), parts_scratch(2 * CP * PIECES)]
        + [pltpu.VMEM((max(spread_rows(6 * FINE + 3 * PIECES, PT_HI), spread_rows(2 * CP * PIECES, sizes.pts)), sizes.obs), bf16)]
        + gather_scratch
        + [pltpu.VMEM((LANES, sizes.cams * sizes.slot), bf16)]
        + [pltpu.VMEM(value.shape, value.dtype) for value in given]
        + [pltpu.SemaphoreType.DMA((len(given),))],
        inputs_at=pl.ANY,
    )
    out, entry, precondition, remainder = call(
        functools.partial(first_owner_kernel, sizes),
        "first_owner",
        [exchange(first)],
        [messages, kept(sizes.pts, LANES, dtype=jnp.int32), owned, owned],
        [owned_scratch] + factors(spread_rows(2 * CP * PIECES, sizes.own_rows), LANES, entries),
        scalars=[column],
    )
    schur_scratch = [pltpu.VMEM((2 * rows, LANES), f32), parts_scratch(CP * PIECES)]
    schur_scratch += [pltpu.VMEM((max(spread_rows(3 * PIECES, PT_HI), spread_rows(CP * PIECES, sizes.pts)), sizes.obs), bf16)]
    schur_scratch += gather_scratch
    at_slot = kept(CP, sizes.pts, LANES)
    product = slots = direction = step = sums = solution_ = None
    for iteration in range(ITERS):
        start, last = iteration == 0, iteration == ITERS - 1
        earlier = [] if start else [product, slots, direction, step, sums]
        if last:
            neighbour = flipped(fields, NEAR)
        arrived = exchange(out)
        if last:
            (both,) = call(
                functools.partial(tail_kernel, sizes),
                "tail",
                [arrived, product, fields, neighbour],
                [kept(4 * CP * sizes.own_rows, LANES)],
                [],
            )
            flips = [1 << bit for bit in range(sizes.pts.bit_length() - 1) if 1 << bit != NEAR]
            flips = flips[1:] + flips[:1]
            early = {flip: flipped(both, flip) for flip in (flips[0], flips[-1])}
        results = call(
            functools.partial(schur_kernel, sizes, start, last),
            "schur_last" if last else "schur",
            [arrived, a, b, inverse, slot, point, place_point, precondition, remainder, gradient]
            + earlier,
            [kept(sizes.devices, LANES) if last else messages, scalar, at_slot, owned, point_table]
            + ([] if start else [point_table]),
            schur_scratch,
            cost=pl.CostEstimate(flops=2_000_000_000, bytes_accessed=10_000_000, transcendentals=0),
        )
        out, product, slots, direction, sums = results[:5]
        if not start:
            gradient = results[5]
        if last:
            early[flips[0]], out = lax.optimization_barrier((early[flips[0]], out))
            gathered, masks = [both], [(0, NEAR)]
            for flip in flips:
                gathered += [early[flip] if value is both and flip in early else flipped(value, flip) for value in gathered]
                masks += [tuple(mask ^ flip for mask in pair) for pair in masks]
            break
        final = iteration == ITERS - 2
        out, remainder, solution_, step, *rest = call(
            functools.partial(owner_kernel, sizes, start, final),
            "owner_final" if final else "owner",
            [exchange(out), entry, precondition, remainder, direction, product] + ([] if start else [solution_]),
            [messages, owned, owned, scalar] + ([kept(3 * CP * sizes.own_rows, LANES)] if final else []),
            [owned_scratch] + factors(spread_rows(CP * PIECES, sizes.own_rows), LANES, entries),
        )
        fields = rest[0] if final else None
    return call(
        functools.partial(final_kernel, sizes, masks),
        "final",
        [exchange(out), product, inverse, gradient, sums] + gathered,
        [shape(CP, CAM_OWN), shape(3, PT_DEV)],
        [pltpu.VMEM((3 * PT_HI, PT_LO), f32)],
        scalars=[lax.axis_index("pts").astype(jnp.int32).reshape(1)],
    )


def solution(mesh):
    return jax.shard_map(
        lambda *arguments: tuple(body(*arguments)),
        mesh=mesh,
        in_specs=(
            P(None, ("pts", "cams")),
            P(None, ("pts", "cams")),
            P(None, ("pts", "cams")),
            P(("pts", "cams")),
            P(("pts", "cams")),
            P(("pts", "cams"), None, None),
        ),
        out_specs=(P(None, "cams"), P(None, ("pts", "cams"))),
        check_vma=False,
    )
```

```python
import functools

import jax
import jax.numpy as jnp
from jax import lax
from jax.experimental import pallas as pl
from jax.experimental.pallas import tpu as pltpu
from jax.sharding import PartitionSpec as P

CP = 9
CAM_OWN = 8192
PT_DEV = 4096
ITERS = 3
LANES = 128
SUB = 8
PT_LO = 256
PT_HI = PT_DEV // PT_LO
PIECES = 2
FINE = 3
NEAR = 2
VMEM_LIMIT = 24 * 1024 * 1024

damping_camera = 1.0
damping_point = 1.0

f32 = jnp.float32
bf16 = jnp.bfloat16


class Sizes:
    def __init__(self, pts, cams, slot, obs):
        self.pts, self.cams, self.slot, self.obs = pts, cams, slot, obs
        self.devices = pts * cams
        self.block = slot // pts
        assert cams * self.block == LANES and LANES % pts == 0
        self.rows = obs // LANES
        self.run = CAM_OWN // pts
        self.run_rows = self.run // LANES
        self.own_rows = max(SUB, self.run_rows)
        self.groups = -(-CP // cams)
        self.first_groups = -(-2 * CP // cams)
        self.message = self.groups
        self.first_message = self.first_groups + 1
        assert self.groups * cams > CP


def sub_iota(rows):
    return lax.broadcasted_iota(jnp.int32, (rows, LANES), 0)


def lane_iota(rows):
    return lax.broadcasted_iota(jnp.int32, (rows, LANES), 1)


def cut(value, pieces=PIECES):
    parts = []
    for _ in range(pieces - 1):
        part = value.astype(bf16).astype(f32)
        parts.append(part)
        value = value - part
    parts.append(value)
    return parts


def swap_blocks(rows, block, wanted):
    which = lane_iota(rows[0].shape[0]) // block
    result = []
    for q in range(wanted):
        total = None
        for c, value in enumerate(rows):
            shift = ((c - q) * block) % LANES
            moved = pltpu.roll(value, shift, axis=1) if shift else value
            total = jnp.where(which == c, moved, 0.0 if total is None else total)
        result.append(total)
    return result


def gather_rows(row, count, high, low, comps):
    result = [None] * comps
    for k in range(count):
        here = high == k
        for c in range(comps):
            source = jnp.broadcast_to(row(c, k), high.shape)
            found = jnp.take_along_axis(source, low, axis=1, mode="promise_in_bounds")
            result[c] = found if k == 0 else jnp.where(here, found, result[c])
    return result


def spread_row(index, parts, high, high_count, spread_ref):
    columns = slice(index * LANES, (index + 1) * LANES)
    mask = jnp.broadcast_to(high, (high_count, LANES)) == sub_iota(high_count)
    together = max(1, 16 // high_count)
    for start in range(0, len(parts), together):
        pieces = [
            jnp.where(mask, jnp.broadcast_to(part, (high_count, LANES)), 0.0)
            for part in parts[start : start + together]
        ]
        while len(pieces) < together:
            pieces.append(jnp.zeros((high_count, LANES), f32))
        tile = pieces[0] if together == 1 else jnp.concatenate(pieces, axis=0)
        spread_ref[start * high_count : start * high_count + tile.shape[0], columns] = tile.astype(bf16)


def place_row(index, low, low_count, place_ref):
    columns = slice(index * LANES, (index + 1) * LANES)
    place = jnp.broadcast_to(low, (low_count, LANES)) == sub_iota(low_count)
    place_ref[:low_count, columns] = jnp.where(place, 1.0, 0.0).astype(bf16)


def keep_parts(parts, group, parts_ref):
    for k, part in enumerate(parts):
        parts_ref[group, k * SUB : (k + 1) * SUB, :] = part


def part_rows(count, group, s, parts_ref):
    return [parts_ref[group, k * SUB + s : k * SUB + s + 1, :] for k in range(count)]


def spread_rows(parts, high_count):
    return -(-parts * high_count // 16) * 16


def scatter(parts, entries, high_count, low_count, spread_ref, place_ref):
    rows = spread_rows(parts, high_count)
    return lax.dot_general(
        spread_ref[:rows, :entries],
        place_ref[:low_count, :entries],
        (((1,), (1,)), ((), ())),
        preferred_element_type=f32,
    )


def joined(result, count, high_count, pieces=None):
    pieces = pieces or [PIECES] * count
    values, first = [], 0
    for number in pieces:
        rows = [result[first + k * high_count : first + (k + 1) * high_count] for k in range(number)]
        first += number * high_count
        total = rows[-1]
        for row in reversed(rows[:-1]):
            total = total + row
        values.append(total)
    return values


def point_gather(ref, point):
    wide = PT_LO // LANES
    row = lambda c, k: ref[c, k // wide : k // wide + 1, (k % wide) * LANES : (k % wide + 1) * LANES]
    return gather_rows(row, PT_HI * wide, point // LANES, point % LANES, 3)


def slot_place(slot, sizes):
    within = slot % sizes.slot
    return within % sizes.pts, (slot // sizes.slot) * sizes.block + within // sizes.pts


def solve(inverse, values):
    first = inverse[0] * values[0] + inverse[1] * values[1] + inverse[2] * values[2]
    second = inverse[1] * values[0] + inverse[3] * values[1] + inverse[4] * values[2]
    third = inverse[2] * values[0] + inverse[4] * values[1] + inverse[5] * values[2]
    return first, second, third


def write_messages(fields, scalar, groups, message, out_refs, column, sizes, extra=None):
    last = lane_iota(sizes.pts) // sizes.block == sizes.cams - 1
    for g in range(message):
        if g < groups:
            rows = swap_blocks(fields[g * sizes.cams : (g + 1) * sizes.cams], sizes.block, sizes.cams)
            if g == groups - 1 and scalar is not None:
                rows = [jnp.where(last, scalar, row) for row in rows]
            bit = 1
            while bit < sizes.cams:
                odd = (column & bit) != 0
                rows = [jnp.where(odd, rows[f ^ bit], rows[f]) for f in range(sizes.cams)]
                bit *= 2
        else:
            rows = [extra] * sizes.cams
        for row, out_ref in zip(rows, out_refs):
            out_ref[pl.ds(g, sizes.pts, stride=message), :] = row


def regroup_kernel(sizes, message, run_ref, *refs):
    in_refs, out_refs = refs[: sizes.cams], refs[sizes.cams :]
    for g, out_ref in enumerate(out_refs):
        first = (run_ref[0] ^ g) * message
        for f, in_ref in enumerate(in_refs):
            for k in range(message):
                out_ref[f * message + k : f * message + k + 1, :] = in_ref[pl.ds(first + k, 1), :]


def sort_messages(in_refs, run, column, message, out_ref, sizes):
    for g, in_ref in enumerate(in_refs):
        for f in range(sizes.cams):
            first = ((run ^ g) * sizes.cams + (column ^ f)) * message
            for k in range(message):
                out_ref[pl.ds(first + k, 1), :] = in_ref[f * message + k : f * message + k + 1, :]


def read_row(in_ref, c, g, message, sizes):
    return in_ref[pl.ds(c * message + g, sizes.pts, stride=sizes.cams * message), :]


def read_messages(in_ref, count, message, sizes):
    fields = []
    group = 0
    while len(fields) < count:
        rows = [read_row(in_ref, c, group, message, sizes) for c in range(sizes.cams)]
        fields += swap_blocks(rows, sizes.block, min(sizes.cams, count - len(fields)))
        group += 1
    return fields


def read_scalar(in_ref, groups, message, sizes):
    total = read_row(in_ref, 0, groups - 1, message, sizes)
    for c in range(1, sizes.cams):
        total = total + read_row(in_ref, c, groups - 1, message, sizes)
    chosen = jnp.where(lane_iota(sizes.pts) == LANES - 1, total, 0.0)
    return jnp.sum(chosen, keepdims=True)


def setup_kernel(sizes, column_ref, *refs):
    sources, refs = refs[:6], refs[6:]
    out_refs, refs = refs[: sizes.cams], refs[sizes.cams :]
    a_ref, b_ref, inv_ref, grad_ref, place_point_ref, new_slot_ref, new_point_ref = refs[:7]
    refs = refs[7:]
    r_ref, parts_ref, spread_ref, table_ref, place_slot_ref, place_list_ref = refs[:6]
    jac_ref, pjac_ref, res_ref, slot_ref, point_ref, list_ref = refs[6:12]
    semaphores = refs[12]
    rows = sizes.rows
    copies = [
        pltpu.make_async_copy(source, target, semaphores.at[k])
        for k, (source, target) in enumerate(zip(sources, refs[6:12]))
    ]
    for copy in copies:
        copy.start()
    for copy in copies:
        copy.wait()
    new_slot_ref[...] = slot_ref[...]
    new_point_ref[...] = point_ref[...]
    for j in range(rows):
        columns = slice(j * LANES, (j + 1) * LANES)
        for start in range(0, 2 * CP, SUB):
            size = min(SUB, 2 * CP - start)
            a_ref[pl.ds(start * rows + j, size, stride=rows), :] = jac_ref[start : start + size, columns]
        b_ref[pl.ds(j, 6, stride=rows), :] = pjac_ref[:, columns]
        r_ref[pl.ds(j, 2, stride=rows), :] = res_ref[:, columns]

    def at(ref, comp, group):
        return ref[comp * rows + group * SUB : comp * rows + (group + 1) * SUB, :]

    normal_pieces = [FINE] * 6 + [PIECES] * 3

    for group in range(rows // SUB):
        b = [at(b_ref, k, group) for k in range(6)]
        r = [at(r_ref, k, group) for k in range(2)]
        values = [b[i] * b[j] + b[3 + i] * b[3 + j] for i, j in ((0, 0), (0, 1), (0, 2), (1, 1), (1, 2), (2, 2))]
        values += [b[i] * r[0] + b[3 + i] * r[1] for i in range(3)]
        parts = [part for value, pieces in zip(values, normal_pieces) for part in cut(value, pieces)]
        keep_parts(parts, group, parts_ref)
        for s in range(SUB):
            row = group * SUB + s
            point = point_ref[row : row + 1, :]
            spread_row(row, part_rows(len(parts), group, s, parts_ref), point >> 8, PT_HI, spread_ref)
            place_row(row, point & (PT_LO - 1), PT_LO, place_point_ref)
    result = scatter(sum(normal_pieces), sizes.obs, PT_HI, PT_LO, spread_ref, place_point_ref)
    normal = joined(result, 9, PT_HI, normal_pieces)
    top_left = normal[0] + damping_point
    top_mid = normal[1]
    top_right = normal[2]
    mid_mid = normal[3] + damping_point
    mid_right = normal[4]
    low_right = normal[5] + damping_point
    adjugate = [
        mid_mid * low_right - mid_right * mid_right,
        top_right * mid_right - top_mid * low_right,
        top_mid * mid_right - top_right * mid_mid,
        top_left * low_right - top_right * top_right,
        top_mid * top_right - top_left * mid_right,
        top_left * mid_mid - top_mid * top_mid,
    ]
    determinant = top_left * adjugate[0] + top_mid * adjugate[1] + top_right * adjugate[2]
    inverse = [value / determinant for value in adjugate]
    for k in range(6):
        inv_ref[k] = inverse[k]
    for k in range(3):
        grad_ref[k] = normal[6 + k]
    eliminated = solve(inverse, normal[6:])
    for k in range(3):
        table_ref[k] = eliminated[k]
    for group in range(rows // SUB):
        at_point = point_gather(table_ref, point_ref[group * SUB : (group + 1) * SUB, :])
        b = [at(b_ref, k, group) for k in range(6)]
        errors = [at(r_ref, i, group) - sum(b[3 * i + k] * at_point[k] for k in range(3)) for i in range(2)]
        a = [at(a_ref, k, group) for k in range(2 * CP)]
        values = [a[k] * errors[0] + a[CP + k] * errors[1] for k in range(CP)]
        values += [a[k] * a[k] + a[CP + k] * a[CP + k] for k in range(CP)]
        parts = [part for value in values for part in cut(value)]
        keep_parts(parts, group, parts_ref)
        for s in range(SUB):
            row = group * SUB + s
            high, low = slot_place(slot_ref[row : row + 1, :], sizes)
            spread_row(row, part_rows(len(parts), group, s, parts_ref), high, sizes.pts, spread_ref)
            place_row(row, low, LANES, place_slot_ref)
    result = scatter(2 * CP * PIECES, sizes.obs, sizes.pts, LANES, spread_ref, place_slot_ref)
    fields = joined(result, 2 * CP, sizes.pts)

    pieces = sizes.slot // LANES
    lane = lane_iota(1)
    for c in range(sizes.cams):
        for half in range(pieces):
            value = list_ref[c : c + 1, half * LANES : (half + 1) * LANES]
            low = c * sizes.block + half * (LANES // sizes.pts) + lane // sizes.pts
            parts = [(value >> 8).astype(f32), (value & 255).astype(f32)]
            spread_row(c * pieces + half, parts, lane % sizes.pts, sizes.pts, spread_ref)
            place_row(c * pieces + half, low, LANES, place_list_ref)
    result = scatter(2, sizes.cams * sizes.slot, sizes.pts, LANES, spread_ref, place_list_ref)
    listed = result[: sizes.pts] * 256.0 + result[sizes.pts : 2 * sizes.pts]
    write_messages(fields, None, sizes.first_groups, sizes.first_message, out_refs, column_ref[0], sizes, extra=listed)


def entries_scatter(fields, entry, sizes, spread_ref, place_ref):
    high, low = entry // LANES, entry % LANES
    parts = [part for value in fields for part in cut(value)]
    for p in range(sizes.pts):
        spread_row(p, [part[p : p + 1] for part in parts], high[p : p + 1], sizes.own_rows, spread_ref)
        place_row(p, low[p : p + 1], LANES, place_ref)
    result = scatter(len(parts), sizes.pts * LANES, sizes.own_rows, LANES, spread_ref, place_ref)
    return joined(result, len(fields), sizes.own_rows)


def send_owned(scaled, partial, entry, out_refs, column, table_ref, sizes):
    for k in range(CP):
        table_ref[k] = scaled[k]
    fields = gather_rows(lambda c, k: table_ref[c, k : k + 1, :], sizes.run_rows, entry // LANES, entry % LANES, CP)
    write_messages(fields, partial, sizes.groups, sizes.message, out_refs, column, sizes)


def dot_fields(left, right):
    return jnp.sum(sum(a * b for a, b in zip(left, right)), keepdims=True)


def first_owner_kernel(sizes, run_ref, column_ref, *refs):
    in_refs, refs = refs[: sizes.pts], refs[sizes.pts :]
    out_refs, refs = refs[: sizes.cams], refs[sizes.cams :]
    entry_ref, pre_ref, rem_ref, table_ref, spread_ref, place_ref, in_ref = refs
    sort_messages(in_refs, run_ref[0], column_ref[0], sizes.first_message, in_ref, sizes)
    listed = jnp.zeros((sizes.pts, LANES), f32)
    for c in range(sizes.cams):
        row = read_row(in_ref, c, sizes.first_groups, sizes.first_message, sizes)
        listed = jnp.where(column_ref[0] == c, row, listed)
    entry = listed.astype(jnp.int32) % sizes.run
    entry_ref[...] = entry
    fields = read_messages(in_ref, 2 * CP, sizes.first_message, sizes)
    sums = entries_scatter(fields, entry, sizes, spread_ref, place_ref)
    remainder = [-value for value in sums[:CP]]
    precondition = [1.0 / (value + damping_camera) for value in sums[CP:]]
    scaled = [p * r for p, r in zip(precondition, remainder)]
    for k in range(CP):
        pre_ref[k] = precondition[k]
        rem_ref[k] = remainder[k]
    send_owned(scaled, dot_fields(remainder, scaled), entry, out_refs, column_ref[0], table_ref, sizes)


def owner_kernel(sizes, start, final, run_ref, column_ref, *refs):
    in_refs, refs = refs[: sizes.pts], refs[sizes.pts :]
    entry_ref, pre_ref, rem_ref, dir_ref, product_ref = refs[:5]
    refs = list(refs[5:])
    sol_ref = None if start else refs.pop(0)
    out_refs, refs = refs[: sizes.cams], refs[sizes.cams :]
    new_rem_ref, new_sol_ref, step_ref = refs[:3]
    fields_ref = refs[3] if final else None
    table_ref, spread_ref, place_ref, in_ref = refs[-4:]
    sort_messages(in_refs, run_ref[0], column_ref[0], sizes.message, in_ref, sizes)
    entry = entry_ref[...]
    fields = read_messages(in_ref, CP, sizes.message, sizes)
    curvature = read_scalar(in_ref, sizes.groups, sizes.message, sizes)
    step = product_ref[...] / jnp.broadcast_to(curvature, (SUB, LANES))
    step_ref[...] = step
    sums = entries_scatter(fields, entry, sizes, spread_ref, place_ref)
    remainder, scaled = [], []
    for k in range(CP):
        direction = dir_ref[k]
        moved = step[:1] * direction
        moved = moved if start else sol_ref[k] + moved
        new_sol_ref[k] = moved
        value = rem_ref[k] - step[:1] * (sums[k] + damping_camera * direction)
        new_rem_ref[k] = value
        remainder.append(value)
        scaled.append(pre_ref[k] * value)
        if final:
            for j, field in enumerate((moved, direction, scaled[k])):
                first = (j * CP + k) * sizes.own_rows
                fields_ref[first : first + sizes.own_rows, :] = field
    send_owned(scaled, dot_fields(remainder, scaled), entry, out_refs, column_ref[0], table_ref, sizes)


def schur_kernel(sizes, start, last, run_ref, column_ref, *refs):
    in_refs, refs = refs[: sizes.pts], list(refs[sizes.pts :])
    a_ref, b_ref, inv_ref, slot_ref, point_ref, place_point_ref, pre_ref, rem_ref, grad_ref = refs[:9]
    refs = refs[9:]
    if not start:
        product_ref, at_slot_ref, dir_ref, step_ref, sum_ref = refs[:5]
        refs = refs[5:]
    out_count = 1 if last else sizes.cams
    out_refs, refs = refs[:out_count], refs[out_count:]
    new_product_ref, new_at_slot_ref, new_dir_ref, new_sum_ref = refs[:4]
    new_grad_ref = None
    refs = refs[4:]
    if not start:
        new_grad_ref = refs.pop(0)
    q_ref, parts_ref, spread_ref, table_ref, place_slot_ref, in_ref = refs
    rows = sizes.rows
    sort_messages(in_refs, run_ref[0], column_ref[0], sizes.message, in_ref, sizes)

    def at(ref, comp, group):
        return ref[comp * rows + group * SUB : comp * rows + (group + 1) * SUB, :]

    renewed = jnp.broadcast_to(read_scalar(in_ref, sizes.groups, sizes.message, sizes), (SUB, LANES))
    new_product_ref[...] = renewed
    fields = read_messages(in_ref, CP, sizes.message, sizes)
    beta = None if start else (renewed / product_ref[...])[:1]
    squares = None
    for k in range(CP):
        direction = pre_ref[k] * rem_ref[k]
        if start:
            new_at_slot_ref[k] = fields[k]
        else:
            new_at_slot_ref[k] = fields[k] + beta * at_slot_ref[k]
            direction = direction + beta * dir_ref[k]
        new_dir_ref[k] = direction
        squares = direction * direction if squares is None else squares + direction * direction

    for group in range(rows // SUB):
        high, low = slot_place(slot_ref[group * SUB : (group + 1) * SUB, :], sizes)
        gathered = gather_rows(lambda c, k: new_at_slot_ref[c, k : k + 1, :], sizes.pts, high, low, CP)
        q = [sum(at(a_ref, i * CP + k, group) * gathered[k] for k in range(CP)) for i in range(2)]
        for i in range(2):
            q_ref[i * rows + group * SUB : i * rows + (group + 1) * SUB, :] = q[i]
        values = [at(b_ref, k, group) * q[0] + at(b_ref, 3 + k, group) * q[1] for k in range(3)]
        parts = [part for value in values for part in cut(value)]
        keep_parts(parts, group, parts_ref)
        for s in range(SUB):
            row = group * SUB + s
            spread_row(row, part_rows(len(parts), group, s, parts_ref), point_ref[row : row + 1, :] >> 8, PT_HI, spread_ref)
    result = scatter(3 * PIECES, sizes.obs, PT_HI, PT_LO, spread_ref, place_point_ref)
    sums = joined(result, 3, PT_HI)
    folded = solve([inv_ref[k] for k in range(6)], sums)
    for k in range(3):
        new_sum_ref[k] = sums[k]
        if not start:
            new_grad_ref[k] = grad_ref[k] + step_ref[:1, :1] * sum_ref[k]

    inner = None
    for k in range(3):
        table_ref[k] = folded[k]
    for group in range(rows // SUB):
        at_point = point_gather(table_ref, point_ref[group * SUB : (group + 1) * SUB, :])
        q = [at(q_ref, i, group) for i in range(2)]
        errors = [q[i] - sum(at(b_ref, 3 * i + k, group) * at_point[k] for k in range(3)) for i in range(2)]
        here = q[0] * errors[0] + q[1] * errors[1]
        inner = here if inner is None else inner + here
        if not last:
            values = [at(a_ref, k, group) * errors[0] + at(a_ref, CP + k, group) * errors[1] for k in range(CP)]
            parts = [part for value in values for part in cut(value)]
            keep_parts(parts, group, parts_ref)
            for s in range(SUB):
                row = group * SUB + s
                high, low = slot_place(slot_ref[row : row + 1, :], sizes)
                spread_row(row, part_rows(len(parts), group, s, parts_ref), high, sizes.pts, spread_ref)
                place_row(row, low, LANES, place_slot_ref)
    partial = jnp.sum(inner, keepdims=True) + damping_camera * jnp.sum(squares, keepdims=True)
    if last:
        out_refs[0][...] = jnp.broadcast_to(partial, (SUB, LANES))
        return
    result = scatter(CP * PIECES, sizes.obs, sizes.pts, LANES, spread_ref, place_slot_ref)
    fields = joined(result, CP, sizes.pts)
    write_messages(fields, partial, sizes.groups, sizes.message, out_refs, column_ref[0], sizes)


def tail_kernel(sizes, run_ref, column_ref, *refs):
    in_refs, refs = refs[: sizes.pts], refs[sizes.pts :]
    product_ref, own_ref, other_ref, out_ref, in_ref = refs
    sort_messages(in_refs, run_ref[0], column_ref[0], sizes.message, in_ref, sizes)
    renewed = jnp.broadcast_to(read_scalar(in_ref, sizes.groups, sizes.message, sizes), (SUB, LANES))
    beta = (renewed / product_ref[...])[:1]
    field = CP * sizes.own_rows
    for j, ref in enumerate((own_ref, other_ref)):
        first = j * 2 * field
        out_ref[first : first + field, :] = ref[:field, :]
        out_ref[first + field : first + 2 * field, :] = ref[2 * field :, :] + beta * ref[field : 2 * field, :]


def final_kernel(sizes, masks, run_ref, in_ref, product_ref, inv_ref, grad_ref, sum_ref, *refs):
    all_refs = refs[: len(masks)]
    cam_ref, pt_ref, table_ref = refs[len(masks) :]
    step = (product_ref[...] / in_ref[...])[:1]
    for all_ref, pair in zip(all_refs, masks):
        for j, mask in enumerate(pair):
            base_column = (run_ref[0] ^ mask) * sizes.run
            for h in range(sizes.run_rows):
                columns = pl.ds(pl.multiple_of(base_column + h * LANES, LANES), LANES)
                for start in range(0, CP, SUB):
                    size = min(SUB, CP - start)
                    first = (j * 2 * CP + start) * sizes.own_rows + h
                    base = all_ref[pl.ds(first, size, stride=sizes.own_rows), :]
                    direction = all_ref[pl.ds(first + CP * sizes.own_rows, size, stride=sizes.own_rows), :]
                    cam_ref[start : start + size, columns] = base + step * direction
    total = [grad_ref[k] + step[:, :1] * sum_ref[k] for k in range(3)]
    solved = solve([inv_ref[k] for k in range(6)], total)
    for k in range(3):
        table_ref[k * PT_HI : (k + 1) * PT_HI, :] = -solved[k]
    for row in range(PT_HI):
        for k in range(3):
            pt_ref[k : k + 1, row * PT_LO : (row + 1) * PT_LO] = table_ref[k * PT_HI + row : k * PT_HI + row + 1, :]


def shape(*dims, dtype=f32):
    return jax.ShapeDtypeStruct(dims, dtype)


def kept(*dims, dtype=f32):
    return pltpu.VMEM(dims, dtype)


def call(kernel, name, inputs, outputs, scratch, scalars=(), inputs_at=pltpu.VMEM, cost=None):
    vmem = pl.BlockSpec(memory_space=pltpu.VMEM)
    given = pl.BlockSpec(memory_space=inputs_at)
    smem = pl.BlockSpec(memory_space=pltpu.SMEM)
    return pl.pallas_call(
        kernel,
        name=name,
        out_shape=outputs,
        in_specs=[smem] * len(scalars) + [given] * len(inputs),
        out_specs=[vmem] * len(outputs),
        scratch_shapes=scratch,
        cost_estimate=cost,
        compiler_params=pltpu.CompilerParams(vmem_limit_bytes=VMEM_LIMIT),
    )(*scalars, *inputs)


def body(camera_jacobian, point_jacobian, residual, observed_slot, observed_point, send_list):
    sizes = Sizes(lax.axis_size("pts"), lax.axis_size("cams"), send_list.shape[2], camera_jacobian.shape[1])
    rows = sizes.rows
    slot = observed_slot.reshape(rows, LANES)
    point = observed_point.reshape(rows, LANES)
    column = lax.axis_index("cams").astype(jnp.int32).reshape(1)
    run = lax.axis_index("pts").astype(jnp.int32).reshape(1)

    def flipped(value, flip, axis="pts"):
        return lax.ppermute(value, axis, [(p, p ^ flip) for p in range(lax.axis_size(axis))])

    def exchange(blocks, message):
        blocks = [flipped(block, f, "cams") if f else block for f, block in enumerate(blocks)]
        blocks = call(
            functools.partial(regroup_kernel, sizes, message),
            "regroup",
            blocks,
            [kept(sizes.cams * message, LANES)] * sizes.pts,
            [],
            scalars=[run],
        )
        return [flipped(block, g) if g else block for g, block in enumerate(blocks)]

    def factors(high_rows, low_rows, entries):
        return [pltpu.VMEM((high_rows, entries), bf16), pltpu.VMEM((low_rows, entries), bf16)]

    point_table = kept(3, PT_HI, PT_LO)
    owned = kept(CP, sizes.own_rows, LANES)
    messages = [kept(sizes.pts * sizes.message, LANES)] * sizes.cams
    inbox = pltpu.VMEM((sizes.devices * sizes.message, LANES), f32)
    place = [run, column]
    scalar = kept(SUB, LANES)
    owned_scratch = pltpu.VMEM((CP, sizes.own_rows, LANES), f32)
    entries = sizes.pts * LANES

    gather_scratch = [pltpu.VMEM((3, PT_HI, PT_LO), f32), pltpu.VMEM((LANES, sizes.obs), bf16)]

    def parts_scratch(count):
        return pltpu.VMEM((rows // SUB, count * SUB, LANES), f32)


    given = [
        pltpu.with_memory_space_constraint(value, pltpu.HBM)
        for value in (camera_jacobian, point_jacobian, residual, slot, point, send_list[0])
    ]
    *first, a, b, inverse, gradient, place_point, slot, point = call(
        functools.partial(setup_kernel, sizes),
        "setup",
        given,
        [kept(sizes.pts * sizes.first_message, LANES)] * sizes.cams
        + [
            kept(2 * CP * rows, LANES),
            kept(6 * rows, LANES),
            kept(6, PT_HI, PT_LO),
            point_table,
            kept(PT_LO, sizes.obs, dtype=bf16),
            kept(rows, LANES, dtype=jnp.int32),
            kept(rows, LANES, dtype=jnp.int32),
        ],
        [pltpu.VMEM((2 * rows, LANES), f32), parts_scratch(2 * CP * PIECES)]
        + [pltpu.VMEM((max(spread_rows(6 * FINE + 3 * PIECES, PT_HI), spread_rows(2 * CP * PIECES, sizes.pts)), sizes.obs), bf16)]
        + gather_scratch
        + [pltpu.VMEM((LANES, sizes.cams * sizes.slot), bf16)]
        + [pltpu.VMEM(value.shape, value.dtype) for value in given]
        + [pltpu.SemaphoreType.DMA((len(given),))],
        scalars=[column],
        inputs_at=pl.ANY,
    )
    *out, entry, precondition, remainder = call(
        functools.partial(first_owner_kernel, sizes),
        "first_owner",
        exchange(first, sizes.first_message),
        messages + [kept(sizes.pts, LANES, dtype=jnp.int32), owned, owned],
        [owned_scratch]
        + factors(spread_rows(2 * CP * PIECES, sizes.own_rows), LANES, entries)
        + [pltpu.VMEM((sizes.devices * sizes.first_message, LANES), f32)],
        scalars=place,
    )
    schur_scratch = [pltpu.VMEM((2 * rows, LANES), f32), parts_scratch(CP * PIECES)]
    schur_scratch += [pltpu.VMEM((max(spread_rows(3 * PIECES, PT_HI), spread_rows(CP * PIECES, sizes.pts)), sizes.obs), bf16)]
    schur_scratch += gather_scratch + [inbox]
    at_slot = kept(CP, sizes.pts, LANES)
    product = slots = direction = step = sums = solution_ = None
    for iteration in range(ITERS):
        start, last = iteration == 0, iteration == ITERS - 1
        earlier = [] if start else [product, slots, direction, step, sums]
        if last:
            neighbour = flipped(fields, NEAR)
        arrived = exchange(out, sizes.message)
        if last:
            (both,) = call(
                functools.partial(tail_kernel, sizes),
                "tail",
                arrived + [product, fields, neighbour],
                [kept(4 * CP * sizes.own_rows, LANES)],
                [inbox],
                scalars=place,
            )
            flips = [1 << bit for bit in range(sizes.pts.bit_length() - 1) if 1 << bit != NEAR]
            flips = flips[1:] + flips[:1]
            early = {flip: flipped(both, flip) for flip in (flips[0], flips[-1])}
        results = call(
            functools.partial(schur_kernel, sizes, start, last),
            "schur_last" if last else "schur",
            arrived + [a, b, inverse, slot, point, place_point, precondition, remainder, gradient] + earlier,
            ([scalar] if last else messages) + [scalar, at_slot, owned, point_table]
            + ([] if start else [point_table]),
            schur_scratch,
            scalars=place,
            cost=pl.CostEstimate(flops=2_000_000_000, bytes_accessed=10_000_000, transcendentals=0),
        )
        count = 1 if last else sizes.cams
        out, results = list(results[:count]), results[count:]
        product, slots, direction, sums = results[:4]
        if not start:
            gradient = results[4]
        if last:
            early[flips[0]], out[0] = lax.optimization_barrier((early[flips[0]], out[0]))
            gathered, masks = [both], [(0, NEAR)]
            for flip in flips:
                gathered += [early[flip] if value is both and flip in early else flipped(value, flip) for value in gathered]
                masks += [tuple(mask ^ flip for mask in pair) for pair in masks]
            break
        final = iteration == ITERS - 2
        results = call(
            functools.partial(owner_kernel, sizes, start, final),
            "owner_final" if final else "owner",
            exchange(out, sizes.message)
            + [entry, precondition, remainder, direction, product]
            + ([] if start else [solution_]),
            messages + [owned, owned, scalar] + ([kept(3 * CP * sizes.own_rows, LANES)] if final else []),
            [owned_scratch] + factors(spread_rows(CP * PIECES, sizes.own_rows), LANES, entries) + [inbox],
            scalars=place,
        )
        out, (remainder, solution_, step, *rest) = results[: sizes.cams], results[sizes.cams :]
        fields = rest[0] if final else None
    curvature = out[0]
    for axis in ("cams", "pts"):
        flips = [1 << bit for bit in range(lax.axis_size(axis).bit_length() - 1)]
        for flip in reversed(flips):
            curvature = curvature + flipped(curvature, flip, axis)
    return call(
        functools.partial(final_kernel, sizes, masks),
        "final",
        [curvature, product, inverse, gradient, sums] + gathered,
        [shape(CP, CAM_OWN), shape(3, PT_DEV)],
        [pltpu.VMEM((3 * PT_HI, PT_LO), f32)],
        scalars=[run],
    )


def solution(mesh):
    return jax.shard_map(
        lambda *arguments: tuple(body(*arguments)),
        mesh=mesh,
        in_specs=(
            P(None, ("pts", "cams")),
            P(None, ("pts", "cams")),
            P(None, ("pts", "cams")),
            P(("pts", "cams")),
            P(("pts", "cams")),
            P(("pts", "cams"), None, None),
        ),
        out_specs=(P(None, "cams"), P(None, ("pts", "cams"))),
        check_vma=False,
    )
```

```python
import functools

import jax
import jax.numpy as jnp
from jax import lax
from jax.experimental import pallas as pl
from jax.experimental.pallas import tpu as pltpu
from jax.sharding import PartitionSpec as P

CP = 9
CAM_OWN = 8192
PT_DEV = 4096
ITERS = 3
LANES = 128
SUB = 8
PT_LO = 256
PT_HI = PT_DEV // PT_LO
PIECES = 2
FINE = 3
VMEM_LIMIT = 24 * 1024 * 1024

damping_camera = 1.0
damping_point = 1.0

f32 = jnp.float32
bf16 = jnp.bfloat16


class Sizes:
    def __init__(self, pts, cams, slot, obs):
        self.pts, self.cams, self.slot, self.obs = pts, cams, slot, obs
        self.devices = pts * cams
        self.block = slot // pts
        assert cams * self.block == LANES and LANES % pts == 0
        self.rows = obs // LANES
        self.run = CAM_OWN // pts
        self.run_rows = self.run // LANES
        self.own_rows = max(SUB, self.run_rows)
        self.groups = -(-CP // cams)
        self.first_groups = -(-2 * CP // cams)
        self.message = self.groups
        self.first_message = self.first_groups + 1
        assert self.groups * cams > CP


def sub_iota(rows):
    return lax.broadcasted_iota(jnp.int32, (rows, LANES), 0)


def lane_iota(rows):
    return lax.broadcasted_iota(jnp.int32, (rows, LANES), 1)


def cut(value, pieces=PIECES):
    parts = []
    for _ in range(pieces - 1):
        part = value.astype(bf16).astype(f32)
        parts.append(part)
        value = value - part
    parts.append(value)
    return parts


def swap_blocks(rows, block, wanted):
    which = lane_iota(rows[0].shape[0]) // block
    result = []
    for q in range(wanted):
        total = None
        for c, value in enumerate(rows):
            shift = ((c - q) * block) % LANES
            moved = pltpu.roll(value, shift, axis=1) if shift else value
            total = jnp.where(which == c, moved, 0.0 if total is None else total)
        result.append(total)
    return result


def gather_rows(row, count, high, low, comps):
    result = [None] * comps
    for k in range(count):
        here = high == k
        for c in range(comps):
            source = jnp.broadcast_to(row(c, k), high.shape)
            found = jnp.take_along_axis(source, low, axis=1, mode="promise_in_bounds")
            result[c] = found if k == 0 else jnp.where(here, found, result[c])
    return result


def spread_row(index, parts, high, high_count, spread_ref):
    columns = slice(index * LANES, (index + 1) * LANES)
    mask = jnp.broadcast_to(high, (high_count, LANES)) == sub_iota(high_count)
    together = max(1, 16 // high_count)
    for start in range(0, len(parts), together):
        pieces = [
            jnp.where(mask, jnp.broadcast_to(part, (high_count, LANES)), 0.0)
            for part in parts[start : start + together]
        ]
        while len(pieces) < together:
            pieces.append(jnp.zeros((high_count, LANES), f32))
        tile = pieces[0] if together == 1 else jnp.concatenate(pieces, axis=0)
        spread_ref[start * high_count : start * high_count + tile.shape[0], columns] = tile.astype(bf16)


def place_row(index, low, low_count, place_ref):
    columns = slice(index * LANES, (index + 1) * LANES)
    place = jnp.broadcast_to(low, (low_count, LANES)) == sub_iota(low_count)
    place_ref[:low_count, columns] = jnp.where(place, 1.0, 0.0).astype(bf16)


def keep_parts(parts, group, parts_ref):
    for k, part in enumerate(parts):
        parts_ref[group, k * SUB : (k + 1) * SUB, :] = part


def part_rows(count, group, s, parts_ref):
    return [parts_ref[group, k * SUB + s : k * SUB + s + 1, :] for k in range(count)]


def spread_rows(parts, high_count):
    return -(-parts * high_count // 16) * 16


def scatter(parts, entries, high_count, low_count, spread_ref, place_ref):
    rows = spread_rows(parts, high_count)
    return lax.dot_general(
        spread_ref[:rows, :entries],
        place_ref[:low_count, :entries],
        (((1,), (1,)), ((), ())),
        preferred_element_type=f32,
    )


def joined(result, count, high_count, pieces=None):
    pieces = pieces or [PIECES] * count
    values, first = [], 0
    for number in pieces:
        rows = [result[first + k * high_count : first + (k + 1) * high_count] for k in range(number)]
        first += number * high_count
        total = rows[-1]
        for row in reversed(rows[:-1]):
            total = total + row
        values.append(total)
    return values


def point_gather(ref, point):
    wide = PT_LO // LANES
    row = lambda c, k: ref[c, k // wide : k // wide + 1, (k % wide) * LANES : (k % wide + 1) * LANES]
    return gather_rows(row, PT_HI * wide, point // LANES, point % LANES, 3)


def slot_place(slot, sizes):
    within = slot % sizes.slot
    return within % sizes.pts, (slot // sizes.slot) * sizes.block + within // sizes.pts


def solve(inverse, values):
    first = inverse[0] * values[0] + inverse[1] * values[1] + inverse[2] * values[2]
    second = inverse[1] * values[0] + inverse[3] * values[1] + inverse[4] * values[2]
    third = inverse[2] * values[0] + inverse[4] * values[1] + inverse[5] * values[2]
    return first, second, third


def write_messages(fields, scalar, groups, message, out_ref, sizes, extra=None):
    which = lane_iota(sizes.pts) // sizes.block
    for g in range(groups):
        rows = fields[g * sizes.cams : (g + 1) * sizes.cams]
        moved = swap_partial(rows, sizes)
        for c in range(sizes.cams):
            value = moved[c]
            if g == groups - 1 and scalar is not None:
                value = jnp.where(which == sizes.cams - 1, scalar, value)
            out_ref[pl.ds(c * message + g, sizes.pts, stride=sizes.cams * message), :] = value
    for g in range(groups, message):
        for c in range(sizes.cams):
            value = extra if (extra is not None and g == groups) else jnp.zeros((sizes.pts, LANES), f32)
            out_ref[pl.ds(c * message + g, sizes.pts, stride=sizes.cams * message), :] = value


def swap_partial(rows, sizes):
    return swap_blocks(rows, sizes.block, sizes.cams)


def read_row(in_ref, c, g, message, sizes):
    return in_ref[pl.ds(c * message + g, sizes.pts, stride=sizes.cams * message), :]


def read_messages(in_ref, count, message, sizes):
    fields = []
    group = 0
    while len(fields) < count:
        rows = [read_row(in_ref, c, group, message, sizes) for c in range(sizes.cams)]
        fields += swap_blocks(rows, sizes.block, min(sizes.cams, count - len(fields)))
        group += 1
    return fields


def read_scalar(in_ref, groups, message, sizes):
    total = read_row(in_ref, 0, groups - 1, message, sizes)
    for c in range(1, sizes.cams):
        total = total + read_row(in_ref, c, groups - 1, message, sizes)
    chosen = jnp.where(lane_iota(sizes.pts) == LANES - 1, total, 0.0)
    return jnp.sum(chosen, keepdims=True)


def setup_kernel(sizes, *refs):
    sources, refs = refs[:6], refs[6:]
    out_ref, a_ref, b_ref, inv_ref, grad_ref, place_point_ref, new_slot_ref, new_point_ref = refs[:8]
    refs = refs[8:]
    r_ref, parts_ref, spread_ref, table_ref, place_slot_ref, place_list_ref = refs[:6]
    jac_ref, pjac_ref, res_ref, slot_ref, point_ref, list_ref = refs[6:12]
    semaphores = refs[12]
    rows = sizes.rows
    copies = [
        pltpu.make_async_copy(source, target, semaphores.at[k])
        for k, (source, target) in enumerate(zip(sources, refs[6:12]))
    ]
    for copy in copies:
        copy.start()
    for copy in copies:
        copy.wait()
    new_slot_ref[...] = slot_ref[...]
    new_point_ref[...] = point_ref[...]
    for j in range(rows):
        columns = slice(j * LANES, (j + 1) * LANES)
        for start in range(0, 2 * CP, SUB):
            size = min(SUB, 2 * CP - start)
            a_ref[pl.ds(start * rows + j, size, stride=rows), :] = jac_ref[start : start + size, columns]
        b_ref[pl.ds(j, 6, stride=rows), :] = pjac_ref[:, columns]
        r_ref[pl.ds(j, 2, stride=rows), :] = res_ref[:, columns]

    def at(ref, comp, group):
        return ref[comp * rows + group * SUB : comp * rows + (group + 1) * SUB, :]

    normal_pieces = [FINE] * 6 + [PIECES] * 3

    for group in range(rows // SUB):
        b = [at(b_ref, k, group) for k in range(6)]
        r = [at(r_ref, k, group) for k in range(2)]
        values = [b[i] * b[j] + b[3 + i] * b[3 + j] for i, j in ((0, 0), (0, 1), (0, 2), (1, 1), (1, 2), (2, 2))]
        values += [b[i] * r[0] + b[3 + i] * r[1] for i in range(3)]
        parts = [part for value, pieces in zip(values, normal_pieces) for part in cut(value, pieces)]
        keep_parts(parts, group, parts_ref)
        for s in range(SUB):
            row = group * SUB + s
            point = point_ref[row : row + 1, :]
            spread_row(row, part_rows(len(parts), group, s, parts_ref), point >> 8, PT_HI, spread_ref)
            place_row(row, point & (PT_LO - 1), PT_LO, place_point_ref)
    result = scatter(sum(normal_pieces), sizes.obs, PT_HI, PT_LO, spread_ref, place_point_ref)
    normal = joined(result, 9, PT_HI, normal_pieces)
    top_left = normal[0] + damping_point
    top_mid = normal[1]
    top_right = normal[2]
    mid_mid = normal[3] + damping_point
    mid_right = normal[4]
    low_right = normal[5] + damping_point
    adjugate = [
        mid_mid * low_right - mid_right * mid_right,
        top_right * mid_right - top_mid * low_right,
        top_mid * mid_right - top_right * mid_mid,
        top_left * low_right - top_right * top_right,
        top_mid * top_right - top_left * mid_right,
        top_left * mid_mid - top_mid * top_mid,
    ]
    determinant = top_left * adjugate[0] + top_mid * adjugate[1] + top_right * adjugate[2]
    inverse = [value / determinant for value in adjugate]
    for k in range(6):
        inv_ref[k] = inverse[k]
    for k in range(3):
        grad_ref[k] = normal[6 + k]
    eliminated = solve(inverse, normal[6:])
    for k in range(3):
        table_ref[k] = eliminated[k]
    for group in range(rows // SUB):
        at_point = point_gather(table_ref, point_ref[group * SUB : (group + 1) * SUB, :])
        b = [at(b_ref, k, group) for k in range(6)]
        errors = [at(r_ref, i, group) - sum(b[3 * i + k] * at_point[k] for k in range(3)) for i in range(2)]
        a = [at(a_ref, k, group) for k in range(2 * CP)]
        values = [a[k] * errors[0] + a[CP + k] * errors[1] for k in range(CP)]
        values += [a[k] * a[k] + a[CP + k] * a[CP + k] for k in range(CP)]
        parts = [part for value in values for part in cut(value)]
        keep_parts(parts, group, parts_ref)
        for s in range(SUB):
            row = group * SUB + s
            high, low = slot_place(slot_ref[row : row + 1, :], sizes)
            spread_row(row, part_rows(len(parts), group, s, parts_ref), high, sizes.pts, spread_ref)
            place_row(row, low, LANES, place_slot_ref)
    result = scatter(2 * CP * PIECES, sizes.obs, sizes.pts, LANES, spread_ref, place_slot_ref)
    fields = joined(result, 2 * CP, sizes.pts)

    pieces = sizes.slot // LANES
    lane = lane_iota(1)
    for c in range(sizes.cams):
        for half in range(pieces):
            value = list_ref[c : c + 1, half * LANES : (half + 1) * LANES]
            low = c * sizes.block + half * (LANES // sizes.pts) + lane // sizes.pts
            parts = [(value >> 8).astype(f32), (value & 255).astype(f32)]
            spread_row(c * pieces + half, parts, lane % sizes.pts, sizes.pts, spread_ref)
            place_row(c * pieces + half, low, LANES, place_list_ref)
    result = scatter(2, sizes.cams * sizes.slot, sizes.pts, LANES, spread_ref, place_list_ref)
    listed = result[: sizes.pts] * 256.0 + result[sizes.pts : 2 * sizes.pts]
    write_messages(fields, None, sizes.first_groups, sizes.first_message, out_ref, sizes, extra=listed)


def entries_scatter(fields, entry, sizes, spread_ref, place_ref):
    high, low = entry // LANES, entry % LANES
    parts = [part for value in fields for part in cut(value)]
    for p in range(sizes.pts):
        spread_row(p, [part[p : p + 1] for part in parts], high[p : p + 1], sizes.own_rows, spread_ref)
        place_row(p, low[p : p + 1], LANES, place_ref)
    result = scatter(len(parts), sizes.pts * LANES, sizes.own_rows, LANES, spread_ref, place_ref)
    return joined(result, len(fields), sizes.own_rows)


def send_owned(scaled, partial, entry, out_ref, table_ref, sizes):
    for k in range(CP):
        table_ref[k] = scaled[k]
    fields = gather_rows(lambda c, k: table_ref[c, k : k + 1, :], sizes.run_rows, entry // LANES, entry % LANES, CP)
    write_messages(fields, partial, sizes.groups, sizes.message, out_ref, sizes)


def dot_fields(left, right):
    return jnp.sum(sum(a * b for a, b in zip(left, right)), keepdims=True)


def first_owner_kernel(sizes, column_ref, in_ref, out_ref, entry_ref, pre_ref, rem_ref, scaled_ref,
                       table_ref, spread_ref, place_ref):
    listed = jnp.zeros((sizes.pts, LANES), f32)
    for c in range(sizes.cams):
        row = read_row(in_ref, c, sizes.first_groups, sizes.first_message, sizes)
        listed = jnp.where(column_ref[0] == c, row, listed)
    entry = listed.astype(jnp.int32) % sizes.run
    entry_ref[...] = entry
    fields = read_messages(in_ref, 2 * CP, sizes.first_message, sizes)
    sums = entries_scatter(fields, entry, sizes, spread_ref, place_ref)
    remainder = [-value for value in sums[:CP]]
    precondition = [1.0 / (value + damping_camera) for value in sums[CP:]]
    scaled = [p * r for p, r in zip(precondition, remainder)]
    for k in range(CP):
        pre_ref[k] = precondition[k]
        rem_ref[k] = remainder[k]
        scaled_ref[k] = scaled[k]
    send_owned(scaled, dot_fields(remainder, scaled), entry, out_ref, table_ref, sizes)


def owner_kernel(sizes, in_ref, entry_ref, pre_ref, rem_ref, dir_ref, product_ref,
                 out_ref, new_rem_ref, scaled_ref, step_ref, table_ref, spread_ref, place_ref):
    entry = entry_ref[...]
    fields = read_messages(in_ref, CP, sizes.message, sizes)
    curvature = read_scalar(in_ref, sizes.groups, sizes.message, sizes)
    step = product_ref[...] / jnp.broadcast_to(curvature, (SUB, LANES))
    step_ref[...] = step
    sums = entries_scatter(fields, entry, sizes, spread_ref, place_ref)
    remainder, scaled = [], []
    for k in range(CP):
        value = rem_ref[k] - step[:1] * (sums[k] + damping_camera * dir_ref[k])
        new_rem_ref[k] = value
        remainder.append(value)
        scaled.append(pre_ref[k] * value)
        scaled_ref[k] = scaled[k]
    send_owned(scaled, dot_fields(remainder, scaled), entry, out_ref, table_ref, sizes)


def schur_kernel(sizes, start, last, in_ref, a_ref, b_ref, inv_ref, slot_ref, point_ref,
                 place_point_ref, scaled_ref, grad_ref, *refs):
    refs = list(refs)
    if not start:
        product_ref, at_slot_ref, dir_ref, step_ref, sum_ref = refs[:5]
        refs = refs[5:]
    out_ref, new_product_ref, new_at_slot_ref, new_dir_ref, new_sum_ref = refs[:5]
    new_grad_ref = None
    refs = refs[5:]
    if not start:
        new_grad_ref = refs.pop(0)
    q_ref, parts_ref, spread_ref, table_ref, place_slot_ref = refs
    rows = sizes.rows

    def at(ref, comp, group):
        return ref[comp * rows + group * SUB : comp * rows + (group + 1) * SUB, :]

    renewed = jnp.broadcast_to(read_scalar(in_ref, sizes.groups, sizes.message, sizes), (SUB, LANES))
    new_product_ref[...] = renewed
    fields = read_messages(in_ref, CP, sizes.message, sizes)
    beta = None if start else (renewed / product_ref[...])[:1]
    squares = None
    for k in range(CP):
        direction = scaled_ref[k]
        if start:
            new_at_slot_ref[k] = fields[k]
        else:
            new_at_slot_ref[k] = fields[k] + beta * at_slot_ref[k]
            direction = direction + beta * dir_ref[k]
        new_dir_ref[k] = direction
        squares = direction * direction if squares is None else squares + direction * direction

    for group in range(rows // SUB):
        high, low = slot_place(slot_ref[group * SUB : (group + 1) * SUB, :], sizes)
        gathered = gather_rows(lambda c, k: new_at_slot_ref[c, k : k + 1, :], sizes.pts, high, low, CP)
        q = [sum(at(a_ref, i * CP + k, group) * gathered[k] for k in range(CP)) for i in range(2)]
        for i in range(2):
            q_ref[i * rows + group * SUB : i * rows + (group + 1) * SUB, :] = q[i]
        values = [at(b_ref, k, group) * q[0] + at(b_ref, 3 + k, group) * q[1] for k in range(3)]
        parts = [part for value in values for part in cut(value)]
        keep_parts(parts, group, parts_ref)
        for s in range(SUB):
            row = group * SUB + s
            spread_row(row, part_rows(len(parts), group, s, parts_ref), point_ref[row : row + 1, :] >> 8, PT_HI, spread_ref)
    result = scatter(3 * PIECES, sizes.obs, PT_HI, PT_LO, spread_ref, place_point_ref)
    sums = joined(result, 3, PT_HI)
    folded = solve([inv_ref[k] for k in range(6)], sums)
    for k in range(3):
        new_sum_ref[k] = sums[k]
        if not start:
            new_grad_ref[k] = grad_ref[k] + step_ref[:1, :1] * sum_ref[k]

    inner = None
    for k in range(3):
        table_ref[k] = folded[k]
    for group in range(rows // SUB):
        at_point = point_gather(table_ref, point_ref[group * SUB : (group + 1) * SUB, :])
        q = [at(q_ref, i, group) for i in range(2)]
        errors = [q[i] - sum(at(b_ref, 3 * i + k, group) * at_point[k] for k in range(3)) for i in range(2)]
        here = q[0] * errors[0] + q[1] * errors[1]
        inner = here if inner is None else inner + here
        if not last:
            values = [at(a_ref, k, group) * errors[0] + at(a_ref, CP + k, group) * errors[1] for k in range(CP)]
            parts = [part for value in values for part in cut(value)]
            keep_parts(parts, group, parts_ref)
            for s in range(SUB):
                row = group * SUB + s
                high, low = slot_place(slot_ref[row : row + 1, :], sizes)
                spread_row(row, part_rows(len(parts), group, s, parts_ref), high, sizes.pts, spread_ref)
                place_row(row, low, LANES, place_slot_ref)
    partial = jnp.sum(inner, keepdims=True) + damping_camera * jnp.sum(squares, keepdims=True)
    if last:
        out_ref[...] = jnp.broadcast_to(partial, (sizes.devices, LANES))
        return
    result = scatter(CP * PIECES, sizes.obs, sizes.pts, LANES, spread_ref, place_slot_ref)
    fields = joined(result, CP, sizes.pts)
    write_messages(fields, partial, sizes.groups, sizes.message, out_ref, sizes)


def final_kernel(sizes, in_ref, inv_ref, grad_ref, sum_ref, early_ref, late_ref, *refs):
    products, steps = [ref[...] for ref in refs[:ITERS]], [ref[...] for ref in refs[ITERS : 2 * ITERS - 1]]
    cam_ref, pt_ref, table_ref = refs[2 * ITERS - 1 :]
    curvature = jnp.sum(jnp.where(lane_iota(sizes.devices) == 0, in_ref[...], 0.0), keepdims=True)
    steps.append(products[-1] / jnp.broadcast_to(curvature, (SUB, LANES)))
    factors = [steps[-1]]
    for k in reversed(range(ITERS - 1)):
        factors.insert(0, steps[k] + factors[0] * (products[k + 1] / products[k]))
    factors = [factor[:1] for factor in factors]
    step = steps[-1][:1]
    for r in range(sizes.pts):
        for h in range(sizes.run_rows):
            columns = slice((r * sizes.run_rows + h) * LANES, (r * sizes.run_rows + h + 1) * LANES)
            for start in range(0, CP, SUB):
                size = min(SUB, CP - start)
                total = None
                for k, factor in enumerate(factors):
                    ref, held, place = (late_ref, 1, 0) if k == ITERS - 1 else (early_ref, ITERS - 1, k)
                    first = ((r * held + place) * CP + start) * sizes.own_rows + h
                    term = factor * ref[pl.ds(first, size, stride=sizes.own_rows), :]
                    total = term if total is None else total + term
                cam_ref[start : start + size, columns] = total
    total = [grad_ref[k] + step[:, :1] * sum_ref[k] for k in range(3)]
    solved = solve([inv_ref[k] for k in range(6)], total)
    for k in range(3):
        table_ref[k * PT_HI : (k + 1) * PT_HI, :] = -solved[k]
    for row in range(PT_HI):
        for k in range(3):
            pt_ref[k : k + 1, row * PT_LO : (row + 1) * PT_LO] = table_ref[k * PT_HI + row : k * PT_HI + row + 1, :]


def shape(*dims, dtype=f32):
    return jax.ShapeDtypeStruct(dims, dtype)


def kept(*dims, dtype=f32):
    return pltpu.VMEM(dims, dtype)


def call(kernel, name, inputs, outputs, scratch, scalars=(), inputs_at=pltpu.VMEM, cost=None):
    vmem = pl.BlockSpec(memory_space=pltpu.VMEM)
    given = pl.BlockSpec(memory_space=inputs_at)
    smem = pl.BlockSpec(memory_space=pltpu.SMEM)
    return pl.pallas_call(
        kernel,
        name=name,
        out_shape=outputs,
        in_specs=[smem] * len(scalars) + [given] * len(inputs),
        out_specs=[vmem] * len(outputs),
        scratch_shapes=scratch,
        cost_estimate=cost,
        compiler_params=pltpu.CompilerParams(vmem_limit_bytes=VMEM_LIMIT),
    )(*scalars, *inputs)


def body(camera_jacobian, point_jacobian, residual, observed_slot, observed_point, send_list):
    sizes = Sizes(lax.axis_size("pts"), lax.axis_size("cams"), send_list.shape[2], camera_jacobian.shape[1])
    axes = ("pts", "cams")
    rows = sizes.rows
    slot = observed_slot.reshape(rows, LANES)
    point = observed_point.reshape(rows, LANES)
    column = lax.axis_index("cams").astype(jnp.int32).reshape(1)

    def exchange(messages):
        width = messages.size // sizes.devices
        flat = messages.reshape(sizes.devices, 1, width)
        return lax.all_to_all(flat, axes, split_axis=0, concat_axis=0, tiled=True).reshape(messages.shape)

    def factors(high_rows, low_rows, entries):
        return [pltpu.VMEM((high_rows, entries), bf16), pltpu.VMEM((low_rows, entries), bf16)]

    point_table = kept(3, PT_HI, PT_LO)
    owned = kept(CP, sizes.own_rows, LANES)
    messages = kept(sizes.devices * sizes.message, LANES)
    scalar = kept(SUB, LANES)
    owned_scratch = pltpu.VMEM((CP, sizes.own_rows, LANES), f32)
    entries = sizes.pts * LANES

    gather_scratch = [pltpu.VMEM((3, PT_HI, PT_LO), f32), pltpu.VMEM((LANES, sizes.obs), bf16)]

    def parts_scratch(count):
        return pltpu.VMEM((rows // SUB, count * SUB, LANES), f32)


    given = [
        pltpu.with_memory_space_constraint(value, pltpu.HBM)
        for value in (camera_jacobian, point_jacobian, residual, slot, point, send_list[0])
    ]
    first, a, b, inverse, gradient, place_point, slot, point = call(
        functools.partial(setup_kernel, sizes),
        "setup",
        given,
        [
            kept(sizes.devices * sizes.first_message, LANES),
            kept(2 * CP * rows, LANES),
            kept(6 * rows, LANES),
            kept(6, PT_HI, PT_LO),
            point_table,
            kept(PT_LO, sizes.obs, dtype=bf16),
            kept(rows, LANES, dtype=jnp.int32),
            kept(rows, LANES, dtype=jnp.int32),
        ],
        [pltpu.VMEM((2 * rows, LANES), f32), parts_scratch(2 * CP * PIECES)]
        + [pltpu.VMEM((max(spread_rows(6 * FINE + 3 * PIECES, PT_HI), spread_rows(2 * CP * PIECES, sizes.pts)), sizes.obs), bf16)]
        + gather_scratch
        + [pltpu.VMEM((LANES, sizes.cams * sizes.slot), bf16)]
        + [pltpu.VMEM(value.shape, value.dtype) for value in given]
        + [pltpu.SemaphoreType.DMA((len(given),))],
        inputs_at=pl.ANY,
    )
    out, entry, precondition, remainder, scaled = call(
        functools.partial(first_owner_kernel, sizes),
        "first_owner",
        [exchange(first)],
        [messages, kept(sizes.pts, LANES, dtype=jnp.int32), owned, owned, owned],
        [owned_scratch] + factors(spread_rows(2 * CP * PIECES, sizes.own_rows), LANES, entries),
        scalars=[column],
    )
    schur_scratch = [pltpu.VMEM((2 * rows, LANES), f32), parts_scratch(CP * PIECES)]
    schur_scratch += [pltpu.VMEM((max(spread_rows(3 * PIECES, PT_HI), spread_rows(CP * PIECES, sizes.pts)), sizes.obs), bf16)]
    schur_scratch += gather_scratch
    at_slot = kept(CP, sizes.pts, LANES)
    product = slots = direction = step = sums = None
    products, steps, everything = [], [], [scaled]

    def over_pts(values):
        rows = jnp.concatenate(values).reshape(-1, LANES)
        return lax.all_gather(rows, "pts", axis=0, tiled=True)

    for iteration in range(ITERS):
        start, last = iteration == 0, iteration == ITERS - 1
        earlier = [] if start else [product, slots, direction, step, sums]
        results = call(
            functools.partial(schur_kernel, sizes, start, last),
            "schur_last" if last else "schur",
            [exchange(out), a, b, inverse, slot, point, place_point, scaled, gradient] + earlier,
            [kept(sizes.devices, LANES) if last else messages, scalar, at_slot, owned, point_table]
            + ([] if start else [point_table]),
            schur_scratch,
            cost=pl.CostEstimate(flops=2_000_000_000, bytes_accessed=10_000_000, transcendentals=0),
        )
        out, product, slots, direction, sums = results[:5]
        products.append(product)
        if not start:
            gradient = results[5]
        if last:
            break
        out, remainder, scaled, step = call(
            functools.partial(owner_kernel, sizes),
            "owner",
            [exchange(out), entry, precondition, remainder, direction, product],
            [messages, owned, owned, scalar],
            [owned_scratch] + factors(spread_rows(CP * PIECES, sizes.own_rows), LANES, entries),
        )
        steps.append(step)
        everything.append(scaled)
    return call(
        functools.partial(final_kernel, sizes),
        "final",
        [exchange(out), inverse, gradient, sums, over_pts(everything[:-1]), over_pts(everything[-1:])] + products + steps,
        [shape(CP, CAM_OWN), shape(3, PT_DEV)],
        [pltpu.VMEM((3 * PT_HI, PT_LO), f32)],
    )


def solution(mesh):
    return jax.shard_map(
        lambda *arguments: tuple(body(*arguments)),
        mesh=mesh,
        in_specs=(
            P(None, ("pts", "cams")),
            P(None, ("pts", "cams")),
            P(None, ("pts", "cams")),
            P(("pts", "cams")),
            P(("pts", "cams")),
            P(("pts", "cams"), None, None),
        ),
        out_specs=(P(None, "cams"), P(None, ("pts", "cams"))),
        check_vma=False,
    )
```

```python
import functools

import jax
import jax.numpy as jnp
from jax import lax
from jax.experimental import pallas as pl
from jax.experimental.pallas import tpu as pltpu
from jax.sharding import PartitionSpec as P

CP = 9
CAM_OWN = 8192
PT_DEV = 4096
ITERS = 3
LANES = 128
SUB = 8
PT_LO = 256
PT_HI = PT_DEV // PT_LO
PIECES = 2
FINE = 3
FIRST = 4
VMEM_LIMIT = 24 * 1024 * 1024

damping_camera = 1.0
damping_point = 1.0

f32 = jnp.float32
bf16 = jnp.bfloat16


class Sizes:
    def __init__(self, pts, cams, slot, obs):
        self.pts, self.cams, self.slot, self.obs = pts, cams, slot, obs
        self.devices = pts * cams
        self.block = slot // pts
        assert cams * self.block == LANES and LANES % pts == 0
        self.rows = obs // LANES
        self.run = CAM_OWN // pts
        self.run_rows = self.run // LANES
        self.own_rows = max(SUB, self.run_rows)
        self.groups = -(-CP // cams)
        self.first_groups = -(-2 * CP // cams)
        self.message = self.groups
        self.first_message = self.first_groups + 1
        assert self.groups * cams > CP


def sub_iota(rows):
    return lax.broadcasted_iota(jnp.int32, (rows, LANES), 0)


def lane_iota(rows):
    return lax.broadcasted_iota(jnp.int32, (rows, LANES), 1)


def cut(value, pieces=PIECES):
    parts = []
    for _ in range(pieces - 1):
        part = value.astype(bf16).astype(f32)
        parts.append(part)
        value = value - part
    parts.append(value)
    return parts


def swap_blocks(rows, block, wanted):
    which = lane_iota(rows[0].shape[0]) // block
    result = []
    for q in range(wanted):
        total = None
        for c, value in enumerate(rows):
            shift = ((c - q) * block) % LANES
            moved = pltpu.roll(value, shift, axis=1) if shift else value
            total = jnp.where(which == c, moved, 0.0 if total is None else total)
        result.append(total)
    return result


def gather_rows(row, count, high, low, comps):
    result = [None] * comps
    for k in range(count):
        here = high == k
        for c in range(comps):
            source = jnp.broadcast_to(row(c, k), high.shape)
            found = jnp.take_along_axis(source, low, axis=1, mode="promise_in_bounds")
            result[c] = found if k == 0 else jnp.where(here, found, result[c])
    return result


def spread_row(index, parts, high, high_count, spread_ref):
    columns = slice(index * LANES, (index + 1) * LANES)
    mask = jnp.broadcast_to(high, (high_count, LANES)) == sub_iota(high_count)
    together = max(1, 16 // high_count)
    for start in range(0, len(parts), together):
        pieces = [
            jnp.where(mask, jnp.broadcast_to(part, (high_count, LANES)), 0.0)
            for part in parts[start : start + together]
        ]
        while len(pieces) < together:
            pieces.append(jnp.zeros((high_count, LANES), f32))
        tile = pieces[0] if together == 1 else jnp.concatenate(pieces, axis=0)
        spread_ref[start * high_count : start * high_count + tile.shape[0], columns] = tile.astype(bf16)


def place_row(index, low, low_count, place_ref):
    columns = slice(index * LANES, (index + 1) * LANES)
    place = jnp.broadcast_to(low, (low_count, LANES)) == sub_iota(low_count)
    place_ref[:low_count, columns] = jnp.where(place, 1.0, 0.0).astype(bf16)


def keep_parts(parts, group, parts_ref):
    for k, part in enumerate(parts):
        parts_ref[group, k * SUB : (k + 1) * SUB, :] = part


def part_rows(count, group, s, parts_ref):
    return [parts_ref[group, k * SUB + s : k * SUB + s + 1, :] for k in range(count)]


def spread_rows(parts, high_count):
    return -(-parts * high_count // 16) * 16


def scatter(parts, entries, high_count, low_count, spread_ref, place_ref):
    rows = spread_rows(parts, high_count)
    return lax.dot_general(
        spread_ref[:rows, :entries],
        place_ref[:low_count, :entries],
        (((1,), (1,)), ((), ())),
        preferred_element_type=f32,
    )


def joined(result, count, high_count, pieces=None):
    pieces = pieces or [PIECES] * count
    values, first = [], 0
    for number in pieces:
        rows = [result[first + k * high_count : first + (k + 1) * high_count] for k in range(number)]
        first += number * high_count
        total = rows[-1]
        for row in reversed(rows[:-1]):
            total = total + row
        values.append(total)
    return values


def point_gather(ref, point):
    wide = PT_LO // LANES
    row = lambda c, k: ref[c, k // wide : k // wide + 1, (k % wide) * LANES : (k % wide + 1) * LANES]
    return gather_rows(row, PT_HI * wide, point // LANES, point % LANES, 3)


def slot_place(slot, sizes):
    within = slot % sizes.slot
    return within % sizes.pts, (slot // sizes.slot) * sizes.block + within // sizes.pts


def solve(inverse, values):
    first = inverse[0] * values[0] + inverse[1] * values[1] + inverse[2] * values[2]
    second = inverse[1] * values[0] + inverse[3] * values[1] + inverse[4] * values[2]
    third = inverse[2] * values[0] + inverse[4] * values[1] + inverse[5] * values[2]
    return first, second, third


def write_messages(fields, scalar, groups, message, out_ref, sizes, extra=None):
    which = lane_iota(sizes.pts) // sizes.block
    for g in range(groups):
        rows = fields[g * sizes.cams : (g + 1) * sizes.cams]
        moved = swap_partial(rows, sizes)
        for c in range(sizes.cams):
            value = moved[c]
            if g == groups - 1 and scalar is not None:
                value = jnp.where(which == sizes.cams - 1, scalar, value)
            out_ref[pl.ds(c * message + g, sizes.pts, stride=sizes.cams * message), :] = value
    for g in range(groups, message):
        for c in range(sizes.cams):
            value = extra if (extra is not None and g == groups) else jnp.zeros((sizes.pts, LANES), f32)
            out_ref[pl.ds(c * message + g, sizes.pts, stride=sizes.cams * message), :] = value


def swap_partial(rows, sizes):
    return swap_blocks(rows, sizes.block, sizes.cams)


def read_row(in_ref, c, g, message, sizes):
    return in_ref[pl.ds(c * message + g, sizes.pts, stride=sizes.cams * message), :]


def read_messages(in_ref, count, message, sizes):
    fields = []
    group = 0
    while len(fields) < count:
        rows = [read_row(in_ref, c, group, message, sizes) for c in range(sizes.cams)]
        fields += swap_blocks(rows, sizes.block, min(sizes.cams, count - len(fields)))
        group += 1
    return fields


def read_scalar(in_ref, groups, message, sizes):
    total = read_row(in_ref, 0, groups - 1, message, sizes)
    for c in range(1, sizes.cams):
        total = total + read_row(in_ref, c, groups - 1, message, sizes)
    chosen = jnp.where(lane_iota(sizes.pts) == LANES - 1, total, 0.0)
    return jnp.sum(chosen, keepdims=True)


def setup_kernel(sizes, *refs):
    sources, refs = refs[:6], refs[6:]
    out_ref, a_ref, b_ref, inv_ref, grad_ref, place_point_ref, new_slot_ref, new_point_ref = refs[:8]
    refs = refs[8:]
    r_ref, parts_ref, spread_ref, table_ref, place_slot_ref, place_list_ref = refs[:6]
    jac_ref, pjac_ref, res_ref, slot_ref, point_ref, list_ref = refs[6:12]
    semaphores = refs[12]
    rows = sizes.rows
    copies = [
        pltpu.make_async_copy(source, target, semaphores.at[k])
        for k, (source, target) in enumerate(zip(sources, refs[6:12]))
    ]
    for copy in copies:
        copy.start()
    for copy in copies:
        copy.wait()
    new_slot_ref[...] = slot_ref[...]
    new_point_ref[...] = point_ref[...]
    for j in range(rows):
        columns = slice(j * LANES, (j + 1) * LANES)
        for start in range(0, 2 * CP, SUB):
            size = min(SUB, 2 * CP - start)
            a_ref[pl.ds(start * rows + j, size, stride=rows), :] = jac_ref[start : start + size, columns]
        b_ref[pl.ds(j, 6, stride=rows), :] = pjac_ref[:, columns]
        r_ref[pl.ds(j, 2, stride=rows), :] = res_ref[:, columns]

    def at(ref, comp, group):
        return ref[comp * rows + group * SUB : comp * rows + (group + 1) * SUB, :]

    normal_pieces = [FINE] * 6 + [PIECES] * 3

    for group in range(rows // SUB):
        b = [at(b_ref, k, group) for k in range(6)]
        r = [at(r_ref, k, group) for k in range(2)]
        values = [b[i] * b[j] + b[3 + i] * b[3 + j] for i, j in ((0, 0), (0, 1), (0, 2), (1, 1), (1, 2), (2, 2))]
        values += [b[i] * r[0] + b[3 + i] * r[1] for i in range(3)]
        parts = [part for value, pieces in zip(values, normal_pieces) for part in cut(value, pieces)]
        keep_parts(parts, group, parts_ref)
        for s in range(SUB):
            row = group * SUB + s
            point = point_ref[row : row + 1, :]
            spread_row(row, part_rows(len(parts), group, s, parts_ref), point >> 8, PT_HI, spread_ref)
            place_row(row, point & (PT_LO - 1), PT_LO, place_point_ref)
    result = scatter(sum(normal_pieces), sizes.obs, PT_HI, PT_LO, spread_ref, place_point_ref)
    normal = joined(result, 9, PT_HI, normal_pieces)
    top_left = normal[0] + damping_point
    top_mid = normal[1]
    top_right = normal[2]
    mid_mid = normal[3] + damping_point
    mid_right = normal[4]
    low_right = normal[5] + damping_point
    adjugate = [
        mid_mid * low_right - mid_right * mid_right,
        top_right * mid_right - top_mid * low_right,
        top_mid * mid_right - top_right * mid_mid,
        top_left * low_right - top_right * top_right,
        top_mid * top_right - top_left * mid_right,
        top_left * mid_mid - top_mid * top_mid,
    ]
    determinant = top_left * adjugate[0] + top_mid * adjugate[1] + top_right * adjugate[2]
    inverse = [value / determinant for value in adjugate]
    for k in range(6):
        inv_ref[k] = inverse[k]
    for k in range(3):
        grad_ref[k] = normal[6 + k]
    eliminated = solve(inverse, normal[6:])
    for k in range(3):
        table_ref[k] = eliminated[k]
    for group in range(rows // SUB):
        at_point = point_gather(table_ref, point_ref[group * SUB : (group + 1) * SUB, :])
        b = [at(b_ref, k, group) for k in range(6)]
        errors = [at(r_ref, i, group) - sum(b[3 * i + k] * at_point[k] for k in range(3)) for i in range(2)]
        a = [at(a_ref, k, group) for k in range(2 * CP)]
        values = [a[k] * errors[0] + a[CP + k] * errors[1] for k in range(CP)]
        values += [a[k] * a[k] + a[CP + k] * a[CP + k] for k in range(CP)]
        parts = [part for value in values for part in cut(value)]
        keep_parts(parts, group, parts_ref)
        for s in range(SUB):
            row = group * SUB + s
            high, low = slot_place(slot_ref[row : row + 1, :], sizes)
            spread_row(row, part_rows(len(parts), group, s, parts_ref), high, sizes.pts, spread_ref)
            place_row(row, low, LANES, place_slot_ref)
    result = scatter(2 * CP * PIECES, sizes.obs, sizes.pts, LANES, spread_ref, place_slot_ref)
    fields = joined(result, 2 * CP, sizes.pts)

    pieces = sizes.slot // LANES
    lane = lane_iota(1)
    for c in range(sizes.cams):
        for half in range(pieces):
            value = list_ref[c : c + 1, half * LANES : (half + 1) * LANES]
            low = c * sizes.block + half * (LANES // sizes.pts) + lane // sizes.pts
            parts = [(value >> 8).astype(f32), (value & 255).astype(f32)]
            spread_row(c * pieces + half, parts, lane % sizes.pts, sizes.pts, spread_ref)
            place_row(c * pieces + half, low, LANES, place_list_ref)
    result = scatter(2, sizes.cams * sizes.slot, sizes.pts, LANES, spread_ref, place_list_ref)
    listed = result[: sizes.pts] * 256.0 + result[sizes.pts : 2 * sizes.pts]
    write_messages(fields, None, sizes.first_groups, sizes.first_message, out_ref, sizes, extra=listed)


def entries_scatter(fields, entry, sizes, spread_ref, place_ref):
    high, low = entry // LANES, entry % LANES
    parts = [part for value in fields for part in cut(value)]
    for p in range(sizes.pts):
        spread_row(p, [part[p : p + 1] for part in parts], high[p : p + 1], sizes.own_rows, spread_ref)
        place_row(p, low[p : p + 1], LANES, place_ref)
    result = scatter(len(parts), sizes.pts * LANES, sizes.own_rows, LANES, spread_ref, place_ref)
    return joined(result, len(fields), sizes.own_rows)


def send_owned(scaled, partial, entry, out_ref, table_ref, sizes):
    for k in range(CP):
        table_ref[k] = scaled[k]
    fields = gather_rows(lambda c, k: table_ref[c, k : k + 1, :], sizes.run_rows, entry // LANES, entry % LANES, CP)
    write_messages(fields, partial, sizes.groups, sizes.message, out_ref, sizes)


def dot_fields(left, right):
    return jnp.sum(sum(a * b for a, b in zip(left, right)), keepdims=True)


def first_owner_kernel(sizes, column_ref, in_ref, out_ref, entry_ref, pre_ref, rem_ref,
                       table_ref, spread_ref, place_ref):
    listed = jnp.zeros((sizes.pts, LANES), f32)
    for c in range(sizes.cams):
        row = read_row(in_ref, c, sizes.first_groups, sizes.first_message, sizes)
        listed = jnp.where(column_ref[0] == c, row, listed)
    entry = listed.astype(jnp.int32) % sizes.run
    entry_ref[...] = entry
    fields = read_messages(in_ref, 2 * CP, sizes.first_message, sizes)
    sums = entries_scatter(fields, entry, sizes, spread_ref, place_ref)
    remainder = [-value for value in sums[:CP]]
    precondition = [1.0 / (value + damping_camera) for value in sums[CP:]]
    scaled = [p * r for p, r in zip(precondition, remainder)]
    for k in range(CP):
        pre_ref[k] = precondition[k]
        rem_ref[k] = remainder[k]
    send_owned(scaled, dot_fields(remainder, scaled), entry, out_ref, table_ref, sizes)


def owner_kernel(sizes, start, final, in_ref, entry_ref, pre_ref, rem_ref, dir_ref, product_ref, *refs):
    refs = list(refs)
    sol_ref = None if start else refs.pop(0)
    out_ref, new_rem_ref, new_sol_ref, step_ref = refs[:4]
    fields_ref = refs[4] if final else None
    table_ref, spread_ref, place_ref = refs[-3:]
    entry = entry_ref[...]
    fields = read_messages(in_ref, CP, sizes.message, sizes)
    curvature = read_scalar(in_ref, sizes.groups, sizes.message, sizes)
    step = product_ref[...] / jnp.broadcast_to(curvature, (SUB, LANES))
    step_ref[...] = step
    sums = entries_scatter(fields, entry, sizes, spread_ref, place_ref)
    remainder, scaled = [], []
    for k in range(CP):
        direction = dir_ref[k]
        moved = step[:1] * direction
        moved = moved if start else sol_ref[k] + moved
        new_sol_ref[k] = moved
        value = rem_ref[k] - step[:1] * (sums[k] + damping_camera * direction)
        new_rem_ref[k] = value
        remainder.append(value)
        scaled.append(pre_ref[k] * value)
        if final:
            for j, field in enumerate((moved, direction, scaled[k])):
                first = (j * CP + k) * sizes.own_rows
                fields_ref[first : first + sizes.own_rows, :] = field
    send_owned(scaled, dot_fields(remainder, scaled), entry, out_ref, table_ref, sizes)


def schur_kernel(sizes, start, last, in_ref, a_ref, b_ref, inv_ref, slot_ref, point_ref,
                 place_point_ref, pre_ref, rem_ref, grad_ref, *refs):
    refs = list(refs)
    if not start:
        product_ref, at_slot_ref, dir_ref, step_ref, sum_ref = refs[:5]
        refs = refs[5:]
    out_ref, new_product_ref, new_at_slot_ref, new_dir_ref, new_sum_ref = refs[:5]
    new_grad_ref = None
    refs = refs[5:]
    if not start:
        new_grad_ref = refs.pop(0)
    q_ref, parts_ref, spread_ref, table_ref, place_slot_ref = refs
    rows = sizes.rows

    def at(ref, comp, group):
        return ref[comp * rows + group * SUB : comp * rows + (group + 1) * SUB, :]

    renewed = jnp.broadcast_to(read_scalar(in_ref, sizes.groups, sizes.message, sizes), (SUB, LANES))
    new_product_ref[...] = renewed
    fields = read_messages(in_ref, CP, sizes.message, sizes)
    beta = None if start else (renewed / product_ref[...])[:1]
    squares = None
    for k in range(CP):
        direction = pre_ref[k] * rem_ref[k]
        if start:
            new_at_slot_ref[k] = fields[k]
        else:
            new_at_slot_ref[k] = fields[k] + beta * at_slot_ref[k]
            direction = direction + beta * dir_ref[k]
        new_dir_ref[k] = direction
        squares = direction * direction if squares is None else squares + direction * direction

    for group in range(rows // SUB):
        high, low = slot_place(slot_ref[group * SUB : (group + 1) * SUB, :], sizes)
        gathered = gather_rows(lambda c, k: new_at_slot_ref[c, k : k + 1, :], sizes.pts, high, low, CP)
        q = [sum(at(a_ref, i * CP + k, group) * gathered[k] for k in range(CP)) for i in range(2)]
        for i in range(2):
            q_ref[i * rows + group * SUB : i * rows + (group + 1) * SUB, :] = q[i]
        values = [at(b_ref, k, group) * q[0] + at(b_ref, 3 + k, group) * q[1] for k in range(3)]
        parts = [part for value in values for part in cut(value)]
        keep_parts(parts, group, parts_ref)
        for s in range(SUB):
            row = group * SUB + s
            spread_row(row, part_rows(len(parts), group, s, parts_ref), point_ref[row : row + 1, :] >> 8, PT_HI, spread_ref)
    result = scatter(3 * PIECES, sizes.obs, PT_HI, PT_LO, spread_ref, place_point_ref)
    sums = joined(result, 3, PT_HI)
    folded = solve([inv_ref[k] for k in range(6)], sums)
    for k in range(3):
        new_sum_ref[k] = sums[k]
        if not start:
            new_grad_ref[k] = grad_ref[k] + step_ref[:1, :1] * sum_ref[k]

    inner = None
    for k in range(3):
        table_ref[k] = folded[k]
    for group in range(rows // SUB):
        at_point = point_gather(table_ref, point_ref[group * SUB : (group + 1) * SUB, :])
        q = [at(q_ref, i, group) for i in range(2)]
        errors = [q[i] - sum(at(b_ref, 3 * i + k, group) * at_point[k] for k in range(3)) for i in range(2)]
        here = q[0] * errors[0] + q[1] * errors[1]
        inner = here if inner is None else inner + here
        if not last:
            values = [at(a_ref, k, group) * errors[0] + at(a_ref, CP + k, group) * errors[1] for k in range(CP)]
            parts = [part for value in values for part in cut(value)]
            keep_parts(parts, group, parts_ref)
            for s in range(SUB):
                row = group * SUB + s
                high, low = slot_place(slot_ref[row : row + 1, :], sizes)
                spread_row(row, part_rows(len(parts), group, s, parts_ref), high, sizes.pts, spread_ref)
                place_row(row, low, LANES, place_slot_ref)
    partial = jnp.sum(inner, keepdims=True) + damping_camera * jnp.sum(squares, keepdims=True)
    if last:
        out_ref[...] = jnp.broadcast_to(partial, (sizes.devices, LANES))
        return
    result = scatter(CP * PIECES, sizes.obs, sizes.pts, LANES, spread_ref, place_slot_ref)
    fields = joined(result, CP, sizes.pts)
    write_messages(fields, partial, sizes.groups, sizes.message, out_ref, sizes)


def tail_kernel(sizes, in_ref, product_ref, own_ref, other_ref, out_ref):
    renewed = jnp.broadcast_to(read_scalar(in_ref, sizes.groups, sizes.message, sizes), (SUB, LANES))
    beta = (renewed / product_ref[...])[:1]
    field = CP * sizes.own_rows
    for j, ref in enumerate((own_ref, other_ref)):
        first = j * 2 * field
        out_ref[first : first + field, :] = ref[:field, :]
        out_ref[first + field : first + 2 * field, :] = ref[2 * field :, :] + beta * ref[field : 2 * field, :]


def final_kernel(sizes, masks, run_ref, in_ref, product_ref, inv_ref, grad_ref, sum_ref, *refs):
    all_refs = refs[: len(masks)]
    cam_ref, pt_ref, table_ref = refs[len(masks) :]
    curvature = jnp.sum(jnp.where(lane_iota(sizes.devices) == 0, in_ref[...], 0.0), keepdims=True)
    step = (product_ref[...] / jnp.broadcast_to(curvature, (SUB, LANES)))[:1]
    for all_ref, pair in zip(all_refs, masks):
        for j, mask in enumerate(pair):
            base_column = (run_ref[0] ^ mask) * sizes.run
            for h in range(sizes.run_rows):
                columns = pl.ds(pl.multiple_of(base_column + h * LANES, LANES), LANES)
                for start in range(0, CP, SUB):
                    size = min(SUB, CP - start)
                    first = (j * 2 * CP + start) * sizes.own_rows + h
                    base = all_ref[pl.ds(first, size, stride=sizes.own_rows), :]
                    direction = all_ref[pl.ds(first + CP * sizes.own_rows, size, stride=sizes.own_rows), :]
                    cam_ref[start : start + size, columns] = base + step * direction
    total = [grad_ref[k] + step[:, :1] * sum_ref[k] for k in range(3)]
    solved = solve([inv_ref[k] for k in range(6)], total)
    for k in range(3):
        table_ref[k * PT_HI : (k + 1) * PT_HI, :] = -solved[k]
    for row in range(PT_HI):
        for k in range(3):
            pt_ref[k : k + 1, row * PT_LO : (row + 1) * PT_LO] = table_ref[k * PT_HI + row : k * PT_HI + row + 1, :]


def shape(*dims, dtype=f32):
    return jax.ShapeDtypeStruct(dims, dtype)


def kept(*dims, dtype=f32):
    return pltpu.VMEM(dims, dtype)


def call(kernel, name, inputs, outputs, scratch, scalars=(), inputs_at=pltpu.VMEM, cost=None):
    vmem = pl.BlockSpec(memory_space=pltpu.VMEM)
    given = pl.BlockSpec(memory_space=inputs_at)
    smem = pl.BlockSpec(memory_space=pltpu.SMEM)
    return pl.pallas_call(
        kernel,
        name=name,
        out_shape=outputs,
        in_specs=[smem] * len(scalars) + [given] * len(inputs),
        out_specs=[vmem] * len(outputs),
        scratch_shapes=scratch,
        cost_estimate=cost,
        compiler_params=pltpu.CompilerParams(vmem_limit_bytes=VMEM_LIMIT),
    )(*scalars, *inputs)


def body(camera_jacobian, point_jacobian, residual, observed_slot, observed_point, send_list):
    sizes = Sizes(lax.axis_size("pts"), lax.axis_size("cams"), send_list.shape[2], camera_jacobian.shape[1])
    axes = ("pts", "cams")
    rows = sizes.rows
    slot = observed_slot.reshape(rows, LANES)
    point = observed_point.reshape(rows, LANES)
    column = lax.axis_index("cams").astype(jnp.int32).reshape(1)

    def exchange(messages):
        width = messages.size // sizes.devices
        flat = messages.reshape(sizes.devices, 1, width)
        return lax.all_to_all(flat, axes, split_axis=0, concat_axis=0, tiled=True).reshape(messages.shape)

    def flipped(value, flip):
        return lax.ppermute(value, "pts", [(p, p ^ flip) for p in range(sizes.pts)])

    def factors(high_rows, low_rows, entries):
        return [pltpu.VMEM((high_rows, entries), bf16), pltpu.VMEM((low_rows, entries), bf16)]

    point_table = kept(3, PT_HI, PT_LO)
    owned = kept(CP, sizes.own_rows, LANES)
    messages = kept(sizes.devices * sizes.message, LANES)
    scalar = kept(SUB, LANES)
    owned_scratch = pltpu.VMEM((CP, sizes.own_rows, LANES), f32)
    entries = sizes.pts * LANES

    gather_scratch = [pltpu.VMEM((3, PT_HI, PT_LO), f32), pltpu.VMEM((LANES, sizes.obs), bf16)]

    def parts_scratch(count):
        return pltpu.VMEM((rows // SUB, count * SUB, LANES), f32)


    given = [
        pltpu.with_memory_space_constraint(value, pltpu.HBM)
        for value in (camera_jacobian, point_jacobian, residual, slot, point, send_list[0])
    ]
    first, a, b, inverse, gradient, place_point, slot, point = call(
        functools.partial(setup_kernel, sizes),
        "setup",
        given,
        [
            kept(sizes.devices * sizes.first_message, LANES),
            kept(2 * CP * rows, LANES),
            kept(6 * rows, LANES),
            kept(6, PT_HI, PT_LO),
            point_table,
            kept(PT_LO, sizes.obs, dtype=bf16),
            kept(rows, LANES, dtype=jnp.int32),
            kept(rows, LANES, dtype=jnp.int32),
        ],
        [pltpu.VMEM((2 * rows, LANES), f32), parts_scratch(2 * CP * PIECES)]
        + [pltpu.VMEM((max(spread_rows(6 * FINE + 3 * PIECES, PT_HI), spread_rows(2 * CP * PIECES, sizes.pts)), sizes.obs), bf16)]
        + gather_scratch
        + [pltpu.VMEM((LANES, sizes.cams * sizes.slot), bf16)]
        + [pltpu.VMEM(value.shape, value.dtype) for value in given]
        + [pltpu.SemaphoreType.DMA((len(given),))],
        inputs_at=pl.ANY,
    )
    out, entry, precondition, remainder = call(
        functools.partial(first_owner_kernel, sizes),
        "first_owner",
        [exchange(first)],
        [messages, kept(sizes.pts, LANES, dtype=jnp.int32), owned, owned],
        [owned_scratch] + factors(spread_rows(2 * CP * PIECES, sizes.own_rows), LANES, entries),
        scalars=[column],
    )
    schur_scratch = [pltpu.VMEM((2 * rows, LANES), f32), parts_scratch(CP * PIECES)]
    schur_scratch += [pltpu.VMEM((max(spread_rows(3 * PIECES, PT_HI), spread_rows(CP * PIECES, sizes.pts)), sizes.obs), bf16)]
    schur_scratch += gather_scratch
    at_slot = kept(CP, sizes.pts, LANES)
    product = slots = direction = step = sums = solution_ = None
    for iteration in range(ITERS):
        start, last = iteration == 0, iteration == ITERS - 1
        earlier = [] if start else [product, slots, direction, step, sums]
        if last:
            neighbour = flipped(fields, FIRST)
        arrived = exchange(out)
        if last:
            (both,) = call(
                functools.partial(tail_kernel, sizes),
                "tail",
                [arrived, product, fields, neighbour],
                [kept(4 * CP * sizes.own_rows, LANES)],
                [],
            )
            flips = [1 << bit for bit in range(sizes.pts.bit_length() - 1) if 1 << bit != FIRST]
            flips = flips[1:] + flips[:1]
            early = {flip: flipped(both, flip) for flip in (flips[0], flips[-1])}
        results = call(
            functools.partial(schur_kernel, sizes, start, last),
            "schur_last" if last else "schur",
            [arrived, a, b, inverse, slot, point, place_point, precondition, remainder, gradient]
            + earlier,
            [kept(sizes.devices, LANES) if last else messages, scalar, at_slot, owned, point_table]
            + ([] if start else [point_table]),
            schur_scratch,
            cost=pl.CostEstimate(flops=2_000_000_000, bytes_accessed=10_000_000, transcendentals=0),
        )
        out, product, slots, direction, sums = results[:5]
        if not start:
            gradient = results[5]
        if last:
            early[flips[0]], out = lax.optimization_barrier((early[flips[0]], out))
            gathered, masks = [both], [(0, FIRST)]
            for flip in flips:
                gathered += [early[flip] if value is both and flip in early else flipped(value, flip) for value in gathered]
                masks += [tuple(mask ^ flip for mask in pair) for pair in masks]
            break
        final = iteration == ITERS - 2
        out, remainder, solution_, step, *rest = call(
            functools.partial(owner_kernel, sizes, start, final),
            "owner_final" if final else "owner",
            [exchange(out), entry, precondition, remainder, direction, product] + ([] if start else [solution_]),
            [messages, owned, owned, scalar] + ([kept(3 * CP * sizes.own_rows, LANES)] if final else []),
            [owned_scratch] + factors(spread_rows(CP * PIECES, sizes.own_rows), LANES, entries),
        )
        fields = rest[0] if final else None
    return call(
        functools.partial(final_kernel, sizes, masks),
        "final",
        [exchange(out), product, inverse, gradient, sums] + gathered,
        [shape(CP, CAM_OWN), shape(3, PT_DEV)],
        [pltpu.VMEM((3 * PT_HI, PT_LO), f32)],
        scalars=[lax.axis_index("pts").astype(jnp.int32).reshape(1)],
    )


def solution(mesh):
    return jax.shard_map(
        lambda *arguments: tuple(body(*arguments)),
        mesh=mesh,
        in_specs=(
            P(None, ("pts", "cams")),
            P(None, ("pts", "cams")),
            P(None, ("pts", "cams")),
            P(("pts", "cams")),
            P(("pts", "cams")),
            P(("pts", "cams"), None, None),
        ),
        out_specs=(P(None, "cams"), P(None, ("pts", "cams"))),
        check_vma=False,
    )
```

```python
import functools

import jax
import jax.numpy as jnp
from jax import lax
from jax.experimental import pallas as pl
from jax.experimental.pallas import tpu as pltpu
from jax.sharding import PartitionSpec as P

CP = 9
CAM_OWN = 8192
PT_DEV = 4096
ITERS = 3
LANES = 128
SUB = 8
PT_LO = 256
PT_HI = PT_DEV // PT_LO
PIECES = 2
FINE = 3
FIRST = 4
VMEM_LIMIT = 24 * 1024 * 1024

damping_camera = 1.0
damping_point = 1.0

f32 = jnp.float32
bf16 = jnp.bfloat16


class Sizes:
    def __init__(self, pts, cams, slot, obs):
        self.pts, self.cams, self.slot, self.obs = pts, cams, slot, obs
        self.devices = pts * cams
        self.block = slot // pts
        assert cams * self.block == LANES and LANES % pts == 0
        self.rows = obs // LANES
        self.run = CAM_OWN // pts
        self.run_rows = self.run // LANES
        self.own_rows = max(SUB, self.run_rows)
        self.groups = -(-CP // cams)
        self.first_groups = -(-2 * CP // cams)
        self.message = self.groups
        self.first_message = self.first_groups + 1
        assert self.groups * cams > CP


def sub_iota(rows):
    return lax.broadcasted_iota(jnp.int32, (rows, LANES), 0)


def lane_iota(rows):
    return lax.broadcasted_iota(jnp.int32, (rows, LANES), 1)


def cut(value, pieces=PIECES):
    parts = []
    for _ in range(pieces - 1):
        part = value.astype(bf16).astype(f32)
        parts.append(part)
        value = value - part
    parts.append(value)
    return parts


def swap_blocks(rows, block, wanted):
    which = lane_iota(rows[0].shape[0]) // block
    result = []
    for q in range(wanted):
        total = None
        for c, value in enumerate(rows):
            shift = ((c - q) * block) % LANES
            moved = pltpu.roll(value, shift, axis=1) if shift else value
            total = jnp.where(which == c, moved, 0.0 if total is None else total)
        result.append(total)
    return result


def gather_rows(row, count, high, low, comps):
    result = [None] * comps
    for k in range(count):
        here = high == k
        for c in range(comps):
            source = jnp.broadcast_to(row(c, k), high.shape)
            found = jnp.take_along_axis(source, low, axis=1, mode="promise_in_bounds")
            result[c] = found if k == 0 else jnp.where(here, found, result[c])
    return result


def spread_row(index, parts, high, high_count, spread_ref):
    columns = slice(index * LANES, (index + 1) * LANES)
    mask = jnp.broadcast_to(high, (high_count, LANES)) == sub_iota(high_count)
    together = max(1, 16 // high_count)
    for start in range(0, len(parts), together):
        pieces = [
            jnp.where(mask, jnp.broadcast_to(part, (high_count, LANES)), 0.0)
            for part in parts[start : start + together]
        ]
        while len(pieces) < together:
            pieces.append(jnp.zeros((high_count, LANES), f32))
        tile = pieces[0] if together == 1 else jnp.concatenate(pieces, axis=0)
        spread_ref[start * high_count : start * high_count + tile.shape[0], columns] = tile.astype(bf16)


def place_row(index, low, low_count, place_ref):
    columns = slice(index * LANES, (index + 1) * LANES)
    place = jnp.broadcast_to(low, (low_count, LANES)) == sub_iota(low_count)
    place_ref[:low_count, columns] = jnp.where(place, 1.0, 0.0).astype(bf16)


def keep_parts(parts, group, parts_ref):
    for k, part in enumerate(parts):
        parts_ref[group, k * SUB : (k + 1) * SUB, :] = part


def part_rows(count, group, s, parts_ref):
    return [parts_ref[group, k * SUB + s : k * SUB + s + 1, :] for k in range(count)]


def spread_rows(parts, high_count):
    return -(-parts * high_count // 16) * 16


def scatter(parts, entries, high_count, low_count, spread_ref, place_ref):
    rows = spread_rows(parts, high_count)
    return lax.dot_general(
        spread_ref[:rows, :entries],
        place_ref[:low_count, :entries],
        (((1,), (1,)), ((), ())),
        preferred_element_type=f32,
    )


def joined(result, count, high_count, pieces=None):
    pieces = pieces or [PIECES] * count
    values, first = [], 0
    for number in pieces:
        rows = [result[first + k * high_count : first + (k + 1) * high_count] for k in range(number)]
        first += number * high_count
        total = rows[-1]
        for row in reversed(rows[:-1]):
            total = total + row
        values.append(total)
    return values


def point_gather(ref, point):
    wide = PT_LO // LANES
    row = lambda c, k: ref[c, k // wide : k // wide + 1, (k % wide) * LANES : (k % wide + 1) * LANES]
    return gather_rows(row, PT_HI * wide, point // LANES, point % LANES, 3)


def slot_place(slot, sizes):
    within = slot % sizes.slot
    return within % sizes.pts, (slot // sizes.slot) * sizes.block + within // sizes.pts


def solve(inverse, values):
    first = inverse[0] * values[0] + inverse[1] * values[1] + inverse[2] * values[2]
    second = inverse[1] * values[0] + inverse[3] * values[1] + inverse[4] * values[2]
    third = inverse[2] * values[0] + inverse[4] * values[1] + inverse[5] * values[2]
    return first, second, third


def write_messages(fields, scalar, groups, message, out_ref, sizes, extra=None, column=None):
    which = lane_iota(sizes.pts) // sizes.block
    for g in range(groups):
        rows = fields[g * sizes.cams : (g + 1) * sizes.cams]
        moved = swap_partial(rows, sizes)
        for c in range(sizes.cams):
            value = moved[c]
            if g == groups - 1 and scalar is not None:
                value = jnp.where(which == sizes.cams - 1, scalar, value)
            out_ref[pl.ds(c * message + g, sizes.pts, stride=sizes.cams * message), :] = value
    for g in range(groups, message):
        for c in range(sizes.cams):
            value = jnp.where(column == c, extra, 0.0)
            out_ref[pl.ds(c * message + g, sizes.pts, stride=sizes.cams * message), :] = value


def swap_partial(rows, sizes):
    return swap_blocks(rows, sizes.block, sizes.cams)


def read_row(in_ref, c, g, message, sizes):
    return in_ref[pl.ds(c * message + g, sizes.pts, stride=sizes.cams * message), :]


def read_messages(in_ref, count, message, sizes):
    fields = []
    group = 0
    while len(fields) < count:
        rows = [read_row(in_ref, c, group, message, sizes) for c in range(sizes.cams)]
        fields += swap_blocks(rows, sizes.block, min(sizes.cams, count - len(fields)))
        group += 1
    return fields


def read_scalar(in_ref, groups, message, sizes):
    total = read_row(in_ref, 0, groups - 1, message, sizes)
    for c in range(1, sizes.cams):
        total = total + read_row(in_ref, c, groups - 1, message, sizes)
    chosen = jnp.where(lane_iota(sizes.pts) == LANES - 1, total, 0.0)
    return jnp.sum(chosen, keepdims=True)


def setup_kernel(sizes, column_ref, *refs):
    sources, refs = refs[:6], refs[6:]
    out_ref, a_ref, b_ref, inv_ref, grad_ref, place_point_ref, new_slot_ref, new_point_ref = refs[:8]
    refs = refs[8:]
    r_ref, parts_ref, spread_ref, table_ref, place_slot_ref, place_list_ref = refs[:6]
    jac_ref, pjac_ref, res_ref, slot_ref, point_ref, list_ref = refs[6:12]
    semaphores = refs[12]
    rows = sizes.rows
    copies = [
        pltpu.make_async_copy(source, target, semaphores.at[k])
        for k, (source, target) in enumerate(zip(sources, refs[6:12]))
    ]
    for copy in copies:
        copy.start()
    for k in (1, 2, 4):
        copies[k].wait()
    new_point_ref[...] = point_ref[...]
    for j in range(rows):
        columns = slice(j * LANES, (j + 1) * LANES)
        b_ref[pl.ds(j, 6, stride=rows), :] = pjac_ref[:, columns]
        r_ref[pl.ds(j, 2, stride=rows), :] = res_ref[:, columns]

    def at(ref, comp, group):
        return ref[comp * rows + group * SUB : comp * rows + (group + 1) * SUB, :]

    normal_pieces = [FINE] * 9

    for group in range(rows // SUB):
        b = [at(b_ref, k, group) for k in range(6)]
        r = [at(r_ref, k, group) for k in range(2)]
        values = [b[i] * b[j] + b[3 + i] * b[3 + j] for i, j in ((0, 0), (0, 1), (0, 2), (1, 1), (1, 2), (2, 2))]
        values += [b[i] * r[0] + b[3 + i] * r[1] for i in range(3)]
        parts = [part for value, pieces in zip(values, normal_pieces) for part in cut(value, pieces)]
        keep_parts(parts, group, parts_ref)
        for s in range(SUB):
            row = group * SUB + s
            point = point_ref[row : row + 1, :]
            spread_row(row, part_rows(len(parts), group, s, parts_ref), point >> 8, PT_HI, spread_ref)
            place_row(row, point & (PT_LO - 1), PT_LO, place_point_ref)
    result = scatter(sum(normal_pieces), sizes.obs, PT_HI, PT_LO, spread_ref, place_point_ref)
    normal = joined(result, 9, PT_HI, normal_pieces)
    top_left = normal[0] + damping_point
    top_mid = normal[1]
    top_right = normal[2]
    mid_mid = normal[3] + damping_point
    mid_right = normal[4]
    low_right = normal[5] + damping_point
    adjugate = [
        mid_mid * low_right - mid_right * mid_right,
        top_right * mid_right - top_mid * low_right,
        top_mid * mid_right - top_right * mid_mid,
        top_left * low_right - top_right * top_right,
        top_mid * top_right - top_left * mid_right,
        top_left * mid_mid - top_mid * top_mid,
    ]
    determinant = top_left * adjugate[0] + top_mid * adjugate[1] + top_right * adjugate[2]
    inverse = [value / determinant for value in adjugate]
    for k in range(6):
        inv_ref[k] = inverse[k]
    for k in range(3):
        grad_ref[k] = normal[6 + k]
    eliminated = solve(inverse, normal[6:])
    for k in range(3):
        table_ref[k] = eliminated[k]
    for k in (0, 3, 5):
        copies[k].wait()
    new_slot_ref[...] = slot_ref[...]
    for j in range(rows):
        for start in range(0, 2 * CP, SUB):
            size = min(SUB, 2 * CP - start)
            a_ref[pl.ds(start * rows + j, size, stride=rows), :] = jac_ref[
                start : start + size, j * LANES : (j + 1) * LANES
            ]

    for group in range(rows // SUB):
        at_point = point_gather(table_ref, point_ref[group * SUB : (group + 1) * SUB, :])
        b = [at(b_ref, k, group) for k in range(6)]
        errors = [at(r_ref, i, group) - sum(b[3 * i + k] * at_point[k] for k in range(3)) for i in range(2)]
        a = [at(a_ref, k, group) for k in range(2 * CP)]
        values = [a[k] * errors[0] + a[CP + k] * errors[1] for k in range(CP)]
        values += [a[k] * a[k] + a[CP + k] * a[CP + k] for k in range(CP)]
        parts = [part for value in values for part in cut(value)]
        keep_parts(parts, group, parts_ref)
        for s in range(SUB):
            row = group * SUB + s
            high, low = slot_place(slot_ref[row : row + 1, :], sizes)
            spread_row(row, part_rows(len(parts), group, s, parts_ref), high, sizes.pts, spread_ref)
            place_row(row, low, LANES, place_slot_ref)
    result = scatter(2 * CP * PIECES, sizes.obs, sizes.pts, LANES, spread_ref, place_slot_ref)
    fields = joined(result, 2 * CP, sizes.pts)

    pieces = sizes.slot // LANES
    lane = lane_iota(1)
    for c in range(sizes.cams):
        for half in range(pieces):
            value = list_ref[c : c + 1, half * LANES : (half + 1) * LANES]
            low = c * sizes.block + half * (LANES // sizes.pts) + lane // sizes.pts
            parts = [(value >> 8).astype(f32), (value & 255).astype(f32)]
            spread_row(c * pieces + half, parts, lane % sizes.pts, sizes.pts, spread_ref)
            place_row(c * pieces + half, low, LANES, place_list_ref)
    result = scatter(2, sizes.cams * sizes.slot, sizes.pts, LANES, spread_ref, place_list_ref)
    listed = result[: sizes.pts] * 256.0 + result[sizes.pts : 2 * sizes.pts]
    write_messages(fields, None, sizes.first_groups, sizes.first_message, out_ref, sizes, extra=listed, column=column_ref[0])


def entries_scatter(fields, entry, sizes, spread_ref, place_ref):
    high, low = entry // LANES, entry % LANES
    parts = [part for value in fields for part in cut(value)]
    for p in range(sizes.pts):
        spread_row(p, [part[p : p + 1] for part in parts], high[p : p + 1], sizes.own_rows, spread_ref)
        place_row(p, low[p : p + 1], LANES, place_ref)
    result = scatter(len(parts), sizes.pts * LANES, sizes.own_rows, LANES, spread_ref, place_ref)
    return joined(result, len(fields), sizes.own_rows)


def send_owned(scaled, partial, entry, out_ref, table_ref, sizes):
    for k in range(CP):
        table_ref[k] = scaled[k]
    fields = gather_rows(lambda c, k: table_ref[c, k : k + 1, :], sizes.run_rows, entry // LANES, entry % LANES, CP)
    write_messages(fields, partial, sizes.groups, sizes.message, out_ref, sizes)


def dot_fields(left, right):
    return jnp.sum(sum(a * b for a, b in zip(left, right)), keepdims=True)


def first_owner_kernel(sizes, in_ref, out_ref, entry_ref, pre_ref, rem_ref,
                       table_ref, spread_ref, place_ref):
    listed = jnp.zeros((sizes.pts, LANES), f32)
    for c in range(sizes.cams):
        listed = listed + read_row(in_ref, c, sizes.first_groups, sizes.first_message, sizes)
    entry = listed.astype(jnp.int32) % sizes.run
    entry_ref[...] = entry
    fields = read_messages(in_ref, 2 * CP, sizes.first_message, sizes)
    sums = entries_scatter(fields, entry, sizes, spread_ref, place_ref)
    remainder = [-value for value in sums[:CP]]
    precondition = [1.0 / (value + damping_camera) for value in sums[CP:]]
    scaled = [p * r for p, r in zip(precondition, remainder)]
    for k in range(CP):
        pre_ref[k] = precondition[k]
        rem_ref[k] = remainder[k]
    send_owned(scaled, dot_fields(remainder, scaled), entry, out_ref, table_ref, sizes)


def owner_kernel(sizes, start, final, in_ref, entry_ref, pre_ref, rem_ref, dir_ref, product_ref, *refs):
    refs = list(refs)
    sol_ref = None if start else refs.pop(0)
    out_ref, new_rem_ref, new_sol_ref, step_ref = refs[:4]
    fields_ref = refs[4] if final else None
    table_ref, spread_ref, place_ref = refs[-3:]
    entry = entry_ref[...]
    fields = read_messages(in_ref, CP, sizes.message, sizes)
    curvature = read_scalar(in_ref, sizes.groups, sizes.message, sizes)
    step = product_ref[...] / jnp.broadcast_to(curvature, (SUB, LANES))
    step_ref[...] = step
    sums = entries_scatter(fields, entry, sizes, spread_ref, place_ref)
    remainder, scaled = [], []
    for k in range(CP):
        direction = dir_ref[k]
        moved = step[:1] * direction
        moved = moved if start else sol_ref[k] + moved
        new_sol_ref[k] = moved
        value = rem_ref[k] - step[:1] * (sums[k] + damping_camera * direction)
        new_rem_ref[k] = value
        remainder.append(value)
        scaled.append(pre_ref[k] * value)
        if final:
            for j, field in enumerate((moved, direction, scaled[k])):
                first = (j * CP + k) * sizes.own_rows
                fields_ref[first : first + sizes.own_rows, :] = field
    send_owned(scaled, dot_fields(remainder, scaled), entry, out_ref, table_ref, sizes)


def schur_kernel(sizes, start, last, in_ref, a_ref, b_ref, inv_ref, slot_ref, point_ref,
                 place_point_ref, pre_ref, rem_ref, grad_ref, *refs):
    refs = list(refs)
    if not start:
        product_ref, at_slot_ref, dir_ref, step_ref, sum_ref = refs[:5]
        refs = refs[5:]
    out_ref, new_product_ref, new_sum_ref = refs[:3]
    refs = refs[3:]
    new_grad_ref = None if start else refs.pop(0)
    q_ref, parts_ref, spread_ref, table_ref, place_slot_ref = refs[-5:]
    new_at_slot_ref, new_dir_ref = (refs[0], None) if last else refs[:2]
    rows = sizes.rows

    def at(ref, comp, group):
        return ref[comp * rows + group * SUB : comp * rows + (group + 1) * SUB, :]

    renewed = jnp.broadcast_to(read_scalar(in_ref, sizes.groups, sizes.message, sizes), (SUB, LANES))
    new_product_ref[...] = renewed
    fields = read_messages(in_ref, CP, sizes.message, sizes)
    beta = None if start else (renewed / product_ref[...])[:1]
    squares = None
    for k in range(CP):
        direction = pre_ref[k] * rem_ref[k]
        if start:
            new_at_slot_ref[k] = fields[k]
        else:
            new_at_slot_ref[k] = fields[k] + beta * at_slot_ref[k]
            direction = direction + beta * dir_ref[k]
        if not last:
            new_dir_ref[k] = direction
        squares = direction * direction if squares is None else squares + direction * direction

    for group in range(rows // SUB):
        high, low = slot_place(slot_ref[group * SUB : (group + 1) * SUB, :], sizes)
        gathered = gather_rows(lambda c, k: new_at_slot_ref[c, k : k + 1, :], sizes.pts, high, low, CP)
        q = [sum(at(a_ref, i * CP + k, group) * gathered[k] for k in range(CP)) for i in range(2)]
        for i in range(2):
            q_ref[i * rows + group * SUB : i * rows + (group + 1) * SUB, :] = q[i]
        values = [at(b_ref, k, group) * q[0] + at(b_ref, 3 + k, group) * q[1] for k in range(3)]
        parts = [part for value in values for part in cut(value, FINE)]
        keep_parts(parts, group, parts_ref)
        for s in range(SUB):
            row = group * SUB + s
            spread_row(row, part_rows(len(parts), group, s, parts_ref), point_ref[row : row + 1, :] >> 8, PT_HI, spread_ref)
    result = scatter(3 * FINE, sizes.obs, PT_HI, PT_LO, spread_ref, place_point_ref)
    sums = joined(result, 3, PT_HI, [FINE] * 3)
    folded = solve([inv_ref[k] for k in range(6)], sums)
    for k in range(3):
        new_sum_ref[k] = sums[k]
        if not start:
            new_grad_ref[k] = grad_ref[k] + step_ref[:1, :1] * sum_ref[k]

    inner = None
    for k in range(3):
        table_ref[k] = folded[k]
    for group in range(rows // SUB):
        at_point = point_gather(table_ref, point_ref[group * SUB : (group + 1) * SUB, :])
        q = [at(q_ref, i, group) for i in range(2)]
        errors = [q[i] - sum(at(b_ref, 3 * i + k, group) * at_point[k] for k in range(3)) for i in range(2)]
        here = q[0] * errors[0] + q[1] * errors[1]
        inner = here if inner is None else inner + here
        if not last:
            values = [at(a_ref, k, group) * errors[0] + at(a_ref, CP + k, group) * errors[1] for k in range(CP)]
            parts = [part for value in values for part in cut(value)]
            keep_parts(parts, group, parts_ref)
            for s in range(SUB):
                row = group * SUB + s
                high, low = slot_place(slot_ref[row : row + 1, :], sizes)
                spread_row(row, part_rows(len(parts), group, s, parts_ref), high, sizes.pts, spread_ref)
                place_row(row, low, LANES, place_slot_ref)
    partial = jnp.sum(inner, keepdims=True) + damping_camera * jnp.sum(squares, keepdims=True)
    if last:
        out_ref[...] = jnp.broadcast_to(partial, (SUB, LANES))
        return
    result = scatter(CP * PIECES, sizes.obs, sizes.pts, LANES, spread_ref, place_slot_ref)
    fields = joined(result, CP, sizes.pts)
    write_messages(fields, partial, sizes.groups, sizes.message, out_ref, sizes)


def tail_kernel(sizes, in_ref, product_ref, own_ref, other_ref, out_ref):
    renewed = jnp.broadcast_to(read_scalar(in_ref, sizes.groups, sizes.message, sizes), (SUB, LANES))
    beta = (renewed / product_ref[...])[:1]
    field = CP * sizes.own_rows
    for j, ref in enumerate((own_ref, other_ref)):
        first = j * 2 * field
        out_ref[first : first + field, :] = ref[:field, :]
        out_ref[first + field : first + 2 * field, :] = ref[2 * field :, :] + beta * ref[field : 2 * field, :]


def final_kernel(sizes, masks, run_ref, in_ref, product_ref, inv_ref, grad_ref, sum_ref, *refs):
    all_refs = refs[: len(masks)]
    cam_ref, pt_ref, table_ref = refs[len(masks) :]
    step = (product_ref[...] / in_ref[...])[:1]
    for all_ref, pair in zip(all_refs, masks):
        for j, mask in enumerate(pair):
            base_column = (run_ref[0] ^ mask) * sizes.run
            for h in range(sizes.run_rows):
                columns = pl.ds(pl.multiple_of(base_column + h * LANES, LANES), LANES)
                for start in range(0, CP, SUB):
                    size = min(SUB, CP - start)
                    first = (j * 2 * CP + start) * sizes.own_rows + h
                    base = all_ref[pl.ds(first, size, stride=sizes.own_rows), :]
                    direction = all_ref[pl.ds(first + CP * sizes.own_rows, size, stride=sizes.own_rows), :]
                    cam_ref[start : start + size, columns] = base + step * direction
    total = [grad_ref[k] + step[:, :1] * sum_ref[k] for k in range(3)]
    solved = solve([inv_ref[k] for k in range(6)], total)
    for k in range(3):
        table_ref[k * PT_HI : (k + 1) * PT_HI, :] = -solved[k]
    for row in range(PT_HI):
        for k in range(3):
            pt_ref[k : k + 1, row * PT_LO : (row + 1) * PT_LO] = table_ref[k * PT_HI + row : k * PT_HI + row + 1, :]


def shape(*dims, dtype=f32):
    return jax.ShapeDtypeStruct(dims, dtype)


def kept(*dims, dtype=f32):
    return pltpu.VMEM(dims, dtype)


def call(kernel, name, inputs, outputs, scratch, scalars=(), inputs_at=pltpu.VMEM, cost=None):
    vmem = pl.BlockSpec(memory_space=pltpu.VMEM)
    given = pl.BlockSpec(memory_space=inputs_at)
    smem = pl.BlockSpec(memory_space=pltpu.SMEM)
    return pl.pallas_call(
        kernel,
        name=name,
        out_shape=outputs,
        in_specs=[smem] * len(scalars) + [given] * len(inputs),
        out_specs=[vmem] * len(outputs),
        scratch_shapes=scratch,
        cost_estimate=cost,
        compiler_params=pltpu.CompilerParams(vmem_limit_bytes=VMEM_LIMIT),
    )(*scalars, *inputs)


def body(camera_jacobian, point_jacobian, residual, observed_slot, observed_point, send_list):
    sizes = Sizes(lax.axis_size("pts"), lax.axis_size("cams"), send_list.shape[2], camera_jacobian.shape[1])
    axes = ("pts", "cams")
    rows = sizes.rows
    slot = observed_slot.reshape(rows, LANES)
    point = observed_point.reshape(rows, LANES)
    column = lax.axis_index("cams").astype(jnp.int32).reshape(1)

    def exchange(messages):
        width = messages.size // sizes.devices
        flat = messages.reshape(sizes.devices, 1, width)
        return lax.all_to_all(flat, axes, split_axis=0, concat_axis=0, tiled=True).reshape(messages.shape)

    def flipped(value, flip):
        return lax.ppermute(value, "pts", [(p, p ^ flip) for p in range(sizes.pts)])

    def factors(high_rows, low_rows, entries):
        return [pltpu.VMEM((high_rows, entries), bf16), pltpu.VMEM((low_rows, entries), bf16)]

    point_table = kept(3, PT_HI, PT_LO)
    owned = kept(CP, sizes.own_rows, LANES)
    messages = kept(sizes.devices * sizes.message, LANES)
    scalar = kept(SUB, LANES)
    owned_scratch = pltpu.VMEM((CP, sizes.own_rows, LANES), f32)
    entries = sizes.pts * LANES

    gather_scratch = [pltpu.VMEM((3, PT_HI, PT_LO), f32), pltpu.VMEM((LANES, sizes.obs), bf16)]

    def parts_scratch(count):
        return pltpu.VMEM((rows // SUB, count * SUB, LANES), f32)


    given = [
        pltpu.with_memory_space_constraint(value, pltpu.HBM)
        for value in (camera_jacobian, point_jacobian, residual, slot, point, send_list[0])
    ]
    first, a, b, inverse, gradient, place_point, slot, point = call(
        functools.partial(setup_kernel, sizes),
        "setup",
        given,
        [
            kept(sizes.devices * sizes.first_message, LANES),
            kept(2 * CP * rows, LANES),
            kept(6 * rows, LANES),
            kept(6, PT_HI, PT_LO),
            point_table,
            kept(PT_LO, sizes.obs, dtype=bf16),
            kept(rows, LANES, dtype=jnp.int32),
            kept(rows, LANES, dtype=jnp.int32),
        ],
        [pltpu.VMEM((2 * rows, LANES), f32), parts_scratch(2 * CP * PIECES)]
        + [pltpu.VMEM((max(spread_rows(9 * FINE, PT_HI), spread_rows(2 * CP * PIECES, sizes.pts)), sizes.obs), bf16)]
        + gather_scratch
        + [pltpu.VMEM((LANES, sizes.cams * sizes.slot), bf16)]
        + [pltpu.VMEM(value.shape, value.dtype) for value in given]
        + [pltpu.SemaphoreType.DMA((len(given),))],
        scalars=[column],
        inputs_at=pl.ANY,
    )
    out, entry, precondition, remainder = call(
        functools.partial(first_owner_kernel, sizes),
        "first_owner",
        [exchange(first)],
        [messages, kept(sizes.pts, LANES, dtype=jnp.int32), owned, owned],
        [owned_scratch] + factors(spread_rows(2 * CP * PIECES, sizes.own_rows), LANES, entries),
    )
    schur_scratch = [pltpu.VMEM((2 * rows, LANES), f32), parts_scratch(CP * PIECES)]
    schur_scratch += [pltpu.VMEM((max(spread_rows(3 * FINE, PT_HI), spread_rows(CP * PIECES, sizes.pts)), sizes.obs), bf16)]
    schur_scratch += gather_scratch
    at_slot = kept(CP, sizes.pts, LANES)
    product = slots = direction = step = sums = solution_ = None
    for iteration in range(ITERS):
        start, last = iteration == 0, iteration == ITERS - 1
        earlier = [] if start else [product, slots, direction, step, sums]
        if last:
            neighbour = flipped(fields, FIRST)
        arrived = exchange(out)
        if last:
            (both,) = call(
                functools.partial(tail_kernel, sizes),
                "tail",
                [arrived, product, fields, neighbour],
                [kept(4 * CP * sizes.own_rows, LANES)],
                [],
            )
            flips = [1 << bit for bit in range(sizes.pts.bit_length() - 1) if 1 << bit != FIRST]
            flips = flips[1:] + flips[:1]
            early = {flip: flipped(both, flip) for flip in (flips[0], flips[-1])}
        results = call(
            functools.partial(schur_kernel, sizes, start, last),
            "schur_last" if last else "schur",
            [arrived, a, b, inverse, slot, point, place_point, precondition, remainder, gradient]
            + earlier,
            [scalar if last else messages, scalar, point_table]
            + ([] if start else [point_table])
            + ([] if last else [at_slot, owned]),
            ([pltpu.VMEM((CP, sizes.pts, LANES), f32)] if last else []) + schur_scratch,
            cost=pl.CostEstimate(flops=2_000_000_000, bytes_accessed=10_000_000, transcendentals=0),
        )
        out, product, sums, *results = results
        if not start:
            gradient, *results = results
        if not last:
            slots, direction = results
        if last:
            early[flips[0]], out = lax.optimization_barrier((early[flips[0]], out))
            gathered, masks = [both], [(0, FIRST)]
            for flip in flips:
                gathered += [early[flip] if value is both and flip in early else flipped(value, flip) for value in gathered]
                masks += [tuple(mask ^ flip for mask in pair) for pair in masks]
            break
        final = iteration == ITERS - 2
        out, remainder, solution_, step, *rest = call(
            functools.partial(owner_kernel, sizes, start, final),
            "owner_final" if final else "owner",
            [exchange(out), entry, precondition, remainder, direction, product] + ([] if start else [solution_]),
            [messages, owned, owned, scalar] + ([kept(3 * CP * sizes.own_rows, LANES)] if final else []),
            [owned_scratch] + factors(spread_rows(CP * PIECES, sizes.own_rows), LANES, entries),
        )
        fields = rest[0] if final else None
    return call(
        functools.partial(final_kernel, sizes, masks),
        "final",
        [lax.psum(out, ("pts", "cams")), product, inverse, gradient, sums] + gathered,
        [shape(CP, CAM_OWN), shape(3, PT_DEV)],
        [pltpu.VMEM((3 * PT_HI, PT_LO), f32)],
        scalars=[lax.axis_index("pts").astype(jnp.int32).reshape(1)],
    )


def solution(mesh):
    return jax.shard_map(
        lambda *arguments: tuple(body(*arguments)),
        mesh=mesh,
        in_specs=(
            P(None, ("pts", "cams")),
            P(None, ("pts", "cams")),
            P(None, ("pts", "cams")),
            P(("pts", "cams")),
            P(("pts", "cams")),
            P(("pts", "cams"), None, None),
        ),
        out_specs=(P(None, "cams"), P(None, ("pts", "cams"))),
        check_vma=False,
    )
```

```python
import functools

import jax
import jax.numpy as jnp
from jax import lax
from jax.experimental import pallas as pl
from jax.experimental.pallas import tpu as pltpu
from jax.sharding import PartitionSpec as P

CP = 9
CAM_OWN = 8192
PT_DEV = 4096
ITERS = 3
LANES = 128
SUB = 8
PT_LO = 256
PT_HI = PT_DEV // PT_LO
PIECES = 2
FINE = 3
FIRST = 4
VMEM_LIMIT = 24 * 1024 * 1024

damping_camera = 1.0
damping_point = 1.0

f32 = jnp.float32
bf16 = jnp.bfloat16


class Sizes:
    def __init__(self, pts, cams, slot, obs):
        self.pts, self.cams, self.slot, self.obs = pts, cams, slot, obs
        self.devices = pts * cams
        self.block = slot // pts
        assert cams * self.block == LANES and LANES % pts == 0
        self.rows = obs // LANES
        self.run = CAM_OWN // pts
        self.run_rows = self.run // LANES
        self.own_rows = max(SUB, self.run_rows)
        self.groups = -(-CP // cams)
        self.first_groups = -(-2 * CP // cams)
        self.message = self.groups
        self.first_message = self.first_groups + 1
        assert self.groups * cams > CP


def sub_iota(rows):
    return lax.broadcasted_iota(jnp.int32, (rows, LANES), 0)


def lane_iota(rows):
    return lax.broadcasted_iota(jnp.int32, (rows, LANES), 1)


def cut(value, pieces=PIECES):
    parts = []
    for _ in range(pieces - 1):
        part = value.astype(bf16).astype(f32)
        parts.append(part)
        value = value - part
    parts.append(value)
    return parts


def swap_blocks(rows, block, wanted):
    which = lane_iota(rows[0].shape[0]) // block
    result = []
    for q in range(wanted):
        total = None
        for c, value in enumerate(rows):
            shift = ((c - q) * block) % LANES
            moved = pltpu.roll(value, shift, axis=1) if shift else value
            total = jnp.where(which == c, moved, 0.0 if total is None else total)
        result.append(total)
    return result


def gather_rows(row, count, high, low, comps):
    result = [None] * comps
    for k in range(count):
        here = high == k
        for c in range(comps):
            source = jnp.broadcast_to(row(c, k), high.shape)
            found = jnp.take_along_axis(source, low, axis=1, mode="promise_in_bounds")
            result[c] = found if k == 0 else jnp.where(here, found, result[c])
    return result


def spread_row(index, parts, high, high_count, spread_ref):
    columns = slice(index * LANES, (index + 1) * LANES)
    mask = jnp.broadcast_to(high, (high_count, LANES)) == sub_iota(high_count)
    together = max(1, 16 // high_count)
    for start in range(0, len(parts), together):
        pieces = [
            jnp.where(mask, jnp.broadcast_to(part, (high_count, LANES)), 0.0)
            for part in parts[start : start + together]
        ]
        while len(pieces) < together:
            pieces.append(jnp.zeros((high_count, LANES), f32))
        tile = pieces[0] if together == 1 else jnp.concatenate(pieces, axis=0)
        spread_ref[start * high_count : start * high_count + tile.shape[0], columns] = tile.astype(bf16)


def place_row(index, low, low_count, place_ref):
    columns = slice(index * LANES, (index + 1) * LANES)
    place = jnp.broadcast_to(low, (low_count, LANES)) == sub_iota(low_count)
    place_ref[:low_count, columns] = jnp.where(place, 1.0, 0.0).astype(bf16)


def keep_parts(parts, group, parts_ref):
    for k, part in enumerate(parts):
        parts_ref[group, k * SUB : (k + 1) * SUB, :] = part


def part_rows(count, group, s, parts_ref):
    return [parts_ref[group, k * SUB + s : k * SUB + s + 1, :] for k in range(count)]


def spread_rows(parts, high_count):
    return -(-parts * high_count // 16) * 16


def scatter(parts, entries, high_count, low_count, spread_ref, place_ref):
    rows = spread_rows(parts, high_count)
    return lax.dot_general(
        spread_ref[:rows, :entries],
        place_ref[:low_count, :entries],
        (((1,), (1,)), ((), ())),
        preferred_element_type=f32,
    )


def joined(result, count, high_count, pieces=None):
    pieces = pieces or [PIECES] * count
    values, first = [], 0
    for number in pieces:
        rows = [result[first + k * high_count : first + (k + 1) * high_count] for k in range(number)]
        first += number * high_count
        total = rows[-1]
        for row in reversed(rows[:-1]):
            total = total + row
        values.append(total)
    return values


def point_gather(ref, point):
    wide = PT_LO // LANES
    row = lambda c, k: ref[c, k // wide : k // wide + 1, (k % wide) * LANES : (k % wide + 1) * LANES]
    return gather_rows(row, PT_HI * wide, point // LANES, point % LANES, 3)


def slot_place(slot, sizes):
    within = slot % sizes.slot
    return within % sizes.pts, (slot // sizes.slot) * sizes.block + within // sizes.pts


def solve(inverse, values):
    first = inverse[0] * values[0] + inverse[1] * values[1] + inverse[2] * values[2]
    second = inverse[1] * values[0] + inverse[3] * values[1] + inverse[4] * values[2]
    third = inverse[2] * values[0] + inverse[4] * values[1] + inverse[5] * values[2]
    return first, second, third


def write_messages(fields, scalar, groups, message, out_ref, sizes, extra=None, column=None):
    which = lane_iota(sizes.pts) // sizes.block
    for g in range(groups):
        rows = fields[g * sizes.cams : (g + 1) * sizes.cams]
        moved = swap_partial(rows, sizes)
        for c in range(sizes.cams):
            value = moved[c]
            if g == groups - 1 and scalar is not None:
                value = jnp.where(which == sizes.cams - 1, scalar, value)
            out_ref[pl.ds(c * message + g, sizes.pts, stride=sizes.cams * message), :] = value
    for g in range(groups, message):
        for c in range(sizes.cams):
            value = jnp.where(column == c, extra, 0.0)
            out_ref[pl.ds(c * message + g, sizes.pts, stride=sizes.cams * message), :] = value


def swap_partial(rows, sizes):
    return swap_blocks(rows, sizes.block, sizes.cams)


def read_row(in_ref, c, g, message, sizes):
    return in_ref[pl.ds(c * message + g, sizes.pts, stride=sizes.cams * message), :]


def read_messages(in_ref, count, message, sizes):
    fields = []
    group = 0
    while len(fields) < count:
        rows = [read_row(in_ref, c, group, message, sizes) for c in range(sizes.cams)]
        fields += swap_blocks(rows, sizes.block, min(sizes.cams, count - len(fields)))
        group += 1
    return fields


def read_scalar(in_ref, groups, message, sizes):
    total = read_row(in_ref, 0, groups - 1, message, sizes)
    for c in range(1, sizes.cams):
        total = total + read_row(in_ref, c, groups - 1, message, sizes)
    chosen = jnp.where(lane_iota(sizes.pts) == LANES - 1, total, 0.0)
    return jnp.sum(chosen, keepdims=True)


def setup_kernel(sizes, column_ref, *refs):
    sources, refs = refs[:6], refs[6:]
    out_ref, a_ref, b_ref, inv_ref, grad_ref, place_point_ref, new_slot_ref, new_point_ref = refs[:8]
    refs = refs[8:]
    r_ref, parts_ref, spread_ref, table_ref, place_slot_ref, place_list_ref = refs[:6]
    jac_ref, pjac_ref, res_ref, slot_ref, point_ref, list_ref = refs[6:12]
    semaphores = refs[12]
    rows = sizes.rows
    copies = [
        pltpu.make_async_copy(source, target, semaphores.at[k])
        for k, (source, target) in enumerate(zip(sources, refs[6:12]))
    ]
    for copy in copies:
        copy.start()
    for k in (1, 2, 4):
        copies[k].wait()
    new_point_ref[...] = point_ref[...]
    for j in range(rows):
        columns = slice(j * LANES, (j + 1) * LANES)
        b_ref[pl.ds(j, 6, stride=rows), :] = pjac_ref[:, columns]
        r_ref[pl.ds(j, 2, stride=rows), :] = res_ref[:, columns]

    def at(ref, comp, group):
        return ref[comp * rows + group * SUB : comp * rows + (group + 1) * SUB, :]

    normal_pieces = [FINE] * 9

    for group in range(rows // SUB):
        b = [at(b_ref, k, group) for k in range(6)]
        r = [at(r_ref, k, group) for k in range(2)]
        values = [b[i] * b[j] + b[3 + i] * b[3 + j] for i, j in ((0, 0), (0, 1), (0, 2), (1, 1), (1, 2), (2, 2))]
        values += [b[i] * r[0] + b[3 + i] * r[1] for i in range(3)]
        parts = [part for value, pieces in zip(values, normal_pieces) for part in cut(value, pieces)]
        keep_parts(parts, group, parts_ref)
        for s in range(SUB):
            row = group * SUB + s
            point = point_ref[row : row + 1, :]
            spread_row(row, part_rows(len(parts), group, s, parts_ref), point >> 8, PT_HI, spread_ref)
            place_row(row, point & (PT_LO - 1), PT_LO, place_point_ref)
    result = scatter(sum(normal_pieces), sizes.obs, PT_HI, PT_LO, spread_ref, place_point_ref)
    normal = joined(result, 9, PT_HI, normal_pieces)
    top_left = normal[0] + damping_point
    top_mid = normal[1]
    top_right = normal[2]
    mid_mid = normal[3] + damping_point
    mid_right = normal[4]
    low_right = normal[5] + damping_point
    adjugate = [
        mid_mid * low_right - mid_right * mid_right,
        top_right * mid_right - top_mid * low_right,
        top_mid * mid_right - top_right * mid_mid,
        top_left * low_right - top_right * top_right,
        top_mid * top_right - top_left * mid_right,
        top_left * mid_mid - top_mid * top_mid,
    ]
    determinant = top_left * adjugate[0] + top_mid * adjugate[1] + top_right * adjugate[2]
    inverse = [value / determinant for value in adjugate]
    for k in range(6):
        inv_ref[k] = inverse[k]
    for k in range(3):
        grad_ref[k] = normal[6 + k]
    eliminated = solve(inverse, normal[6:])
    for k in range(3):
        table_ref[k] = eliminated[k]
    for k in (0, 3, 5):
        copies[k].wait()
    new_slot_ref[...] = slot_ref[...]
    for j in range(rows):
        for start in range(0, 2 * CP, SUB):
            size = min(SUB, 2 * CP - start)
            a_ref[pl.ds(start * rows + j, size, stride=rows), :] = jac_ref[
                start : start + size, j * LANES : (j + 1) * LANES
            ]

    for group in range(rows // SUB):
        at_point = point_gather(table_ref, point_ref[group * SUB : (group + 1) * SUB, :])
        b = [at(b_ref, k, group) for k in range(6)]
        errors = [at(r_ref, i, group) - sum(b[3 * i + k] * at_point[k] for k in range(3)) for i in range(2)]
        a = [at(a_ref, k, group) for k in range(2 * CP)]
        values = [a[k] * errors[0] + a[CP + k] * errors[1] for k in range(CP)]
        values += [a[k] * a[k] + a[CP + k] * a[CP + k] for k in range(CP)]
        parts = [part for value in values for part in cut(value)]
        keep_parts(parts, group, parts_ref)
        for s in range(SUB):
            row = group * SUB + s
            high, low = slot_place(slot_ref[row : row + 1, :], sizes)
            spread_row(row, part_rows(len(parts), group, s, parts_ref), high, sizes.pts, spread_ref)
            place_row(row, low, LANES, place_slot_ref)
    result = scatter(2 * CP * PIECES, sizes.obs, sizes.pts, LANES, spread_ref, place_slot_ref)
    fields = joined(result, 2 * CP, sizes.pts)

    pieces = sizes.slot // LANES
    lane = lane_iota(1)
    for c in range(sizes.cams):
        for half in range(pieces):
            value = list_ref[c : c + 1, half * LANES : (half + 1) * LANES]
            low = c * sizes.block + half * (LANES // sizes.pts) + lane // sizes.pts
            parts = [(value >> 8).astype(f32), (value & 255).astype(f32)]
            spread_row(c * pieces + half, parts, lane % sizes.pts, sizes.pts, spread_ref)
            place_row(c * pieces + half, low, LANES, place_list_ref)
    result = scatter(2, sizes.cams * sizes.slot, sizes.pts, LANES, spread_ref, place_list_ref)
    listed = result[: sizes.pts] * 256.0 + result[sizes.pts : 2 * sizes.pts]
    write_messages(fields, None, sizes.first_groups, sizes.first_message, out_ref, sizes, extra=listed, column=column_ref[0])


def entries_scatter(fields, entry, sizes, spread_ref, place_ref):
    high, low = entry // LANES, entry % LANES
    parts = [part for value in fields for part in cut(value)]
    for p in range(sizes.pts):
        spread_row(p, [part[p : p + 1] for part in parts], high[p : p + 1], sizes.own_rows, spread_ref)
        place_row(p, low[p : p + 1], LANES, place_ref)
    result = scatter(len(parts), sizes.pts * LANES, sizes.own_rows, LANES, spread_ref, place_ref)
    return joined(result, len(fields), sizes.own_rows)


def send_owned(scaled, partial, entry, out_ref, table_ref, sizes):
    for k in range(CP):
        table_ref[k] = scaled[k]
    fields = gather_rows(lambda c, k: table_ref[c, k : k + 1, :], sizes.run_rows, entry // LANES, entry % LANES, CP)
    write_messages(fields, partial, sizes.groups, sizes.message, out_ref, sizes)


def dot_fields(left, right):
    return jnp.sum(sum(a * b for a, b in zip(left, right)), keepdims=True)


def first_owner_kernel(sizes, in_ref, out_ref, entry_ref, pre_ref, rem_ref,
                       table_ref, spread_ref, place_ref):
    listed = jnp.zeros((sizes.pts, LANES), f32)
    for c in range(sizes.cams):
        listed = listed + read_row(in_ref, c, sizes.first_groups, sizes.first_message, sizes)
    entry = listed.astype(jnp.int32) % sizes.run
    entry_ref[...] = entry
    fields = read_messages(in_ref, 2 * CP, sizes.first_message, sizes)
    sums = entries_scatter(fields, entry, sizes, spread_ref, place_ref)
    remainder = [-value for value in sums[:CP]]
    precondition = [1.0 / (value + damping_camera) for value in sums[CP:]]
    scaled = [p * r for p, r in zip(precondition, remainder)]
    for k in range(CP):
        pre_ref[k] = precondition[k]
        rem_ref[k] = remainder[k]
    send_owned(scaled, dot_fields(remainder, scaled), entry, out_ref, table_ref, sizes)


def owner_kernel(sizes, start, final, in_ref, entry_ref, pre_ref, rem_ref, dir_ref, product_ref, *refs):
    refs = list(refs)
    sol_ref = None if start else refs.pop(0)
    out_ref, new_rem_ref, new_sol_ref, step_ref = refs[:4]
    fields_ref = refs[4] if final else None
    table_ref, spread_ref, place_ref = refs[-3:]
    entry = entry_ref[...]
    fields = read_messages(in_ref, CP, sizes.message, sizes)
    curvature = read_scalar(in_ref, sizes.groups, sizes.message, sizes)
    step = product_ref[...] / jnp.broadcast_to(curvature, (SUB, LANES))
    step_ref[...] = step
    sums = entries_scatter(fields, entry, sizes, spread_ref, place_ref)
    remainder, scaled = [], []
    for k in range(CP):
        direction = dir_ref[k]
        moved = step[:1] * direction
        moved = moved if start else sol_ref[k] + moved
        new_sol_ref[k] = moved
        value = rem_ref[k] - step[:1] * (sums[k] + damping_camera * direction)
        new_rem_ref[k] = value
        remainder.append(value)
        scaled.append(pre_ref[k] * value)
        if final:
            for j, field in enumerate((moved, direction, scaled[k])):
                first = (j * CP + k) * sizes.own_rows
                fields_ref[first : first + sizes.own_rows, :] = field
    send_owned(scaled, dot_fields(remainder, scaled), entry, out_ref, table_ref, sizes)


def schur_kernel(sizes, start, last, in_ref, a_ref, b_ref, inv_ref, slot_ref, point_ref,
                 place_point_ref, pre_ref, rem_ref, grad_ref, *refs):
    refs = list(refs)
    if not start:
        product_ref, at_slot_ref, dir_ref, step_ref, sum_ref = refs[:5]
        refs = refs[5:]
    out_ref, new_product_ref, new_sum_ref = refs[:3]
    refs = refs[3:]
    new_grad_ref = None if start else refs.pop(0)
    q_ref, parts_ref, spread_ref, table_ref, place_slot_ref = refs[-5:]
    new_at_slot_ref, new_dir_ref = (refs[0], None) if last else refs[:2]
    rows = sizes.rows

    def at(ref, comp, group):
        return ref[comp * rows + group * SUB : comp * rows + (group + 1) * SUB, :]

    renewed = jnp.broadcast_to(read_scalar(in_ref, sizes.groups, sizes.message, sizes), (SUB, LANES))
    new_product_ref[...] = renewed
    fields = read_messages(in_ref, CP, sizes.message, sizes)
    beta = None if start else (renewed / product_ref[...])[:1]
    squares = None
    for k in range(CP):
        direction = pre_ref[k] * rem_ref[k]
        if start:
            new_at_slot_ref[k] = fields[k]
        else:
            new_at_slot_ref[k] = fields[k] + beta * at_slot_ref[k]
            direction = direction + beta * dir_ref[k]
        if not last:
            new_dir_ref[k] = direction
        squares = direction * direction if squares is None else squares + direction * direction

    for group in range(rows // SUB):
        high, low = slot_place(slot_ref[group * SUB : (group + 1) * SUB, :], sizes)
        gathered = gather_rows(lambda c, k: new_at_slot_ref[c, k : k + 1, :], sizes.pts, high, low, CP)
        q = [sum(at(a_ref, i * CP + k, group) * gathered[k] for k in range(CP)) for i in range(2)]
        for i in range(2):
            q_ref[i * rows + group * SUB : i * rows + (group + 1) * SUB, :] = q[i]
        values = [at(b_ref, k, group) * q[0] + at(b_ref, 3 + k, group) * q[1] for k in range(3)]
        parts = [part for value in values for part in cut(value, FINE)]
        keep_parts(parts, group, parts_ref)
        for s in range(SUB):
            row = group * SUB + s
            spread_row(row, part_rows(len(parts), group, s, parts_ref), point_ref[row : row + 1, :] >> 8, PT_HI, spread_ref)
    result = scatter(3 * FINE, sizes.obs, PT_HI, PT_LO, spread_ref, place_point_ref)
    sums = joined(result, 3, PT_HI, [FINE] * 3)
    folded = solve([inv_ref[k] for k in range(6)], sums)
    for k in range(3):
        new_sum_ref[k] = sums[k]
        if not start:
            new_grad_ref[k] = grad_ref[k] + step_ref[:1, :1] * sum_ref[k]

    inner = None
    for k in range(3):
        table_ref[k] = folded[k]
    for group in range(rows // SUB):
        at_point = point_gather(table_ref, point_ref[group * SUB : (group + 1) * SUB, :])
        q = [at(q_ref, i, group) for i in range(2)]
        errors = [q[i] - sum(at(b_ref, 3 * i + k, group) * at_point[k] for k in range(3)) for i in range(2)]
        here = q[0] * errors[0] + q[1] * errors[1]
        inner = here if inner is None else inner + here
        if not last:
            values = [at(a_ref, k, group) * errors[0] + at(a_ref, CP + k, group) * errors[1] for k in range(CP)]
            parts = [part for value in values for part in cut(value)]
            keep_parts(parts, group, parts_ref)
            for s in range(SUB):
                row = group * SUB + s
                high, low = slot_place(slot_ref[row : row + 1, :], sizes)
                spread_row(row, part_rows(len(parts), group, s, parts_ref), high, sizes.pts, spread_ref)
                place_row(row, low, LANES, place_slot_ref)
    partial = jnp.sum(inner, keepdims=True) + damping_camera * jnp.sum(squares, keepdims=True)
    if last:
        out_ref[...] = jnp.broadcast_to(partial, (sizes.devices, LANES))
        return
    result = scatter(CP * PIECES, sizes.obs, sizes.pts, LANES, spread_ref, place_slot_ref)
    fields = joined(result, CP, sizes.pts)
    write_messages(fields, partial, sizes.groups, sizes.message, out_ref, sizes)


def tail_kernel(sizes, in_ref, product_ref, own_ref, other_ref, out_ref):
    renewed = jnp.broadcast_to(read_scalar(in_ref, sizes.groups, sizes.message, sizes), (SUB, LANES))
    beta = (renewed / product_ref[...])[:1]
    field = CP * sizes.own_rows
    for j, ref in enumerate((own_ref, other_ref)):
        first = j * 2 * field
        out_ref[first : first + field, :] = ref[:field, :]
        out_ref[first + field : first + 2 * field, :] = ref[2 * field :, :] + beta * ref[field : 2 * field, :]


def final_kernel(sizes, masks, run_ref, in_ref, product_ref, inv_ref, grad_ref, sum_ref, *refs):
    all_refs = refs[: len(masks)]
    cam_ref, pt_ref, table_ref = refs[len(masks) :]
    curvature = jnp.sum(jnp.where(lane_iota(sizes.devices) == 0, in_ref[...], 0.0), keepdims=True)
    step = (product_ref[...] / jnp.broadcast_to(curvature, (SUB, LANES)))[:1]
    for all_ref, pair in zip(all_refs, masks):
        for j, mask in enumerate(pair):
            base_column = (run_ref[0] ^ mask) * sizes.run
            for h in range(sizes.run_rows):
                columns = pl.ds(pl.multiple_of(base_column + h * LANES, LANES), LANES)
                for start in range(0, CP, SUB):
                    size = min(SUB, CP - start)
                    first = (j * 2 * CP + start) * sizes.own_rows + h
                    base = all_ref[pl.ds(first, size, stride=sizes.own_rows), :]
                    direction = all_ref[pl.ds(first + CP * sizes.own_rows, size, stride=sizes.own_rows), :]
                    cam_ref[start : start + size, columns] = base + step * direction
    total = [grad_ref[k] + step[:, :1] * sum_ref[k] for k in range(3)]
    solved = solve([inv_ref[k] for k in range(6)], total)
    for k in range(3):
        table_ref[k * PT_HI : (k + 1) * PT_HI, :] = -solved[k]
    for row in range(PT_HI):
        for k in range(3):
            pt_ref[k : k + 1, row * PT_LO : (row + 1) * PT_LO] = table_ref[k * PT_HI + row : k * PT_HI + row + 1, :]


def shape(*dims, dtype=f32):
    return jax.ShapeDtypeStruct(dims, dtype)


def kept(*dims, dtype=f32):
    return pltpu.VMEM(dims, dtype)


def call(kernel, name, inputs, outputs, scratch, scalars=(), inputs_at=pltpu.VMEM, cost=None):
    vmem = pl.BlockSpec(memory_space=pltpu.VMEM)
    given = pl.BlockSpec(memory_space=inputs_at)
    smem = pl.BlockSpec(memory_space=pltpu.SMEM)
    return pl.pallas_call(
        kernel,
        name=name,
        out_shape=outputs,
        in_specs=[smem] * len(scalars) + [given] * len(inputs),
        out_specs=[vmem] * len(outputs),
        scratch_shapes=scratch,
        cost_estimate=cost,
        compiler_params=pltpu.CompilerParams(vmem_limit_bytes=VMEM_LIMIT),
    )(*scalars, *inputs)


def body(camera_jacobian, point_jacobian, residual, observed_slot, observed_point, send_list):
    sizes = Sizes(lax.axis_size("pts"), lax.axis_size("cams"), send_list.shape[2], camera_jacobian.shape[1])
    axes = ("pts", "cams")
    rows = sizes.rows
    slot = observed_slot.reshape(rows, LANES)
    point = observed_point.reshape(rows, LANES)
    column = lax.axis_index("cams").astype(jnp.int32).reshape(1)

    def exchange(messages):
        width = messages.size // sizes.devices
        flat = messages.reshape(sizes.devices, 1, width)
        return lax.all_to_all(flat, axes, split_axis=0, concat_axis=0, tiled=True).reshape(messages.shape)

    def flipped(value, flip):
        return lax.ppermute(value, "pts", [(p, p ^ flip) for p in range(sizes.pts)])

    def factors(high_rows, low_rows, entries):
        return [pltpu.VMEM((high_rows, entries), bf16), pltpu.VMEM((low_rows, entries), bf16)]

    point_table = kept(3, PT_HI, PT_LO)
    owned = kept(CP, sizes.own_rows, LANES)
    messages = kept(sizes.devices * sizes.message, LANES)
    scalar = kept(SUB, LANES)
    owned_scratch = pltpu.VMEM((CP, sizes.own_rows, LANES), f32)
    entries = sizes.pts * LANES

    gather_scratch = [pltpu.VMEM((3, PT_HI, PT_LO), f32), pltpu.VMEM((LANES, sizes.obs), bf16)]

    def parts_scratch(count):
        return pltpu.VMEM((rows // SUB, count * SUB, LANES), f32)


    given = [
        pltpu.with_memory_space_constraint(value, pltpu.HBM)
        for value in (camera_jacobian, point_jacobian, residual, slot, point, send_list[0])
    ]
    first, a, b, inverse, gradient, place_point, slot, point = call(
        functools.partial(setup_kernel, sizes),
        "setup",
        given,
        [
            kept(sizes.devices * sizes.first_message, LANES),
            kept(2 * CP * rows, LANES),
            kept(6 * rows, LANES),
            kept(6, PT_HI, PT_LO),
            point_table,
            kept(PT_LO, sizes.obs, dtype=bf16),
            kept(rows, LANES, dtype=jnp.int32),
            kept(rows, LANES, dtype=jnp.int32),
        ],
        [pltpu.VMEM((2 * rows, LANES), f32), parts_scratch(2 * CP * PIECES)]
        + [pltpu.VMEM((max(spread_rows(9 * FINE, PT_HI), spread_rows(2 * CP * PIECES, sizes.pts)), sizes.obs), bf16)]
        + gather_scratch
        + [pltpu.VMEM((LANES, sizes.cams * sizes.slot), bf16)]
        + [pltpu.VMEM(value.shape, value.dtype) for value in given]
        + [pltpu.SemaphoreType.DMA((len(given),))],
        scalars=[column],
        inputs_at=pl.ANY,
    )
    out, entry, precondition, remainder = call(
        functools.partial(first_owner_kernel, sizes),
        "first_owner",
        [exchange(first)],
        [messages, kept(sizes.pts, LANES, dtype=jnp.int32), owned, owned],
        [owned_scratch] + factors(spread_rows(2 * CP * PIECES, sizes.own_rows), LANES, entries),
    )
    schur_scratch = [pltpu.VMEM((2 * rows, LANES), f32), parts_scratch(CP * PIECES)]
    schur_scratch += [pltpu.VMEM((max(spread_rows(3 * FINE, PT_HI), spread_rows(CP * PIECES, sizes.pts)), sizes.obs), bf16)]
    schur_scratch += gather_scratch
    at_slot = kept(CP, sizes.pts, LANES)
    product = slots = direction = step = sums = solution_ = None
    for iteration in range(ITERS):
        start, last = iteration == 0, iteration == ITERS - 1
        earlier = [] if start else [product, slots, direction, step, sums]
        if last:
            neighbour = flipped(fields, FIRST)
        arrived = exchange(out)
        if last:
            (both,) = call(
                functools.partial(tail_kernel, sizes),
                "tail",
                [arrived, product, fields, neighbour],
                [kept(4 * CP * sizes.own_rows, LANES)],
                [],
            )
            flips = [1 << bit for bit in range(sizes.pts.bit_length() - 1) if 1 << bit != FIRST]
            flips = flips[1:] + flips[:1]
            early = {flip: flipped(both, flip) for flip in (flips[0], flips[-1])}
        results = call(
            functools.partial(schur_kernel, sizes, start, last),
            "schur_last" if last else "schur",
            [arrived, a, b, inverse, slot, point, place_point, precondition, remainder, gradient]
            + earlier,
            [kept(sizes.devices, LANES) if last else messages, scalar, point_table]
            + ([] if start else [point_table])
            + ([] if last else [at_slot, owned]),
            ([pltpu.VMEM((CP, sizes.pts, LANES), f32)] if last else []) + schur_scratch,
            cost=pl.CostEstimate(flops=2_000_000_000, bytes_accessed=10_000_000, transcendentals=0),
        )
        out, product, sums, *results = results
        if not start:
            gradient, *results = results
        if not last:
            slots, direction = results
        if last:
            early[flips[0]], out = lax.optimization_barrier((early[flips[0]], out))
            gathered, masks = [both], [(0, FIRST)]
            for flip in flips:
                gathered += [early[flip] if value is both and flip in early else flipped(value, flip) for value in gathered]
                masks += [tuple(mask ^ flip for mask in pair) for pair in masks]
            break
        final = iteration == ITERS - 2
        out, remainder, solution_, step, *rest = call(
            functools.partial(owner_kernel, sizes, start, final),
            "owner_final" if final else "owner",
            [exchange(out), entry, precondition, remainder, direction, product] + ([] if start else [solution_]),
            [messages, owned, owned, scalar] + ([kept(3 * CP * sizes.own_rows, LANES)] if final else []),
            [owned_scratch] + factors(spread_rows(CP * PIECES, sizes.own_rows), LANES, entries),
        )
        fields = rest[0] if final else None
    return call(
        functools.partial(final_kernel, sizes, masks),
        "final",
        [exchange(out), product, inverse, gradient, sums] + gathered,
        [shape(CP, CAM_OWN), shape(3, PT_DEV)],
        [pltpu.VMEM((3 * PT_HI, PT_LO), f32)],
        scalars=[lax.axis_index("pts").astype(jnp.int32).reshape(1)],
    )


def solution(mesh):
    return jax.shard_map(
        lambda *arguments: tuple(body(*arguments)),
        mesh=mesh,
        in_specs=(
            P(None, ("pts", "cams")),
            P(None, ("pts", "cams")),
            P(None, ("pts", "cams")),
            P(("pts", "cams")),
            P(("pts", "cams")),
            P(("pts", "cams"), None, None),
        ),
        out_specs=(P(None, "cams"), P(None, ("pts", "cams"))),
        check_vma=False,
    )
```

```python
import functools

import jax
import jax.numpy as jnp
from jax import lax
from jax.experimental import pallas as pl
from jax.experimental.pallas import tpu as pltpu
from jax.sharding import PartitionSpec as P

CP = 9
CAM_OWN = 8192
PT_DEV = 4096
ITERS = 3
LANES = 128
SUB = 8
PT_ROWS = PT_DEV // LANES
PT_LO = 256
PT_HI = PT_DEV // PT_LO
PIECES = 2
FINE = 3
FIRST = 4
VMEM_LIMIT = 24 * 1024 * 1024

damping_camera = 1.0
damping_point = 1.0

f32 = jnp.float32
bf16 = jnp.bfloat16


class Sizes:
    def __init__(self, pts, cams, slot, obs):
        self.pts, self.cams, self.slot, self.obs = pts, cams, slot, obs
        self.devices = pts * cams
        self.block = slot // pts
        assert cams * self.block == LANES and LANES % pts == 0
        self.rows = obs // LANES
        self.run = CAM_OWN // pts
        self.run_rows = self.run // LANES
        self.own_rows = max(SUB, self.run_rows)
        self.groups = -(-CP // cams)
        self.first_groups = -(-2 * CP // cams)
        self.message = self.groups
        self.first_message = self.first_groups + 1
        assert self.groups * cams > CP


def sub_iota(rows):
    return lax.broadcasted_iota(jnp.int32, (rows, LANES), 0)


def lane_iota(rows):
    return lax.broadcasted_iota(jnp.int32, (rows, LANES), 1)


def cut(value, pieces=PIECES):
    parts = []
    for _ in range(pieces - 1):
        part = value.astype(bf16).astype(f32)
        parts.append(part)
        value = value - part
    parts.append(value)
    return parts


def swap_blocks(rows, block, wanted):
    which = lane_iota(rows[0].shape[0]) // block
    result = []
    for q in range(wanted):
        total = None
        for c, value in enumerate(rows):
            shift = ((c - q) * block) % LANES
            moved = pltpu.roll(value, shift, axis=1) if shift else value
            total = jnp.where(which == c, moved, 0.0 if total is None else total)
        result.append(total)
    return result


def gather_rows(row, count, high, low, comps):
    result = [None] * comps
    for k in range(count):
        here = high == k
        for c in range(comps):
            source = jnp.broadcast_to(row(c, k), high.shape)
            found = jnp.take_along_axis(source, low, axis=1, mode="promise_in_bounds")
            result[c] = found if k == 0 else jnp.where(here, found, result[c])
    return result


def spread_row(index, parts, high, high_count, spread_ref):
    columns = slice(index * LANES, (index + 1) * LANES)
    mask = jnp.broadcast_to(high, (high_count, LANES)) == sub_iota(high_count)
    together = max(1, 16 // high_count)
    for start in range(0, len(parts), together):
        pieces = [
            jnp.where(mask, jnp.broadcast_to(part, (high_count, LANES)), 0.0)
            for part in parts[start : start + together]
        ]
        while len(pieces) < together:
            pieces.append(jnp.zeros((high_count, LANES), f32))
        tile = pieces[0] if together == 1 else jnp.concatenate(pieces, axis=0)
        spread_ref[start * high_count : start * high_count + tile.shape[0], columns] = tile.astype(bf16)


def place_row(index, low, low_count, place_ref):
    columns = slice(index * LANES, (index + 1) * LANES)
    place = jnp.broadcast_to(low, (low_count, LANES)) == sub_iota(low_count)
    place_ref[:low_count, columns] = jnp.where(place, 1.0, 0.0).astype(bf16)


def keep_parts(parts, group, parts_ref):
    for k, part in enumerate(parts):
        parts_ref[group, k * SUB : (k + 1) * SUB, :] = part


def part_rows(count, group, s, parts_ref):
    return [parts_ref[group, k * SUB + s : k * SUB + s + 1, :] for k in range(count)]


def spread_rows(parts, high_count):
    return -(-parts * high_count // 16) * 16


def scatter(parts, entries, high_count, low_count, spread_ref, place_ref):
    rows = spread_rows(parts, high_count)
    return lax.dot_general(
        spread_ref[:rows, :entries],
        place_ref[:low_count, :entries],
        (((1,), (1,)), ((), ())),
        preferred_element_type=f32,
    )


def joined(result, count, high_count, pieces=None):
    pieces = pieces or [PIECES] * count
    values, first = [], 0
    for number in pieces:
        rows = [result[first + k * high_count : first + (k + 1) * high_count] for k in range(number)]
        first += number * high_count
        total = rows[-1]
        for row in reversed(rows[:-1]):
            total = total + row
        values.append(total)
    return values


def point_gather(ref, point):
    return gather_rows(lambda c, k: ref[c, k : k + 1, :], PT_ROWS, point // LANES, point % LANES, 3)


def narrow(ref, k, value):
    parts = PT_LO // LANES
    for part in range(parts):
        ref[k, pl.ds(part, PT_HI, stride=parts), :] = value[:, part * LANES : (part + 1) * LANES]


def slot_place(slot, sizes):
    within = slot % sizes.slot
    return within % sizes.pts, (slot // sizes.slot) * sizes.block + within // sizes.pts


def solve(inverse, values):
    first = inverse[0] * values[0] + inverse[1] * values[1] + inverse[2] * values[2]
    second = inverse[1] * values[0] + inverse[3] * values[1] + inverse[4] * values[2]
    third = inverse[2] * values[0] + inverse[4] * values[1] + inverse[5] * values[2]
    return first, second, third


def write_messages(fields, scalar, groups, message, out_ref, sizes, extra=None, column=None):
    which = lane_iota(sizes.pts) // sizes.block
    for g in range(groups):
        rows = fields[g * sizes.cams : (g + 1) * sizes.cams]
        moved = swap_partial(rows, sizes)
        for c in range(sizes.cams):
            value = moved[c]
            if g == groups - 1 and scalar is not None:
                value = jnp.where(which == sizes.cams - 1, scalar, value)
            out_ref[pl.ds(c * message + g, sizes.pts, stride=sizes.cams * message), :] = value
    for g in range(groups, message):
        for c in range(sizes.cams):
            value = jnp.where(column == c, extra, 0.0)
            out_ref[pl.ds(c * message + g, sizes.pts, stride=sizes.cams * message), :] = value


def swap_partial(rows, sizes):
    return swap_blocks(rows, sizes.block, sizes.cams)


def read_row(in_ref, c, g, message, sizes):
    return in_ref[pl.ds(c * message + g, sizes.pts, stride=sizes.cams * message), :]


def read_messages(in_ref, count, message, sizes):
    fields = []
    group = 0
    while len(fields) < count:
        rows = [read_row(in_ref, c, group, message, sizes) for c in range(sizes.cams)]
        fields += swap_blocks(rows, sizes.block, min(sizes.cams, count - len(fields)))
        group += 1
    return fields


def read_scalar(in_ref, groups, message, sizes):
    total = read_row(in_ref, 0, groups - 1, message, sizes)
    for c in range(1, sizes.cams):
        total = total + read_row(in_ref, c, groups - 1, message, sizes)
    chosen = jnp.where(lane_iota(sizes.pts) == LANES - 1, total, 0.0)
    return jnp.sum(chosen, keepdims=True)


def setup_kernel(sizes, column_ref, *refs):
    sources, refs = refs[:6], refs[6:]
    out_ref, a_ref, b_ref, inv_ref, grad_ref, place_point_ref, place_slot_ref, new_slot_ref, new_point_ref = refs[:9]
    refs = refs[9:]
    r_ref, parts_ref, spread_ref, table_ref, place_wide_ref, place_list_ref = refs[:6]
    jac_ref, pjac_ref, res_ref, slot_ref, point_ref, list_ref = refs[6:12]
    semaphores = refs[12]
    rows = sizes.rows
    copies = [
        pltpu.make_async_copy(source, target, semaphores.at[k])
        for k, (source, target) in enumerate(zip(sources, refs[6:12]))
    ]
    for copy in copies:
        copy.start()
    for k in (1, 2, 4):
        copies[k].wait()
    new_point_ref[...] = point_ref[...]
    for j in range(rows):
        columns = slice(j * LANES, (j + 1) * LANES)
        b_ref[pl.ds(j, 6, stride=rows), :] = pjac_ref[:, columns]
        r_ref[pl.ds(j, 2, stride=rows), :] = res_ref[:, columns]

    def at(ref, comp, group):
        return ref[comp * rows + group * SUB : comp * rows + (group + 1) * SUB, :]

    normal_pieces = [FINE] * 9

    for group in range(rows // SUB):
        b = [at(b_ref, k, group) for k in range(6)]
        r = [at(r_ref, k, group) for k in range(2)]
        values = [b[i] * b[j] + b[3 + i] * b[3 + j] for i, j in ((0, 0), (0, 1), (0, 2), (1, 1), (1, 2), (2, 2))]
        values += [b[i] * r[0] + b[3 + i] * r[1] for i in range(3)]
        parts = [part for value, pieces in zip(values, normal_pieces) for part in cut(value, pieces)]
        keep_parts(parts, group, parts_ref)
        for s in range(SUB):
            row = group * SUB + s
            point = point_ref[row : row + 1, :]
            spread_row(row, part_rows(len(parts), group, s, parts_ref), point >> 8, PT_HI, spread_ref)
            place_row(row, point & (PT_LO - 1), PT_LO, place_wide_ref)
    result = scatter(sum(normal_pieces), sizes.obs, PT_HI, PT_LO, spread_ref, place_wide_ref)
    normal = joined(result, 9, PT_HI, normal_pieces)
    top_left = normal[0] + damping_point
    top_mid = normal[1]
    top_right = normal[2]
    mid_mid = normal[3] + damping_point
    mid_right = normal[4]
    low_right = normal[5] + damping_point
    adjugate = [
        mid_mid * low_right - mid_right * mid_right,
        top_right * mid_right - top_mid * low_right,
        top_mid * mid_right - top_right * mid_mid,
        top_left * low_right - top_right * top_right,
        top_mid * top_right - top_left * mid_right,
        top_left * mid_mid - top_mid * top_mid,
    ]
    determinant = top_left * adjugate[0] + top_mid * adjugate[1] + top_right * adjugate[2]
    inverse = [value / determinant for value in adjugate]
    for k in range(6):
        narrow(inv_ref, k, inverse[k])
    for k in range(3):
        narrow(grad_ref, k, normal[6 + k])
    eliminated = solve(inverse, normal[6:])
    for k in range(3):
        narrow(table_ref, k, eliminated[k])
    place_point_ref[...] = place_wide_ref[:LANES, :] + place_wide_ref[LANES:, :]
    for k in (0, 3, 5):
        copies[k].wait()
    new_slot_ref[...] = slot_ref[...]
    for j in range(rows):
        for start in range(0, 2 * CP, SUB):
            size = min(SUB, 2 * CP - start)
            a_ref[pl.ds(start * rows + j, size, stride=rows), :] = jac_ref[
                start : start + size, j * LANES : (j + 1) * LANES
            ]

    for group in range(rows // SUB):
        at_point = point_gather(table_ref, point_ref[group * SUB : (group + 1) * SUB, :])
        b = [at(b_ref, k, group) for k in range(6)]
        errors = [at(r_ref, i, group) - sum(b[3 * i + k] * at_point[k] for k in range(3)) for i in range(2)]
        a = [at(a_ref, k, group) for k in range(2 * CP)]
        values = [a[k] * errors[0] + a[CP + k] * errors[1] for k in range(CP)]
        values += [a[k] * a[k] + a[CP + k] * a[CP + k] for k in range(CP)]
        parts = [part for value in values for part in cut(value)]
        keep_parts(parts, group, parts_ref)
        for s in range(SUB):
            row = group * SUB + s
            high, low = slot_place(slot_ref[row : row + 1, :], sizes)
            spread_row(row, part_rows(len(parts), group, s, parts_ref), high, sizes.pts, spread_ref)
            place_row(row, low, LANES, place_slot_ref)
    result = scatter(2 * CP * PIECES, sizes.obs, sizes.pts, LANES, spread_ref, place_slot_ref)
    fields = joined(result, 2 * CP, sizes.pts)

    pieces = sizes.slot // LANES
    lane = lane_iota(1)
    for c in range(sizes.cams):
        for half in range(pieces):
            value = list_ref[c : c + 1, half * LANES : (half + 1) * LANES]
            low = c * sizes.block + half * (LANES // sizes.pts) + lane // sizes.pts
            parts = [(value >> 8).astype(f32), (value & 255).astype(f32)]
            spread_row(c * pieces + half, parts, lane % sizes.pts, sizes.pts, spread_ref)
            place_row(c * pieces + half, low, LANES, place_list_ref)
    result = scatter(2, sizes.cams * sizes.slot, sizes.pts, LANES, spread_ref, place_list_ref)
    listed = result[: sizes.pts] * 256.0 + result[sizes.pts : 2 * sizes.pts]
    write_messages(fields, None, sizes.first_groups, sizes.first_message, out_ref, sizes, extra=listed, column=column_ref[0])


def entries_scatter(fields, entry, sizes, spread_ref, place_ref):
    high, low = entry // LANES, entry % LANES
    parts = [part for value in fields for part in cut(value)]
    for p in range(sizes.pts):
        spread_row(p, [part[p : p + 1] for part in parts], high[p : p + 1], sizes.own_rows, spread_ref)
        place_row(p, low[p : p + 1], LANES, place_ref)
    result = scatter(len(parts), sizes.pts * LANES, sizes.own_rows, LANES, spread_ref, place_ref)
    return joined(result, len(fields), sizes.own_rows)


def send_owned(scaled, partial, entry, out_ref, table_ref, sizes):
    for k in range(CP):
        table_ref[k] = scaled[k]
    fields = gather_rows(lambda c, k: table_ref[c, k : k + 1, :], sizes.run_rows, entry // LANES, entry % LANES, CP)
    write_messages(fields, partial, sizes.groups, sizes.message, out_ref, sizes)


def dot_fields(left, right):
    return jnp.sum(sum(a * b for a, b in zip(left, right)), keepdims=True)


def first_owner_kernel(sizes, in_ref, out_ref, entry_ref, pre_ref, rem_ref,
                       table_ref, spread_ref, place_ref):
    listed = jnp.zeros((sizes.pts, LANES), f32)
    for c in range(sizes.cams):
        listed = listed + read_row(in_ref, c, sizes.first_groups, sizes.first_message, sizes)
    entry = listed.astype(jnp.int32) % sizes.run
    entry_ref[...] = entry
    fields = read_messages(in_ref, 2 * CP, sizes.first_message, sizes)
    sums = entries_scatter(fields, entry, sizes, spread_ref, place_ref)
    remainder = [-value for value in sums[:CP]]
    precondition = [1.0 / (value + damping_camera) for value in sums[CP:]]
    scaled = [p * r for p, r in zip(precondition, remainder)]
    for k in range(CP):
        pre_ref[k] = precondition[k]
        rem_ref[k] = remainder[k]
    send_owned(scaled, dot_fields(remainder, scaled), entry, out_ref, table_ref, sizes)


def owner_kernel(sizes, start, final, in_ref, entry_ref, pre_ref, rem_ref, dir_ref, product_ref, *refs):
    refs = list(refs)
    sol_ref = None if start else refs.pop(0)
    out_ref, new_rem_ref, new_sol_ref, step_ref = refs[:4]
    fields_ref = refs[4] if final else None
    table_ref, spread_ref, place_ref = refs[-3:]
    entry = entry_ref[...]
    fields = read_messages(in_ref, CP, sizes.message, sizes)
    curvature = read_scalar(in_ref, sizes.groups, sizes.message, sizes)
    step = product_ref[...] / jnp.broadcast_to(curvature, (SUB, LANES))
    step_ref[...] = step
    sums = entries_scatter(fields, entry, sizes, spread_ref, place_ref)
    remainder, scaled = [], []
    for k in range(CP):
        direction = dir_ref[k]
        moved = step[:1] * direction
        moved = moved if start else sol_ref[k] + moved
        new_sol_ref[k] = moved
        value = rem_ref[k] - step[:1] * (sums[k] + damping_camera * direction)
        new_rem_ref[k] = value
        remainder.append(value)
        scaled.append(pre_ref[k] * value)
        if final:
            for j, field in enumerate((moved, direction, scaled[k])):
                first = (j * CP + k) * sizes.own_rows
                fields_ref[first : first + sizes.own_rows, :] = field
    send_owned(scaled, dot_fields(remainder, scaled), entry, out_ref, table_ref, sizes)


def schur_kernel(sizes, start, last, in_ref, a_ref, b_ref, inv_ref, slot_ref, point_ref,
                 place_point_ref, place_slot_ref, pre_ref, rem_ref, grad_ref, *refs):
    refs = list(refs)
    if not start:
        product_ref, at_slot_ref, dir_ref, step_ref, sum_ref = refs[:5]
        refs = refs[5:]
    out_ref, new_product_ref, new_sum_ref = refs[:3]
    refs = refs[3:]
    new_grad_ref = None if start else refs.pop(0)
    q_ref, parts_ref, spread_ref, table_ref = refs[-4:]
    new_at_slot_ref, new_dir_ref = (refs[0], None) if last else refs[:2]
    rows = sizes.rows

    def at(ref, comp, group):
        return ref[comp * rows + group * SUB : comp * rows + (group + 1) * SUB, :]

    renewed = jnp.broadcast_to(read_scalar(in_ref, sizes.groups, sizes.message, sizes), (SUB, LANES))
    new_product_ref[...] = renewed
    fields = read_messages(in_ref, CP, sizes.message, sizes)
    beta = None if start else (renewed / product_ref[...])[:1]
    squares = None
    for k in range(CP):
        direction = pre_ref[k] * rem_ref[k]
        if start:
            new_at_slot_ref[k] = fields[k]
        else:
            new_at_slot_ref[k] = fields[k] + beta * at_slot_ref[k]
            direction = direction + beta * dir_ref[k]
        if not last:
            new_dir_ref[k] = direction
        squares = direction * direction if squares is None else squares + direction * direction

    for group in range(rows // SUB):
        high, low = slot_place(slot_ref[group * SUB : (group + 1) * SUB, :], sizes)
        gathered = gather_rows(lambda c, k: new_at_slot_ref[c, k : k + 1, :], sizes.pts, high, low, CP)
        q = [sum(at(a_ref, i * CP + k, group) * gathered[k] for k in range(CP)) for i in range(2)]
        for i in range(2):
            q_ref[i * rows + group * SUB : i * rows + (group + 1) * SUB, :] = q[i]
        values = [at(b_ref, k, group) * q[0] + at(b_ref, 3 + k, group) * q[1] for k in range(3)]
        parts = [part for value in values for part in cut(value, FINE)]
        keep_parts(parts, group, parts_ref)
        for s in range(SUB):
            row = group * SUB + s
            spread_row(row, part_rows(len(parts), group, s, parts_ref), point_ref[row : row + 1, :] // LANES, PT_ROWS, spread_ref)
    result = scatter(3 * FINE, sizes.obs, PT_ROWS, LANES, spread_ref, place_point_ref)
    sums = joined(result, 3, PT_ROWS, [FINE] * 3)
    folded = solve([inv_ref[k] for k in range(6)], sums)
    for k in range(3):
        new_sum_ref[k] = sums[k]
        if not start:
            new_grad_ref[k] = grad_ref[k] + step_ref[:1, :1] * sum_ref[k]

    inner = None
    for k in range(3):
        table_ref[k] = folded[k]
    for group in range(rows // SUB):
        at_point = point_gather(table_ref, point_ref[group * SUB : (group + 1) * SUB, :])
        q = [at(q_ref, i, group) for i in range(2)]
        errors = [q[i] - sum(at(b_ref, 3 * i + k, group) * at_point[k] for k in range(3)) for i in range(2)]
        here = q[0] * errors[0] + q[1] * errors[1]
        inner = here if inner is None else inner + here
        if not last:
            values = [at(a_ref, k, group) * errors[0] + at(a_ref, CP + k, group) * errors[1] for k in range(CP)]
            parts = [part for value in values for part in cut(value)]
            keep_parts(parts, group, parts_ref)
            for s in range(SUB):
                row = group * SUB + s
                high, _ = slot_place(slot_ref[row : row + 1, :], sizes)
                spread_row(row, part_rows(len(parts), group, s, parts_ref), high, sizes.pts, spread_ref)
    partial = jnp.sum(inner, keepdims=True) + damping_camera * jnp.sum(squares, keepdims=True)
    if last:
        out_ref[...] = jnp.broadcast_to(partial, (sizes.devices, LANES))
        return
    result = scatter(CP * PIECES, sizes.obs, sizes.pts, LANES, spread_ref, place_slot_ref)
    fields = joined(result, CP, sizes.pts)
    write_messages(fields, partial, sizes.groups, sizes.message, out_ref, sizes)


def tail_kernel(sizes, in_ref, product_ref, own_ref, other_ref, out_ref):
    renewed = jnp.broadcast_to(read_scalar(in_ref, sizes.groups, sizes.message, sizes), (SUB, LANES))
    beta = (renewed / product_ref[...])[:1]
    field = CP * sizes.own_rows
    for j, ref in enumerate((own_ref, other_ref)):
        first = j * 2 * field
        out_ref[first : first + field, :] = ref[:field, :]
        out_ref[first + field : first + 2 * field, :] = ref[2 * field :, :] + beta * ref[field : 2 * field, :]


def final_kernel(sizes, masks, run_ref, in_ref, product_ref, inv_ref, grad_ref, sum_ref, *refs):
    all_refs = refs[: len(masks)]
    cam_ref, pt_ref, table_ref = refs[len(masks) :]
    curvature = jnp.sum(jnp.where(lane_iota(sizes.devices) == 0, in_ref[...], 0.0), keepdims=True)
    step = (product_ref[...] / jnp.broadcast_to(curvature, (SUB, LANES)))[:1]
    for all_ref, pair in zip(all_refs, masks):
        for j, mask in enumerate(pair):
            base_column = (run_ref[0] ^ mask) * sizes.run
            for h in range(sizes.run_rows):
                columns = pl.ds(pl.multiple_of(base_column + h * LANES, LANES), LANES)
                for start in range(0, CP, SUB):
                    size = min(SUB, CP - start)
                    first = (j * 2 * CP + start) * sizes.own_rows + h
                    base = all_ref[pl.ds(first, size, stride=sizes.own_rows), :]
                    direction = all_ref[pl.ds(first + CP * sizes.own_rows, size, stride=sizes.own_rows), :]
                    cam_ref[start : start + size, columns] = base + step * direction
    total = [grad_ref[k] + step[:, :1] * sum_ref[k] for k in range(3)]
    solved = solve([inv_ref[k] for k in range(6)], total)
    for k in range(3):
        table_ref[k * PT_ROWS : (k + 1) * PT_ROWS, :] = -solved[k]
    for row in range(PT_ROWS):
        pt_ref[:, row * LANES : (row + 1) * LANES] = table_ref[pl.ds(row, 3, stride=PT_ROWS), :]


def shape(*dims, dtype=f32):
    return jax.ShapeDtypeStruct(dims, dtype)


def kept(*dims, dtype=f32):
    return pltpu.VMEM(dims, dtype)


def call(kernel, name, inputs, outputs, scratch, scalars=(), inputs_at=pltpu.VMEM, cost=None):
    vmem = pl.BlockSpec(memory_space=pltpu.VMEM)
    given = pl.BlockSpec(memory_space=inputs_at)
    smem = pl.BlockSpec(memory_space=pltpu.SMEM)
    return pl.pallas_call(
        kernel,
        name=name,
        out_shape=outputs,
        in_specs=[smem] * len(scalars) + [given] * len(inputs),
        out_specs=[vmem] * len(outputs),
        scratch_shapes=scratch,
        cost_estimate=cost,
        compiler_params=pltpu.CompilerParams(vmem_limit_bytes=VMEM_LIMIT),
    )(*scalars, *inputs)


def body(camera_jacobian, point_jacobian, residual, observed_slot, observed_point, send_list):
    sizes = Sizes(lax.axis_size("pts"), lax.axis_size("cams"), send_list.shape[2], camera_jacobian.shape[1])
    axes = ("pts", "cams")
    rows = sizes.rows
    slot = observed_slot.reshape(rows, LANES)
    point = observed_point.reshape(rows, LANES)
    column = lax.axis_index("cams").astype(jnp.int32).reshape(1)

    def exchange(messages):
        width = messages.size // sizes.devices
        flat = messages.reshape(sizes.devices, 1, width)
        return lax.all_to_all(flat, axes, split_axis=0, concat_axis=0, tiled=True).reshape(messages.shape)

    def flipped(value, flip):
        return lax.ppermute(value, "pts", [(p, p ^ flip) for p in range(sizes.pts)])

    def factors(high_rows, low_rows, entries):
        return [pltpu.VMEM((high_rows, entries), bf16), pltpu.VMEM((low_rows, entries), bf16)]

    point_table = kept(3, PT_ROWS, LANES)
    owned = kept(CP, sizes.own_rows, LANES)
    messages = kept(sizes.devices * sizes.message, LANES)
    scalar = kept(SUB, LANES)
    owned_scratch = pltpu.VMEM((CP, sizes.own_rows, LANES), f32)
    entries = sizes.pts * LANES

    point_scratch = pltpu.VMEM((3, PT_ROWS, LANES), f32)

    def parts_scratch(count):
        return pltpu.VMEM((rows // SUB, count * SUB, LANES), f32)


    given = [
        pltpu.with_memory_space_constraint(value, pltpu.HBM)
        for value in (camera_jacobian, point_jacobian, residual, slot, point, send_list[0])
    ]
    first, a, b, inverse, gradient, place_point, place_slot, slot, point = call(
        functools.partial(setup_kernel, sizes),
        "setup",
        given,
        [
            kept(sizes.devices * sizes.first_message, LANES),
            kept(2 * CP * rows, LANES),
            kept(6 * rows, LANES),
            kept(6, PT_ROWS, LANES),
            point_table,
            kept(LANES, sizes.obs, dtype=bf16),
            kept(LANES, sizes.obs, dtype=bf16),
            kept(rows, LANES, dtype=jnp.int32),
            kept(rows, LANES, dtype=jnp.int32),
        ],
        [pltpu.VMEM((2 * rows, LANES), f32), parts_scratch(2 * CP * PIECES)]
        + [pltpu.VMEM((max(spread_rows(9 * FINE, PT_HI), spread_rows(2 * CP * PIECES, sizes.pts)), sizes.obs), bf16)]
        + [point_scratch, pltpu.VMEM((PT_LO, sizes.obs), bf16), pltpu.VMEM((LANES, sizes.cams * sizes.slot), bf16)]
        + [pltpu.VMEM(value.shape, value.dtype) for value in given]
        + [pltpu.SemaphoreType.DMA((len(given),))],
        scalars=[column],
        inputs_at=pl.ANY,
    )
    out, entry, precondition, remainder = call(
        functools.partial(first_owner_kernel, sizes),
        "first_owner",
        [exchange(first)],
        [messages, kept(sizes.pts, LANES, dtype=jnp.int32), owned, owned],
        [owned_scratch] + factors(spread_rows(2 * CP * PIECES, sizes.own_rows), LANES, entries),
    )
    schur_scratch = [pltpu.VMEM((2 * rows, LANES), f32), parts_scratch(CP * PIECES)]
    schur_scratch += [pltpu.VMEM((max(spread_rows(3 * FINE, PT_ROWS), spread_rows(CP * PIECES, sizes.pts)), sizes.obs), bf16)]
    schur_scratch += [point_scratch]
    at_slot = kept(CP, sizes.pts, LANES)
    product = slots = direction = step = sums = solution_ = None
    for iteration in range(ITERS):
        start, last = iteration == 0, iteration == ITERS - 1
        earlier = [] if start else [product, slots, direction, step, sums]
        if last:
            neighbour = flipped(fields, FIRST)
        arrived = exchange(out)
        if last:
            (both,) = call(
                functools.partial(tail_kernel, sizes),
                "tail",
                [arrived, product, fields, neighbour],
                [kept(4 * CP * sizes.own_rows, LANES)],
                [],
            )
            flips = [1 << bit for bit in range(sizes.pts.bit_length() - 1) if 1 << bit != FIRST]
            flips = flips[1:] + flips[:1]
            early = {flip: flipped(both, flip) for flip in (flips[0], flips[-1])}
        results = call(
            functools.partial(schur_kernel, sizes, start, last),
            "schur_last" if last else "schur",
            [arrived, a, b, inverse, slot, point, place_point, place_slot, precondition, remainder, gradient]
            + earlier,
            [kept(sizes.devices, LANES) if last else messages, scalar, point_table]
            + ([] if start else [point_table])
            + ([] if last else [at_slot, owned]),
            ([pltpu.VMEM((CP, sizes.pts, LANES), f32)] if last else []) + schur_scratch,
            cost=pl.CostEstimate(flops=2_000_000_000, bytes_accessed=10_000_000, transcendentals=0),
        )
        out, product, sums, *results = results
        if not start:
            gradient, *results = results
        if not last:
            slots, direction = results
        if last:
            early, out = lax.optimization_barrier((early, out))
            gathered, masks = [both], [(0, FIRST)]
            for flip in flips:
                gathered += [early[flip] if value is both and flip in early else flipped(value, flip) for value in gathered]
                masks += [tuple(mask ^ flip for mask in pair) for pair in masks]
            break
        final = iteration == ITERS - 2
        out, remainder, solution_, step, *rest = call(
            functools.partial(owner_kernel, sizes, start, final),
            "owner_final" if final else "owner",
            [exchange(out), entry, precondition, remainder, direction, product] + ([] if start else [solution_]),
            [messages, owned, owned, scalar] + ([kept(3 * CP * sizes.own_rows, LANES)] if final else []),
            [owned_scratch] + factors(spread_rows(CP * PIECES, sizes.own_rows), LANES, entries),
        )
        fields = rest[0] if final else None
    return call(
        functools.partial(final_kernel, sizes, masks),
        "final",
        [exchange(out), product, inverse, gradient, sums] + gathered,
        [shape(CP, CAM_OWN), shape(3, PT_DEV)],
        [pltpu.VMEM((3 * PT_ROWS, LANES), f32)],
        scalars=[lax.axis_index("pts").astype(jnp.int32).reshape(1)],
    )


def solution(mesh):
    return jax.shard_map(
        lambda *arguments: tuple(body(*arguments)),
        mesh=mesh,
        in_specs=(
            P(None, ("pts", "cams")),
            P(None, ("pts", "cams")),
            P(None, ("pts", "cams")),
            P(("pts", "cams")),
            P(("pts", "cams")),
            P(("pts", "cams"), None, None),
        ),
        out_specs=(P(None, "cams"), P(None, ("pts", "cams"))),
        check_vma=False,
    )
```

```python
import functools

import jax
import jax.numpy as jnp
from jax import lax
from jax.experimental import pallas as pl
from jax.experimental.pallas import tpu as pltpu
from jax.sharding import PartitionSpec as P

CP = 9
CAM_OWN = 8192
PT_DEV = 4096
ITERS = 3
LANES = 128
SUB = 8
PT_ROWS = PT_DEV // LANES
PT_LO = 256
PT_HI = PT_DEV // PT_LO
PIECES = 2
FINE = 3
FIRST = 4
VMEM_LIMIT = 24 * 1024 * 1024

damping_camera = 1.0
damping_point = 1.0

f32 = jnp.float32
bf16 = jnp.bfloat16


class Sizes:
    def __init__(self, pts, cams, slot, obs):
        self.pts, self.cams, self.slot, self.obs = pts, cams, slot, obs
        self.devices = pts * cams
        self.block = slot // pts
        assert cams * self.block == LANES and LANES % pts == 0
        self.rows = obs // LANES
        self.run = CAM_OWN // pts
        self.run_rows = self.run // LANES
        self.own_rows = max(SUB, self.run_rows)
        self.groups = -(-CP // cams)
        self.first_groups = -(-2 * CP // cams)
        self.message = self.groups
        self.first_message = self.first_groups + 1
        assert self.groups * cams > CP


def sub_iota(rows):
    return lax.broadcasted_iota(jnp.int32, (rows, LANES), 0)


def lane_iota(rows):
    return lax.broadcasted_iota(jnp.int32, (rows, LANES), 1)


def cut(value, pieces=PIECES):
    parts = []
    for _ in range(pieces - 1):
        part = value.astype(bf16).astype(f32)
        parts.append(part)
        value = value - part
    parts.append(value)
    return parts


def swap_blocks(rows, block, wanted):
    which = lane_iota(rows[0].shape[0]) // block
    result = []
    for q in range(wanted):
        total = None
        for c, value in enumerate(rows):
            shift = ((c - q) * block) % LANES
            moved = pltpu.roll(value, shift, axis=1) if shift else value
            total = jnp.where(which == c, moved, 0.0 if total is None else total)
        result.append(total)
    return result


def gather_rows(row, count, high, low, comps):
    result = [None] * comps
    for k in range(count):
        here = high == k
        for c in range(comps):
            source = jnp.broadcast_to(row(c, k), high.shape)
            found = jnp.take_along_axis(source, low, axis=1, mode="promise_in_bounds")
            result[c] = found if k == 0 else jnp.where(here, found, result[c])
    return result


def spread_row(index, parts, high, high_count, spread_ref):
    columns = slice(index * LANES, (index + 1) * LANES)
    mask = jnp.broadcast_to(high, (high_count, LANES)) == sub_iota(high_count)
    together = max(1, 16 // high_count)
    for start in range(0, len(parts), together):
        pieces = [
            jnp.where(mask, jnp.broadcast_to(part, (high_count, LANES)), 0.0)
            for part in parts[start : start + together]
        ]
        while len(pieces) < together:
            pieces.append(jnp.zeros((high_count, LANES), f32))
        tile = pieces[0] if together == 1 else jnp.concatenate(pieces, axis=0)
        spread_ref[start * high_count : start * high_count + tile.shape[0], columns] = tile.astype(bf16)


def place_row(index, low, low_count, place_ref):
    columns = slice(index * LANES, (index + 1) * LANES)
    place = jnp.broadcast_to(low, (low_count, LANES)) == sub_iota(low_count)
    place_ref[:low_count, columns] = jnp.where(place, 1.0, 0.0).astype(bf16)


def keep_parts(parts, group, parts_ref):
    for k, part in enumerate(parts):
        parts_ref[group, k * SUB : (k + 1) * SUB, :] = part


def part_rows(count, group, s, parts_ref):
    return [parts_ref[group, k * SUB + s : k * SUB + s + 1, :] for k in range(count)]


def spread_rows(parts, high_count):
    return -(-parts * high_count // 16) * 16


def scatter(parts, entries, high_count, low_count, spread_ref, place_ref):
    rows = spread_rows(parts, high_count)
    return lax.dot_general(
        spread_ref[:rows, :entries],
        place_ref[:low_count, :entries],
        (((1,), (1,)), ((), ())),
        preferred_element_type=f32,
    )


def joined(result, count, high_count, pieces=None):
    pieces = pieces or [PIECES] * count
    values, first = [], 0
    for number in pieces:
        rows = [result[first + k * high_count : first + (k + 1) * high_count] for k in range(number)]
        first += number * high_count
        total = rows[-1]
        for row in reversed(rows[:-1]):
            total = total + row
        values.append(total)
    return values


def point_gather(ref, point):
    return gather_rows(lambda c, k: ref[c, k : k + 1, :], PT_ROWS, point // LANES, point % LANES, 3)


def narrow(ref, k, value):
    parts = PT_LO // LANES
    for part in range(parts):
        ref[k, pl.ds(part, PT_HI, stride=parts), :] = value[:, part * LANES : (part + 1) * LANES]


def slot_place(slot, sizes):
    within = slot % sizes.slot
    return within % sizes.pts, (slot // sizes.slot) * sizes.block + within // sizes.pts


def solve(inverse, values):
    first = inverse[0] * values[0] + inverse[1] * values[1] + inverse[2] * values[2]
    second = inverse[1] * values[0] + inverse[3] * values[1] + inverse[4] * values[2]
    third = inverse[2] * values[0] + inverse[4] * values[1] + inverse[5] * values[2]
    return first, second, third


def write_messages(fields, scalar, groups, message, out_ref, sizes, extra=None, column=None):
    which = lane_iota(sizes.pts) // sizes.block
    for g in range(groups):
        rows = fields[g * sizes.cams : (g + 1) * sizes.cams]
        moved = swap_partial(rows, sizes)
        for c in range(sizes.cams):
            value = moved[c]
            if g == groups - 1 and scalar is not None:
                value = jnp.where(which == sizes.cams - 1, scalar, value)
            out_ref[pl.ds(c * message + g, sizes.pts, stride=sizes.cams * message), :] = value
    for g in range(groups, message):
        for c in range(sizes.cams):
            value = jnp.where(column == c, extra, 0.0)
            out_ref[pl.ds(c * message + g, sizes.pts, stride=sizes.cams * message), :] = value


def swap_partial(rows, sizes):
    return swap_blocks(rows, sizes.block, sizes.cams)


def read_row(in_ref, c, g, message, sizes):
    return in_ref[pl.ds(c * message + g, sizes.pts, stride=sizes.cams * message), :]


def read_messages(in_ref, count, message, sizes):
    fields = []
    group = 0
    while len(fields) < count:
        rows = [read_row(in_ref, c, group, message, sizes) for c in range(sizes.cams)]
        fields += swap_blocks(rows, sizes.block, min(sizes.cams, count - len(fields)))
        group += 1
    return fields


def read_scalar(in_ref, groups, message, sizes):
    total = read_row(in_ref, 0, groups - 1, message, sizes)
    for c in range(1, sizes.cams):
        total = total + read_row(in_ref, c, groups - 1, message, sizes)
    chosen = jnp.where(lane_iota(sizes.pts) == LANES - 1, total, 0.0)
    return jnp.sum(chosen, keepdims=True)


def setup_kernel(sizes, run_ref, column_ref, *refs):
    del run_ref
    sources, refs = refs[:6], refs[6:]
    out_ref, a_ref, b_ref, inv_ref, grad_ref, place_point_ref, place_slot_ref, new_slot_ref, new_point_ref = refs[:9]
    refs = refs[9:]
    r_ref, parts_ref, spread_ref, table_ref, place_wide_ref, place_list_ref = refs[:6]
    jac_ref, pjac_ref, res_ref, slot_ref, point_ref, list_ref = refs[6:12]
    semaphores = refs[12]
    rows = sizes.rows
    copies = [
        pltpu.make_async_copy(source, target, semaphores.at[k])
        for k, (source, target) in enumerate(zip(sources, refs[6:12]))
    ]
    for copy in copies:
        copy.start()
    for k in (1, 2, 4):
        copies[k].wait()
    new_point_ref[...] = point_ref[...]
    for j in range(rows):
        columns = slice(j * LANES, (j + 1) * LANES)
        b_ref[pl.ds(j, 6, stride=rows), :] = pjac_ref[:, columns]
        r_ref[pl.ds(j, 2, stride=rows), :] = res_ref[:, columns]

    def at(ref, comp, group):
        return ref[comp * rows + group * SUB : comp * rows + (group + 1) * SUB, :]

    normal_pieces = [FINE] * 9

    for group in range(rows // SUB):
        b = [at(b_ref, k, group) for k in range(6)]
        r = [at(r_ref, k, group) for k in range(2)]
        values = [b[i] * b[j] + b[3 + i] * b[3 + j] for i, j in ((0, 0), (0, 1), (0, 2), (1, 1), (1, 2), (2, 2))]
        values += [b[i] * r[0] + b[3 + i] * r[1] for i in range(3)]
        parts = [part for value, pieces in zip(values, normal_pieces) for part in cut(value, pieces)]
        keep_parts(parts, group, parts_ref)
        for s in range(SUB):
            row = group * SUB + s
            point = point_ref[row : row + 1, :]
            spread_row(row, part_rows(len(parts), group, s, parts_ref), point >> 8, PT_HI, spread_ref)
            place_row(row, point & (PT_LO - 1), PT_LO, place_wide_ref)
    result = scatter(sum(normal_pieces), sizes.obs, PT_HI, PT_LO, spread_ref, place_wide_ref)
    normal = joined(result, 9, PT_HI, normal_pieces)
    top_left = normal[0] + damping_point
    top_mid = normal[1]
    top_right = normal[2]
    mid_mid = normal[3] + damping_point
    mid_right = normal[4]
    low_right = normal[5] + damping_point
    adjugate = [
        mid_mid * low_right - mid_right * mid_right,
        top_right * mid_right - top_mid * low_right,
        top_mid * mid_right - top_right * mid_mid,
        top_left * low_right - top_right * top_right,
        top_mid * top_right - top_left * mid_right,
        top_left * mid_mid - top_mid * top_mid,
    ]
    determinant = top_left * adjugate[0] + top_mid * adjugate[1] + top_right * adjugate[2]
    inverse = [value / determinant for value in adjugate]
    for k in range(6):
        narrow(inv_ref, k, inverse[k])
    for k in range(3):
        narrow(grad_ref, k, normal[6 + k])
    eliminated = solve(inverse, normal[6:])
    for k in range(3):
        narrow(table_ref, k, eliminated[k])
    place_point_ref[...] = place_wide_ref[:LANES, :] + place_wide_ref[LANES:, :]
    for k in (0, 3, 5):
        copies[k].wait()
    new_slot_ref[...] = slot_ref[...]
    for j in range(rows):
        for start in range(0, 2 * CP, SUB):
            size = min(SUB, 2 * CP - start)
            a_ref[pl.ds(start * rows + j, size, stride=rows), :] = jac_ref[
                start : start + size, j * LANES : (j + 1) * LANES
            ]

    for group in range(rows // SUB):
        at_point = point_gather(table_ref, point_ref[group * SUB : (group + 1) * SUB, :])
        b = [at(b_ref, k, group) for k in range(6)]
        errors = [at(r_ref, i, group) - sum(b[3 * i + k] * at_point[k] for k in range(3)) for i in range(2)]
        a = [at(a_ref, k, group) for k in range(2 * CP)]
        values = [a[k] * errors[0] + a[CP + k] * errors[1] for k in range(CP)]
        values += [a[k] * a[k] + a[CP + k] * a[CP + k] for k in range(CP)]
        parts = [part for value in values for part in cut(value)]
        keep_parts(parts, group, parts_ref)
        for s in range(SUB):
            row = group * SUB + s
            high, low = slot_place(slot_ref[row : row + 1, :], sizes)
            spread_row(row, part_rows(len(parts), group, s, parts_ref), high, sizes.pts, spread_ref)
            place_row(row, low, LANES, place_slot_ref)
    result = scatter(2 * CP * PIECES, sizes.obs, sizes.pts, LANES, spread_ref, place_slot_ref)
    fields = joined(result, 2 * CP, sizes.pts)

    pieces = sizes.slot // LANES
    lane = lane_iota(1)
    for c in range(sizes.cams):
        for half in range(pieces):
            value = list_ref[c : c + 1, half * LANES : (half + 1) * LANES]
            low = c * sizes.block + half * (LANES // sizes.pts) + lane // sizes.pts
            parts = [(value >> 8).astype(f32), (value & 255).astype(f32)]
            spread_row(c * pieces + half, parts, lane % sizes.pts, sizes.pts, spread_ref)
            place_row(c * pieces + half, low, LANES, place_list_ref)
    result = scatter(2, sizes.cams * sizes.slot, sizes.pts, LANES, spread_ref, place_list_ref)
    listed = result[: sizes.pts] * 256.0 + result[sizes.pts : 2 * sizes.pts]
    write_messages(fields, None, sizes.first_groups, sizes.first_message, out_ref, sizes, extra=listed, column=column_ref[0])


def entries_scatter(fields, entry, sizes, spread_ref, place_ref):
    high, low = entry // LANES, entry % LANES
    parts = [part for value in fields for part in cut(value)]
    for p in range(sizes.pts):
        spread_row(p, [part[p : p + 1] for part in parts], high[p : p + 1], sizes.own_rows, spread_ref)
        place_row(p, low[p : p + 1], LANES, place_ref)
    result = scatter(len(parts), sizes.pts * LANES, sizes.own_rows, LANES, spread_ref, place_ref)
    return joined(result, len(fields), sizes.own_rows)


def send_owned(scaled, partial, entry, out_ref, table_ref, sizes):
    for k in range(CP):
        table_ref[k] = scaled[k]
    fields = gather_rows(lambda c, k: table_ref[c, k : k + 1, :], sizes.run_rows, entry // LANES, entry % LANES, CP)
    write_messages(fields, partial, sizes.groups, sizes.message, out_ref, sizes)


def dot_fields(left, right):
    return jnp.sum(sum(a * b for a, b in zip(left, right)), keepdims=True)


def first_owner_kernel(sizes, in_ref, out_ref, entry_ref, pre_ref, rem_ref,
                       table_ref, spread_ref, place_ref):
    listed = jnp.zeros((sizes.pts, LANES), f32)
    for c in range(sizes.cams):
        listed = listed + read_row(in_ref, c, sizes.first_groups, sizes.first_message, sizes)
    entry = listed.astype(jnp.int32) % sizes.run
    entry_ref[...] = entry
    fields = read_messages(in_ref, 2 * CP, sizes.first_message, sizes)
    sums = entries_scatter(fields, entry, sizes, spread_ref, place_ref)
    remainder = [-value for value in sums[:CP]]
    precondition = [1.0 / (value + damping_camera) for value in sums[CP:]]
    scaled = [p * r for p, r in zip(precondition, remainder)]
    for k in range(CP):
        pre_ref[k] = precondition[k]
        rem_ref[k] = remainder[k]
    send_owned(scaled, dot_fields(remainder, scaled), entry, out_ref, table_ref, sizes)


def owner_kernel(sizes, start, final, in_ref, entry_ref, pre_ref, rem_ref, dir_ref, product_ref, *refs):
    refs = list(refs)
    sol_ref = None if start else refs.pop(0)
    out_ref, new_rem_ref, step_ref, new_sol_ref = refs[:4]
    table_ref, spread_ref, place_ref = refs[-3:]
    entry = entry_ref[...]
    fields = read_messages(in_ref, CP, sizes.message, sizes)
    curvature = read_scalar(in_ref, sizes.groups, sizes.message, sizes)
    step = product_ref[...] / jnp.broadcast_to(curvature, (SUB, LANES))
    step_ref[...] = step
    sums = entries_scatter(fields, entry, sizes, spread_ref, place_ref)
    remainder, scaled = [], []
    for k in range(CP):
        direction = dir_ref[k]
        moved = step[:1] * direction
        moved = moved if start else sol_ref[k] + moved
        if not final:
            new_sol_ref[k] = moved
        value = rem_ref[k] - step[:1] * (sums[k] + damping_camera * direction)
        new_rem_ref[k] = value
        remainder.append(value)
        scaled.append(pre_ref[k] * value)
        if final:
            for j, field in enumerate((moved, direction, scaled[k])):
                first = (j * CP + k) * sizes.own_rows
                new_sol_ref[first : first + sizes.own_rows, :] = field
    send_owned(scaled, dot_fields(remainder, scaled), entry, out_ref, table_ref, sizes)


def schur_kernel(sizes, start, last, in_ref, a_ref, b_ref, inv_ref, slot_ref, point_ref,
                 place_point_ref, place_slot_ref, pre_ref, rem_ref, grad_ref, *refs):
    refs = list(refs)
    if not start:
        product_ref, at_slot_ref, dir_ref, step_ref, sum_ref = refs[:5]
        refs = refs[5:]
    out_ref, new_product_ref, new_sum_ref = refs[:3]
    refs = refs[3:]
    new_grad_ref = None if start else refs.pop(0)
    q_ref, parts_ref, spread_ref, table_ref = refs[-4:]
    new_at_slot_ref, new_dir_ref = (refs[0], None) if last else refs[:2]
    rows = sizes.rows

    def at(ref, comp, group):
        return ref[comp * rows + group * SUB : comp * rows + (group + 1) * SUB, :]

    renewed = jnp.broadcast_to(read_scalar(in_ref, sizes.groups, sizes.message, sizes), (SUB, LANES))
    new_product_ref[...] = renewed
    fields = read_messages(in_ref, CP, sizes.message, sizes)
    beta = None if start else (renewed / product_ref[...])[:1]
    squares = None
    for k in range(CP):
        direction = pre_ref[k] * rem_ref[k]
        if start:
            new_at_slot_ref[k] = fields[k]
        else:
            new_at_slot_ref[k] = fields[k] + beta * at_slot_ref[k]
            direction = direction + beta * dir_ref[k]
        if not last:
            new_dir_ref[k] = direction
        squares = direction * direction if squares is None else squares + direction * direction

    for group in range(rows // SUB):
        high, low = slot_place(slot_ref[group * SUB : (group + 1) * SUB, :], sizes)
        gathered = gather_rows(lambda c, k: new_at_slot_ref[c, k : k + 1, :], sizes.pts, high, low, CP)
        q = [sum(at(a_ref, i * CP + k, group) * gathered[k] for k in range(CP)) for i in range(2)]
        for i in range(2):
            q_ref[i * rows + group * SUB : i * rows + (group + 1) * SUB, :] = q[i]
        values = [at(b_ref, k, group) * q[0] + at(b_ref, 3 + k, group) * q[1] for k in range(3)]
        parts = [part for value in values for part in cut(value, FINE)]
        keep_parts(parts, group, parts_ref)
        for s in range(SUB):
            row = group * SUB + s
            spread_row(row, part_rows(len(parts), group, s, parts_ref), point_ref[row : row + 1, :] // LANES, PT_ROWS, spread_ref)
    result = scatter(3 * FINE, sizes.obs, PT_ROWS, LANES, spread_ref, place_point_ref)
    sums = joined(result, 3, PT_ROWS, [FINE] * 3)
    folded = solve([inv_ref[k] for k in range(6)], sums)
    for k in range(3):
        new_sum_ref[k] = sums[k]
        if not start:
            new_grad_ref[k] = grad_ref[k] + step_ref[:1, :1] * sum_ref[k]

    inner = None
    for k in range(3):
        table_ref[k] = folded[k]
    for group in range(rows // SUB):
        at_point = point_gather(table_ref, point_ref[group * SUB : (group + 1) * SUB, :])
        q = [at(q_ref, i, group) for i in range(2)]
        errors = [q[i] - sum(at(b_ref, 3 * i + k, group) * at_point[k] for k in range(3)) for i in range(2)]
        here = q[0] * errors[0] + q[1] * errors[1]
        inner = here if inner is None else inner + here
        if not last:
            values = [at(a_ref, k, group) * errors[0] + at(a_ref, CP + k, group) * errors[1] for k in range(CP)]
            parts = [part for value in values for part in cut(value)]
            keep_parts(parts, group, parts_ref)
            for s in range(SUB):
                row = group * SUB + s
                high, _ = slot_place(slot_ref[row : row + 1, :], sizes)
                spread_row(row, part_rows(len(parts), group, s, parts_ref), high, sizes.pts, spread_ref)
    partial = jnp.sum(inner, keepdims=True) + damping_camera * jnp.sum(squares, keepdims=True)
    if last:
        out_ref[...] = jnp.broadcast_to(partial, (sizes.devices, LANES))
        return
    result = scatter(CP * PIECES, sizes.obs, sizes.pts, LANES, spread_ref, place_slot_ref)
    fields = joined(result, CP, sizes.pts)
    write_messages(fields, partial, sizes.groups, sizes.message, out_ref, sizes)


def tail_kernel(sizes, in_ref, product_ref, own_ref, other_ref, out_ref):
    renewed = jnp.broadcast_to(read_scalar(in_ref, sizes.groups, sizes.message, sizes), (SUB, LANES))
    beta = (renewed / product_ref[...])[:1]
    field = CP * sizes.own_rows
    for j, ref in enumerate((own_ref, other_ref)):
        first = j * 2 * field
        out_ref[first : first + field, :] = ref[:field, :]
        out_ref[first + field : first + 2 * field, :] = ref[2 * field :, :] + beta * ref[field : 2 * field, :]


def final_kernel(sizes, masks, run_ref, in_ref, product_ref, inv_ref, grad_ref, sum_ref, *refs):
    all_refs = refs[: len(masks)]
    cam_ref, pt_ref, table_ref = refs[len(masks) :]
    curvature = jnp.sum(jnp.where(lane_iota(sizes.devices) == 0, in_ref[...], 0.0), keepdims=True)
    step = (product_ref[...] / jnp.broadcast_to(curvature, (SUB, LANES)))[:1]
    for all_ref, pair in zip(all_refs, masks):
        for j, mask in enumerate(pair):
            base_column = (run_ref[0] ^ mask) * sizes.run
            for h in range(sizes.run_rows):
                columns = pl.ds(pl.multiple_of(base_column + h * LANES, LANES), LANES)
                for start in range(0, CP, SUB):
                    size = min(SUB, CP - start)
                    first = (j * 2 * CP + start) * sizes.own_rows + h
                    base = all_ref[pl.ds(first, size, stride=sizes.own_rows), :]
                    direction = all_ref[pl.ds(first + CP * sizes.own_rows, size, stride=sizes.own_rows), :]
                    cam_ref[start : start + size, columns] = base + step * direction
    total = [grad_ref[k] + step[:, :1] * sum_ref[k] for k in range(3)]
    solved = solve([inv_ref[k] for k in range(6)], total)
    for k in range(3):
        table_ref[k * PT_ROWS : (k + 1) * PT_ROWS, :] = -solved[k]
    for row in range(PT_ROWS):
        pt_ref[:, row * LANES : (row + 1) * LANES] = table_ref[pl.ds(row, 3, stride=PT_ROWS), :]


def shape(*dims, dtype=f32):
    return jax.ShapeDtypeStruct(dims, dtype)


def kept(*dims, dtype=f32):
    return pltpu.VMEM(dims, dtype)


def call(kernel, name, inputs, outputs, scratch, scalars=(), inputs_at=pltpu.VMEM, cost=None):
    vmem = pl.BlockSpec(memory_space=pltpu.VMEM)
    given = pl.BlockSpec(memory_space=inputs_at)
    smem = pl.BlockSpec(memory_space=pltpu.SMEM)
    return pl.pallas_call(
        kernel,
        name=name,
        out_shape=outputs,
        in_specs=[smem] * len(scalars) + [given] * len(inputs),
        out_specs=[vmem] * len(outputs),
        scratch_shapes=scratch,
        cost_estimate=cost,
        compiler_params=pltpu.CompilerParams(vmem_limit_bytes=VMEM_LIMIT),
    )(*scalars, *inputs)


def body(camera_jacobian, point_jacobian, residual, observed_slot, observed_point, send_list):
    sizes = Sizes(lax.axis_size("pts"), lax.axis_size("cams"), send_list.shape[2], camera_jacobian.shape[1])
    axes = ("pts", "cams")
    rows = sizes.rows
    slot = observed_slot.reshape(rows, LANES)
    point = observed_point.reshape(rows, LANES)
    column = lax.axis_index("cams").astype(jnp.int32).reshape(1)
    run = lax.axis_index("pts").astype(jnp.int32).reshape(1)

    def exchange(messages):
        width = messages.size // sizes.devices
        flat = messages.reshape(sizes.devices, 1, width)
        return lax.all_to_all(flat, axes, split_axis=0, concat_axis=0, tiled=True).reshape(messages.shape)

    def flipped(value, flip):
        return lax.ppermute(value, "pts", [(p, p ^ flip) for p in range(sizes.pts)])

    def factors(high_rows, low_rows, entries):
        return [pltpu.VMEM((high_rows, entries), bf16), pltpu.VMEM((low_rows, entries), bf16)]

    point_table = kept(3, PT_ROWS, LANES)
    owned = kept(CP, sizes.own_rows, LANES)
    messages = kept(sizes.devices * sizes.message, LANES)
    scalar = kept(SUB, LANES)
    owned_scratch = pltpu.VMEM((CP, sizes.own_rows, LANES), f32)
    entries = sizes.pts * LANES

    point_scratch = pltpu.VMEM((3, PT_ROWS, LANES), f32)

    def parts_scratch(count):
        return pltpu.VMEM((rows // SUB, count * SUB, LANES), f32)


    given = [
        pltpu.with_memory_space_constraint(value, pltpu.HBM)
        for value in (camera_jacobian, point_jacobian, residual, slot, point, send_list[0])
    ]
    first, a, b, inverse, gradient, place_point, place_slot, slot, point = call(
        functools.partial(setup_kernel, sizes),
        "setup",
        given,
        [
            kept(sizes.devices * sizes.first_message, LANES),
            kept(2 * CP * rows, LANES),
            kept(6 * rows, LANES),
            kept(6, PT_ROWS, LANES),
            point_table,
            kept(LANES, sizes.obs, dtype=bf16),
            kept(LANES, sizes.obs, dtype=bf16),
            kept(rows, LANES, dtype=jnp.int32),
            kept(rows, LANES, dtype=jnp.int32),
        ],
        [pltpu.VMEM((2 * rows, LANES), f32), parts_scratch(2 * CP * PIECES)]
        + [pltpu.VMEM((max(spread_rows(9 * FINE, PT_HI), spread_rows(2 * CP * PIECES, sizes.pts)), sizes.obs), bf16)]
        + [point_scratch, pltpu.VMEM((PT_LO, sizes.obs), bf16), pltpu.VMEM((LANES, sizes.cams * sizes.slot), bf16)]
        + [pltpu.VMEM(value.shape, value.dtype) for value in given]
        + [pltpu.SemaphoreType.DMA((len(given),))],
        scalars=[run, column],
        inputs_at=pl.ANY,
    )
    out, entry, precondition, remainder = call(
        functools.partial(first_owner_kernel, sizes),
        "first_owner",
        [exchange(first)],
        [messages, kept(sizes.pts, LANES, dtype=jnp.int32), owned, owned],
        [owned_scratch] + factors(spread_rows(2 * CP * PIECES, sizes.own_rows), LANES, entries),
    )
    schur_scratch = [pltpu.VMEM((2 * rows, LANES), f32), parts_scratch(CP * PIECES)]
    schur_scratch += [pltpu.VMEM((max(spread_rows(3 * FINE, PT_ROWS), spread_rows(CP * PIECES, sizes.pts)), sizes.obs), bf16)]
    schur_scratch += [point_scratch]
    at_slot = kept(CP, sizes.pts, LANES)
    product = slots = direction = step = sums = solution_ = None
    for iteration in range(ITERS):
        start, last = iteration == 0, iteration == ITERS - 1
        earlier = [] if start else [product, slots, direction, step, sums]
        if last:
            neighbour = flipped(fields, FIRST)
        arrived = exchange(out)
        if last:
            (both,) = call(
                functools.partial(tail_kernel, sizes),
                "tail",
                [arrived, product, fields, neighbour],
                [kept(4 * CP * sizes.own_rows, LANES)],
                [],
            )
            flips = [1 << bit for bit in range(sizes.pts.bit_length() - 1) if 1 << bit != FIRST]
            flips = flips[1:] + flips[:1]
            early = {flip: flipped(both, flip) for flip in (flips[0], flips[-1])}
        results = call(
            functools.partial(schur_kernel, sizes, start, last),
            "schur_last" if last else "schur",
            [arrived, a, b, inverse, slot, point, place_point, place_slot, precondition, remainder, gradient]
            + earlier,
            [kept(sizes.devices, LANES) if last else messages, scalar, point_table]
            + ([] if start else [point_table])
            + ([] if last else [at_slot, owned]),
            ([pltpu.VMEM((CP, sizes.pts, LANES), f32)] if last else []) + schur_scratch,
            cost=pl.CostEstimate(flops=2_000_000_000, bytes_accessed=10_000_000, transcendentals=0),
        )
        out, product, sums, *results = results
        if not start:
            gradient, *results = results
        if not last:
            slots, direction = results
        if last:
            early, out = lax.optimization_barrier((early, out))
            gathered, masks = [both], [(0, FIRST)]
            for flip in flips:
                gathered += [early[flip] if value is both and flip in early else flipped(value, flip) for value in gathered]
                masks += [tuple(mask ^ flip for mask in pair) for pair in masks]
            break
        final = iteration == ITERS - 2
        out, remainder, step, solution_ = call(
            functools.partial(owner_kernel, sizes, start, final),
            "owner_final" if final else "owner",
            [exchange(out), entry, precondition, remainder, direction, product] + ([] if start else [solution_]),
            [messages, owned, scalar, kept(3 * CP * sizes.own_rows, LANES) if final else owned],
            [owned_scratch] + factors(spread_rows(CP * PIECES, sizes.own_rows), LANES, entries),
        )
        fields = solution_
    return call(
        functools.partial(final_kernel, sizes, masks),
        "final",
        [exchange(out), product, inverse, gradient, sums] + gathered,
        [shape(CP, CAM_OWN), shape(3, PT_DEV)],
        [pltpu.VMEM((3 * PT_ROWS, LANES), f32)],
        scalars=[run],
    )


def solution(mesh):
    return jax.shard_map(
        lambda *arguments: tuple(body(*arguments)),
        mesh=mesh,
        in_specs=(
            P(None, ("pts", "cams")),
            P(None, ("pts", "cams")),
            P(None, ("pts", "cams")),
            P(("pts", "cams")),
            P(("pts", "cams")),
            P(("pts", "cams"), None, None),
        ),
        out_specs=(P(None, "cams"), P(None, ("pts", "cams"))),
        check_vma=False,
    )
```

```python
import functools

import jax
import jax.numpy as jnp
from jax import lax
from jax.experimental import pallas as pl
from jax.experimental.pallas import tpu as pltpu
from jax.sharding import PartitionSpec as P

CP = 9
CAM_OWN = 8192
PT_DEV = 4096
ITERS = 3
LANES = 128
SUB = 8
PT_ROWS = PT_DEV // LANES
PT_LO = 256
PT_HI = PT_DEV // PT_LO
PIECES = 2
FINE = 3
FAR, NEAR = 4, 2
VMEM_LIMIT = 24 * 1024 * 1024

damping_camera = 1.0
damping_point = 1.0

f32 = jnp.float32
bf16 = jnp.bfloat16


class Sizes:
    def __init__(self, pts, cams, slot, obs):
        self.pts, self.cams, self.slot, self.obs = pts, cams, slot, obs
        self.devices = pts * cams
        self.block = slot // pts
        assert cams * self.block == LANES and LANES % pts == 0
        self.rows = obs // LANES
        self.run = CAM_OWN // pts
        self.run_rows = self.run // LANES
        self.own_rows = max(SUB, self.run_rows)
        self.groups = -(-CP // cams)
        self.first_groups = -(-2 * CP // cams)
        self.message = self.groups
        self.first_message = self.first_groups + 1
        assert self.groups * cams > CP


def sub_iota(rows):
    return lax.broadcasted_iota(jnp.int32, (rows, LANES), 0)


def lane_iota(rows):
    return lax.broadcasted_iota(jnp.int32, (rows, LANES), 1)


def cut(value, pieces=PIECES):
    parts = []
    for _ in range(pieces - 1):
        part = value.astype(bf16).astype(f32)
        parts.append(part)
        value = value - part
    parts.append(value)
    return parts


def swap_blocks(rows, block, wanted):
    which = lane_iota(rows[0].shape[0]) // block
    result = []
    for q in range(wanted):
        total = None
        for c, value in enumerate(rows):
            shift = ((c - q) * block) % LANES
            moved = pltpu.roll(value, shift, axis=1) if shift else value
            total = jnp.where(which == c, moved, 0.0 if total is None else total)
        result.append(total)
    return result


def gather_rows(row, count, high, low, comps):
    result = [None] * comps
    for k in range(count):
        here = high == k
        for c in range(comps):
            source = jnp.broadcast_to(row(c, k), high.shape)
            found = jnp.take_along_axis(source, low, axis=1, mode="promise_in_bounds")
            result[c] = found if k == 0 else jnp.where(here, found, result[c])
    return result


def spread_row(index, parts, high, high_count, spread_ref):
    columns = slice(index * LANES, (index + 1) * LANES)
    mask = jnp.broadcast_to(high, (high_count, LANES)) == sub_iota(high_count)
    together = max(1, 16 // high_count)
    for start in range(0, len(parts), together):
        pieces = [
            jnp.where(mask, jnp.broadcast_to(part, (high_count, LANES)), 0.0)
            for part in parts[start : start + together]
        ]
        while len(pieces) < together:
            pieces.append(jnp.zeros((high_count, LANES), f32))
        tile = pieces[0] if together == 1 else jnp.concatenate(pieces, axis=0)
        spread_ref[start * high_count : start * high_count + tile.shape[0], columns] = tile.astype(bf16)


def place_row(index, low, low_count, place_ref):
    columns = slice(index * LANES, (index + 1) * LANES)
    place = jnp.broadcast_to(low, (low_count, LANES)) == sub_iota(low_count)
    place_ref[:low_count, columns] = jnp.where(place, 1.0, 0.0).astype(bf16)


def keep_parts(parts, group, parts_ref):
    for k, part in enumerate(parts):
        parts_ref[group, k * SUB : (k + 1) * SUB, :] = part


def part_rows(count, group, s, parts_ref):
    return [parts_ref[group, k * SUB + s : k * SUB + s + 1, :] for k in range(count)]


def spread_rows(parts, high_count):
    return -(-parts * high_count // 16) * 16


def scatter(parts, entries, high_count, low_count, spread_ref, place_ref):
    rows = spread_rows(parts, high_count)
    return lax.dot_general(
        spread_ref[:rows, :entries],
        place_ref[:low_count, :entries],
        (((1,), (1,)), ((), ())),
        preferred_element_type=f32,
    )


def joined(result, count, high_count, pieces=None):
    pieces = pieces or [PIECES] * count
    values, first = [], 0
    for number in pieces:
        rows = [result[first + k * high_count : first + (k + 1) * high_count] for k in range(number)]
        first += number * high_count
        total = rows[-1]
        for row in reversed(rows[:-1]):
            total = total + row
        values.append(total)
    return values


def point_gather(ref, point):
    return gather_rows(lambda c, k: ref[c, k : k + 1, :], PT_ROWS, point // LANES, point % LANES, 3)


def narrow(ref, k, value):
    parts = PT_LO // LANES
    for part in range(parts):
        ref[k, pl.ds(part, PT_HI, stride=parts), :] = value[:, part * LANES : (part + 1) * LANES]


def slot_place(slot, sizes):
    within = slot % sizes.slot
    return within % sizes.pts, (slot // sizes.slot) * sizes.block + within // sizes.pts


def solve(inverse, values):
    first = inverse[0] * values[0] + inverse[1] * values[1] + inverse[2] * values[2]
    second = inverse[1] * values[0] + inverse[3] * values[1] + inverse[4] * values[2]
    third = inverse[2] * values[0] + inverse[4] * values[1] + inverse[5] * values[2]
    return first, second, third


def write_messages(fields, scalar, groups, message, out_ref, sizes, extra=None, column=None):
    which = lane_iota(sizes.pts) // sizes.block
    for g in range(groups):
        rows = fields[g * sizes.cams : (g + 1) * sizes.cams]
        moved = swap_partial(rows, sizes)
        for c in range(sizes.cams):
            value = moved[c]
            if g == groups - 1 and scalar is not None:
                value = jnp.where(which == sizes.cams - 1, scalar, value)
            out_ref[pl.ds(c * message + g, sizes.pts, stride=sizes.cams * message), :] = value
    for g in range(groups, message):
        for c in range(sizes.cams):
            value = jnp.where(column == c, extra, 0.0)
            out_ref[pl.ds(c * message + g, sizes.pts, stride=sizes.cams * message), :] = value


def swap_partial(rows, sizes):
    return swap_blocks(rows, sizes.block, sizes.cams)


def read_row(in_ref, c, g, message, sizes):
    return in_ref[pl.ds(c * message + g, sizes.pts, stride=sizes.cams * message), :]


def read_messages(in_ref, count, message, sizes):
    fields = []
    group = 0
    while len(fields) < count:
        rows = [read_row(in_ref, c, group, message, sizes) for c in range(sizes.cams)]
        fields += swap_blocks(rows, sizes.block, min(sizes.cams, count - len(fields)))
        group += 1
    return fields


def read_scalar(in_ref, groups, message, sizes):
    total = read_row(in_ref, 0, groups - 1, message, sizes)
    for c in range(1, sizes.cams):
        total = total + read_row(in_ref, c, groups - 1, message, sizes)
    chosen = jnp.where(lane_iota(sizes.pts) == LANES - 1, total, 0.0)
    return jnp.sum(chosen, keepdims=True)


def own_lists(sizes, list_ref, spread_ref, place_ref):
    pieces = sizes.slot // LANES
    lane = lane_iota(1)
    for c in range(sizes.cams):
        for half in range(pieces):
            value = list_ref[c : c + 1, half * LANES : (half + 1) * LANES]
            low = c * sizes.block + half * (LANES // sizes.pts) + lane // sizes.pts
            parts = [(value >> 8).astype(f32), (value & 255).astype(f32)]
            spread_row(c * pieces + half, parts, lane % sizes.pts, sizes.pts, spread_ref)
            place_row(c * pieces + half, low, LANES, place_ref)
    result = scatter(2, sizes.cams * sizes.slot, sizes.pts, LANES, spread_ref, place_ref)
    return result[: sizes.pts] * 256.0 + result[sizes.pts : 2 * sizes.pts]


def setup_kernel(sizes, run_ref, column_ref, *refs):
    del run_ref
    sources, refs = refs[:6], refs[6:]
    out_ref, a_ref, b_ref, inv_ref, grad_ref, place_point_ref, place_slot_ref, new_slot_ref, new_point_ref = refs[:9]
    refs = refs[9:]
    r_ref, parts_ref, spread_ref, table_ref, place_wide_ref, place_list_ref = refs[:6]
    jac_ref, pjac_ref, res_ref, slot_ref, point_ref, list_ref = refs[6:12]
    semaphores = refs[12]
    rows = sizes.rows
    copies = [
        pltpu.make_async_copy(source, target, semaphores.at[k])
        for k, (source, target) in enumerate(zip(sources, refs[6:12]))
    ]
    for copy in copies:
        copy.start()
    for k in (3, 4, 5):
        copies[k].wait()
    new_slot_ref[...] = slot_ref[...]
    new_point_ref[...] = point_ref[...]
    for row in range(rows):
        place_row(row, point_ref[row : row + 1, :] & (PT_LO - 1), PT_LO, place_wide_ref)
        place_row(row, slot_place(slot_ref[row : row + 1, :], sizes)[1], LANES, place_slot_ref)
    place_point_ref[...] = place_wide_ref[:LANES, :] + place_wide_ref[LANES:, :]
    listed = own_lists(sizes, list_ref, spread_ref, place_list_ref)
    for k in (1, 2):
        copies[k].wait()
    for j in range(rows):
        columns = slice(j * LANES, (j + 1) * LANES)
        b_ref[pl.ds(j, 6, stride=rows), :] = pjac_ref[:, columns]
        r_ref[pl.ds(j, 2, stride=rows), :] = res_ref[:, columns]

    def at(ref, comp, group):
        return ref[comp * rows + group * SUB : comp * rows + (group + 1) * SUB, :]

    normal_pieces = [FINE] * 9

    for group in range(rows // SUB):
        b = [at(b_ref, k, group) for k in range(6)]
        r = [at(r_ref, k, group) for k in range(2)]
        values = [b[i] * b[j] + b[3 + i] * b[3 + j] for i, j in ((0, 0), (0, 1), (0, 2), (1, 1), (1, 2), (2, 2))]
        values += [b[i] * r[0] + b[3 + i] * r[1] for i in range(3)]
        parts = [part for value, pieces in zip(values, normal_pieces) for part in cut(value, pieces)]
        keep_parts(parts, group, parts_ref)
        for s in range(SUB):
            row = group * SUB + s
            high = point_ref[row : row + 1, :] // PT_LO
            spread_row(row, part_rows(len(parts), group, s, parts_ref), high, PT_HI, spread_ref)
    result = scatter(sum(normal_pieces), sizes.obs, PT_HI, PT_LO, spread_ref, place_wide_ref)
    normal = joined(result, 9, PT_HI, normal_pieces)
    top_left = normal[0] + damping_point
    top_mid = normal[1]
    top_right = normal[2]
    mid_mid = normal[3] + damping_point
    mid_right = normal[4]
    low_right = normal[5] + damping_point
    adjugate = [
        mid_mid * low_right - mid_right * mid_right,
        top_right * mid_right - top_mid * low_right,
        top_mid * mid_right - top_right * mid_mid,
        top_left * low_right - top_right * top_right,
        top_mid * top_right - top_left * mid_right,
        top_left * mid_mid - top_mid * top_mid,
    ]
    determinant = top_left * adjugate[0] + top_mid * adjugate[1] + top_right * adjugate[2]
    inverse = [value / determinant for value in adjugate]
    for k in range(6):
        narrow(inv_ref, k, inverse[k])
    for k in range(3):
        narrow(grad_ref, k, normal[6 + k])
    eliminated = solve(inverse, normal[6:])
    for k in range(3):
        narrow(table_ref, k, eliminated[k])
    copies[0].wait()
    for j in range(rows):
        for start in range(0, 2 * CP, SUB):
            size = min(SUB, 2 * CP - start)
            a_ref[pl.ds(start * rows + j, size, stride=rows), :] = jac_ref[
                start : start + size, j * LANES : (j + 1) * LANES
            ]

    for group in range(rows // SUB):
        at_point = point_gather(table_ref, point_ref[group * SUB : (group + 1) * SUB, :])
        b = [at(b_ref, k, group) for k in range(6)]
        errors = [at(r_ref, i, group) - sum(b[3 * i + k] * at_point[k] for k in range(3)) for i in range(2)]
        a = [at(a_ref, k, group) for k in range(2 * CP)]
        values = [a[k] * errors[0] + a[CP + k] * errors[1] for k in range(CP)]
        values += [a[k] * a[k] + a[CP + k] * a[CP + k] for k in range(CP)]
        parts = [part for value in values for part in cut(value)]
        keep_parts(parts, group, parts_ref)
        for s in range(SUB):
            row = group * SUB + s
            high, _ = slot_place(slot_ref[row : row + 1, :], sizes)
            spread_row(row, part_rows(len(parts), group, s, parts_ref), high, sizes.pts, spread_ref)
    result = scatter(2 * CP * PIECES, sizes.obs, sizes.pts, LANES, spread_ref, place_slot_ref)
    fields = joined(result, 2 * CP, sizes.pts)

    write_messages(fields, None, sizes.first_groups, sizes.first_message, out_ref, sizes, extra=listed, column=column_ref[0])


def entries_scatter(fields, entry, sizes, spread_ref, place_ref):
    high, low = entry // LANES, entry % LANES
    parts = [part for value in fields for part in cut(value)]
    for p in range(sizes.pts):
        spread_row(p, [part[p : p + 1] for part in parts], high[p : p + 1], sizes.own_rows, spread_ref)
        place_row(p, low[p : p + 1], LANES, place_ref)
    result = scatter(len(parts), sizes.pts * LANES, sizes.own_rows, LANES, spread_ref, place_ref)
    return joined(result, len(fields), sizes.own_rows)


def send_owned(scaled, partial, entry, out_ref, table_ref, sizes):
    for k in range(CP):
        table_ref[k] = scaled[k]
    fields = gather_rows(lambda c, k: table_ref[c, k : k + 1, :], sizes.run_rows, entry // LANES, entry % LANES, CP)
    write_messages(fields, partial, sizes.groups, sizes.message, out_ref, sizes)


def dot_fields(left, right):
    return jnp.sum(sum(a * b for a, b in zip(left, right)), keepdims=True)


def first_owner_kernel(sizes, in_ref, out_ref, entry_ref, pre_ref, rem_ref,
                       table_ref, spread_ref, place_ref):
    listed = jnp.zeros((sizes.pts, LANES), f32)
    for c in range(sizes.cams):
        listed = listed + read_row(in_ref, c, sizes.first_groups, sizes.first_message, sizes)
    entry = listed.astype(jnp.int32) % sizes.run
    entry_ref[...] = entry
    fields = read_messages(in_ref, 2 * CP, sizes.first_message, sizes)
    sums = entries_scatter(fields, entry, sizes, spread_ref, place_ref)
    remainder = [-value for value in sums[:CP]]
    precondition = [1.0 / (value + damping_camera) for value in sums[CP:]]
    scaled = [p * r for p, r in zip(precondition, remainder)]
    for k in range(CP):
        pre_ref[k] = precondition[k]
        rem_ref[k] = remainder[k]
    send_owned(scaled, dot_fields(remainder, scaled), entry, out_ref, table_ref, sizes)


def owner_kernel(sizes, start, final, in_ref, entry_ref, pre_ref, rem_ref, dir_ref, product_ref, *refs):
    refs = list(refs)
    sol_ref = None if start else refs.pop(0)
    out_ref, new_rem_ref, step_ref, new_sol_ref = refs[:4]
    table_ref, spread_ref, place_ref = refs[-3:]
    entry = entry_ref[...]
    fields = read_messages(in_ref, CP, sizes.message, sizes)
    curvature = read_scalar(in_ref, sizes.groups, sizes.message, sizes)
    step = product_ref[...] / jnp.broadcast_to(curvature, (SUB, LANES))
    step_ref[...] = step
    sums = entries_scatter(fields, entry, sizes, spread_ref, place_ref)
    remainder, scaled = [], []
    for k in range(CP):
        direction = dir_ref[k]
        moved = step[:1] * direction
        moved = moved if start else sol_ref[k] + moved
        if not final:
            new_sol_ref[k] = moved
        value = rem_ref[k] - step[:1] * (sums[k] + damping_camera * direction)
        new_rem_ref[k] = value
        remainder.append(value)
        scaled.append(pre_ref[k] * value)
        if final:
            for j, field in enumerate((moved, direction, scaled[k])):
                first = (j * CP + k) * sizes.own_rows
                new_sol_ref[first : first + sizes.own_rows, :] = field
    send_owned(scaled, dot_fields(remainder, scaled), entry, out_ref, table_ref, sizes)


def schur_kernel(sizes, start, last, in_ref, a_ref, b_ref, inv_ref, slot_ref, point_ref,
                 place_point_ref, place_slot_ref, pre_ref, rem_ref, grad_ref, *refs):
    refs = list(refs)
    if not start:
        product_ref, at_slot_ref, dir_ref, step_ref, sum_ref = refs[:5]
        refs = refs[5:]
    out_ref, new_product_ref, new_sum_ref = refs[:3]
    refs = refs[3:]
    new_grad_ref = None if start else refs.pop(0)
    q_ref, parts_ref, spread_ref, table_ref = refs[-4:]
    new_at_slot_ref, new_dir_ref = (refs[0], None) if last else refs[:2]
    rows = sizes.rows

    def at(ref, comp, group):
        return ref[comp * rows + group * SUB : comp * rows + (group + 1) * SUB, :]

    renewed = jnp.broadcast_to(read_scalar(in_ref, sizes.groups, sizes.message, sizes), (SUB, LANES))
    new_product_ref[...] = renewed
    fields = read_messages(in_ref, CP, sizes.message, sizes)
    beta = None if start else (renewed / product_ref[...])[:1]
    squares = None
    for k in range(CP):
        direction = pre_ref[k] * rem_ref[k]
        if start:
            new_at_slot_ref[k] = fields[k]
        else:
            new_at_slot_ref[k] = fields[k] + beta * at_slot_ref[k]
            direction = direction + beta * dir_ref[k]
        if not last:
            new_dir_ref[k] = direction
        squares = direction * direction if squares is None else squares + direction * direction

    for group in range(rows // SUB):
        high, low = slot_place(slot_ref[group * SUB : (group + 1) * SUB, :], sizes)
        gathered = gather_rows(lambda c, k: new_at_slot_ref[c, k : k + 1, :], sizes.pts, high, low, CP)
        q = [sum(at(a_ref, i * CP + k, group) * gathered[k] for k in range(CP)) for i in range(2)]
        for i in range(2):
            q_ref[i * rows + group * SUB : i * rows + (group + 1) * SUB, :] = q[i]
        values = [at(b_ref, k, group) * q[0] + at(b_ref, 3 + k, group) * q[1] for k in range(3)]
        parts = [part for value in values for part in cut(value, FINE)]
        keep_parts(parts, group, parts_ref)
        for s in range(SUB):
            row = group * SUB + s
            spread_row(row, part_rows(len(parts), group, s, parts_ref), point_ref[row : row + 1, :] // LANES, PT_ROWS, spread_ref)
    result = scatter(3 * FINE, sizes.obs, PT_ROWS, LANES, spread_ref, place_point_ref)
    sums = joined(result, 3, PT_ROWS, [FINE] * 3)
    folded = solve([inv_ref[k] for k in range(6)], sums)
    for k in range(3):
        new_sum_ref[k] = sums[k]
        if not start:
            new_grad_ref[k] = grad_ref[k] + step_ref[:1, :1] * sum_ref[k]

    inner = None
    for k in range(3):
        table_ref[k] = folded[k]
    for group in range(rows // SUB):
        at_point = point_gather(table_ref, point_ref[group * SUB : (group + 1) * SUB, :])
        q = [at(q_ref, i, group) for i in range(2)]
        errors = [q[i] - sum(at(b_ref, 3 * i + k, group) * at_point[k] for k in range(3)) for i in range(2)]
        here = q[0] * errors[0] + q[1] * errors[1]
        inner = here if inner is None else inner + here
        if not last:
            values = [at(a_ref, k, group) * errors[0] + at(a_ref, CP + k, group) * errors[1] for k in range(CP)]
            parts = [part for value in values for part in cut(value)]
            keep_parts(parts, group, parts_ref)
            for s in range(SUB):
                row = group * SUB + s
                high, _ = slot_place(slot_ref[row : row + 1, :], sizes)
                spread_row(row, part_rows(len(parts), group, s, parts_ref), high, sizes.pts, spread_ref)
    partial = jnp.sum(inner, keepdims=True) + damping_camera * jnp.sum(squares, keepdims=True)
    if last:
        out_ref[...] = jnp.broadcast_to(partial, (sizes.devices, LANES))
        return
    result = scatter(CP * PIECES, sizes.obs, sizes.pts, LANES, spread_ref, place_slot_ref)
    fields = joined(result, CP, sizes.pts)
    write_messages(fields, partial, sizes.groups, sizes.message, out_ref, sizes)


def tail_kernel(sizes, in_ref, product_ref, own_ref, far_ref, near_ref, out_ref, far_out_ref):
    renewed = jnp.broadcast_to(read_scalar(in_ref, sizes.groups, sizes.message, sizes), (SUB, LANES))
    beta = (renewed / product_ref[...])[:1]
    field = CP * sizes.own_rows
    for j, ref in enumerate((own_ref, far_ref, near_ref)):
        base = ref[:field, :]
        direction = ref[2 * field :, :] + beta * ref[field : 2 * field, :]
        for target, first in [(out_ref, j * 2 * field)] + ([(far_out_ref, 0)] if ref is far_ref else []):
            target[first : first + field, :] = base
            target[first + field : first + 2 * field, :] = direction


def final_kernel(sizes, masks, run_ref, in_ref, product_ref, inv_ref, grad_ref, sum_ref, *refs):
    all_refs = refs[: len(masks)]
    cam_ref, pt_ref, table_ref, run_out_ref, semaphores = refs[len(masks) :]
    curvature = jnp.sum(jnp.where(lane_iota(sizes.devices) == 0, in_ref[...], 0.0), keepdims=True)
    step = (product_ref[...] / jnp.broadcast_to(curvature, (SUB, LANES)))[:1]
    copies = []
    for all_ref, group in zip(all_refs, masks):
        for j, mask in enumerate(group):
            slot = len(copies)
            for h in range(sizes.run_rows):
                columns = slice(h * LANES, (h + 1) * LANES)
                for start in range(0, CP, SUB):
                    size = min(SUB, CP - start)
                    first = (j * 2 * CP + start) * sizes.own_rows + h
                    base = all_ref[pl.ds(first, size, stride=sizes.own_rows), :]
                    direction = all_ref[pl.ds(first + CP * sizes.own_rows, size, stride=sizes.own_rows), :]
                    run_out_ref[slot, start : start + size, columns] = base + step * direction
            columns = pl.ds(pl.multiple_of((run_ref[0] ^ mask) * sizes.run, LANES), sizes.run)
            copies.append(pltpu.make_async_copy(run_out_ref.at[slot], cam_ref.at[:, columns], semaphores.at[slot]))
            copies[-1].start()
    total = [grad_ref[k] + step[:, :1] * sum_ref[k] for k in range(3)]
    solved = solve([inv_ref[k] for k in range(6)], total)
    for k in range(3):
        table_ref[k * PT_ROWS : (k + 1) * PT_ROWS, :] = -solved[k]
    for row in range(PT_ROWS):
        pt_ref[:, row * LANES : (row + 1) * LANES] = table_ref[pl.ds(row, 3, stride=PT_ROWS), :]
    for copy in copies:
        copy.wait()


def shape(*dims, dtype=f32):
    return jax.ShapeDtypeStruct(dims, dtype)


def kept(*dims, dtype=f32):
    return pltpu.VMEM(dims, dtype)


def call(kernel, name, inputs, outputs, scratch, scalars=(), inputs_at=pltpu.VMEM, outputs_at=None, cost=None):
    given = pl.BlockSpec(memory_space=inputs_at)
    smem = pl.BlockSpec(memory_space=pltpu.SMEM)
    return pl.pallas_call(
        kernel,
        name=name,
        out_shape=outputs,
        in_specs=[smem] * len(scalars) + [given] * len(inputs),
        out_specs=[pl.BlockSpec(memory_space=space) for space in outputs_at or [pltpu.VMEM] * len(outputs)],
        scratch_shapes=scratch,
        cost_estimate=cost,
        compiler_params=pltpu.CompilerParams(vmem_limit_bytes=VMEM_LIMIT),
    )(*scalars, *inputs)


def body(camera_jacobian, point_jacobian, residual, observed_slot, observed_point, send_list):
    sizes = Sizes(lax.axis_size("pts"), lax.axis_size("cams"), send_list.shape[2], camera_jacobian.shape[1])
    axes = ("pts", "cams")
    rows = sizes.rows
    slot = observed_slot.reshape(rows, LANES)
    point = observed_point.reshape(rows, LANES)
    column = lax.axis_index("cams").astype(jnp.int32).reshape(1)
    run = lax.axis_index("pts").astype(jnp.int32).reshape(1)

    def exchange(messages):
        width = messages.size // sizes.devices
        flat = messages.reshape(sizes.devices, 1, width)
        return lax.all_to_all(flat, axes, split_axis=0, concat_axis=0, tiled=True).reshape(messages.shape)

    def flipped(value, flip):
        return lax.ppermute(value, "pts", [(p, p ^ flip) for p in range(sizes.pts)])

    def factors(high_rows, low_rows, entries):
        return [pltpu.VMEM((high_rows, entries), bf16), pltpu.VMEM((low_rows, entries), bf16)]

    point_table = kept(3, PT_ROWS, LANES)
    owned = kept(CP, sizes.own_rows, LANES)
    messages = kept(sizes.devices * sizes.message, LANES)
    scalar = kept(SUB, LANES)
    owned_scratch = pltpu.VMEM((CP, sizes.own_rows, LANES), f32)
    entries = sizes.pts * LANES

    point_scratch = pltpu.VMEM((3, PT_ROWS, LANES), f32)

    def parts_scratch(count):
        return pltpu.VMEM((rows // SUB, count * SUB, LANES), f32)


    given = [
        pltpu.with_memory_space_constraint(value, pltpu.HBM)
        for value in (camera_jacobian, point_jacobian, residual, slot, point, send_list[0])
    ]
    first, a, b, inverse, gradient, place_point, place_slot, slot, point = call(
        functools.partial(setup_kernel, sizes),
        "setup",
        given,
        [
            kept(sizes.devices * sizes.first_message, LANES),
            kept(2 * CP * rows, LANES),
            kept(6 * rows, LANES),
            kept(6, PT_ROWS, LANES),
            point_table,
            kept(LANES, sizes.obs, dtype=bf16),
            kept(LANES, sizes.obs, dtype=bf16),
            kept(rows, LANES, dtype=jnp.int32),
            kept(rows, LANES, dtype=jnp.int32),
        ],
        [pltpu.VMEM((2 * rows, LANES), f32), parts_scratch(2 * CP * PIECES)]
        + [pltpu.VMEM((max(spread_rows(9 * FINE, PT_HI), spread_rows(2 * CP * PIECES, sizes.pts)), sizes.obs), bf16)]
        + [point_scratch, pltpu.VMEM((PT_LO, sizes.obs), bf16), pltpu.VMEM((LANES, sizes.cams * sizes.slot), bf16)]
        + [pltpu.VMEM(value.shape, value.dtype) for value in given]
        + [pltpu.SemaphoreType.DMA((len(given),))],
        scalars=[run, column],
        inputs_at=pl.ANY,
    )
    out, entry, precondition, remainder = call(
        functools.partial(first_owner_kernel, sizes),
        "first_owner",
        [exchange(first)],
        [messages, kept(sizes.pts, LANES, dtype=jnp.int32), owned, owned],
        [owned_scratch] + factors(spread_rows(2 * CP * PIECES, sizes.own_rows), LANES, entries),
    )
    schur_scratch = [pltpu.VMEM((2 * rows, LANES), f32), parts_scratch(CP * PIECES)]
    schur_scratch += [pltpu.VMEM((max(spread_rows(3 * FINE, PT_ROWS), spread_rows(CP * PIECES, sizes.pts)), sizes.obs), bf16)]
    schur_scratch += [point_scratch]
    at_slot = kept(CP, sizes.pts, LANES)
    product = slots = direction = step = sums = solution_ = None
    for iteration in range(ITERS):
        start, last = iteration == 0, iteration == ITERS - 1
        earlier = [] if start else [product, slots, direction, step, sums]
        if last:
            neighbours = [flipped(fields, FAR), flipped(fields, NEAR)]
        arrived = exchange(out)
        if last:
            near_side, far_block = call(
                functools.partial(tail_kernel, sizes),
                "tail",
                [arrived, product, fields] + neighbours,
                [kept(6 * CP * sizes.own_rows, LANES), kept(2 * CP * sizes.own_rows, LANES)],
                [],
            )
            flips = [1 << bit for bit in reversed(range(sizes.pts.bit_length() - 1)) if 1 << bit not in (FAR, NEAR)]
            early = [flipped(far_block, NEAR), flipped(near_side, flips[0])]
        results = call(
            functools.partial(schur_kernel, sizes, start, last),
            "schur_last" if last else "schur",
            [arrived, a, b, inverse, slot, point, place_point, place_slot, precondition, remainder, gradient]
            + earlier,
            [kept(sizes.devices, LANES) if last else messages, scalar, point_table]
            + ([] if start else [point_table])
            + ([] if last else [at_slot, owned]),
            ([pltpu.VMEM((CP, sizes.pts, LANES), f32)] if last else []) + schur_scratch,
            cost=pl.CostEstimate(flops=2_000_000_000, bytes_accessed=10_000_000, transcendentals=0),
        )
        out, product, sums, *results = results
        if not start:
            gradient, *results = results
        if not last:
            slots, direction = results
        if last:
            early[0], out = lax.optimization_barrier((early[0], out))
            gathered, masks = [near_side, early[0]], [(0, FAR, NEAR), (FAR ^ NEAR,)]
            for flip in flips:
                gathered += [
                    early[1] if value is near_side and flip == flips[0] else flipped(value, flip) for value in gathered
                ]
                masks += [tuple(mask ^ flip for mask in group) for group in masks]
            break
        final = iteration == ITERS - 2
        out, remainder, step, solution_ = call(
            functools.partial(owner_kernel, sizes, start, final),
            "owner_final" if final else "owner",
            [exchange(out), entry, precondition, remainder, direction, product] + ([] if start else [solution_]),
            [messages, owned, scalar, kept(3 * CP * sizes.own_rows, LANES) if final else owned],
            [owned_scratch] + factors(spread_rows(CP * PIECES, sizes.own_rows), LANES, entries),
        )
        fields = solution_
    return call(
        functools.partial(final_kernel, sizes, masks),
        "final",
        [exchange(out), product, inverse, gradient, sums] + gathered,
        [shape(CP, CAM_OWN), shape(3, PT_DEV)],
        [
            pltpu.VMEM((3 * PT_ROWS, LANES), f32),
            pltpu.VMEM((sizes.pts, CP, sizes.run), f32),
            pltpu.SemaphoreType.DMA((sizes.pts,)),
        ],
        outputs_at=[pl.ANY, pltpu.VMEM],
        scalars=[run],
    )


def solution(mesh):
    return jax.shard_map(
        lambda *arguments: tuple(body(*arguments)),
        mesh=mesh,
        in_specs=(
            P(None, ("pts", "cams")),
            P(None, ("pts", "cams")),
            P(None, ("pts", "cams")),
            P(("pts", "cams")),
            P(("pts", "cams")),
            P(("pts", "cams"), None, None),
        ),
        out_specs=(P(None, "cams"), P(None, ("pts", "cams"))),
        check_vma=False,
    )
```

```python
import functools

import jax
import jax.numpy as jnp
from jax import lax
from jax.experimental import pallas as pl
from jax.experimental.pallas import tpu as pltpu
from jax.sharding import PartitionSpec as P

CP = 9
CAM_OWN = 8192
PT_DEV = 4096
ITERS = 3
LANES = 128
SUB = 8
PT_ROWS = PT_DEV // LANES
PT_LO = 256
PT_HI = PT_DEV // PT_LO
PIECES = 2
FINE = 3
FAR, NEAR = 4, 2
VMEM_LIMIT = 24 * 1024 * 1024

damping_camera = 1.0
damping_point = 1.0

f32 = jnp.float32
bf16 = jnp.bfloat16


class Sizes:
    def __init__(self, pts, cams, slot, obs):
        self.pts, self.cams, self.slot, self.obs = pts, cams, slot, obs
        self.devices = pts * cams
        self.block = slot // pts
        assert cams * self.block == LANES and LANES % pts == 0
        self.rows = obs // LANES
        self.run = CAM_OWN // pts
        self.run_rows = self.run // LANES
        self.own_rows = max(SUB, self.run_rows)
        self.groups = -(-CP // cams)
        self.first_groups = -(-2 * CP // cams)
        self.message = self.groups
        self.first_message = self.first_groups + 1
        assert self.groups * cams > CP


def sub_iota(rows):
    return lax.broadcasted_iota(jnp.int32, (rows, LANES), 0)


def lane_iota(rows):
    return lax.broadcasted_iota(jnp.int32, (rows, LANES), 1)


def cut(value, pieces=PIECES):
    parts = []
    for _ in range(pieces - 1):
        part = value.astype(bf16).astype(f32)
        parts.append(part)
        value = value - part
    parts.append(value)
    return parts


def swap_blocks(rows, block, wanted):
    which = lane_iota(rows[0].shape[0]) // block
    result = []
    for q in range(wanted):
        total = None
        for c, value in enumerate(rows):
            shift = ((c - q) * block) % LANES
            moved = pltpu.roll(value, shift, axis=1) if shift else value
            total = jnp.where(which == c, moved, 0.0 if total is None else total)
        result.append(total)
    return result


def gather_rows(row, count, high, low, comps):
    result = [None] * comps
    for k in range(count):
        here = high == k
        for c in range(comps):
            source = jnp.broadcast_to(row(c, k), high.shape)
            found = jnp.take_along_axis(source, low, axis=1, mode="promise_in_bounds")
            result[c] = found if k == 0 else jnp.where(here, found, result[c])
    return result


def spread_row(index, parts, high, high_count, spread_ref, base=0):
    columns = slice(index * LANES, (index + 1) * LANES)
    mask = jnp.broadcast_to(high, (high_count, LANES)) == sub_iota(high_count)
    together = max(1, 16 // high_count)
    for start in range(0, len(parts), together):
        pieces = [
            jnp.where(mask, jnp.broadcast_to(part, (high_count, LANES)), 0.0)
            for part in parts[start : start + together]
        ]
        while len(pieces) < together:
            pieces.append(jnp.zeros((high_count, LANES), f32))
        tile = pieces[0] if together == 1 else jnp.concatenate(pieces, axis=0)
        first = base + start * high_count
        spread_ref[first : first + tile.shape[0], columns] = tile.astype(bf16)


def place_row(index, low, low_count, place_ref):
    columns = slice(index * LANES, (index + 1) * LANES)
    place = jnp.broadcast_to(low, (low_count, LANES)) == sub_iota(low_count)
    place_ref[:low_count, columns] = jnp.where(place, 1.0, 0.0).astype(bf16)


def keep_parts(parts, group, parts_ref, base=0):
    for k, part in enumerate(parts, base):
        parts_ref[group, k * SUB : (k + 1) * SUB, :] = part


def part_rows(count, group, s, parts_ref, base=0):
    return [parts_ref[group, k * SUB + s : k * SUB + s + 1, :] for k in range(base, base + count)]


def spread_rows(parts, high_count):
    return -(-parts * high_count // 16) * 16


def scatter(parts, entries, high_count, low_count, spread_ref, place_ref):
    rows = spread_rows(parts, high_count)
    return lax.dot_general(
        spread_ref[:rows, :entries],
        place_ref[:low_count, :entries],
        (((1,), (1,)), ((), ())),
        preferred_element_type=f32,
    )


def joined(result, count, high_count, pieces=None):
    pieces = pieces or [PIECES] * count
    values, first = [], 0
    for number in pieces:
        rows = [result[first + k * high_count : first + (k + 1) * high_count] for k in range(number)]
        first += number * high_count
        total = rows[-1]
        for row in reversed(rows[:-1]):
            total = total + row
        values.append(total)
    return values


def point_gather(ref, point):
    return gather_rows(lambda c, k: ref[c, k : k + 1, :], PT_ROWS, point // LANES, point % LANES, 3)


def narrow(ref, k, value):
    parts = PT_LO // LANES
    for part in range(parts):
        ref[k, pl.ds(part, PT_HI, stride=parts), :] = value[:, part * LANES : (part + 1) * LANES]


def slot_place(slot, sizes):
    within = slot % sizes.slot
    return within % sizes.pts, (slot // sizes.slot) * sizes.block + within // sizes.pts


def solve(inverse, values):
    first = inverse[0] * values[0] + inverse[1] * values[1] + inverse[2] * values[2]
    second = inverse[1] * values[0] + inverse[3] * values[1] + inverse[4] * values[2]
    third = inverse[2] * values[0] + inverse[4] * values[1] + inverse[5] * values[2]
    return first, second, third


def write_messages(fields, scalar, groups, message, out_ref, sizes, extra=None, column=None):
    which = lane_iota(sizes.pts) // sizes.block
    for g in range(groups):
        rows = fields[g * sizes.cams : (g + 1) * sizes.cams]
        moved = swap_partial(rows, sizes)
        for c in range(sizes.cams):
            value = moved[c]
            if g == groups - 1 and scalar is not None:
                value = jnp.where(which == sizes.cams - 1, scalar, value)
            out_ref[pl.ds(c * message + g, sizes.pts, stride=sizes.cams * message), :] = value
    for g in range(groups, message):
        for c in range(sizes.cams):
            value = jnp.where(column == c, extra, 0.0)
            out_ref[pl.ds(c * message + g, sizes.pts, stride=sizes.cams * message), :] = value


def swap_partial(rows, sizes):
    return swap_blocks(rows, sizes.block, sizes.cams)


def read_row(in_ref, c, g, message, sizes):
    return in_ref[pl.ds(c * message + g, sizes.pts, stride=sizes.cams * message), :]


def read_messages(in_ref, count, message, sizes):
    fields = []
    group = 0
    while len(fields) < count:
        rows = [read_row(in_ref, c, group, message, sizes) for c in range(sizes.cams)]
        fields += swap_blocks(rows, sizes.block, min(sizes.cams, count - len(fields)))
        group += 1
    return fields


def read_scalar(in_ref, groups, message, sizes):
    total = read_row(in_ref, 0, groups - 1, message, sizes)
    for c in range(1, sizes.cams):
        total = total + read_row(in_ref, c, groups - 1, message, sizes)
    chosen = jnp.where(lane_iota(sizes.pts) == LANES - 1, total, 0.0)
    return jnp.sum(chosen, keepdims=True)


def setup_kernel(sizes, run_ref, column_ref, *refs):
    del run_ref
    sources, refs = refs[:6], refs[6:]
    out_ref, a_ref, b_ref, inv_ref, grad_ref, place_point_ref, place_slot_ref, new_slot_ref, new_point_ref = refs[:9]
    refs = refs[9:]
    r_ref, parts_ref, spread_ref, table_ref, place_wide_ref, place_list_ref, slot_parts_ref, spread_slot_ref, spread_list_ref = refs[:9]
    jac_ref, pjac_ref, res_ref, slot_ref, point_ref, list_ref = refs[9:15]
    semaphores = refs[15]
    rows = sizes.rows
    copies = [
        pltpu.make_async_copy(source, target, semaphores.at[k])
        for k, (source, target) in enumerate(zip(sources, refs[9:15]))
    ]
    for copy in copies:
        copy.start()
    for k in (1, 2, 4):
        copies[k].wait()
    new_point_ref[...] = point_ref[...]
    for j in range(rows):
        columns = slice(j * LANES, (j + 1) * LANES)
        b_ref[pl.ds(j, 6, stride=rows), :] = pjac_ref[:, columns]
        r_ref[pl.ds(j, 2, stride=rows), :] = res_ref[:, columns]

    def at(ref, comp, group):
        return ref[comp * rows + group * SUB : comp * rows + (group + 1) * SUB, :]

    normal_pieces = [FINE] * 9

    for group in range(rows // SUB):
        b = [at(b_ref, k, group) for k in range(6)]
        r = [at(r_ref, k, group) for k in range(2)]
        values = [b[i] * b[j] + b[3 + i] * b[3 + j] for i, j in ((0, 0), (0, 1), (0, 2), (1, 1), (1, 2), (2, 2))]
        values += [b[i] * r[0] + b[3 + i] * r[1] for i in range(3)]
        parts = [part for value, pieces in zip(values, normal_pieces) for part in cut(value, pieces)]
        keep_parts(parts, group, parts_ref)
        for s in range(SUB):
            row = group * SUB + s
            point = point_ref[row : row + 1, :]
            spread_row(row, part_rows(len(parts), group, s, parts_ref), point >> 8, PT_HI, spread_ref)
            place_row(row, point & (PT_LO - 1), PT_LO, place_wide_ref)
    for k in (0, 3, 5):
        copies[k].wait()
    new_slot_ref[...] = slot_ref[...]
    for j in range(rows):
        for start in range(0, 2 * CP, SUB):
            size = min(SUB, 2 * CP - start)
            a_ref[pl.ds(start * rows + j, size, stride=rows), :] = jac_ref[
                start : start + size, j * LANES : (j + 1) * LANES
            ]

    count = CP * PIECES
    for group in range(rows // SUB):
        a = [at(a_ref, k, group) for k in range(2 * CP)]
        values = [a[k] * a[k] + a[CP + k] * a[CP + k] for k in range(CP)]
        keep_parts([part for value in values for part in cut(value)], group, slot_parts_ref, count)
        for s in range(SUB):
            row = group * SUB + s
            high, low = slot_place(slot_ref[row : row + 1, :], sizes)
            parts = part_rows(count, group, s, slot_parts_ref, count)
            spread_row(row, parts, high, sizes.pts, spread_slot_ref, count * sizes.pts)
            place_row(row, low, LANES, place_slot_ref)

    pieces = sizes.slot // LANES
    lane = lane_iota(1)
    for c in range(sizes.cams):
        for half in range(pieces):
            value = list_ref[c : c + 1, half * LANES : (half + 1) * LANES]
            low = c * sizes.block + half * (LANES // sizes.pts) + lane // sizes.pts
            parts = [(value >> 8).astype(f32), (value & 255).astype(f32)]
            spread_row(c * pieces + half, parts, lane % sizes.pts, sizes.pts, spread_list_ref)
            place_row(c * pieces + half, low, LANES, place_list_ref)
    result = scatter(2, sizes.cams * sizes.slot, sizes.pts, LANES, spread_list_ref, place_list_ref)
    listed = result[: sizes.pts] * 256.0 + result[sizes.pts : 2 * sizes.pts]
    result = scatter(sum(normal_pieces), sizes.obs, PT_HI, PT_LO, spread_ref, place_wide_ref)
    normal = joined(result, 9, PT_HI, normal_pieces)
    top_left = normal[0] + damping_point
    top_mid = normal[1]
    top_right = normal[2]
    mid_mid = normal[3] + damping_point
    mid_right = normal[4]
    low_right = normal[5] + damping_point
    adjugate = [
        mid_mid * low_right - mid_right * mid_right,
        top_right * mid_right - top_mid * low_right,
        top_mid * mid_right - top_right * mid_mid,
        top_left * low_right - top_right * top_right,
        top_mid * top_right - top_left * mid_right,
        top_left * mid_mid - top_mid * top_mid,
    ]
    determinant = top_left * adjugate[0] + top_mid * adjugate[1] + top_right * adjugate[2]
    inverse = [value / determinant for value in adjugate]
    for k in range(6):
        narrow(inv_ref, k, inverse[k])
    for k in range(3):
        narrow(grad_ref, k, normal[6 + k])
    eliminated = solve(inverse, normal[6:])
    for k in range(3):
        narrow(table_ref, k, eliminated[k])
    place_point_ref[...] = place_wide_ref[:LANES, :] + place_wide_ref[LANES:, :]
    for group in range(rows // SUB):
        at_point = point_gather(table_ref, point_ref[group * SUB : (group + 1) * SUB, :])
        b = [at(b_ref, k, group) for k in range(6)]
        errors = [at(r_ref, i, group) - sum(b[3 * i + k] * at_point[k] for k in range(3)) for i in range(2)]
        a = [at(a_ref, k, group) for k in range(2 * CP)]
        values = [a[k] * errors[0] + a[CP + k] * errors[1] for k in range(CP)]
        keep_parts([part for value in values for part in cut(value)], group, slot_parts_ref)
        for s in range(SUB):
            row = group * SUB + s
            high, _ = slot_place(slot_ref[row : row + 1, :], sizes)
            spread_row(row, part_rows(count, group, s, slot_parts_ref), high, sizes.pts, spread_slot_ref)
    result = scatter(2 * count, sizes.obs, sizes.pts, LANES, spread_slot_ref, place_slot_ref)
    fields = joined(result, 2 * CP, sizes.pts)

    write_messages(fields, None, sizes.first_groups, sizes.first_message, out_ref, sizes, extra=listed, column=column_ref[0])


def entries_scatter(fields, entry, sizes, spread_ref, place_ref):
    high, low = entry // LANES, entry % LANES
    parts = [part for value in fields for part in cut(value)]
    for p in range(sizes.pts):
        spread_row(p, [part[p : p + 1] for part in parts], high[p : p + 1], sizes.own_rows, spread_ref)
        place_row(p, low[p : p + 1], LANES, place_ref)
    result = scatter(len(parts), sizes.pts * LANES, sizes.own_rows, LANES, spread_ref, place_ref)
    return joined(result, len(fields), sizes.own_rows)


def send_owned(scaled, partial, entry, out_ref, table_ref, sizes):
    for k in range(CP):
        table_ref[k] = scaled[k]
    fields = gather_rows(lambda c, k: table_ref[c, k : k + 1, :], sizes.run_rows, entry // LANES, entry % LANES, CP)
    write_messages(fields, partial, sizes.groups, sizes.message, out_ref, sizes)


def dot_fields(left, right):
    return jnp.sum(sum(a * b for a, b in zip(left, right)), keepdims=True)


def first_owner_kernel(sizes, in_ref, out_ref, entry_ref, pre_ref, rem_ref,
                       table_ref, spread_ref, place_ref):
    listed = jnp.zeros((sizes.pts, LANES), f32)
    for c in range(sizes.cams):
        listed = listed + read_row(in_ref, c, sizes.first_groups, sizes.first_message, sizes)
    entry = listed.astype(jnp.int32) % sizes.run
    entry_ref[...] = entry
    fields = read_messages(in_ref, 2 * CP, sizes.first_message, sizes)
    sums = entries_scatter(fields, entry, sizes, spread_ref, place_ref)
    remainder = [-value for value in sums[:CP]]
    precondition = [1.0 / (value + damping_camera) for value in sums[CP:]]
    scaled = [p * r for p, r in zip(precondition, remainder)]
    for k in range(CP):
        pre_ref[k] = precondition[k]
        rem_ref[k] = remainder[k]
    send_owned(scaled, dot_fields(remainder, scaled), entry, out_ref, table_ref, sizes)


def owner_kernel(sizes, start, final, in_ref, entry_ref, pre_ref, rem_ref, dir_ref, product_ref, *refs):
    refs = list(refs)
    sol_ref = None if start else refs.pop(0)
    out_ref, new_rem_ref, step_ref, new_sol_ref = refs[:4]
    table_ref, spread_ref, place_ref = refs[-3:]
    entry = entry_ref[...]
    fields = read_messages(in_ref, CP, sizes.message, sizes)
    curvature = read_scalar(in_ref, sizes.groups, sizes.message, sizes)
    step = product_ref[...] / jnp.broadcast_to(curvature, (SUB, LANES))
    step_ref[...] = step
    sums = entries_scatter(fields, entry, sizes, spread_ref, place_ref)
    remainder, scaled = [], []
    for k in range(CP):
        direction = dir_ref[k]
        moved = step[:1] * direction
        moved = moved if start else sol_ref[k] + moved
        if not final:
            new_sol_ref[k] = moved
        value = rem_ref[k] - step[:1] * (sums[k] + damping_camera * direction)
        new_rem_ref[k] = value
        remainder.append(value)
        scaled.append(pre_ref[k] * value)
        if final:
            for j, field in enumerate((moved, direction, scaled[k])):
                first = (j * CP + k) * sizes.own_rows
                new_sol_ref[first : first + sizes.own_rows, :] = field
    send_owned(scaled, dot_fields(remainder, scaled), entry, out_ref, table_ref, sizes)


def schur_kernel(sizes, start, last, in_ref, a_ref, b_ref, inv_ref, slot_ref, point_ref,
                 place_point_ref, place_slot_ref, pre_ref, rem_ref, grad_ref, *refs):
    refs = list(refs)
    if not start:
        product_ref, at_slot_ref, dir_ref, step_ref, sum_ref = refs[:5]
        refs = refs[5:]
    out_ref, new_product_ref, new_sum_ref = refs[:3]
    refs = refs[3:]
    new_grad_ref = None if start else refs.pop(0)
    q_ref, parts_ref, spread_ref, table_ref = refs[-4:]
    new_at_slot_ref, new_dir_ref = (refs[0], None) if last else refs[:2]
    rows = sizes.rows

    def at(ref, comp, group):
        return ref[comp * rows + group * SUB : comp * rows + (group + 1) * SUB, :]

    renewed = jnp.broadcast_to(read_scalar(in_ref, sizes.groups, sizes.message, sizes), (SUB, LANES))
    new_product_ref[...] = renewed
    fields = read_messages(in_ref, CP, sizes.message, sizes)
    beta = None if start else (renewed / product_ref[...])[:1]
    squares = None
    for k in range(CP):
        direction = pre_ref[k] * rem_ref[k]
        if start:
            new_at_slot_ref[k] = fields[k]
        else:
            new_at_slot_ref[k] = fields[k] + beta * at_slot_ref[k]
            direction = direction + beta * dir_ref[k]
        if not last:
            new_dir_ref[k] = direction
        squares = direction * direction if squares is None else squares + direction * direction

    for group in range(rows // SUB):
        high, low = slot_place(slot_ref[group * SUB : (group + 1) * SUB, :], sizes)
        gathered = gather_rows(lambda c, k: new_at_slot_ref[c, k : k + 1, :], sizes.pts, high, low, CP)
        q = [sum(at(a_ref, i * CP + k, group) * gathered[k] for k in range(CP)) for i in range(2)]
        for i in range(2):
            q_ref[i * rows + group * SUB : i * rows + (group + 1) * SUB, :] = q[i]
        values = [at(b_ref, k, group) * q[0] + at(b_ref, 3 + k, group) * q[1] for k in range(3)]
        parts = [part for value in values for part in cut(value, FINE)]
        keep_parts(parts, group, parts_ref)
        for s in range(SUB):
            row = group * SUB + s
            spread_row(row, part_rows(len(parts), group, s, parts_ref), point_ref[row : row + 1, :] // LANES, PT_ROWS, spread_ref)
    result = scatter(3 * FINE, sizes.obs, PT_ROWS, LANES, spread_ref, place_point_ref)
    sums = joined(result, 3, PT_ROWS, [FINE] * 3)
    folded = solve([inv_ref[k] for k in range(6)], sums)
    for k in range(3):
        new_sum_ref[k] = sums[k]
        if not start:
            new_grad_ref[k] = grad_ref[k] + step_ref[:1, :1] * sum_ref[k]

    inner = None
    for k in range(3):
        table_ref[k] = folded[k]
    for group in range(rows // SUB):
        at_point = point_gather(table_ref, point_ref[group * SUB : (group + 1) * SUB, :])
        q = [at(q_ref, i, group) for i in range(2)]
        errors = [q[i] - sum(at(b_ref, 3 * i + k, group) * at_point[k] for k in range(3)) for i in range(2)]
        here = q[0] * errors[0] + q[1] * errors[1]
        inner = here if inner is None else inner + here
        if not last:
            values = [at(a_ref, k, group) * errors[0] + at(a_ref, CP + k, group) * errors[1] for k in range(CP)]
            parts = [part for value in values for part in cut(value)]
            keep_parts(parts, group, parts_ref)
            for s in range(SUB):
                row = group * SUB + s
                high, _ = slot_place(slot_ref[row : row + 1, :], sizes)
                spread_row(row, part_rows(len(parts), group, s, parts_ref), high, sizes.pts, spread_ref)
    partial = jnp.sum(inner, keepdims=True) + damping_camera * jnp.sum(squares, keepdims=True)
    if last:
        out_ref[...] = jnp.broadcast_to(partial, (sizes.devices, LANES))
        return
    result = scatter(CP * PIECES, sizes.obs, sizes.pts, LANES, spread_ref, place_slot_ref)
    fields = joined(result, CP, sizes.pts)
    write_messages(fields, partial, sizes.groups, sizes.message, out_ref, sizes)


def tail_kernel(sizes, in_ref, product_ref, own_ref, far_ref, near_ref, out_ref, far_out_ref):
    renewed = jnp.broadcast_to(read_scalar(in_ref, sizes.groups, sizes.message, sizes), (SUB, LANES))
    beta = (renewed / product_ref[...])[:1]
    field = CP * sizes.own_rows
    for j, ref in enumerate((own_ref, far_ref, near_ref)):
        base = ref[:field, :]
        direction = ref[2 * field :, :] + beta * ref[field : 2 * field, :]
        for target, first in [(out_ref, j * 2 * field)] + ([(far_out_ref, 0)] if ref is far_ref else []):
            target[first : first + field, :] = base
            target[first + field : first + 2 * field, :] = direction


def final_kernel(sizes, masks, run_ref, in_ref, product_ref, inv_ref, grad_ref, sum_ref, *refs):
    all_refs = refs[: len(masks)]
    cam_ref, pt_ref, table_ref = refs[len(masks) :]
    curvature = jnp.sum(jnp.where(lane_iota(sizes.devices) == 0, in_ref[...], 0.0), keepdims=True)
    step = (product_ref[...] / jnp.broadcast_to(curvature, (SUB, LANES)))[:1]
    for all_ref, pair in zip(all_refs, masks):
        for j, mask in enumerate(pair):
            base_column = (run_ref[0] ^ mask) * sizes.run
            for h in range(sizes.run_rows):
                columns = pl.ds(pl.multiple_of(base_column + h * LANES, LANES), LANES)
                for start in range(0, CP, SUB):
                    size = min(SUB, CP - start)
                    first = (j * 2 * CP + start) * sizes.own_rows + h
                    base = all_ref[pl.ds(first, size, stride=sizes.own_rows), :]
                    direction = all_ref[pl.ds(first + CP * sizes.own_rows, size, stride=sizes.own_rows), :]
                    cam_ref[start : start + size, columns] = base + step * direction
    total = [grad_ref[k] + step[:, :1] * sum_ref[k] for k in range(3)]
    solved = solve([inv_ref[k] for k in range(6)], total)
    for k in range(3):
        table_ref[k * PT_ROWS : (k + 1) * PT_ROWS, :] = -solved[k]
    for row in range(PT_ROWS):
        pt_ref[:, row * LANES : (row + 1) * LANES] = table_ref[pl.ds(row, 3, stride=PT_ROWS), :]


def shape(*dims, dtype=f32):
    return jax.ShapeDtypeStruct(dims, dtype)


def kept(*dims, dtype=f32):
    return pltpu.VMEM(dims, dtype)


def call(kernel, name, inputs, outputs, scratch, scalars=(), inputs_at=pltpu.VMEM, cost=None):
    vmem = pl.BlockSpec(memory_space=pltpu.VMEM)
    given = pl.BlockSpec(memory_space=inputs_at)
    smem = pl.BlockSpec(memory_space=pltpu.SMEM)
    return pl.pallas_call(
        kernel,
        name=name,
        out_shape=outputs,
        in_specs=[smem] * len(scalars) + [given] * len(inputs),
        out_specs=[vmem] * len(outputs),
        scratch_shapes=scratch,
        cost_estimate=cost,
        compiler_params=pltpu.CompilerParams(vmem_limit_bytes=VMEM_LIMIT),
    )(*scalars, *inputs)


def body(camera_jacobian, point_jacobian, residual, observed_slot, observed_point, send_list):
    sizes = Sizes(lax.axis_size("pts"), lax.axis_size("cams"), send_list.shape[2], camera_jacobian.shape[1])
    axes = ("pts", "cams")
    rows = sizes.rows
    slot = observed_slot.reshape(rows, LANES)
    point = observed_point.reshape(rows, LANES)
    column = lax.axis_index("cams").astype(jnp.int32).reshape(1)
    run = lax.axis_index("pts").astype(jnp.int32).reshape(1)

    def exchange(messages):
        width = messages.size // sizes.devices
        flat = messages.reshape(sizes.devices, 1, width)
        return lax.all_to_all(flat, axes, split_axis=0, concat_axis=0, tiled=True).reshape(messages.shape)

    def flipped(value, flip):
        return lax.ppermute(value, "pts", [(p, p ^ flip) for p in range(sizes.pts)])

    def factors(high_rows, low_rows, entries):
        return [pltpu.VMEM((high_rows, entries), bf16), pltpu.VMEM((low_rows, entries), bf16)]

    point_table = kept(3, PT_ROWS, LANES)
    owned = kept(CP, sizes.own_rows, LANES)
    messages = kept(sizes.devices * sizes.message, LANES)
    scalar = kept(SUB, LANES)
    owned_scratch = pltpu.VMEM((CP, sizes.own_rows, LANES), f32)
    entries = sizes.pts * LANES

    point_scratch = pltpu.VMEM((3, PT_ROWS, LANES), f32)

    def parts_scratch(count):
        return pltpu.VMEM((rows // SUB, count * SUB, LANES), f32)


    given = [
        pltpu.with_memory_space_constraint(value, pltpu.HBM)
        for value in (camera_jacobian, point_jacobian, residual, slot, point, send_list[0])
    ]
    first, a, b, inverse, gradient, place_point, place_slot, slot, point = call(
        functools.partial(setup_kernel, sizes),
        "setup",
        given,
        [
            kept(sizes.devices * sizes.first_message, LANES),
            kept(2 * CP * rows, LANES),
            kept(6 * rows, LANES),
            kept(6, PT_ROWS, LANES),
            point_table,
            kept(LANES, sizes.obs, dtype=bf16),
            kept(LANES, sizes.obs, dtype=bf16),
            kept(rows, LANES, dtype=jnp.int32),
            kept(rows, LANES, dtype=jnp.int32),
        ],
        [pltpu.VMEM((2 * rows, LANES), f32), parts_scratch(9 * FINE)]
        + [pltpu.VMEM((spread_rows(9 * FINE, PT_HI), sizes.obs), bf16)]
        + [point_scratch, pltpu.VMEM((PT_LO, sizes.obs), bf16), pltpu.VMEM((LANES, sizes.cams * sizes.slot), bf16)]
        + [parts_scratch(2 * CP * PIECES), pltpu.VMEM((spread_rows(2 * CP * PIECES, sizes.pts), sizes.obs), bf16)]
        + [pltpu.VMEM((spread_rows(2, sizes.pts), sizes.cams * sizes.slot), bf16)]
        + [pltpu.VMEM(value.shape, value.dtype) for value in given]
        + [pltpu.SemaphoreType.DMA((len(given),))],
        scalars=[run, column],
        inputs_at=pl.ANY,
    )
    out, entry, precondition, remainder = call(
        functools.partial(first_owner_kernel, sizes),
        "first_owner",
        [exchange(first)],
        [messages, kept(sizes.pts, LANES, dtype=jnp.int32), owned, owned],
        [owned_scratch] + factors(spread_rows(2 * CP * PIECES, sizes.own_rows), LANES, entries),
    )
    schur_scratch = [pltpu.VMEM((2 * rows, LANES), f32), parts_scratch(CP * PIECES)]
    schur_scratch += [pltpu.VMEM((max(spread_rows(3 * FINE, PT_ROWS), spread_rows(CP * PIECES, sizes.pts)), sizes.obs), bf16)]
    schur_scratch += [point_scratch]
    at_slot = kept(CP, sizes.pts, LANES)
    product = slots = direction = step = sums = solution_ = None
    for iteration in range(ITERS):
        start, last = iteration == 0, iteration == ITERS - 1
        earlier = [] if start else [product, slots, direction, step, sums]
        if last:
            neighbours = [flipped(fields, FAR), flipped(fields, NEAR)]
        arrived = exchange(out)
        if last:
            near_side, far_block = call(
                functools.partial(tail_kernel, sizes),
                "tail",
                [arrived, product, fields] + neighbours,
                [kept(6 * CP * sizes.own_rows, LANES), kept(2 * CP * sizes.own_rows, LANES)],
                [],
            )
            flips = [1 << bit for bit in reversed(range(sizes.pts.bit_length() - 1)) if 1 << bit not in (FAR, NEAR)]
            early = [flipped(far_block, NEAR), flipped(near_side, flips[0])]
        results = call(
            functools.partial(schur_kernel, sizes, start, last),
            "schur_last" if last else "schur",
            [arrived, a, b, inverse, slot, point, place_point, place_slot, precondition, remainder, gradient]
            + earlier,
            [kept(sizes.devices, LANES) if last else messages, scalar, point_table]
            + ([] if start else [point_table])
            + ([] if last else [at_slot, owned]),
            ([pltpu.VMEM((CP, sizes.pts, LANES), f32)] if last else []) + schur_scratch,
            cost=pl.CostEstimate(flops=2_000_000_000, bytes_accessed=10_000_000, transcendentals=0),
        )
        out, product, sums, *results = results
        if not start:
            gradient, *results = results
        if not last:
            slots, direction = results
        if last:
            early[0], out = lax.optimization_barrier((early[0], out))
            gathered, masks = [near_side, early[0]], [(0, FAR, NEAR), (FAR ^ NEAR,)]
            for flip in flips:
                gathered += [
                    early[1] if value is near_side and flip == flips[0] else flipped(value, flip) for value in gathered
                ]
                masks += [tuple(mask ^ flip for mask in group) for group in masks]
            break
        final = iteration == ITERS - 2
        out, remainder, step, solution_ = call(
            functools.partial(owner_kernel, sizes, start, final),
            "owner_final" if final else "owner",
            [exchange(out), entry, precondition, remainder, direction, product] + ([] if start else [solution_]),
            [messages, owned, scalar, kept(3 * CP * sizes.own_rows, LANES) if final else owned],
            [owned_scratch] + factors(spread_rows(CP * PIECES, sizes.own_rows), LANES, entries),
        )
        fields = solution_
    return call(
        functools.partial(final_kernel, sizes, masks),
        "final",
        [exchange(out), product, inverse, gradient, sums] + gathered,
        [shape(CP, CAM_OWN), shape(3, PT_DEV)],
        [pltpu.VMEM((3 * PT_ROWS, LANES), f32)],
        scalars=[run],
    )


def solution(mesh):
    return jax.shard_map(
        lambda *arguments: tuple(body(*arguments)),
        mesh=mesh,
        in_specs=(
            P(None, ("pts", "cams")),
            P(None, ("pts", "cams")),
            P(None, ("pts", "cams")),
            P(("pts", "cams")),
            P(("pts", "cams")),
            P(("pts", "cams"), None, None),
        ),
        out_specs=(P(None, "cams"), P(None, ("pts", "cams"))),
        check_vma=False,
    )
```

```python
import functools

import jax
import jax.numpy as jnp
from jax import lax
from jax.experimental import pallas as pl
from jax.experimental.pallas import tpu as pltpu
from jax.sharding import PartitionSpec as P

CP = 9
CAM_OWN = 8192
PT_DEV = 4096
ITERS = 3
LANES = 128
SUB = 8
PT_ROWS = PT_DEV // LANES
PT_LO = 256
PT_HI = PT_DEV // PT_LO
PIECES = 2
FINE = 3
FAR, NEAR = 4, 2
VMEM_LIMIT = 24 * 1024 * 1024

damping_camera = 1.0
damping_point = 1.0

f32 = jnp.float32
bf16 = jnp.bfloat16


class Sizes:
    def __init__(self, pts, cams, slot, obs):
        self.pts, self.cams, self.slot, self.obs = pts, cams, slot, obs
        self.devices = pts * cams
        self.block = slot // pts
        assert cams * self.block == LANES and LANES % pts == 0
        self.rows = obs // LANES
        self.run = CAM_OWN // pts
        self.run_rows = self.run // LANES
        self.own_rows = max(SUB, self.run_rows)
        self.groups = -(-CP // cams)
        self.first_groups = -(-2 * CP // cams)
        self.message = self.groups
        self.first_message = self.first_groups + 1
        assert self.groups * cams > CP


def sub_iota(rows):
    return lax.broadcasted_iota(jnp.int32, (rows, LANES), 0)


def lane_iota(rows):
    return lax.broadcasted_iota(jnp.int32, (rows, LANES), 1)


def cut(value, pieces=PIECES):
    parts = []
    for _ in range(pieces - 1):
        part = value.astype(bf16).astype(f32)
        parts.append(part)
        value = value - part
    parts.append(value)
    return parts


def swap_blocks(rows, block, wanted):
    which = lane_iota(rows[0].shape[0]) // block
    result = []
    for q in range(wanted):
        total = None
        for c, value in enumerate(rows):
            shift = ((c - q) * block) % LANES
            moved = pltpu.roll(value, shift, axis=1) if shift else value
            total = jnp.where(which == c, moved, 0.0 if total is None else total)
        result.append(total)
    return result


def gather_rows(row, count, high, low, comps):
    result = [None] * comps
    for k in range(count):
        here = high == k
        for c in range(comps):
            source = jnp.broadcast_to(row(c, k), high.shape)
            found = jnp.take_along_axis(source, low, axis=1, mode="promise_in_bounds")
            result[c] = found if k == 0 else jnp.where(here, found, result[c])
    return result


def spread_row(index, parts, high, high_count, spread_ref):
    columns = slice(index * LANES, (index + 1) * LANES)
    mask = jnp.broadcast_to(high, (high_count, LANES)) == sub_iota(high_count)
    together = max(1, 16 // high_count)
    for start in range(0, len(parts), together):
        pieces = [
            jnp.where(mask, jnp.broadcast_to(part, (high_count, LANES)), 0.0)
            for part in parts[start : start + together]
        ]
        while len(pieces) < together:
            pieces.append(jnp.zeros((high_count, LANES), f32))
        tile = pieces[0] if together == 1 else jnp.concatenate(pieces, axis=0)
        spread_ref[start * high_count : start * high_count + tile.shape[0], columns] = tile.astype(bf16)


def place_row(index, low, low_count, place_ref):
    columns = slice(index * LANES, (index + 1) * LANES)
    place = jnp.broadcast_to(low, (low_count, LANES)) == sub_iota(low_count)
    place_ref[:low_count, columns] = jnp.where(place, 1.0, 0.0).astype(bf16)


def keep_parts(parts, group, parts_ref):
    for k, part in enumerate(parts):
        parts_ref[group, k * SUB : (k + 1) * SUB, :] = part


def part_rows(count, group, s, parts_ref):
    return [parts_ref[group, k * SUB + s : k * SUB + s + 1, :] for k in range(count)]


def spread_rows(parts, high_count):
    return -(-parts * high_count // 16) * 16


def scatter(parts, entries, high_count, low_count, spread_ref, place_ref):
    rows = spread_rows(parts, high_count)
    return lax.dot_general(
        spread_ref[:rows, :entries],
        place_ref[:low_count, :entries],
        (((1,), (1,)), ((), ())),
        preferred_element_type=f32,
    )


def joined(result, count, high_count, pieces=None):
    pieces = pieces or [PIECES] * count
    values, first = [], 0
    for number in pieces:
        rows = [result[first + k * high_count : first + (k + 1) * high_count] for k in range(number)]
        first += number * high_count
        total = rows[-1]
        for row in reversed(rows[:-1]):
            total = total + row
        values.append(total)
    return values


def point_gather(ref, point):
    return gather_rows(lambda c, k: ref[c, k : k + 1, :], PT_ROWS, point // LANES, point % LANES, 3)


def narrow(ref, k, value):
    parts = PT_LO // LANES
    for part in range(parts):
        ref[k, pl.ds(part, PT_HI, stride=parts), :] = value[:, part * LANES : (part + 1) * LANES]


def slot_place(slot, sizes):
    within = slot % sizes.slot
    return within % sizes.pts, (slot // sizes.slot) * sizes.block + within // sizes.pts


def solve(inverse, values):
    first = inverse[0] * values[0] + inverse[1] * values[1] + inverse[2] * values[2]
    second = inverse[1] * values[0] + inverse[3] * values[1] + inverse[4] * values[2]
    third = inverse[2] * values[0] + inverse[4] * values[1] + inverse[5] * values[2]
    return first, second, third


def write_messages(fields, scalar, groups, message, out_ref, sizes, extra=None, column=None):
    which = lane_iota(sizes.pts) // sizes.block
    for g in range(groups):
        rows = fields[g * sizes.cams : (g + 1) * sizes.cams]
        moved = swap_partial(rows, sizes)
        for c in range(sizes.cams):
            value = moved[c]
            if g == groups - 1 and scalar is not None:
                value = jnp.where(which == sizes.cams - 1, scalar, value)
            out_ref[pl.ds(c * message + g, sizes.pts, stride=sizes.cams * message), :] = value
    for g in range(groups, message):
        for c in range(sizes.cams):
            value = jnp.where(column == c, extra, 0.0)
            out_ref[pl.ds(c * message + g, sizes.pts, stride=sizes.cams * message), :] = value


def swap_partial(rows, sizes):
    return swap_blocks(rows, sizes.block, sizes.cams)


def read_row(in_ref, c, g, message, sizes):
    return in_ref[pl.ds(c * message + g, sizes.pts, stride=sizes.cams * message), :]


def read_messages(in_ref, count, message, sizes):
    fields = []
    group = 0
    while len(fields) < count:
        rows = [read_row(in_ref, c, group, message, sizes) for c in range(sizes.cams)]
        fields += swap_blocks(rows, sizes.block, min(sizes.cams, count - len(fields)))
        group += 1
    return fields


def read_scalar(in_ref, groups, message, sizes):
    total = read_row(in_ref, 0, groups - 1, message, sizes)
    for c in range(1, sizes.cams):
        total = total + read_row(in_ref, c, groups - 1, message, sizes)
    chosen = jnp.where(lane_iota(sizes.pts) == LANES - 1, total, 0.0)
    return jnp.sum(chosen, keepdims=True)


def setup_kernel(sizes, run_ref, column_ref, *refs):
    del run_ref
    sources, refs = refs[:6], refs[6:]
    out_ref, a_ref, b_ref, inv_ref, grad_ref, place_point_ref, place_slot_ref, new_slot_ref, new_point_ref = refs[:9]
    refs = refs[9:]
    r_ref, parts_ref, spread_ref, table_ref, place_wide_ref, place_list_ref, spread_list_ref = refs[:7]
    jac_ref, pjac_ref, res_ref, slot_ref, point_ref, list_ref = refs[7:13]
    semaphores = refs[13]
    rows = sizes.rows
    copies = [
        pltpu.make_async_copy(source, target, semaphores.at[k])
        for k, (source, target) in enumerate(zip(sources, refs[7:13]))
    ]
    for copy in copies:
        copy.start()
    for k in (1, 2, 4):
        copies[k].wait()
    new_point_ref[...] = point_ref[...]
    for j in range(rows):
        columns = slice(j * LANES, (j + 1) * LANES)
        b_ref[pl.ds(j, 6, stride=rows), :] = pjac_ref[:, columns]
        r_ref[pl.ds(j, 2, stride=rows), :] = res_ref[:, columns]

    def at(ref, comp, group):
        return ref[comp * rows + group * SUB : comp * rows + (group + 1) * SUB, :]

    normal_pieces = [FINE] * 9

    for group in range(rows // SUB):
        b = [at(b_ref, k, group) for k in range(6)]
        r = [at(r_ref, k, group) for k in range(2)]
        values = [b[i] * b[j] + b[3 + i] * b[3 + j] for i, j in ((0, 0), (0, 1), (0, 2), (1, 1), (1, 2), (2, 2))]
        values += [b[i] * r[0] + b[3 + i] * r[1] for i in range(3)]
        parts = [part for value, pieces in zip(values, normal_pieces) for part in cut(value, pieces)]
        keep_parts(parts, group, parts_ref)
        for s in range(SUB):
            row = group * SUB + s
            point = point_ref[row : row + 1, :]
            spread_row(row, part_rows(len(parts), group, s, parts_ref), point >> 8, PT_HI, spread_ref)
            place_row(row, point & (PT_LO - 1), PT_LO, place_wide_ref)
    result = scatter(sum(normal_pieces), sizes.obs, PT_HI, PT_LO, spread_ref, place_wide_ref)
    normal = joined(result, 9, PT_HI, normal_pieces)
    top_left = normal[0] + damping_point
    top_mid = normal[1]
    top_right = normal[2]
    mid_mid = normal[3] + damping_point
    mid_right = normal[4]
    low_right = normal[5] + damping_point
    adjugate = [
        mid_mid * low_right - mid_right * mid_right,
        top_right * mid_right - top_mid * low_right,
        top_mid * mid_right - top_right * mid_mid,
        top_left * low_right - top_right * top_right,
        top_mid * top_right - top_left * mid_right,
        top_left * mid_mid - top_mid * top_mid,
    ]
    determinant = top_left * adjugate[0] + top_mid * adjugate[1] + top_right * adjugate[2]
    inverse = [value / determinant for value in adjugate]
    for k in range(6):
        narrow(inv_ref, k, inverse[k])
    for k in range(3):
        narrow(grad_ref, k, normal[6 + k])
    eliminated = solve(inverse, normal[6:])
    for k in range(3):
        narrow(table_ref, k, eliminated[k])
    place_point_ref[...] = place_wide_ref[:LANES, :] + place_wide_ref[LANES:, :]
    for k in (0, 3, 5):
        copies[k].wait()
    new_slot_ref[...] = slot_ref[...]
    for j in range(rows):
        for start in range(0, 2 * CP, SUB):
            size = min(SUB, 2 * CP - start)
            a_ref[pl.ds(start * rows + j, size, stride=rows), :] = jac_ref[
                start : start + size, j * LANES : (j + 1) * LANES
            ]

    for group in range(rows // SUB):
        at_point = point_gather(table_ref, point_ref[group * SUB : (group + 1) * SUB, :])
        b = [at(b_ref, k, group) for k in range(6)]
        errors = [at(r_ref, i, group) - sum(b[3 * i + k] * at_point[k] for k in range(3)) for i in range(2)]
        a = [at(a_ref, k, group) for k in range(2 * CP)]
        values = [a[k] * errors[0] + a[CP + k] * errors[1] for k in range(CP)]
        values += [a[k] * a[k] + a[CP + k] * a[CP + k] for k in range(CP)]
        parts = [part for value in values for part in cut(value)]
        keep_parts(parts, group, parts_ref)
        for s in range(SUB):
            row = group * SUB + s
            high, low = slot_place(slot_ref[row : row + 1, :], sizes)
            spread_row(row, part_rows(len(parts), group, s, parts_ref), high, sizes.pts, spread_ref)
            place_row(row, low, LANES, place_slot_ref)
    result = scatter(2 * CP * PIECES, sizes.obs, sizes.pts, LANES, spread_ref, place_slot_ref)
    fields = joined(result, 2 * CP, sizes.pts)

    pieces = sizes.slot // LANES
    lane = lane_iota(1)
    for c in range(sizes.cams):
        for half in range(pieces):
            value = list_ref[c : c + 1, half * LANES : (half + 1) * LANES]
            low = c * sizes.block + half * (LANES // sizes.pts) + lane // sizes.pts
            parts = [(value >> 8).astype(f32), (value & 255).astype(f32)]
            spread_row(c * pieces + half, parts, lane % sizes.pts, sizes.pts, spread_list_ref)
            place_row(c * pieces + half, low, LANES, place_list_ref)
    result = scatter(2, sizes.cams * sizes.slot, sizes.pts, LANES, spread_list_ref, place_list_ref)
    listed = result[: sizes.pts] * 256.0 + result[sizes.pts : 2 * sizes.pts]
    write_messages(fields, None, sizes.first_groups, sizes.first_message, out_ref, sizes, extra=listed, column=column_ref[0])


def entries_scatter(fields, entry, sizes, spread_ref, place_ref):
    high, low = entry // LANES, entry % LANES
    parts = [part for value in fields for part in cut(value)]
    for p in range(sizes.pts):
        spread_row(p, [part[p : p + 1] for part in parts], high[p : p + 1], sizes.own_rows, spread_ref)
        place_row(p, low[p : p + 1], LANES, place_ref)
    result = scatter(len(parts), sizes.pts * LANES, sizes.own_rows, LANES, spread_ref, place_ref)
    return joined(result, len(fields), sizes.own_rows)


def send_owned(scaled, partial, entry, out_ref, table_ref, sizes):
    for k in range(CP):
        table_ref[k] = scaled[k]
    fields = gather_rows(lambda c, k: table_ref[c, k : k + 1, :], sizes.run_rows, entry // LANES, entry % LANES, CP)
    write_messages(fields, partial, sizes.groups, sizes.message, out_ref, sizes)


def dot_fields(left, right):
    return jnp.sum(sum(a * b for a, b in zip(left, right)), keepdims=True)


def first_owner_kernel(sizes, in_ref, out_ref, entry_ref, pre_ref, rem_ref,
                       table_ref, spread_ref, place_ref):
    listed = jnp.zeros((sizes.pts, LANES), f32)
    for c in range(sizes.cams):
        listed = listed + read_row(in_ref, c, sizes.first_groups, sizes.first_message, sizes)
    entry = listed.astype(jnp.int32) % sizes.run
    entry_ref[...] = entry
    fields = read_messages(in_ref, 2 * CP, sizes.first_message, sizes)
    sums = entries_scatter(fields, entry, sizes, spread_ref, place_ref)
    remainder = [-value for value in sums[:CP]]
    precondition = [1.0 / (value + damping_camera) for value in sums[CP:]]
    scaled = [p * r for p, r in zip(precondition, remainder)]
    for k in range(CP):
        pre_ref[k] = precondition[k]
        rem_ref[k] = remainder[k]
    send_owned(scaled, dot_fields(remainder, scaled), entry, out_ref, table_ref, sizes)


def owner_kernel(sizes, start, final, in_ref, entry_ref, pre_ref, rem_ref, dir_ref, product_ref, *refs):
    refs = list(refs)
    sol_ref = None if start else refs.pop(0)
    out_ref, new_rem_ref, step_ref, new_sol_ref = refs[:4]
    table_ref, spread_ref, place_ref = refs[-3:]
    entry = entry_ref[...]
    fields = read_messages(in_ref, CP, sizes.message, sizes)
    curvature = read_scalar(in_ref, sizes.groups, sizes.message, sizes)
    step = product_ref[...] / jnp.broadcast_to(curvature, (SUB, LANES))
    step_ref[...] = step
    sums = entries_scatter(fields, entry, sizes, spread_ref, place_ref)
    remainder, scaled = [], []
    for k in range(CP):
        direction = dir_ref[k]
        moved = step[:1] * direction
        moved = moved if start else sol_ref[k] + moved
        if not final:
            new_sol_ref[k] = moved
        value = rem_ref[k] - step[:1] * (sums[k] + damping_camera * direction)
        new_rem_ref[k] = value
        remainder.append(value)
        scaled.append(pre_ref[k] * value)
        if final:
            for j, field in enumerate((moved, direction, scaled[k])):
                first = (j * CP + k) * sizes.own_rows
                new_sol_ref[first : first + sizes.own_rows, :] = field
    send_owned(scaled, dot_fields(remainder, scaled), entry, out_ref, table_ref, sizes)


def schur_kernel(sizes, start, last, in_ref, a_ref, b_ref, inv_ref, slot_ref, point_ref,
                 place_point_ref, place_slot_ref, pre_ref, rem_ref, grad_ref, *refs):
    refs = list(refs)
    if not start:
        product_ref, at_slot_ref, dir_ref, step_ref, sum_ref = refs[:5]
        refs = refs[5:]
    out_ref, new_product_ref, new_sum_ref = refs[:3]
    refs = refs[3:]
    new_grad_ref = None if start else refs.pop(0)
    q_ref, parts_ref, spread_ref, table_ref = refs[-4:]
    new_at_slot_ref, new_dir_ref = (refs[0], None) if last else refs[:2]
    rows = sizes.rows

    def at(ref, comp, group):
        return ref[comp * rows + group * SUB : comp * rows + (group + 1) * SUB, :]

    renewed = jnp.broadcast_to(read_scalar(in_ref, sizes.groups, sizes.message, sizes), (SUB, LANES))
    new_product_ref[...] = renewed
    fields = read_messages(in_ref, CP, sizes.message, sizes)
    beta = None if start else (renewed / product_ref[...])[:1]
    squares = None
    for k in range(CP):
        direction = pre_ref[k] * rem_ref[k]
        if start:
            new_at_slot_ref[k] = fields[k]
        else:
            new_at_slot_ref[k] = fields[k] + beta * at_slot_ref[k]
            direction = direction + beta * dir_ref[k]
        if not last:
            new_dir_ref[k] = direction
        squares = direction * direction if squares is None else squares + direction * direction

    for group in range(rows // SUB):
        high, low = slot_place(slot_ref[group * SUB : (group + 1) * SUB, :], sizes)
        gathered = gather_rows(lambda c, k: new_at_slot_ref[c, k : k + 1, :], sizes.pts, high, low, CP)
        q = [sum(at(a_ref, i * CP + k, group) * gathered[k] for k in range(CP)) for i in range(2)]
        for i in range(2):
            q_ref[i * rows + group * SUB : i * rows + (group + 1) * SUB, :] = q[i]
        values = [at(b_ref, k, group) * q[0] + at(b_ref, 3 + k, group) * q[1] for k in range(3)]
        parts = [part for value in values for part in cut(value, FINE)]
        keep_parts(parts, group, parts_ref)
        for s in range(SUB):
            row = group * SUB + s
            spread_row(row, part_rows(len(parts), group, s, parts_ref), point_ref[row : row + 1, :] // LANES, PT_ROWS, spread_ref)
    result = scatter(3 * FINE, sizes.obs, PT_ROWS, LANES, spread_ref, place_point_ref)
    sums = joined(result, 3, PT_ROWS, [FINE] * 3)
    folded = solve([inv_ref[k] for k in range(6)], sums)
    for k in range(3):
        new_sum_ref[k] = sums[k]
        if not start:
            new_grad_ref[k] = grad_ref[k] + step_ref[:1, :1] * sum_ref[k]

    inner = None
    for k in range(3):
        table_ref[k] = folded[k]
    for group in range(rows // SUB):
        at_point = point_gather(table_ref, point_ref[group * SUB : (group + 1) * SUB, :])
        q = [at(q_ref, i, group) for i in range(2)]
        errors = [q[i] - sum(at(b_ref, 3 * i + k, group) * at_point[k] for k in range(3)) for i in range(2)]
        here = q[0] * errors[0] + q[1] * errors[1]
        inner = here if inner is None else inner + here
        if not last:
            values = [at(a_ref, k, group) * errors[0] + at(a_ref, CP + k, group) * errors[1] for k in range(CP)]
            parts = [part for value in values for part in cut(value)]
            keep_parts(parts, group, parts_ref)
            for s in range(SUB):
                row = group * SUB + s
                high, _ = slot_place(slot_ref[row : row + 1, :], sizes)
                spread_row(row, part_rows(len(parts), group, s, parts_ref), high, sizes.pts, spread_ref)
    partial = jnp.sum(inner, keepdims=True) + damping_camera * jnp.sum(squares, keepdims=True)
    if last:
        out_ref[...] = jnp.broadcast_to(partial, (sizes.devices, LANES))
        return
    result = scatter(CP * PIECES, sizes.obs, sizes.pts, LANES, spread_ref, place_slot_ref)
    fields = joined(result, CP, sizes.pts)
    write_messages(fields, partial, sizes.groups, sizes.message, out_ref, sizes)


def tail_kernel(sizes, in_ref, product_ref, own_ref, far_ref, near_ref, out_ref, far_out_ref):
    renewed = jnp.broadcast_to(read_scalar(in_ref, sizes.groups, sizes.message, sizes), (SUB, LANES))
    beta = (renewed / product_ref[...])[:1]
    field = CP * sizes.own_rows
    for j, ref in enumerate((own_ref, far_ref, near_ref)):
        base = ref[:field, :]
        direction = ref[2 * field :, :] + beta * ref[field : 2 * field, :]
        for target, first in [(out_ref, j * 2 * field)] + ([(far_out_ref, 0)] if ref is far_ref else []):
            target[first : first + field, :] = base
            target[first + field : first + 2 * field, :] = direction


def final_kernel(sizes, masks, run_ref, in_ref, product_ref, inv_ref, grad_ref, sum_ref, *refs):
    all_refs = refs[: len(masks)]
    cam_ref, pt_ref, table_ref = refs[len(masks) :]
    curvature = jnp.sum(jnp.where(lane_iota(sizes.devices) == 0, in_ref[...], 0.0), keepdims=True)
    step = (product_ref[...] / jnp.broadcast_to(curvature, (SUB, LANES)))[:1]
    for all_ref, pair in zip(all_refs, masks):
        for j, mask in enumerate(pair):
            base_column = (run_ref[0] ^ mask) * sizes.run
            for h in range(sizes.run_rows):
                columns = pl.ds(pl.multiple_of(base_column + h * LANES, LANES), LANES)
                for start in range(0, CP, SUB):
                    size = min(SUB, CP - start)
                    first = (j * 2 * CP + start) * sizes.own_rows + h
                    base = all_ref[pl.ds(first, size, stride=sizes.own_rows), :]
                    direction = all_ref[pl.ds(first + CP * sizes.own_rows, size, stride=sizes.own_rows), :]
                    cam_ref[start : start + size, columns] = base + step * direction
    total = [grad_ref[k] + step[:, :1] * sum_ref[k] for k in range(3)]
    solved = solve([inv_ref[k] for k in range(6)], total)
    for k in range(3):
        table_ref[k * PT_ROWS : (k + 1) * PT_ROWS, :] = -solved[k]
    for row in range(PT_ROWS):
        pt_ref[:, row * LANES : (row + 1) * LANES] = table_ref[pl.ds(row, 3, stride=PT_ROWS), :]


def shape(*dims, dtype=f32):
    return jax.ShapeDtypeStruct(dims, dtype)


def kept(*dims, dtype=f32):
    return pltpu.VMEM(dims, dtype)


def call(kernel, name, inputs, outputs, scratch, scalars=(), inputs_at=pltpu.VMEM, cost=None):
    vmem = pl.BlockSpec(memory_space=pltpu.VMEM)
    given = pl.BlockSpec(memory_space=inputs_at)
    smem = pl.BlockSpec(memory_space=pltpu.SMEM)
    return pl.pallas_call(
        kernel,
        name=name,
        out_shape=outputs,
        in_specs=[smem] * len(scalars) + [given] * len(inputs),
        out_specs=[vmem] * len(outputs),
        scratch_shapes=scratch,
        cost_estimate=cost,
        compiler_params=pltpu.CompilerParams(vmem_limit_bytes=VMEM_LIMIT),
    )(*scalars, *inputs)


def body(camera_jacobian, point_jacobian, residual, observed_slot, observed_point, send_list):
    sizes = Sizes(lax.axis_size("pts"), lax.axis_size("cams"), send_list.shape[2], camera_jacobian.shape[1])
    axes = ("pts", "cams")
    rows = sizes.rows
    slot = observed_slot.reshape(rows, LANES)
    point = observed_point.reshape(rows, LANES)
    column = lax.axis_index("cams").astype(jnp.int32).reshape(1)
    run = lax.axis_index("pts").astype(jnp.int32).reshape(1)

    def exchange(messages):
        width = messages.size // sizes.devices
        flat = messages.reshape(sizes.devices, 1, width)
        return lax.all_to_all(flat, axes, split_axis=0, concat_axis=0, tiled=True).reshape(messages.shape)

    def flipped(value, flip):
        return lax.ppermute(value, "pts", [(p, p ^ flip) for p in range(sizes.pts)])

    def factors(high_rows, low_rows, entries):
        return [pltpu.VMEM((high_rows, entries), bf16), pltpu.VMEM((low_rows, entries), bf16)]

    point_table = kept(3, PT_ROWS, LANES)
    owned = kept(CP, sizes.own_rows, LANES)
    messages = kept(sizes.devices * sizes.message, LANES)
    scalar = kept(SUB, LANES)
    owned_scratch = pltpu.VMEM((CP, sizes.own_rows, LANES), f32)
    entries = sizes.pts * LANES

    point_scratch = pltpu.VMEM((3, PT_ROWS, LANES), f32)

    def parts_scratch(count):
        return pltpu.VMEM((rows // SUB, count * SUB, LANES), f32)


    given = [
        pltpu.with_memory_space_constraint(value, pltpu.HBM)
        for value in (camera_jacobian, point_jacobian, residual, slot, point, send_list[0])
    ]
    first, a, b, inverse, gradient, place_point, place_slot, slot, point = call(
        functools.partial(setup_kernel, sizes),
        "setup",
        given,
        [
            kept(sizes.devices * sizes.first_message, LANES),
            kept(2 * CP * rows, LANES),
            kept(6 * rows, LANES),
            kept(6, PT_ROWS, LANES),
            point_table,
            kept(LANES, sizes.obs, dtype=bf16),
            kept(LANES, sizes.obs, dtype=bf16),
            kept(rows, LANES, dtype=jnp.int32),
            kept(rows, LANES, dtype=jnp.int32),
        ],
        [pltpu.VMEM((2 * rows, LANES), f32), parts_scratch(2 * CP * PIECES)]
        + [pltpu.VMEM((max(spread_rows(9 * FINE, PT_HI), spread_rows(2 * CP * PIECES, sizes.pts)), sizes.obs), bf16)]
        + [point_scratch, pltpu.VMEM((PT_LO, sizes.obs), bf16), pltpu.VMEM((LANES, sizes.cams * sizes.slot), bf16)]
        + [pltpu.VMEM((spread_rows(2, sizes.pts), sizes.cams * sizes.slot), bf16)]
        + [pltpu.VMEM(value.shape, value.dtype) for value in given]
        + [pltpu.SemaphoreType.DMA((len(given),))],
        scalars=[run, column],
        inputs_at=pl.ANY,
    )
    out, entry, precondition, remainder = call(
        functools.partial(first_owner_kernel, sizes),
        "first_owner",
        [exchange(first)],
        [messages, kept(sizes.pts, LANES, dtype=jnp.int32), owned, owned],
        [owned_scratch] + factors(spread_rows(2 * CP * PIECES, sizes.own_rows), LANES, entries),
    )
    schur_scratch = [pltpu.VMEM((2 * rows, LANES), f32), parts_scratch(CP * PIECES)]
    schur_scratch += [pltpu.VMEM((max(spread_rows(3 * FINE, PT_ROWS), spread_rows(CP * PIECES, sizes.pts)), sizes.obs), bf16)]
    schur_scratch += [point_scratch]
    at_slot = kept(CP, sizes.pts, LANES)
    product = slots = direction = step = sums = solution_ = None
    for iteration in range(ITERS):
        start, last = iteration == 0, iteration == ITERS - 1
        earlier = [] if start else [product, slots, direction, step, sums]
        if last:
            neighbours = [flipped(fields, FAR), flipped(fields, NEAR)]
        arrived = exchange(out)
        if last:
            near_side, far_block = call(
                functools.partial(tail_kernel, sizes),
                "tail",
                [arrived, product, fields] + neighbours,
                [kept(6 * CP * sizes.own_rows, LANES), kept(2 * CP * sizes.own_rows, LANES)],
                [],
            )
            flips = [1 << bit for bit in reversed(range(sizes.pts.bit_length() - 1)) if 1 << bit not in (FAR, NEAR)]
            early = [flipped(far_block, NEAR), flipped(near_side, flips[0])]
        results = call(
            functools.partial(schur_kernel, sizes, start, last),
            "schur_last" if last else "schur",
            [arrived, a, b, inverse, slot, point, place_point, place_slot, precondition, remainder, gradient]
            + earlier,
            [kept(sizes.devices, LANES) if last else messages, scalar, point_table]
            + ([] if start else [point_table])
            + ([] if last else [at_slot, owned]),
            ([pltpu.VMEM((CP, sizes.pts, LANES), f32)] if last else []) + schur_scratch,
            cost=pl.CostEstimate(flops=2_000_000_000, bytes_accessed=10_000_000, transcendentals=0),
        )
        out, product, sums, *results = results
        if not start:
            gradient, *results = results
        if not last:
            slots, direction = results
        if last:
            early[0], out = lax.optimization_barrier((early[0], out))
            gathered, masks = [near_side, early[0]], [(0, FAR, NEAR), (FAR ^ NEAR,)]
            for flip in flips:
                gathered += [
                    early[1] if value is near_side and flip == flips[0] else flipped(value, flip) for value in gathered
                ]
                masks += [tuple(mask ^ flip for mask in group) for group in masks]
            break
        final = iteration == ITERS - 2
        out, remainder, step, solution_ = call(
            functools.partial(owner_kernel, sizes, start, final),
            "owner_final" if final else "owner",
            [exchange(out), entry, precondition, remainder, direction, product] + ([] if start else [solution_]),
            [messages, owned, scalar, kept(3 * CP * sizes.own_rows, LANES) if final else owned],
            [owned_scratch] + factors(spread_rows(CP * PIECES, sizes.own_rows), LANES, entries),
        )
        fields = solution_
    return call(
        functools.partial(final_kernel, sizes, masks),
        "final",
        [exchange(out), product, inverse, gradient, sums] + gathered,
        [shape(CP, CAM_OWN), shape(3, PT_DEV)],
        [pltpu.VMEM((3 * PT_ROWS, LANES), f32)],
        scalars=[run],
    )


def solution(mesh):
    return jax.shard_map(
        lambda *arguments: tuple(body(*arguments)),
        mesh=mesh,
        in_specs=(
            P(None, ("pts", "cams")),
            P(None, ("pts", "cams")),
            P(None, ("pts", "cams")),
            P(("pts", "cams")),
            P(("pts", "cams")),
            P(("pts", "cams"), None, None),
        ),
        out_specs=(P(None, "cams"), P(None, ("pts", "cams"))),
        check_vma=False,
    )
```

```python
import functools

import jax
import jax.numpy as jnp
from jax import lax
from jax.experimental import pallas as pl
from jax.experimental.pallas import tpu as pltpu
from jax.sharding import PartitionSpec as P

CP = 9
CAM_OWN = 8192
PT_DEV = 4096
ITERS = 3
LANES = 128
SUB = 8
PT_ROWS = PT_DEV // LANES
PIECES = 2
FINE = 3
FAR, NEAR = 4, 2
VMEM_LIMIT = 24 * 1024 * 1024

damping_camera = 1.0
damping_point = 1.0

f32 = jnp.float32
bf16 = jnp.bfloat16


class Sizes:
    def __init__(self, pts, cams, slot, obs):
        self.pts, self.cams, self.slot, self.obs = pts, cams, slot, obs
        self.devices = pts * cams
        self.block = slot // pts
        assert cams * self.block == LANES and LANES % pts == 0
        self.rows = obs // LANES
        self.run = CAM_OWN // pts
        self.run_rows = self.run // LANES
        self.own_rows = max(SUB, self.run_rows)
        self.groups = -(-CP // cams)
        self.first_groups = -(-2 * CP // cams)
        self.message = self.groups
        self.first_message = self.first_groups + 1
        assert self.groups * cams > CP


def sub_iota(rows):
    return lax.broadcasted_iota(jnp.int32, (rows, LANES), 0)


def lane_iota(rows):
    return lax.broadcasted_iota(jnp.int32, (rows, LANES), 1)


def cut(value, pieces=PIECES):
    parts = []
    for _ in range(pieces - 1):
        part = value.astype(bf16).astype(f32)
        parts.append(part)
        value = value - part
    parts.append(value)
    return parts


def swap_blocks(rows, block, wanted):
    which = lane_iota(rows[0].shape[0]) // block
    result = []
    for q in range(wanted):
        total = None
        for c, value in enumerate(rows):
            shift = ((c - q) * block) % LANES
            moved = pltpu.roll(value, shift, axis=1) if shift else value
            total = jnp.where(which == c, moved, 0.0 if total is None else total)
        result.append(total)
    return result


def gather_rows(row, count, high, low, comps):
    result = [None] * comps
    for k in range(count):
        here = high == k
        for c in range(comps):
            source = jnp.broadcast_to(row(c, k), high.shape)
            found = jnp.take_along_axis(source, low, axis=1, mode="promise_in_bounds")
            result[c] = found if k == 0 else jnp.where(here, found, result[c])
    return result


def spread_row(index, parts, high, high_count, spread_ref):
    columns = slice(index * LANES, (index + 1) * LANES)
    mask = jnp.broadcast_to(high, (high_count, LANES)) == sub_iota(high_count)
    together = max(1, 16 // high_count)
    for start in range(0, len(parts), together):
        pieces = [
            jnp.where(mask, jnp.broadcast_to(part, (high_count, LANES)), 0.0)
            for part in parts[start : start + together]
        ]
        while len(pieces) < together:
            pieces.append(jnp.zeros((high_count, LANES), f32))
        tile = pieces[0] if together == 1 else jnp.concatenate(pieces, axis=0)
        spread_ref[start * high_count : start * high_count + tile.shape[0], columns] = tile.astype(bf16)


def place_row(index, low, low_count, place_ref):
    columns = slice(index * LANES, (index + 1) * LANES)
    place = jnp.broadcast_to(low, (low_count, LANES)) == sub_iota(low_count)
    place_ref[:low_count, columns] = jnp.where(place, 1.0, 0.0).astype(bf16)


def keep_parts(parts, group, parts_ref):
    for k, part in enumerate(parts):
        parts_ref[group, k * SUB : (k + 1) * SUB, :] = part


def part_rows(count, group, s, parts_ref):
    return [parts_ref[group, k * SUB + s : k * SUB + s + 1, :] for k in range(count)]


def spread_rows(parts, high_count):
    return -(-parts * high_count // 16) * 16


def scatter(parts, entries, high_count, low_count, spread_ref, place_ref):
    rows = spread_rows(parts, high_count)
    return lax.dot_general(
        spread_ref[:rows, :entries],
        place_ref[:low_count, :entries],
        (((1,), (1,)), ((), ())),
        preferred_element_type=f32,
    )


def joined(result, count, high_count, pieces=None):
    pieces = pieces or [PIECES] * count
    values, first = [], 0
    for number in pieces:
        rows = [result[first + k * high_count : first + (k + 1) * high_count] for k in range(number)]
        first += number * high_count
        total = rows[-1]
        for row in reversed(rows[:-1]):
            total = total + row
        values.append(total)
    return values


def point_gather(ref, point):
    return gather_rows(lambda c, k: ref[c, k : k + 1, :], PT_ROWS, point // LANES, point % LANES, 3)


def slot_place(slot, sizes):
    within = slot % sizes.slot
    return within % sizes.pts, (slot // sizes.slot) * sizes.block + within // sizes.pts


def solve(inverse, values):
    first = inverse[0] * values[0] + inverse[1] * values[1] + inverse[2] * values[2]
    second = inverse[1] * values[0] + inverse[3] * values[1] + inverse[4] * values[2]
    third = inverse[2] * values[0] + inverse[4] * values[1] + inverse[5] * values[2]
    return first, second, third


def write_messages(fields, scalar, groups, message, out_ref, sizes, extra=None, column=None):
    which = lane_iota(sizes.pts) // sizes.block
    for g in range(groups):
        rows = fields[g * sizes.cams : (g + 1) * sizes.cams]
        moved = swap_partial(rows, sizes)
        for c in range(sizes.cams):
            value = moved[c]
            if g == groups - 1 and scalar is not None:
                value = jnp.where(which == sizes.cams - 1, scalar, value)
            out_ref[pl.ds(c * message + g, sizes.pts, stride=sizes.cams * message), :] = value
    for g in range(groups, message):
        for c in range(sizes.cams):
            value = jnp.where(column == c, extra, 0.0)
            out_ref[pl.ds(c * message + g, sizes.pts, stride=sizes.cams * message), :] = value


def swap_partial(rows, sizes):
    return swap_blocks(rows, sizes.block, sizes.cams)


def read_row(in_ref, c, g, message, sizes):
    return in_ref[pl.ds(c * message + g, sizes.pts, stride=sizes.cams * message), :]


def read_messages(in_ref, count, message, sizes):
    fields = []
    group = 0
    while len(fields) < count:
        rows = [read_row(in_ref, c, group, message, sizes) for c in range(sizes.cams)]
        fields += swap_blocks(rows, sizes.block, min(sizes.cams, count - len(fields)))
        group += 1
    return fields


def read_scalar(in_ref, groups, message, sizes):
    total = read_row(in_ref, 0, groups - 1, message, sizes)
    for c in range(1, sizes.cams):
        total = total + read_row(in_ref, c, groups - 1, message, sizes)
    chosen = jnp.where(lane_iota(sizes.pts) == LANES - 1, total, 0.0)
    return jnp.sum(chosen, keepdims=True)


def setup_kernel(sizes, run_ref, column_ref, *refs):
    del run_ref
    sources, refs = refs[:6], refs[6:]
    out_ref, a_ref, b_ref, inv_ref, grad_ref, place_point_ref, place_slot_ref, new_slot_ref, new_point_ref = refs[:9]
    refs = refs[9:]
    r_ref, parts_ref, spread_ref, table_ref, place_list_ref, spread_list_ref = refs[:6]
    jac_ref, pjac_ref, res_ref, slot_ref, point_ref, list_ref = refs[6:12]
    semaphores = refs[12]
    rows = sizes.rows
    copies = [
        pltpu.make_async_copy(source, target, semaphores.at[k])
        for k, (source, target) in enumerate(zip(sources, refs[6:12]))
    ]
    for copy in copies:
        copy.start()
    for k in (1, 2, 4):
        copies[k].wait()
    new_point_ref[...] = point_ref[...]
    for j in range(rows):
        columns = slice(j * LANES, (j + 1) * LANES)
        b_ref[pl.ds(j, 6, stride=rows), :] = pjac_ref[:, columns]
        r_ref[pl.ds(j, 2, stride=rows), :] = res_ref[:, columns]

    def at(ref, comp, group):
        return ref[comp * rows + group * SUB : comp * rows + (group + 1) * SUB, :]

    normal_pieces = [FINE] * 9

    for group in range(rows // SUB):
        b = [at(b_ref, k, group) for k in range(6)]
        r = [at(r_ref, k, group) for k in range(2)]
        values = [b[i] * b[j] + b[3 + i] * b[3 + j] for i, j in ((0, 0), (0, 1), (0, 2), (1, 1), (1, 2), (2, 2))]
        values += [b[i] * r[0] + b[3 + i] * r[1] for i in range(3)]
        parts = [part for value, pieces in zip(values, normal_pieces) for part in cut(value, pieces)]
        keep_parts(parts, group, parts_ref)
        for s in range(SUB):
            row = group * SUB + s
            point = point_ref[row : row + 1, :]
            spread_row(row, part_rows(len(parts), group, s, parts_ref), point // LANES, PT_ROWS, spread_ref)
            place_row(row, point % LANES, LANES, place_point_ref)
    result = scatter(sum(normal_pieces), sizes.obs, PT_ROWS, LANES, spread_ref, place_point_ref)
    normal = joined(result, 9, PT_ROWS, normal_pieces)
    top_left = normal[0] + damping_point
    top_mid = normal[1]
    top_right = normal[2]
    mid_mid = normal[3] + damping_point
    mid_right = normal[4]
    low_right = normal[5] + damping_point
    adjugate = [
        mid_mid * low_right - mid_right * mid_right,
        top_right * mid_right - top_mid * low_right,
        top_mid * mid_right - top_right * mid_mid,
        top_left * low_right - top_right * top_right,
        top_mid * top_right - top_left * mid_right,
        top_left * mid_mid - top_mid * top_mid,
    ]
    determinant = top_left * adjugate[0] + top_mid * adjugate[1] + top_right * adjugate[2]
    inverse = [value / determinant for value in adjugate]
    for k in range(6):
        inv_ref[k] = inverse[k]
    for k in range(3):
        grad_ref[k] = normal[6 + k]
    eliminated = solve(inverse, normal[6:])
    for k in range(3):
        table_ref[k] = eliminated[k]
    for k in (0, 3, 5):
        copies[k].wait()
    new_slot_ref[...] = slot_ref[...]
    for j in range(rows):
        for start in range(0, 2 * CP, SUB):
            size = min(SUB, 2 * CP - start)
            a_ref[pl.ds(start * rows + j, size, stride=rows), :] = jac_ref[
                start : start + size, j * LANES : (j + 1) * LANES
            ]

    for group in range(rows // SUB):
        at_point = point_gather(table_ref, point_ref[group * SUB : (group + 1) * SUB, :])
        b = [at(b_ref, k, group) for k in range(6)]
        errors = [at(r_ref, i, group) - sum(b[3 * i + k] * at_point[k] for k in range(3)) for i in range(2)]
        a = [at(a_ref, k, group) for k in range(2 * CP)]
        values = [a[k] * errors[0] + a[CP + k] * errors[1] for k in range(CP)]
        values += [a[k] * a[k] + a[CP + k] * a[CP + k] for k in range(CP)]
        parts = [part for value in values for part in cut(value)]
        keep_parts(parts, group, parts_ref)
        for s in range(SUB):
            row = group * SUB + s
            high, low = slot_place(slot_ref[row : row + 1, :], sizes)
            spread_row(row, part_rows(len(parts), group, s, parts_ref), high, sizes.pts, spread_ref)
            place_row(row, low, LANES, place_slot_ref)
    result = scatter(2 * CP * PIECES, sizes.obs, sizes.pts, LANES, spread_ref, place_slot_ref)
    fields = joined(result, 2 * CP, sizes.pts)

    pieces = sizes.slot // LANES
    lane = lane_iota(1)
    for c in range(sizes.cams):
        for half in range(pieces):
            value = list_ref[c : c + 1, half * LANES : (half + 1) * LANES]
            low = c * sizes.block + half * (LANES // sizes.pts) + lane // sizes.pts
            parts = [(value >> 8).astype(f32), (value & 255).astype(f32)]
            spread_row(c * pieces + half, parts, lane % sizes.pts, sizes.pts, spread_list_ref)
            place_row(c * pieces + half, low, LANES, place_list_ref)
    result = scatter(2, sizes.cams * sizes.slot, sizes.pts, LANES, spread_list_ref, place_list_ref)
    listed = result[: sizes.pts] * 256.0 + result[sizes.pts : 2 * sizes.pts]
    write_messages(fields, None, sizes.first_groups, sizes.first_message, out_ref, sizes, extra=listed, column=column_ref[0])


def entries_scatter(fields, entry, sizes, spread_ref, place_ref):
    high, low = entry // LANES, entry % LANES
    parts = [part for value in fields for part in cut(value)]
    for p in range(sizes.pts):
        spread_row(p, [part[p : p + 1] for part in parts], high[p : p + 1], sizes.own_rows, spread_ref)
        place_row(p, low[p : p + 1], LANES, place_ref)
    result = scatter(len(parts), sizes.pts * LANES, sizes.own_rows, LANES, spread_ref, place_ref)
    return joined(result, len(fields), sizes.own_rows)


def send_owned(scaled, partial, entry, out_ref, table_ref, sizes):
    for k in range(CP):
        table_ref[k] = scaled[k]
    fields = gather_rows(lambda c, k: table_ref[c, k : k + 1, :], sizes.run_rows, entry // LANES, entry % LANES, CP)
    write_messages(fields, partial, sizes.groups, sizes.message, out_ref, sizes)


def dot_fields(left, right):
    return jnp.sum(sum(a * b for a, b in zip(left, right)), keepdims=True)


def first_owner_kernel(sizes, in_ref, out_ref, entry_ref, pre_ref, rem_ref,
                       table_ref, spread_ref, place_ref):
    listed = jnp.zeros((sizes.pts, LANES), f32)
    for c in range(sizes.cams):
        listed = listed + read_row(in_ref, c, sizes.first_groups, sizes.first_message, sizes)
    entry = listed.astype(jnp.int32) % sizes.run
    entry_ref[...] = entry
    fields = read_messages(in_ref, 2 * CP, sizes.first_message, sizes)
    sums = entries_scatter(fields, entry, sizes, spread_ref, place_ref)
    remainder = [-value for value in sums[:CP]]
    precondition = [1.0 / (value + damping_camera) for value in sums[CP:]]
    scaled = [p * r for p, r in zip(precondition, remainder)]
    for k in range(CP):
        pre_ref[k] = precondition[k]
        rem_ref[k] = remainder[k]
    send_owned(scaled, dot_fields(remainder, scaled), entry, out_ref, table_ref, sizes)


def owner_kernel(sizes, start, final, in_ref, entry_ref, pre_ref, rem_ref, dir_ref, product_ref, *refs):
    refs = list(refs)
    sol_ref = None if start else refs.pop(0)
    out_ref, new_rem_ref, step_ref, new_sol_ref = refs[:4]
    table_ref, spread_ref, place_ref = refs[-3:]
    entry = entry_ref[...]
    fields = read_messages(in_ref, CP, sizes.message, sizes)
    curvature = read_scalar(in_ref, sizes.groups, sizes.message, sizes)
    step = product_ref[...] / jnp.broadcast_to(curvature, (SUB, LANES))
    step_ref[...] = step
    sums = entries_scatter(fields, entry, sizes, spread_ref, place_ref)
    remainder, scaled = [], []
    for k in range(CP):
        direction = dir_ref[k]
        moved = step[:1] * direction
        moved = moved if start else sol_ref[k] + moved
        if not final:
            new_sol_ref[k] = moved
        value = rem_ref[k] - step[:1] * (sums[k] + damping_camera * direction)
        new_rem_ref[k] = value
        remainder.append(value)
        scaled.append(pre_ref[k] * value)
        if final:
            for j, field in enumerate((moved, direction, scaled[k])):
                first = (j * CP + k) * sizes.own_rows
                new_sol_ref[first : first + sizes.own_rows, :] = field
    send_owned(scaled, dot_fields(remainder, scaled), entry, out_ref, table_ref, sizes)


def schur_kernel(sizes, start, last, in_ref, a_ref, b_ref, inv_ref, slot_ref, point_ref,
                 place_point_ref, place_slot_ref, pre_ref, rem_ref, grad_ref, *refs):
    refs = list(refs)
    if not start:
        product_ref, at_slot_ref, dir_ref, step_ref, sum_ref = refs[:5]
        refs = refs[5:]
    out_ref, new_product_ref, new_sum_ref = refs[:3]
    refs = refs[3:]
    new_grad_ref = None if start else refs.pop(0)
    q_ref, parts_ref, spread_ref, table_ref = refs[-4:]
    new_at_slot_ref, new_dir_ref = (refs[0], None) if last else refs[:2]
    rows = sizes.rows

    def at(ref, comp, group):
        return ref[comp * rows + group * SUB : comp * rows + (group + 1) * SUB, :]

    renewed = jnp.broadcast_to(read_scalar(in_ref, sizes.groups, sizes.message, sizes), (SUB, LANES))
    new_product_ref[...] = renewed
    fields = read_messages(in_ref, CP, sizes.message, sizes)
    beta = None if start else (renewed / product_ref[...])[:1]
    squares = None
    for k in range(CP):
        direction = pre_ref[k] * rem_ref[k]
        if start:
            new_at_slot_ref[k] = fields[k]
        else:
            new_at_slot_ref[k] = fields[k] + beta * at_slot_ref[k]
            direction = direction + beta * dir_ref[k]
        if not last:
            new_dir_ref[k] = direction
        squares = direction * direction if squares is None else squares + direction * direction

    for group in range(rows // SUB):
        high, low = slot_place(slot_ref[group * SUB : (group + 1) * SUB, :], sizes)
        gathered = gather_rows(lambda c, k: new_at_slot_ref[c, k : k + 1, :], sizes.pts, high, low, CP)
        q = [sum(at(a_ref, i * CP + k, group) * gathered[k] for k in range(CP)) for i in range(2)]
        for i in range(2):
            q_ref[i * rows + group * SUB : i * rows + (group + 1) * SUB, :] = q[i]
        values = [at(b_ref, k, group) * q[0] + at(b_ref, 3 + k, group) * q[1] for k in range(3)]
        parts = [part for value in values for part in cut(value, FINE)]
        keep_parts(parts, group, parts_ref)
        for s in range(SUB):
            row = group * SUB + s
            spread_row(row, part_rows(len(parts), group, s, parts_ref), point_ref[row : row + 1, :] // LANES, PT_ROWS, spread_ref)
    result = scatter(3 * FINE, sizes.obs, PT_ROWS, LANES, spread_ref, place_point_ref)
    sums = joined(result, 3, PT_ROWS, [FINE] * 3)
    folded = solve([inv_ref[k] for k in range(6)], sums)
    for k in range(3):
        new_sum_ref[k] = sums[k]
        if not start:
            new_grad_ref[k] = grad_ref[k] + step_ref[:1, :1] * sum_ref[k]

    inner = None
    for k in range(3):
        table_ref[k] = folded[k]
    for group in range(rows // SUB):
        at_point = point_gather(table_ref, point_ref[group * SUB : (group + 1) * SUB, :])
        q = [at(q_ref, i, group) for i in range(2)]
        errors = [q[i] - sum(at(b_ref, 3 * i + k, group) * at_point[k] for k in range(3)) for i in range(2)]
        here = q[0] * errors[0] + q[1] * errors[1]
        inner = here if inner is None else inner + here
        if not last:
            values = [at(a_ref, k, group) * errors[0] + at(a_ref, CP + k, group) * errors[1] for k in range(CP)]
            parts = [part for value in values for part in cut(value)]
            keep_parts(parts, group, parts_ref)
            for s in range(SUB):
                row = group * SUB + s
                high, _ = slot_place(slot_ref[row : row + 1, :], sizes)
                spread_row(row, part_rows(len(parts), group, s, parts_ref), high, sizes.pts, spread_ref)
    partial = jnp.sum(inner, keepdims=True) + damping_camera * jnp.sum(squares, keepdims=True)
    if last:
        out_ref[...] = jnp.broadcast_to(partial, (sizes.devices, LANES))
        return
    result = scatter(CP * PIECES, sizes.obs, sizes.pts, LANES, spread_ref, place_slot_ref)
    fields = joined(result, CP, sizes.pts)
    write_messages(fields, partial, sizes.groups, sizes.message, out_ref, sizes)


def tail_kernel(sizes, in_ref, product_ref, own_ref, far_ref, near_ref, out_ref, far_out_ref):
    renewed = jnp.broadcast_to(read_scalar(in_ref, sizes.groups, sizes.message, sizes), (SUB, LANES))
    beta = (renewed / product_ref[...])[:1]
    field = CP * sizes.own_rows
    for j, ref in enumerate((own_ref, far_ref, near_ref)):
        base = ref[:field, :]
        direction = ref[2 * field :, :] + beta * ref[field : 2 * field, :]
        for target, first in [(out_ref, j * 2 * field)] + ([(far_out_ref, 0)] if ref is far_ref else []):
            target[first : first + field, :] = base
            target[first + field : first + 2 * field, :] = direction


def final_kernel(sizes, masks, run_ref, in_ref, product_ref, inv_ref, grad_ref, sum_ref, *refs):
    all_refs = refs[: len(masks)]
    cam_ref, pt_ref, table_ref = refs[len(masks) :]
    curvature = jnp.sum(jnp.where(lane_iota(sizes.devices) == 0, in_ref[...], 0.0), keepdims=True)
    step = (product_ref[...] / jnp.broadcast_to(curvature, (SUB, LANES)))[:1]
    for all_ref, pair in zip(all_refs, masks):
        for j, mask in enumerate(pair):
            base_column = (run_ref[0] ^ mask) * sizes.run
            for h in range(sizes.run_rows):
                columns = pl.ds(pl.multiple_of(base_column + h * LANES, LANES), LANES)
                for start in range(0, CP, SUB):
                    size = min(SUB, CP - start)
                    first = (j * 2 * CP + start) * sizes.own_rows + h
                    base = all_ref[pl.ds(first, size, stride=sizes.own_rows), :]
                    direction = all_ref[pl.ds(first + CP * sizes.own_rows, size, stride=sizes.own_rows), :]
                    cam_ref[start : start + size, columns] = base + step * direction
    total = [grad_ref[k] + step[:, :1] * sum_ref[k] for k in range(3)]
    solved = solve([inv_ref[k] for k in range(6)], total)
    for k in range(3):
        table_ref[k * PT_ROWS : (k + 1) * PT_ROWS, :] = -solved[k]
    for row in range(PT_ROWS):
        pt_ref[:, row * LANES : (row + 1) * LANES] = table_ref[pl.ds(row, 3, stride=PT_ROWS), :]


def shape(*dims, dtype=f32):
    return jax.ShapeDtypeStruct(dims, dtype)


def kept(*dims, dtype=f32):
    return pltpu.VMEM(dims, dtype)


def call(kernel, name, inputs, outputs, scratch, scalars=(), inputs_at=pltpu.VMEM, cost=None):
    vmem = pl.BlockSpec(memory_space=pltpu.VMEM)
    given = pl.BlockSpec(memory_space=inputs_at)
    smem = pl.BlockSpec(memory_space=pltpu.SMEM)
    return pl.pallas_call(
        kernel,
        name=name,
        out_shape=outputs,
        in_specs=[smem] * len(scalars) + [given] * len(inputs),
        out_specs=[vmem] * len(outputs),
        scratch_shapes=scratch,
        cost_estimate=cost,
        compiler_params=pltpu.CompilerParams(vmem_limit_bytes=VMEM_LIMIT),
    )(*scalars, *inputs)


def body(camera_jacobian, point_jacobian, residual, observed_slot, observed_point, send_list):
    sizes = Sizes(lax.axis_size("pts"), lax.axis_size("cams"), send_list.shape[2], camera_jacobian.shape[1])
    axes = ("pts", "cams")
    rows = sizes.rows
    slot = observed_slot.reshape(rows, LANES)
    point = observed_point.reshape(rows, LANES)
    column = lax.axis_index("cams").astype(jnp.int32).reshape(1)
    run = lax.axis_index("pts").astype(jnp.int32).reshape(1)

    def exchange(messages):
        width = messages.size // sizes.devices
        flat = messages.reshape(sizes.devices, 1, width)
        return lax.all_to_all(flat, axes, split_axis=0, concat_axis=0, tiled=True).reshape(messages.shape)

    def flipped(value, flip):
        return lax.ppermute(value, "pts", [(p, p ^ flip) for p in range(sizes.pts)])

    def factors(high_rows, low_rows, entries):
        return [pltpu.VMEM((high_rows, entries), bf16), pltpu.VMEM((low_rows, entries), bf16)]

    point_table = kept(3, PT_ROWS, LANES)
    owned = kept(CP, sizes.own_rows, LANES)
    messages = kept(sizes.devices * sizes.message, LANES)
    scalar = kept(SUB, LANES)
    owned_scratch = pltpu.VMEM((CP, sizes.own_rows, LANES), f32)
    entries = sizes.pts * LANES

    point_scratch = pltpu.VMEM((3, PT_ROWS, LANES), f32)

    def parts_scratch(count):
        return pltpu.VMEM((rows // SUB, count * SUB, LANES), f32)


    given = [
        pltpu.with_memory_space_constraint(value, pltpu.HBM)
        for value in (camera_jacobian, point_jacobian, residual, slot, point, send_list[0])
    ]
    first, a, b, inverse, gradient, place_point, place_slot, slot, point = call(
        functools.partial(setup_kernel, sizes),
        "setup",
        given,
        [
            kept(sizes.devices * sizes.first_message, LANES),
            kept(2 * CP * rows, LANES),
            kept(6 * rows, LANES),
            kept(6, PT_ROWS, LANES),
            point_table,
            kept(LANES, sizes.obs, dtype=bf16),
            kept(LANES, sizes.obs, dtype=bf16),
            kept(rows, LANES, dtype=jnp.int32),
            kept(rows, LANES, dtype=jnp.int32),
        ],
        [pltpu.VMEM((2 * rows, LANES), f32), parts_scratch(2 * CP * PIECES)]
        + [pltpu.VMEM((max(spread_rows(9 * FINE, PT_ROWS), spread_rows(2 * CP * PIECES, sizes.pts)), sizes.obs), bf16)]
        + [point_scratch, pltpu.VMEM((LANES, sizes.cams * sizes.slot), bf16)]
        + [pltpu.VMEM((spread_rows(2, sizes.pts), sizes.cams * sizes.slot), bf16)]
        + [pltpu.VMEM(value.shape, value.dtype) for value in given]
        + [pltpu.SemaphoreType.DMA((len(given),))],
        scalars=[run, column],
        inputs_at=pl.ANY,
    )
    out, entry, precondition, remainder = call(
        functools.partial(first_owner_kernel, sizes),
        "first_owner",
        [exchange(first)],
        [messages, kept(sizes.pts, LANES, dtype=jnp.int32), owned, owned],
        [owned_scratch] + factors(spread_rows(2 * CP * PIECES, sizes.own_rows), LANES, entries),
    )
    schur_scratch = [pltpu.VMEM((2 * rows, LANES), f32), parts_scratch(CP * PIECES)]
    schur_scratch += [pltpu.VMEM((max(spread_rows(3 * FINE, PT_ROWS), spread_rows(CP * PIECES, sizes.pts)), sizes.obs), bf16)]
    schur_scratch += [point_scratch]
    at_slot = kept(CP, sizes.pts, LANES)
    product = slots = direction = step = sums = solution_ = None
    for iteration in range(ITERS):
        start, last = iteration == 0, iteration == ITERS - 1
        earlier = [] if start else [product, slots, direction, step, sums]
        if last:
            neighbours = [flipped(fields, FAR), flipped(fields, NEAR)]
        arrived = exchange(out)
        if last:
            near_side, far_block = call(
                functools.partial(tail_kernel, sizes),
                "tail",
                [arrived, product, fields] + neighbours,
                [kept(6 * CP * sizes.own_rows, LANES), kept(2 * CP * sizes.own_rows, LANES)],
                [],
            )
            flips = [1 << bit for bit in reversed(range(sizes.pts.bit_length() - 1)) if 1 << bit not in (FAR, NEAR)]
            early = [flipped(far_block, NEAR), flipped(near_side, flips[0])]
        results = call(
            functools.partial(schur_kernel, sizes, start, last),
            "schur_last" if last else "schur",
            [arrived, a, b, inverse, slot, point, place_point, place_slot, precondition, remainder, gradient]
            + earlier,
            [kept(sizes.devices, LANES) if last else messages, scalar, point_table]
            + ([] if start else [point_table])
            + ([] if last else [at_slot, owned]),
            ([pltpu.VMEM((CP, sizes.pts, LANES), f32)] if last else []) + schur_scratch,
            cost=pl.CostEstimate(flops=2_000_000_000, bytes_accessed=10_000_000, transcendentals=0),
        )
        out, product, sums, *results = results
        if not start:
            gradient, *results = results
        if not last:
            slots, direction = results
        if last:
            early[0], out = lax.optimization_barrier((early[0], out))
            gathered, masks = [near_side, early[0]], [(0, FAR, NEAR), (FAR ^ NEAR,)]
            for flip in flips:
                gathered += [
                    early[1] if value is near_side and flip == flips[0] else flipped(value, flip) for value in gathered
                ]
                masks += [tuple(mask ^ flip for mask in group) for group in masks]
            break
        final = iteration == ITERS - 2
        out, remainder, step, solution_ = call(
            functools.partial(owner_kernel, sizes, start, final),
            "owner_final" if final else "owner",
            [exchange(out), entry, precondition, remainder, direction, product] + ([] if start else [solution_]),
            [messages, owned, scalar, kept(3 * CP * sizes.own_rows, LANES) if final else owned],
            [owned_scratch] + factors(spread_rows(CP * PIECES, sizes.own_rows), LANES, entries),
        )
        fields = solution_
    return call(
        functools.partial(final_kernel, sizes, masks),
        "final",
        [exchange(out), product, inverse, gradient, sums] + gathered,
        [shape(CP, CAM_OWN), shape(3, PT_DEV)],
        [pltpu.VMEM((3 * PT_ROWS, LANES), f32)],
        scalars=[run],
    )


def solution(mesh):
    return jax.shard_map(
        lambda *arguments: tuple(body(*arguments)),
        mesh=mesh,
        in_specs=(
            P(None, ("pts", "cams")),
            P(None, ("pts", "cams")),
            P(None, ("pts", "cams")),
            P(("pts", "cams")),
            P(("pts", "cams")),
            P(("pts", "cams"), None, None),
        ),
        out_specs=(P(None, "cams"), P(None, ("pts", "cams"))),
        check_vma=False,
    )
```
